32 devices in a mesh: group: 4 (over y, core), member: 8 (over z, x).
Axes of the slice: x: 2, y: 2, z: 4, core: 2. Of those that a mesh axis runs over, the one named last changes fastest.
Arguments:
- heads: bfloat16 [65536, 768], P(('group', 'member')), may hold values from -16 to 16
- new_heads: bfloat16 [64, 768], P('group'), may hold values from -16 to 16
- vectors: bfloat16 [32, 128, 768], P(('group', 'member')), may hold values from -16 to 16
- near_ids: int32 [32, 64], P(('group', 'member')), may hold values from 0 to 16383, as said below
Outputs:
- density: float32 [64], P('group')
- spread: float32 [64], P('group')
- reassign: float32 [32, 64, 128], P(('group', 'member'))
The draws below stay inside these ranges and needn't reach their ends.
Inputs may be any that keep to these rules, and one draw needn't show every extreme that they name: `near_ids`: each row holds 64 different numbers; of one row at most 16 lie in one range j * 2048 to (j + 1) * 2048 - 1, and exactly 16 in some such range.
All inputs are finite; a program needn't handle non-finite values.
Results may differ from the reference program's by a relative error of at most 0.0003.
Values may be sent and summed in bfloat16 or wider, within the bound.
No kernel may reach another device: no remote copies, remote signals or barrier semaphores. Data moves between devices by JAX's collectives and lax.ppermute only.
A program may use at most 64 MiB of HBM per device.

```python
import jax
import jax.numpy as jnp
from jax import lax

D = 768
HEAD_DEV = 2048
BLOCK = 128
NEAR = 64
GROUP_HEADS = 16384
HEADS_ALL = 65536
POSTS_GRP = 8
NEW = 64
SPLITS = 32
NEAR_MOST = 16


centre_total = 32


def head_labels(key):
    key = jax.random.fold_in(key, 101)
    first, second, third = jax.random.split(key, 3)
    anywhere = jax.random.randint(first, (HEADS_ALL,), 0, centre_total)
    group_of = jnp.arange(HEADS_ALL, dtype=jnp.int32) // GROUP_HEADS
    nearby = (group_of * 5 + jax.random.randint(second, (HEADS_ALL,), 0, centre_total // 4)) % centre_total
    coin = jax.random.randint(third, (HEADS_ALL,), 0, 2)
    return jnp.where(coin == 1, anywhere, nearby).astype(jnp.int32)


def head_centres(key):
    key = jax.random.fold_in(key, 103)
    first, second = jax.random.split(key, 2)
    scales = jnp.exp(jax.random.uniform(second, (centre_total, 1), jnp.float32, jnp.log(1.0), jnp.log(2.4)))
    return jax.random.truncated_normal(first, -4.0, 4.0, (centre_total, D), jnp.float32) * scales


def listed_ids(key):
    key = jax.random.fold_in(key, 107)
    keys = jax.random.split(key, 5)
    members = GROUP_HEADS // HEAD_DEV
    units = (members - 1) * NEAR_MOST
    home = jax.random.randint(keys[0], (SPLITS, 1), 0, members)
    scores = jax.random.randint(keys[1], (SPLITS, units), 0, 2 ** 20) * units + jnp.arange(units, dtype=jnp.int32)[None, :]
    order = jnp.argsort(scores, axis=1)[:, :NEAR - NEAR_MOST].astype(jnp.int32)
    other_member = (home + 1 + order // NEAR_MOST) % members
    other_rank = order % NEAR_MOST
    home_member = jnp.broadcast_to(home, (SPLITS, NEAR_MOST))
    home_rank = jnp.broadcast_to(jnp.arange(NEAR_MOST, dtype=jnp.int32)[None, :], (SPLITS, NEAR_MOST))
    member = jnp.concatenate([home_member, other_member], axis=1).astype(jnp.int32)
    rank = jnp.concatenate([home_rank, other_rank], axis=1).astype(jnp.int32)
    stride = HEAD_DEV // NEAR_MOST
    offset = jax.random.randint(keys[2], (SPLITS, members), 0, HEAD_DEV)
    jitter = jax.random.randint(keys[3], (SPLITS, NEAR), 0, stride)
    base = jnp.take_along_axis(offset, member, axis=1)
    local = (base + rank * stride + jitter) % HEAD_DEV
    ids = member * HEAD_DEV + local
    shuffle_scores = jax.random.randint(keys[4], (SPLITS, NEAR), 0, 2 ** 20) * NEAR + jnp.arange(NEAR, dtype=jnp.int32)[None, :]
    shuffle = jnp.argsort(shuffle_scores, axis=1).astype(jnp.int32)
    return jnp.take_along_axis(ids, shuffle, axis=1).astype(jnp.int32)


def chosen_heads(ids, posting, slot):
    group_of = posting // POSTS_GRP
    return (ids[posting, slot] + group_of * GROUP_HEADS).astype(jnp.int32)


def draw_heads(key, part):
    labels = head_labels(key)
    centres = head_centres(key)
    key = jax.random.fold_in(key, 7)
    noise = 0.35 * jax.random.truncated_normal(key, -4.0, 4.0, (HEADS_ALL, D), jnp.float32)
    return (centres[labels] + noise).astype(jnp.bfloat16)


def draw_new_heads(key, part):
    labels = head_labels(key)
    ids = listed_ids(key)
    centres = head_centres(key)
    key = jax.random.fold_in(key, 11)
    count = jnp.arange(NEW, dtype=jnp.int32)
    chosen = chosen_heads(ids, count // 2, count % 2)
    noise = 0.25 * jax.random.truncated_normal(key, -4.0, 4.0, (NEW, D), jnp.float32)
    return (centres[labels[chosen]] + noise).astype(jnp.bfloat16)


def draw_vectors(key, part):
    labels = head_labels(key)
    ids = listed_ids(key)
    centres = head_centres(key)
    key = jax.random.fold_in(key, 13)
    posting = jnp.broadcast_to(jnp.arange(SPLITS, dtype=jnp.int32)[:, None], (SPLITS, BLOCK))
    slot = jnp.broadcast_to((jnp.arange(BLOCK, dtype=jnp.int32) % 2)[None, :], (SPLITS, BLOCK))
    chosen = chosen_heads(ids, posting, slot)
    noise = 0.5 * jax.random.truncated_normal(key, -4.0, 4.0, (SPLITS, BLOCK, D), jnp.float32)
    return (centres[labels[chosen]] + noise).astype(jnp.bfloat16)


def draw_near_ids(key, part):
    ids = listed_ids(key)
    return ids


def setup_inputs(seed: int = 0) -> dict:
    splits = jax.random.split(jax.random.key(seed), 5)
    return {
        "heads": draw_heads(jax.random.fold_in(splits[4], 71), 0),
        "new_heads": draw_new_heads(jax.random.fold_in(splits[4], 71), 0),
        "vectors": draw_vectors(jax.random.fold_in(splits[4], 71), 0),
        "near_ids": draw_near_ids(jax.random.fold_in(splits[4], 71), 0),
    }


def reference(heads, new_heads, vectors, near_ids):
    query_sq = jnp.sum(jnp.square(new_heads.astype(jnp.float32)), axis=1)
    stacked = heads.reshape(HEADS_ALL // HEAD_DEV, HEAD_DEV, D)

    def fold(carry, block):
        block_sq = jnp.sum(jnp.square(block.astype(jnp.float32)), axis=1)
        dots = jnp.dot(new_heads, block.T, preferred_element_type=jnp.float32)
        excess = (query_sq[:, None] + block_sq[None, :] - 2.0 * dots) / D
        weight = 1.0 / jnp.square(1.0 + excess)
        return (carry[0] + jnp.sum(weight, axis=1), carry[1] + jnp.sum(weight * excess, axis=1)), None

    start = jnp.zeros((NEW,), jnp.float32)
    (total_w, total_we), unused = lax.scan(fold, (start, start), stacked)
    density = jnp.log(total_w / HEADS_ALL)
    spread = total_we / total_w

    owner_group = (jnp.arange(SPLITS) // POSTS_GRP).astype(jnp.int32)
    global_ids = (near_ids + owner_group[:, None] * GROUP_HEADS).astype(jnp.int32)
    listed = heads[global_ids].astype(jnp.float32)
    vec32 = vectors.astype(jnp.float32)
    vec_sq = jnp.sum(jnp.square(vec32), axis=2)
    head_sq = jnp.sum(jnp.square(listed), axis=2)
    dots = jnp.einsum("pbd,pkd->pkb", vec32, listed)
    reassign = (head_sq[:, :, None] + vec_sq[:, None, :] - 2.0 * dots) / D
    return density, spread, reassign
```

```python
import jax
import jax.numpy as jnp
from jax import lax
from jax.sharding import PartitionSpec as P


def from_partner(value, axis, mask):
    count = lax.axis_size(axis)
    return lax.ppermute(value, axis, [(source, source ^ mask) for source in range(count)])


def tree_sum(parts):
    while len(parts) > 1:
        parts = [parts[i] + parts[i + 1] for i in range(0, len(parts), 2)]
    return parts[0]


def per_device(heads, new_heads, vectors, near_ids):
    head_dev, width = heads.shape
    new_count = new_heads.shape[0]
    near = near_ids.shape[1]
    groups = lax.axis_size("group")
    members = lax.axis_size("member")
    most = 2 * near // members
    me = lax.axis_index("member")

    lists = [near_ids] + [from_partner(near_ids, "member", mask) for mask in range(1, members)]
    blocks = [new_heads] + [from_partner(new_heads, "group", mask) for mask in range(1, groups)]

    head_sq = jnp.sum(jnp.square(heads.astype(jnp.float32)), axis=1)

    ids = jnp.concatenate(lists, axis=0)
    local = ids - me * head_dev
    owned = (local >= 0) & (local < head_dev)
    rank = jnp.cumsum(owned.astype(jnp.int32), axis=1) - 1
    slots = jnp.arange(most, dtype=jnp.int32)
    pick = owned[:, None, :] & (rank[:, None, :] == slots[None, :, None])
    wanted = jnp.sum(jnp.where(pick, local[:, None, :] + 1, 0), axis=2).reshape(-1) - 1
    onehot = (wanted[:, None] == jnp.arange(head_dev, dtype=jnp.int32)[None, :]).astype(jnp.bfloat16)
    rows = jnp.dot(onehot, heads, preferred_element_type=jnp.float32).astype(jnp.bfloat16)
    rows = rows.reshape(members, most, width)
    listed = [rows[0]] + [from_partner(rows[mask], "member", mask) for mask in range(1, members)]

    queries = jnp.concatenate(blocks, axis=0)
    query_sq = jnp.sum(jnp.square(queries.astype(jnp.float32)), axis=1)
    dots = lax.dot_general(
        queries, heads, (((1,), (1,)), ((), ())), preferred_element_type=jnp.float32
    )
    excess = (query_sq[:, None] + head_sq[None, :] - 2.0 * dots) / width
    weight = 1.0 / jnp.square(1.0 + excess)
    sums = jnp.stack([jnp.sum(weight, axis=1), jnp.sum(weight * excess, axis=1)])
    sums = sums.reshape(2, groups, new_count)
    mine = tree_sum(
        [sums[:, 0]] + [from_partner(sums[:, mask], "group", mask) for mask in range(1, groups)]
    )
    mine = tree_sum([mine] + [from_partner(mine, "member", mask) for mask in range(1, members)])
    total_heads = float(head_dev * groups * members)
    density = jnp.log(mine[0] / total_heads)
    spread = mine[1] / mine[0]

    owner = near_ids[0] // head_dev
    earlier = jnp.tril(jnp.ones((near, near), jnp.bool_), -1)
    place = jnp.sum((earlier & (owner[:, None] == owner[None, :])).astype(jnp.int32), axis=1)
    source = (owner ^ me) * most + place
    back = (source[:, None] == jnp.arange(members * most, dtype=jnp.int32)[None, :]).astype(jnp.bfloat16)
    near_rows = jnp.dot(
        back, jnp.concatenate(listed, axis=0), preferred_element_type=jnp.float32
    ).astype(jnp.bfloat16)
    vec = vectors[0]
    vec_sq = jnp.sum(jnp.square(vec.astype(jnp.float32)), axis=1)
    row_sq = jnp.sum(jnp.square(near_rows.astype(jnp.float32)), axis=1)
    dots = lax.dot_general(
        near_rows, vec, (((1,), (1,)), ((), ())), preferred_element_type=jnp.float32
    )
    reassign = (row_sq[:, None] + vec_sq[None, :] - 2.0 * dots) / width
    return (density, spread, reassign[None])


def solution(mesh):
    placed = (
        P(("group", "member"), None),
        P("group", None),
        P(("group", "member"), None, None),
        P(("group", "member"), None),
    )
    return jax.shard_map(
        per_device,
        mesh=mesh,
        in_specs=placed,
        out_specs=(P("group"), P("group"), P(("group", "member"), None, None)),
        check_vma=False,
    )
```

```python
import jax
import jax.numpy as jnp
from jax import lax
from jax.sharding import PartitionSpec as P


def to_each(value, axis):
    return lax.all_to_all(value, axis, 0, 0, tiled=True)


def per_device(heads, new_heads, vectors, near_ids):
    head_dev, width = heads.shape
    new_count = new_heads.shape[0]
    near = near_ids.shape[1]
    groups = lax.axis_size("group")
    members = lax.axis_size("member")
    most = 2 * near // members
    me = lax.axis_index("member")

    ids = to_each(jnp.broadcast_to(near_ids, (members, near)), "member")
    queries = to_each(jnp.tile(new_heads, (groups, 1)), "group")

    head_sq = jnp.sum(jnp.square(heads.astype(jnp.float32)), axis=1)

    local = ids - me * head_dev
    owned = (local >= 0) & (local < head_dev)
    rank = jnp.cumsum(owned.astype(jnp.int32), axis=1) - 1
    slots = jnp.arange(most, dtype=jnp.int32)
    pick = owned[:, None, :] & (rank[:, None, :] == slots[None, :, None])
    wanted = jnp.sum(jnp.where(pick, local[:, None, :] + 1, 0), axis=2).reshape(-1) - 1
    onehot = (wanted[:, None] == jnp.arange(head_dev, dtype=jnp.int32)[None, :]).astype(jnp.bfloat16)
    rows = jnp.dot(onehot, heads, preferred_element_type=jnp.float32).astype(jnp.bfloat16)
    listed = to_each(rows, "member")

    query_sq = jnp.sum(jnp.square(queries.astype(jnp.float32)), axis=1)
    dots = lax.dot_general(
        queries, heads, (((1,), (1,)), ((), ())), preferred_element_type=jnp.float32
    )
    excess = (query_sq[:, None] + head_sq[None, :] - 2.0 * dots) / width
    weight = 1.0 / jnp.square(1.0 + excess)
    sums = jnp.stack([jnp.sum(weight, axis=1), jnp.sum(weight * excess, axis=1)])
    sums = jnp.transpose(sums.reshape(2, groups, new_count), (1, 0, 2))
    sums = jnp.broadcast_to(sums[:, None], (groups, members, 2, new_count))
    sums = to_each(sums.reshape(groups * members, 2, new_count), ("group", "member"))
    mine = jnp.sum(sums, axis=0)
    total_heads = float(head_dev * groups * members)
    density = jnp.log(mine[0] / total_heads)
    spread = mine[1] / mine[0]

    owner = near_ids[0] // head_dev
    earlier = jnp.tril(jnp.ones((near, near), jnp.bool_), -1)
    place = jnp.sum((earlier & (owner[:, None] == owner[None, :])).astype(jnp.int32), axis=1)
    source = owner * most + place
    back = (source[:, None] == jnp.arange(members * most, dtype=jnp.int32)[None, :]).astype(jnp.bfloat16)
    near_rows = jnp.dot(
        back, listed, preferred_element_type=jnp.float32
    ).astype(jnp.bfloat16)
    vec = vectors[0]
    vec_sq = jnp.sum(jnp.square(vec.astype(jnp.float32)), axis=1)
    row_sq = jnp.sum(jnp.square(near_rows.astype(jnp.float32)), axis=1)
    dots = lax.dot_general(
        near_rows, vec, (((1,), (1,)), ((), ())), preferred_element_type=jnp.float32
    )
    reassign = (row_sq[:, None] + vec_sq[None, :] - 2.0 * dots) / width
    return (density, spread, reassign[None])


def solution(mesh):
    placed = (
        P(("group", "member"), None),
        P("group", None),
        P(("group", "member"), None, None),
        P(("group", "member"), None),
    )
    return jax.shard_map(
        per_device,
        mesh=mesh,
        in_specs=placed,
        out_specs=(P("group"), P("group"), P(("group", "member"), None, None)),
        check_vma=False,
    )
```

```python
import functools

import jax
import jax.numpy as jnp
from jax import lax
from jax.experimental import pallas as pl
from jax.experimental.pallas import tpu as pltpu
from jax.sharding import PartitionSpec as P

VMEM = pltpu.MemorySpace.VMEM
LANES = 128
LIMIT = 24 * 2**20


def from_partner(value, axis, mask):
    count = lax.axis_size(axis)
    return lax.ppermute(value, axis, [(source, source ^ mask) for source in range(count)])


def to_each(value, axis):
    return lax.all_to_all(value, axis, 0, 0, tiled=True)


def call(body, shapes, operands, flops, moved):
    return pl.pallas_call(
        body,
        out_shape=shapes,
        in_specs=[pl.BlockSpec(memory_space=VMEM)] * len(operands),
        out_specs=jax.tree.map(lambda unused: pl.BlockSpec(memory_space=VMEM), shapes),
        compiler_params=pltpu.CompilerParams(vmem_limit_bytes=LIMIT),
        cost_estimate=pl.CostEstimate(flops=flops, bytes_accessed=moved, transcendentals=0),
    )(*operands)


def iota(shape, dim):
    return lax.broadcasted_iota(jnp.int32, shape, dim)


def gather_kernel(members, most, ids_ref, heads_ref, rows_ref):
    head_dev = heads_ref.shape[0]
    near = ids_ref.shape[1]
    me = lax.axis_index("member")
    ids = jnp.concatenate([ids_ref[pl.ds(me ^ member, 1), :] for member in range(members)], axis=0)
    local = ids - me * head_dev
    owned = (local >= 0) & (local < head_dev)
    earlier = (iota((near, near), 0) < iota((near, near), 1)).astype(jnp.bfloat16)
    rank = jnp.dot(owned.astype(jnp.bfloat16), earlier, preferred_element_type=jnp.float32)
    rank = jnp.where(owned, rank.astype(jnp.int32), -1)
    shape = (members, most, near)
    pick = jnp.broadcast_to(rank[:, None, :], shape) == iota(shape, 1)
    wanted = jnp.sum(
        jnp.where(pick, jnp.broadcast_to(local[:, None, :] + 1, shape), 0), axis=2, keepdims=True
    ).reshape(members * most, 1)
    onehot = (wanted == iota((members * most, head_dev), 1) + 1).astype(jnp.bfloat16)
    rows_ref[...] = jnp.dot(
        onehot, heads_ref[...], preferred_element_type=jnp.float32
    ).astype(jnp.bfloat16)


def crowd_kernel(groups, members, heads_ref, *refs):
    query_refs, sums_ref = refs[:groups], refs[groups]
    head_dev, width = heads_ref.shape
    new_count = query_refs[0].shape[0]
    here = lax.axis_index("group")
    queries = jnp.concatenate([ref[...] for ref in query_refs], axis=0)
    squares = jnp.square(queries.astype(jnp.float32))
    query_sq = jnp.sum(squares, axis=1, keepdims=True)
    total_w = jnp.zeros((groups * new_count, 1), jnp.float32)
    total_we = jnp.zeros((groups * new_count, 1), jnp.float32)
    tile = 512
    for start in range(0, head_dev, tile):
        block = heads_ref[start:start + tile, :]
        dots = lax.dot_general(
            queries, block, (((1,), (1,)), ((), ())), preferred_element_type=jnp.float32
        )
        parts = jnp.square(block.astype(jnp.float32))
        folded = parts[:, :LANES]
        for column in range(LANES, width, LANES):
            folded = folded + parts[:, column:column + LANES]
        head_sq = jnp.sum(folded.T, axis=0, keepdims=True)
        excess = (query_sq + head_sq - 2.0 * dots) * (1.0 / width)
        inverse = 1.0 / (1.0 + excess)
        weight = inverse * inverse
        total_w = total_w + jnp.sum(weight, axis=1, keepdims=True)
        total_we = total_we + jnp.sum(weight * excess, axis=1, keepdims=True)
    shape = (new_count, LANES)
    lane = iota(shape, 1)
    row = iota(shape, 0)
    for mask in range(groups):
        part = slice(mask * new_count, (mask + 1) * new_count)
        spread_out = jnp.where(lane == row, total_w[part], 0.0) + jnp.where(
            lane == row + new_count, total_we[part], 0.0
        )
        message = jnp.sum(spread_out, axis=0, keepdims=True)
        first = pl.multiple_of((here ^ mask) * members, members)
        sums_ref[pl.ds(first, members), :] = jnp.broadcast_to(message, (members, LANES))


def near_kernel(most, head_dev, ids_ref, listed_ref, vectors_ref, out_ref):
    near = ids_ref.shape[1]
    width = vectors_ref.shape[2]
    block = vectors_ref.shape[1]
    square = (near, near)
    owner_row = jnp.broadcast_to(lax.div(ids_ref[...], head_dev), square)
    eye = iota(square, 0) == iota(square, 1)
    owner = jnp.sum(jnp.where(eye, owner_row, 0), axis=1, keepdims=True)
    before = (owner_row == owner) & (iota(square, 1) < iota(square, 0))
    place = jnp.sum(before.astype(jnp.int32), axis=1, keepdims=True)
    source = owner * most + place
    back = (source == iota((near, listed_ref.shape[0]), 1)).astype(jnp.bfloat16)
    rows32 = jnp.dot(back, listed_ref[...], preferred_element_type=jnp.float32)
    row_sq = jnp.sum(jnp.square(rows32), axis=1, keepdims=True)
    vec = vectors_ref[0]
    vec_sq = jnp.sum(jnp.square(vec.astype(jnp.float32)), axis=1, keepdims=True)
    turned = iota((block, block), 0) == iota((block, block), 1)
    vec_sq = jnp.sum(jnp.where(turned, vec_sq, 0.0), axis=0, keepdims=True)
    dots = lax.dot_general(
        rows32.astype(jnp.bfloat16), vec, (((1,), (1,)), ((), ())),
        preferred_element_type=jnp.float32,
    )
    out_ref[0] = (row_sq + vec_sq - 2.0 * dots) * (1.0 / width)


def final_kernel(new_count, total_heads, sums_ref, density_ref, spread_ref):
    total = jnp.sum(sums_ref[...], axis=0, keepdims=True)
    total_w = total[:, :new_count]
    total_we = total[:, new_count:2 * new_count]
    density_ref[...] = jnp.log(total_w * (1.0 / total_heads))
    spread_ref[...] = total_we / total_w


def per_device(heads, new_heads, vectors, near_ids):
    head_dev, width = heads.shape
    new_count = new_heads.shape[0]
    near = near_ids.shape[1]
    groups = lax.axis_size("group")
    members = lax.axis_size("member")
    most = 2 * near // members

    ids = near_ids
    blocks = [new_heads]
    mask = 1
    while mask < members:
        ids = jnp.concatenate([ids, from_partner(ids, "member", mask)], axis=0)
        mask *= 2
    for mask in range(1, groups):
        blocks.append(from_partner(new_heads, "group", mask))

    rows = call(
        functools.partial(gather_kernel, members, most),
        jax.ShapeDtypeStruct((members * most, width), jnp.bfloat16),
        (ids, heads),
        2 * members * most * head_dev * width,
        heads.size * 2,
    )
    listed = to_each(rows, "member")

    sums = call(
        functools.partial(crowd_kernel, groups, members),
        jax.ShapeDtypeStruct((groups * members, LANES), jnp.float32),
        (heads, *blocks),
        2 * groups * new_count * head_dev * width,
        heads.size * 2,
    )
    sums = to_each(sums, ("group", "member"))
    density, spread = call(
        functools.partial(final_kernel, new_count, float(head_dev * groups * members)),
        (jax.ShapeDtypeStruct((1, new_count), jnp.float32),) * 2,
        (sums,),
        groups * members * LANES,
        groups * members * LANES * 4,
    )
    reassign = call(
        functools.partial(near_kernel, most, head_dev),
        jax.ShapeDtypeStruct((1, near, vectors.shape[1]), jnp.float32),
        (near_ids, listed, vectors),
        4 * near * vectors.shape[1] * width,
        vectors.size * 4,
    )
    return (density[0], spread[0], reassign)


def solution(mesh):
    placed = (
        P(("group", "member"), None),
        P("group", None),
        P(("group", "member"), None, None),
        P(("group", "member"), None),
    )
    return jax.shard_map(
        per_device,
        mesh=mesh,
        in_specs=placed,
        out_specs=(P("group"), P("group"), P(("group", "member"), None, None)),
        check_vma=False,
    )
```

```python
import functools

import jax
import jax.numpy as jnp
from jax import lax
from jax.experimental import pallas as pl
from jax.experimental.pallas import tpu as pltpu
from jax.sharding import PartitionSpec as P

VMEM = pltpu.MemorySpace.VMEM
LANES = 128
LIMIT = 24 * 2**20


def from_partner(value, axis, mask):
    count = lax.axis_size(axis)
    return lax.ppermute(value, axis, [(source, source ^ mask) for source in range(count)])


def to_each(value, axis):
    return lax.all_to_all(value, axis, 0, 0, tiled=True)


def call(body, shapes, operands, flops, moved, unread=0):
    spaces = [VMEM] * (len(operands) - unread) + [pl.ANY] * unread
    return pl.pallas_call(
        body,
        out_shape=shapes,
        in_specs=[pl.BlockSpec(memory_space=space) for space in spaces],
        out_specs=jax.tree.map(lambda unused: pl.BlockSpec(memory_space=VMEM), shapes),
        compiler_params=pltpu.CompilerParams(vmem_limit_bytes=LIMIT),
        cost_estimate=pl.CostEstimate(flops=flops, bytes_accessed=moved, transcendentals=0),
    )(*operands)


def iota(shape, dim):
    return lax.broadcasted_iota(jnp.int32, shape, dim)


def tile_kernel(ids_ref, new_ref, out_ref, kept_ref):
    near = ids_ref.shape[1]
    out_ref[:, :near] = jnp.broadcast_to(ids_ref[...], (out_ref.shape[0], near))
    kept_ref[...] = new_ref[...]
    out_ref[:, near:] = jnp.zeros((out_ref.shape[0], out_ref.shape[1] - near), jnp.int32)


def squares_kernel(heads_ref, kept_ref, head_sq_ref, *sems):
    head_dev, width = heads_ref.shape
    tile = head_dev // len(sems)
    parts = [pl.ds(i * tile, tile) for i in range(len(sems))]
    copies = [
        pltpu.make_async_copy(heads_ref.at[part], kept_ref.at[part], sem)
        for part, sem in zip(parts, sems)
    ]
    for copy in copies:
        copy.start()
    for i, copy in enumerate(copies):
        copy.wait()
        for first in range(i * tile, (i + 1) * tile, LANES):
            block = jnp.square(kept_ref[first:first + LANES, :].astype(jnp.float32))
            folded = block[:, :LANES]
            for column in range(LANES, width, LANES):
                folded = folded + block[:, column:column + LANES]
            head_sq_ref[:, first:first + LANES] = jnp.sum(folded.T, axis=0, keepdims=True)


def gather_kernel(members, most, near, ids_ref, heads_ref, rows_ref):
    head_dev = heads_ref.shape[0]
    me = lax.axis_index("member")
    ids = ids_ref[:, :near]
    local = ids - me * head_dev
    owned = (local >= 0) & (local < head_dev)
    earlier = (iota((near, near), 0) < iota((near, near), 1)).astype(jnp.bfloat16)
    rank = jnp.dot(owned.astype(jnp.bfloat16), earlier, preferred_element_type=jnp.float32)
    rank = jnp.where(owned, rank.astype(jnp.int32), -1)
    shape = (members, most, near)
    pick = jnp.broadcast_to(rank[:, None, :], shape) == iota(shape, 1)
    wanted = jnp.sum(
        jnp.where(pick, jnp.broadcast_to(local[:, None, :] + 1, shape), 0), axis=2, keepdims=True
    ).reshape(members * most, 1)
    onehot = (wanted == iota((members * most, head_dev), 1) + 1).astype(jnp.bfloat16)
    rows_ref[...] = jnp.dot(
        onehot, heads_ref[...], preferred_element_type=jnp.float32
    ).astype(jnp.bfloat16)


def crowd_kernel(groups, members, heads_ref, head_sq_ref, *refs):
    query_refs, sums_ref = refs[:groups], refs[-1]
    head_dev, width = heads_ref.shape
    new_count = query_refs[0].shape[0]
    here = lax.axis_index("group")
    queries = jnp.concatenate([ref[...] for ref in query_refs], axis=0)
    squares = jnp.square(queries.astype(jnp.float32))
    query_sq = jnp.sum(squares, axis=1, keepdims=True)
    total_w = jnp.zeros((groups * new_count, 1), jnp.float32)
    total_we = jnp.zeros((groups * new_count, 1), jnp.float32)
    tile = 512
    for start in range(0, head_dev, tile):
        dots = lax.dot_general(
            queries, heads_ref[start:start + tile, :], (((1,), (1,)), ((), ())),
            preferred_element_type=jnp.float32,
        )
        head_sq = head_sq_ref[:, start:start + tile]
        excess = (query_sq + head_sq - 2.0 * dots) * (1.0 / width)
        inverse = 1.0 / (1.0 + excess)
        weight = inverse * inverse
        total_w = total_w + jnp.sum(weight, axis=1, keepdims=True)
        total_we = total_we + jnp.sum(weight * excess, axis=1, keepdims=True)
    shape = (new_count, LANES)
    lane = iota(shape, 1)
    row = iota(shape, 0)
    for mask in range(groups):
        part = slice(mask * new_count, (mask + 1) * new_count)
        spread_out = jnp.where(lane == row, total_w[part], 0.0) + jnp.where(
            lane == row + new_count, total_we[part], 0.0
        )
        message = jnp.sum(spread_out, axis=0, keepdims=True)
        first = pl.multiple_of((here ^ mask) * members, members)
        sums_ref[pl.ds(first, members), :] = jnp.broadcast_to(message, (members, LANES))


def near_kernel(most, head_dev, ids_ref, listed_ref, vectors_ref, out_ref):
    near = ids_ref.shape[1]
    width = vectors_ref.shape[2]
    block = vectors_ref.shape[1]
    square = (near, near)
    owner_row = jnp.broadcast_to(lax.div(ids_ref[...], head_dev), square)
    eye = iota(square, 0) == iota(square, 1)
    owner = jnp.sum(jnp.where(eye, owner_row, 0), axis=1, keepdims=True)
    before = (owner_row == owner) & (iota(square, 1) < iota(square, 0))
    place = jnp.sum(before.astype(jnp.int32), axis=1, keepdims=True)
    source = owner * most + place
    back = (source == iota((near, listed_ref.shape[0]), 1)).astype(jnp.bfloat16)
    rows32 = jnp.dot(back, listed_ref[...], preferred_element_type=jnp.float32)
    row_sq = jnp.sum(jnp.square(rows32), axis=1, keepdims=True)
    vec = vectors_ref[0]
    vec_sq = jnp.sum(jnp.square(vec.astype(jnp.float32)), axis=1, keepdims=True)
    turned = iota((block, block), 0) == iota((block, block), 1)
    vec_sq = jnp.sum(jnp.where(turned, vec_sq, 0.0), axis=0, keepdims=True)
    dots = lax.dot_general(
        rows32.astype(jnp.bfloat16), vec, (((1,), (1,)), ((), ())),
        preferred_element_type=jnp.float32,
    )
    out_ref[0] = (row_sq + vec_sq - 2.0 * dots) * (1.0 / width)


def final_kernel(new_count, total_heads, sums_ref, density_ref, spread_ref):
    total = jnp.sum(sums_ref[...], axis=0, keepdims=True)
    total_w = total[:, :new_count]
    total_we = total[:, new_count:2 * new_count]
    density_ref[...] = jnp.log(total_w * (1.0 / total_heads))
    spread_ref[...] = total_we / total_w


def per_device(heads, new_heads, vectors, near_ids):
    head_dev, width = heads.shape
    new_count = new_heads.shape[0]
    near = near_ids.shape[1]
    groups = lax.axis_size("group")
    members = lax.axis_size("member")
    most = 2 * near // members

    ids, new_heads = call(
        tile_kernel,
        (
            jax.ShapeDtypeStruct((members, LANES), jnp.int32),
            jax.ShapeDtypeStruct(new_heads.shape, new_heads.dtype),
        ),
        (near_ids, new_heads),
        0,
        near * 4,
    )
    ids = to_each(ids, "member")
    blocks = [new_heads] + [from_partner(new_heads, "group", mask) for mask in range(1, groups)]
    heads, head_sq = pl.pallas_call(
        squares_kernel,
        out_shape=(
            jax.ShapeDtypeStruct((head_dev, width), jnp.bfloat16),
            jax.ShapeDtypeStruct((1, head_dev), jnp.float32),
        ),
        in_specs=[pl.BlockSpec(memory_space=pltpu.MemorySpace.HBM)],
        out_specs=(pl.BlockSpec(memory_space=VMEM),) * 2,
        scratch_shapes=[pltpu.SemaphoreType.DMA] * 4,
        compiler_params=pltpu.CompilerParams(vmem_limit_bytes=LIMIT),
        cost_estimate=pl.CostEstimate(
            flops=heads.size * 2, bytes_accessed=heads.size * 2, transcendentals=0
        ),
    )(pltpu.with_memory_space_constraint(heads, pltpu.MemorySpace.HBM))

    rows = call(
        functools.partial(gather_kernel, members, most, near),
        jax.ShapeDtypeStruct((members * most, width), jnp.bfloat16),
        (ids, heads),
        2 * members * most * head_dev * width,
        heads.size * 2,
    )
    listed = to_each(rows, "member")

    sums = call(
        functools.partial(crowd_kernel, groups, members),
        jax.ShapeDtypeStruct((groups * members, LANES), jnp.float32),
        (heads, head_sq, *blocks, rows),
        2 * groups * new_count * head_dev * width,
        heads.size * 2,
        unread=1,
    )
    sums = to_each(sums, ("group", "member"))
    density, spread = call(
        functools.partial(final_kernel, new_count, float(head_dev * groups * members)),
        (jax.ShapeDtypeStruct((1, new_count), jnp.float32),) * 2,
        (sums,),
        groups * members * LANES,
        groups * members * LANES * 4,
    )
    reassign = call(
        functools.partial(near_kernel, most, head_dev),
        jax.ShapeDtypeStruct((1, near, vectors.shape[1]), jnp.float32),
        (near_ids, listed, vectors),
        4 * near * vectors.shape[1] * width,
        vectors.size * 4,
    )
    return (density[0], spread[0], reassign)


def solution(mesh):
    placed = (
        P(("group", "member"), None),
        P("group", None),
        P(("group", "member"), None, None),
        P(("group", "member"), None),
    )
    return jax.shard_map(
        per_device,
        mesh=mesh,
        in_specs=placed,
        out_specs=(P("group"), P("group"), P(("group", "member"), None, None)),
        check_vma=False,
    )
```

```python
import functools

import jax
import jax.numpy as jnp
from jax import lax
from jax.experimental import pallas as pl
from jax.experimental.pallas import tpu as pltpu
from jax.sharding import PartitionSpec as P

VMEM = pltpu.MemorySpace.VMEM
LANES = 128
LIMIT = 24 * 2**20


def from_partner(value, axis, mask):
    count = lax.axis_size(axis)
    return lax.ppermute(value, axis, [(source, source ^ mask) for source in range(count)])


def to_each(value, axis):
    return lax.all_to_all(value, axis, 0, 0, tiled=True)


def call(body, shapes, operands, flops, moved, unread=0):
    spaces = [VMEM] * (len(operands) - unread) + [pl.ANY] * unread
    return pl.pallas_call(
        body,
        out_shape=shapes,
        in_specs=[pl.BlockSpec(memory_space=space) for space in spaces],
        out_specs=jax.tree.map(lambda unused: pl.BlockSpec(memory_space=VMEM), shapes),
        compiler_params=pltpu.CompilerParams(vmem_limit_bytes=LIMIT),
        cost_estimate=pl.CostEstimate(flops=flops, bytes_accessed=moved, transcendentals=0),
    )(*operands)


def iota(shape, dim):
    return lax.broadcasted_iota(jnp.int32, shape, dim)


def tile_kernel(ids_ref, new_ref, out_ref, kept_ref):
    near = ids_ref.shape[1]
    out_ref[:, :near] = jnp.broadcast_to(ids_ref[...], (out_ref.shape[0], near))
    kept_ref[...] = new_ref[...]
    out_ref[:, near:] = jnp.zeros((out_ref.shape[0], out_ref.shape[1] - near), jnp.int32)


def squares_kernel(heads_ref, kept_ref, head_sq_ref, *sems):
    head_dev, width = heads_ref.shape
    tile = head_dev // len(sems)
    parts = [pl.ds(i * tile, tile) for i in range(len(sems))]
    copies = [
        pltpu.make_async_copy(heads_ref.at[part], kept_ref.at[part], sem)
        for part, sem in zip(parts, sems)
    ]
    for copy in copies:
        copy.start()
    for i, copy in enumerate(copies):
        copy.wait()
        for first in range(i * tile, (i + 1) * tile, LANES):
            block = jnp.square(kept_ref[first:first + LANES, :].astype(jnp.float32))
            folded = block[:, :LANES]
            for column in range(LANES, width, LANES):
                folded = folded + block[:, column:column + LANES]
            head_sq_ref[:, first:first + LANES] = jnp.sum(folded.T, axis=0, keepdims=True)


def gather_kernel(members, most, near, ids_ref, heads_ref, rows_ref):
    head_dev = heads_ref.shape[0]
    me = lax.axis_index("member")
    ids = ids_ref[:, :near]
    local = ids - me * head_dev
    owned = (local >= 0) & (local < head_dev)
    earlier = (iota((near, near), 0) < iota((near, near), 1)).astype(jnp.bfloat16)
    rank = jnp.dot(owned.astype(jnp.bfloat16), earlier, preferred_element_type=jnp.float32)
    rank = jnp.where(owned, rank.astype(jnp.int32), -1)
    shape = (members, most, near)
    pick = jnp.broadcast_to(rank[:, None, :], shape) == iota(shape, 1)
    wanted = jnp.sum(
        jnp.where(pick, jnp.broadcast_to(local[:, None, :] + 1, shape), 0), axis=2, keepdims=True
    ).reshape(members * most, 1)
    onehot = (wanted == iota((members * most, head_dev), 1) + 1).astype(jnp.bfloat16)
    rows_ref[...] = jnp.dot(
        onehot, heads_ref[...], preferred_element_type=jnp.float32
    ).astype(jnp.bfloat16)


def crowd_kernel(groups, members, heads_ref, head_sq_ref, *refs):
    query_refs, sums_ref = refs[:groups], refs[-1]
    head_dev, width = heads_ref.shape
    new_count = query_refs[0].shape[0]
    here = lax.axis_index("group")
    queries = jnp.concatenate([ref[...] for ref in query_refs], axis=0)
    squares = jnp.square(queries.astype(jnp.float32))
    query_sq = jnp.sum(squares, axis=1, keepdims=True)
    total_w = jnp.zeros((groups * new_count, 1), jnp.float32)
    total_we = jnp.zeros((groups * new_count, 1), jnp.float32)
    tile = 512
    for start in range(0, head_dev, tile):
        dots = lax.dot_general(
            queries, heads_ref[start:start + tile, :], (((1,), (1,)), ((), ())),
            preferred_element_type=jnp.float32,
        )
        head_sq = head_sq_ref[:, start:start + tile]
        excess = (query_sq + head_sq - 2.0 * dots) * (1.0 / width)
        inverse = 1.0 / (1.0 + excess)
        weight = inverse * inverse
        total_w = total_w + jnp.sum(weight, axis=1, keepdims=True)
        total_we = total_we + jnp.sum(weight * excess, axis=1, keepdims=True)
    shape = (new_count, LANES)
    lane = iota(shape, 1)
    row = iota(shape, 0)
    for mask in range(groups):
        part = slice(mask * new_count, (mask + 1) * new_count)
        spread_out = jnp.where(lane == row, total_w[part], 0.0) + jnp.where(
            lane == row + new_count, total_we[part], 0.0
        )
        message = jnp.sum(spread_out, axis=0, keepdims=True)
        first = pl.multiple_of((here ^ mask) * members, members)
        sums_ref[pl.ds(first, members), :] = jnp.broadcast_to(message, (members, LANES))


def near_kernel(most, head_dev, ids_ref, listed_ref, vectors_ref, out_ref):
    near = ids_ref.shape[1]
    width = vectors_ref.shape[2]
    block = vectors_ref.shape[1]
    square = (near, near)
    owner_row = jnp.broadcast_to(lax.div(ids_ref[...], head_dev), square)
    eye = iota(square, 0) == iota(square, 1)
    owner = jnp.sum(jnp.where(eye, owner_row, 0), axis=1, keepdims=True)
    before = (owner_row == owner) & (iota(square, 1) < iota(square, 0))
    place = jnp.sum(before.astype(jnp.int32), axis=1, keepdims=True)
    source = owner * most + place
    back = (source == iota((near, listed_ref.shape[0]), 1)).astype(jnp.bfloat16)
    rows32 = jnp.dot(back, listed_ref[...], preferred_element_type=jnp.float32)
    row_sq = jnp.sum(jnp.square(rows32), axis=1, keepdims=True)
    vec = vectors_ref[0]
    vec_sq = jnp.sum(jnp.square(vec.astype(jnp.float32)), axis=1, keepdims=True)
    turned = iota((block, block), 0) == iota((block, block), 1)
    vec_sq = jnp.sum(jnp.where(turned, vec_sq, 0.0), axis=0, keepdims=True)
    dots = lax.dot_general(
        rows32.astype(jnp.bfloat16), vec, (((1,), (1,)), ((), ())),
        preferred_element_type=jnp.float32,
    )
    out_ref[0] = (row_sq + vec_sq - 2.0 * dots) * (1.0 / width)


def final_kernel(new_count, total_heads, sums_ref, unused, density_ref, spread_ref):
    total = jnp.sum(sums_ref[...], axis=0, keepdims=True)
    total_w = total[:, :new_count]
    total_we = total[:, new_count:2 * new_count]
    density_ref[...] = jnp.log(total_w * (1.0 / total_heads))
    spread_ref[...] = total_we / total_w


def per_device(heads, new_heads, vectors, near_ids):
    head_dev, width = heads.shape
    new_count = new_heads.shape[0]
    near = near_ids.shape[1]
    groups = lax.axis_size("group")
    members = lax.axis_size("member")
    most = 2 * near // members

    ids, new_heads = call(
        tile_kernel,
        (
            jax.ShapeDtypeStruct((members, LANES), jnp.int32),
            jax.ShapeDtypeStruct(new_heads.shape, new_heads.dtype),
        ),
        (near_ids, new_heads),
        0,
        near * 4,
    )
    ids = to_each(ids, "member")
    blocks = [new_heads] + [from_partner(new_heads, "group", mask) for mask in range(1, groups)]
    heads, head_sq = pl.pallas_call(
        squares_kernel,
        out_shape=(
            jax.ShapeDtypeStruct((head_dev, width), jnp.bfloat16),
            jax.ShapeDtypeStruct((1, head_dev), jnp.float32),
        ),
        in_specs=[pl.BlockSpec(memory_space=pltpu.MemorySpace.HBM)],
        out_specs=(pl.BlockSpec(memory_space=VMEM),) * 2,
        scratch_shapes=[pltpu.SemaphoreType.DMA] * 4,
        compiler_params=pltpu.CompilerParams(vmem_limit_bytes=LIMIT),
        cost_estimate=pl.CostEstimate(
            flops=heads.size * 2, bytes_accessed=heads.size * 2, transcendentals=0
        ),
    )(pltpu.with_memory_space_constraint(heads, pltpu.MemorySpace.HBM))

    rows = call(
        functools.partial(gather_kernel, members, most, near),
        jax.ShapeDtypeStruct((members * most, width), jnp.bfloat16),
        (ids, heads),
        2 * members * most * head_dev * width,
        heads.size * 2,
    )
    listed = to_each(rows, "member")

    sums = call(
        functools.partial(crowd_kernel, groups, members),
        jax.ShapeDtypeStruct((groups * members, LANES), jnp.float32),
        (heads, head_sq, *blocks, rows),
        2 * groups * new_count * head_dev * width,
        heads.size * 2,
        unread=1,
    )
    sums = to_each(sums, ("group", "member"))
    reassign = call(
        functools.partial(near_kernel, most, head_dev),
        jax.ShapeDtypeStruct((1, near, vectors.shape[1]), jnp.float32),
        (near_ids, listed, vectors),
        4 * near * vectors.shape[1] * width,
        vectors.size * 4,
    )
    density, spread = call(
        functools.partial(final_kernel, new_count, float(head_dev * groups * members)),
        (jax.ShapeDtypeStruct((1, new_count), jnp.float32),) * 2,
        (sums, reassign),
        groups * members * LANES,
        groups * members * LANES * 4,
        unread=1,
    )
    return (density[0], spread[0], reassign)


def solution(mesh):
    placed = (
        P(("group", "member"), None),
        P("group", None),
        P(("group", "member"), None, None),
        P(("group", "member"), None),
    )
    return jax.shard_map(
        per_device,
        mesh=mesh,
        in_specs=placed,
        out_specs=(P("group"), P("group"), P(("group", "member"), None, None)),
        check_vma=False,
    )
```

```python
import functools

import jax
import jax.numpy as jnp
from jax import lax
from jax.experimental import pallas as pl
from jax.experimental.pallas import tpu as pltpu
from jax.sharding import PartitionSpec as P

VMEM = pltpu.MemorySpace.VMEM
HBM = pltpu.MemorySpace.HBM
LANES = 128
LIMIT = 24 * 2**20


def from_partner(value, axis, mask):
    count = lax.axis_size(axis)
    return lax.ppermute(value, axis, [(source, source ^ mask) for source in range(count)])


def to_each(value, axis):
    return lax.all_to_all(value, axis, 0, 0, tiled=True)


def in_hbm(value):
    return pltpu.with_memory_space_constraint(value, HBM)


def call(body, shapes, operands, flops, moved, unread=0):
    spaces = [VMEM] * (len(operands) - unread) + [pl.ANY] * unread
    return pl.pallas_call(
        body,
        out_shape=shapes,
        in_specs=[pl.BlockSpec(memory_space=space) for space in spaces],
        out_specs=jax.tree.map(lambda unused: pl.BlockSpec(memory_space=VMEM), shapes),
        compiler_params=pltpu.CompilerParams(vmem_limit_bytes=LIMIT),
        cost_estimate=pl.CostEstimate(flops=flops, bytes_accessed=moved, transcendentals=0),
    )(*operands)


def iota(shape, dim):
    return lax.broadcasted_iota(jnp.int32, shape, dim)


def squares_kernel(heads_ref, new_ref, kept_ref, head_sq_ref, kept_new_ref, new_sem, *sems):
    head_dev, width = heads_ref.shape
    tile = head_dev // len(sems)
    parts = [pl.ds(i * tile, tile) for i in range(len(sems))]
    copies = [
        pltpu.make_async_copy(heads_ref.at[part], kept_ref.at[part], sem)
        for part, sem in zip(parts, sems)
    ]
    for copy in copies:
        copy.start()
    new_copy = pltpu.make_async_copy(new_ref, kept_new_ref, new_sem)
    new_copy.start()
    for i, copy in enumerate(copies):
        copy.wait()
        for first in range(i * tile, (i + 1) * tile, LANES):
            block = jnp.square(kept_ref[first:first + LANES, :].astype(jnp.float32))
            folded = block[:, :LANES]
            for column in range(LANES, width, LANES):
                folded = folded + block[:, column:column + LANES]
            head_sq_ref[:, first:first + LANES] = jnp.sum(folded.T, axis=0, keepdims=True)
    new_copy.wait()


def gather_kernel(members, most, ids_ref, heads_ref, *refs):
    rows_ref = refs[-1]
    head_dev = heads_ref.shape[0]
    near = ids_ref.shape[1]
    me = lax.axis_index("member")
    ids = jnp.concatenate([ids_ref[pl.ds(me ^ member, 1), :] for member in range(members)], axis=0)
    local = ids - me * head_dev
    owned = (local >= 0) & (local < head_dev)
    earlier = (iota((near, near), 0) < iota((near, near), 1)).astype(jnp.bfloat16)
    rank = jnp.dot(owned.astype(jnp.bfloat16), earlier, preferred_element_type=jnp.float32)
    rank = jnp.where(owned, rank.astype(jnp.int32), -1)
    shape = (members, most, near)
    pick = jnp.broadcast_to(rank[:, None, :], shape) == iota(shape, 1)
    wanted = jnp.sum(
        jnp.where(pick, jnp.broadcast_to(local[:, None, :] + 1, shape), 0), axis=2, keepdims=True
    ).reshape(members * most, 1)
    onehot = (wanted == iota((members * most, head_dev), 1) + 1).astype(jnp.bfloat16)
    rows_ref[...] = jnp.dot(
        onehot, heads_ref[...], preferred_element_type=jnp.float32
    ).astype(jnp.bfloat16)


def crowd_kernel(groups, members, heads_ref, head_sq_ref, *refs):
    query_refs, sums_ref = refs[:groups], refs[-1]
    head_dev, width = heads_ref.shape
    new_count = query_refs[0].shape[0]
    here = lax.axis_index("group")
    queries = jnp.concatenate([ref[...] for ref in query_refs], axis=0)
    squares = jnp.square(queries.astype(jnp.float32))
    query_sq = jnp.sum(squares, axis=1, keepdims=True)
    total_w = jnp.zeros((groups * new_count, 1), jnp.float32)
    total_we = jnp.zeros((groups * new_count, 1), jnp.float32)
    tile = 512
    for start in range(0, head_dev, tile):
        dots = lax.dot_general(
            queries, heads_ref[start:start + tile, :], (((1,), (1,)), ((), ())),
            preferred_element_type=jnp.float32,
        )
        head_sq = head_sq_ref[:, start:start + tile]
        excess = (query_sq + head_sq - 2.0 * dots) * (1.0 / width)
        inverse = 1.0 / (1.0 + excess)
        weight = inverse * inverse
        total_w = total_w + jnp.sum(weight, axis=1, keepdims=True)
        total_we = total_we + jnp.sum(weight * excess, axis=1, keepdims=True)
    shape = (new_count, LANES)
    lane = iota(shape, 1)
    row = iota(shape, 0)
    for mask in range(groups):
        part = slice(mask * new_count, (mask + 1) * new_count)
        spread_out = jnp.where(lane == row, total_w[part], 0.0) + jnp.where(
            lane == row + new_count, total_we[part], 0.0
        )
        message = jnp.sum(spread_out, axis=0, keepdims=True)
        first = pl.multiple_of((here ^ mask) * members, members)
        sums_ref[pl.ds(first, members), :] = jnp.broadcast_to(message, (members, LANES))


def near_kernel(most, head_dev, ids_ref, listed_ref, vectors_ref, out_ref):
    near = ids_ref.shape[1]
    width = vectors_ref.shape[2]
    block = vectors_ref.shape[1]
    square = (near, near)
    owner_row = jnp.broadcast_to(lax.div(ids_ref[...], head_dev), square)
    eye = iota(square, 0) == iota(square, 1)
    owner = jnp.sum(jnp.where(eye, owner_row, 0), axis=1, keepdims=True)
    before = (owner_row == owner) & (iota(square, 1) < iota(square, 0))
    place = jnp.sum(before.astype(jnp.int32), axis=1, keepdims=True)
    source = owner * most + place
    back = (source == iota((near, listed_ref.shape[0]), 1)).astype(jnp.bfloat16)
    rows32 = jnp.dot(back, listed_ref[...], preferred_element_type=jnp.float32)
    row_sq = jnp.sum(jnp.square(rows32), axis=1, keepdims=True)
    vec = vectors_ref[0]
    vec_sq = jnp.sum(jnp.square(vec.astype(jnp.float32)), axis=1, keepdims=True)
    turned = iota((block, block), 0) == iota((block, block), 1)
    vec_sq = jnp.sum(jnp.where(turned, vec_sq, 0.0), axis=0, keepdims=True)
    dots = lax.dot_general(
        rows32.astype(jnp.bfloat16), vec, (((1,), (1,)), ((), ())),
        preferred_element_type=jnp.float32,
    )
    out_ref[0] = (row_sq + vec_sq - 2.0 * dots) * (1.0 / width)


def final_kernel(new_count, total_heads, sums_ref, unused, density_ref, spread_ref):
    total = jnp.sum(sums_ref[...], axis=0, keepdims=True)
    total_w = total[:, :new_count]
    total_we = total[:, new_count:2 * new_count]
    density_ref[...] = jnp.log(total_w * (1.0 / total_heads))
    spread_ref[...] = total_we / total_w


def per_device(heads, new_heads, vectors, near_ids):
    head_dev, width = heads.shape
    new_count = new_heads.shape[0]
    near = near_ids.shape[1]
    groups = lax.axis_size("group")
    members = lax.axis_size("member")
    most = 2 * near // members

    ids = lax.optimization_barrier(jnp.maximum(near_ids, 0))
    mask = 1
    while mask < members:
        ids = jnp.concatenate([ids, from_partner(ids, "member", mask)], axis=0)
        mask *= 2
    others = [from_partner(new_heads, "group", mask) for mask in range(1, groups)]
    heads, head_sq, new_heads = pl.pallas_call(
        squares_kernel,
        out_shape=(
            jax.ShapeDtypeStruct((head_dev, width), jnp.bfloat16),
            jax.ShapeDtypeStruct((1, head_dev), jnp.float32),
            jax.ShapeDtypeStruct(new_heads.shape, new_heads.dtype),
        ),
        in_specs=[pl.BlockSpec(memory_space=HBM)] * 2,
        out_specs=(pl.BlockSpec(memory_space=VMEM),) * 3,
        scratch_shapes=[pltpu.SemaphoreType.DMA] * 5,
        compiler_params=pltpu.CompilerParams(vmem_limit_bytes=LIMIT),
        cost_estimate=pl.CostEstimate(
            flops=heads.size * 2, bytes_accessed=heads.size * 2, transcendentals=0
        ),
    )(in_hbm(heads), in_hbm(new_heads))

    rows = call(
        functools.partial(gather_kernel, members, most),
        jax.ShapeDtypeStruct((members * most, width), jnp.bfloat16),
        (ids, heads, *others),
        2 * members * most * head_dev * width,
        heads.size * 2,
        unread=len(others),
    )
    listed = to_each(rows, "member")

    sums = call(
        functools.partial(crowd_kernel, groups, members),
        jax.ShapeDtypeStruct((groups * members, LANES), jnp.float32),
        (heads, head_sq, new_heads, *others, rows),
        2 * groups * new_count * head_dev * width,
        heads.size * 2,
        unread=1,
    )
    sums = to_each(sums, ("group", "member"))
    reassign = call(
        functools.partial(near_kernel, most, head_dev),
        jax.ShapeDtypeStruct((1, near, vectors.shape[1]), jnp.float32),
        (near_ids, listed, vectors),
        4 * near * vectors.shape[1] * width,
        vectors.size * 4,
    )
    density, spread = call(
        functools.partial(final_kernel, new_count, float(head_dev * groups * members)),
        (jax.ShapeDtypeStruct((1, new_count), jnp.float32),) * 2,
        (sums, in_hbm(reassign)),
        groups * members * LANES,
        groups * members * LANES * 4,
        unread=1,
    )
    return (density[0], spread[0], reassign)


def solution(mesh):
    placed = (
        P(("group", "member"), None),
        P("group", None),
        P(("group", "member"), None, None),
        P(("group", "member"), None),
    )
    return jax.shard_map(
        per_device,
        mesh=mesh,
        in_specs=placed,
        out_specs=(P("group"), P("group"), P(("group", "member"), None, None)),
        check_vma=False,
    )
```

```python
import functools

import jax
import jax.numpy as jnp
from jax import lax
from jax.experimental import pallas as pl
from jax.experimental.pallas import tpu as pltpu
from jax.sharding import PartitionSpec as P

VMEM = pltpu.MemorySpace.VMEM
HBM = pltpu.MemorySpace.HBM
LANES = 128
PACK = 16
PARTS = 3
LIMIT = 24 * 2**20


def from_partner(value, axis, mask):
    count = lax.axis_size(axis)
    return lax.ppermute(value, axis, [(source, source ^ mask) for source in range(count)])


def in_hbm(value):
    return pltpu.with_memory_space_constraint(value, HBM)


def call(body, shapes, operands, cost, scratch=(), spaces=None):
    return pl.pallas_call(
        body,
        out_shape=shapes,
        in_specs=[pl.BlockSpec(memory_space=space) for space in spaces or [VMEM] * len(operands)],
        out_specs=jax.tree.map(lambda unused: pl.BlockSpec(memory_space=VMEM), shapes),
        scratch_shapes=scratch,
        compiler_params=pltpu.CompilerParams(vmem_limit_bytes=LIMIT),
        cost_estimate=pl.CostEstimate(flops=cost[0], bytes_accessed=cost[1], transcendentals=0),
    )(*operands)


def iota(shape, dim):
    return lax.broadcasted_iota(jnp.int32, shape, dim)


def early_kernel(
    heads_ref, new_ref, ids_ref, other_ref, kept_ref, head_sq_ref, pair_ref, kept_ids_ref, sems
):
    head_dev, width = heads_ref.shape
    new_count = new_ref.shape[0]
    tiles = 4
    tile = head_dev // tiles
    parts = [pl.ds(i * tile, tile) for i in range(tiles)]
    copies = [
        pltpu.make_async_copy(heads_ref.at[part], kept_ref.at[part], sems.at[i])
        for i, part in enumerate(parts)
    ]
    copies += [
        pltpu.make_async_copy(new_ref, pair_ref.at[pl.ds(0, new_count)], sems.at[tiles]),
        pltpu.make_async_copy(ids_ref, kept_ids_ref, sems.at[tiles + 1]),
    ]
    for copy in copies:
        copy.start()
    pair_ref[new_count:, :] = other_ref[...]
    for i in range(tiles):
        copies[i].wait()
        for first in range(i * tile, (i + 1) * tile, LANES):
            block = jnp.square(kept_ref[first:first + LANES, :].astype(jnp.float32))
            folded = block[:, :LANES]
            for column in range(LANES, width, LANES):
                folded = folded + block[:, column:column + LANES]
            head_sq_ref[:, first:first + LANES] = jnp.sum(folded.T, axis=0, keepdims=True)
    for copy in copies[tiles:]:
        copy.wait()


def listed_rows(ids, me, slots, heads_ref):
    members, near = ids.shape
    head_dev = heads_ref.shape[0]
    local = ids - me * head_dev
    owned = (local >= 0) & (local < head_dev)
    earlier = (iota((near, near), 0) < iota((near, near), 1)).astype(jnp.bfloat16)
    rank = jnp.dot(owned.astype(jnp.bfloat16), earlier, preferred_element_type=jnp.float32)
    rank = jnp.where(owned, rank.astype(jnp.int32), -1)
    shape = (members, slots, near)
    pick = jnp.broadcast_to(rank[:, None, :], shape) == iota(shape, 1)
    wanted = jnp.sum(
        jnp.where(pick, jnp.broadcast_to(local[:, None, :] + 1, shape), 0), axis=2, keepdims=True
    ).reshape(members * slots, 1)
    onehot = (wanted == iota((members * slots, head_dev), 1) + 1).astype(jnp.bfloat16)
    return jnp.dot(
        onehot, heads_ref[...], preferred_element_type=jnp.float32
    ).astype(jnp.bfloat16)


def crowding(queries, heads_ref, head_sq_ref):
    head_dev, width = heads_ref.shape
    query_sq = jnp.sum(jnp.square(queries.astype(jnp.float32)), axis=1, keepdims=True)
    total_w = jnp.zeros((queries.shape[0], 1), jnp.float32)
    total_we = jnp.zeros((queries.shape[0], 1), jnp.float32)
    tile = 512
    for start in range(0, head_dev, tile):
        dots = lax.dot_general(
            queries, heads_ref[start:start + tile, :], (((1,), (1,)), ((), ())),
            preferred_element_type=jnp.float32,
        )
        head_sq = head_sq_ref[:, start:start + tile]
        excess = (query_sq + head_sq - 2.0 * dots) * (1.0 / width)
        inverse = 1.0 / (1.0 + excess)
        weight = inverse * inverse
        total_w = total_w + jnp.sum(weight, axis=1, keepdims=True)
        total_we = total_we + jnp.sum(weight * excess, axis=1, keepdims=True)
    return total_w, total_we


def message_kernel(groups, members, slots, ids_ref, heads_ref, head_sq_ref, *refs):
    query_refs, out_ref = refs[:-1], refs[-1]
    width = heads_ref.shape[1]
    here = lax.axis_index("group")
    me = lax.axis_index("member")
    ids = jnp.concatenate([ids_ref[pl.ds(me ^ member, 1), :] for member in range(members)], axis=0)
    rows = listed_rows(ids, me, slots, heads_ref)
    chunks = width // LANES
    for member in range(members):
        for chunk in range(chunks):
            out_ref[member, chunk * slots:(chunk + 1) * slots, :] = rows[
                member * slots:(member + 1) * slots, chunk * LANES:(chunk + 1) * LANES
            ]

    queries = jnp.concatenate([ref[...] for ref in query_refs], axis=0)
    new_count = queries.shape[0] // groups
    totals = crowding(queries, heads_ref, head_sq_ref)
    lines = 2 * groups * new_count // LANES
    lane = iota((new_count, LANES), 1)
    row = iota((new_count, LANES), 0)
    line = iota((lines, LANES), 0)
    sums = jnp.zeros((lines, LANES), jnp.float32)
    for mask in range(groups):
        part = slice(mask * new_count, (mask + 1) * new_count)
        for kind in range(2):
            place = (kind * groups + (here ^ mask)) * new_count
            spread_out = jnp.where(lane == row + place % LANES, totals[kind][part], 0.0)
            spread_out = jnp.sum(spread_out, axis=0, keepdims=True)
            sums = sums + jnp.where(line == place // LANES, spread_out, 0.0)
    coded = []
    for unused in range(PARTS):
        coded.append(sums.astype(jnp.bfloat16).astype(jnp.float32))
        sums = sums - coded[-1]
    extra = out_ref.shape[1] - chunks * slots
    if extra > PARTS * lines:
        coded.append(jnp.zeros((extra - PARTS * lines, LANES), jnp.float32))
    tail = jnp.concatenate(coded, axis=0).astype(jnp.bfloat16)
    for member in range(members):
        out_ref[member, chunks * slots:, :] = tail


def near_kernel(most, slots, head_dev, ids_ref, listed_ref, vectors_ref, out_ref):
    near = ids_ref.shape[1]
    members = listed_ref.shape[0]
    block, width = vectors_ref.shape[1:]
    square = (near, near)
    owner_row = jnp.broadcast_to(lax.div(ids_ref[...], head_dev), square)
    eye = iota(square, 0) == iota(square, 1)
    owner = jnp.sum(jnp.where(eye, owner_row, 0), axis=1, keepdims=True)
    before = (owner_row == owner) & (iota(square, 1) < iota(square, 0))
    place = jnp.sum(before.astype(jnp.int32), axis=1, keepdims=True)
    source = owner * slots + place
    back = (source == iota((near, members * slots), 1)).astype(jnp.bfloat16)
    rows = []
    for chunk in range(width // LANES):
        part = listed_ref[:, chunk * slots:(chunk + 1) * slots, :].reshape(members * slots, LANES)
        rows.append(jnp.dot(back, part, preferred_element_type=jnp.float32))
    rows = jnp.concatenate(rows, axis=1)
    row_sq = jnp.sum(jnp.square(rows), axis=1, keepdims=True)
    vec = vectors_ref[0]
    vec_sq = jnp.sum(jnp.square(vec.astype(jnp.float32)), axis=1, keepdims=True)
    turned = iota((block, block), 0) == iota((block, block), 1)
    vec_sq = jnp.sum(jnp.where(turned, vec_sq, 0.0), axis=0, keepdims=True)
    dots = lax.dot_general(
        rows.astype(jnp.bfloat16), vec, (((1,), (1,)), ((), ())),
        preferred_element_type=jnp.float32,
    )
    out_ref[0] = (row_sq + vec_sq - 2.0 * dots) * (1.0 / width)


def final_kernel(groups, new_count, total_heads, mine_ref, other_ref, density_ref, spread_ref):
    here = lax.axis_index("group")
    total = mine_ref[...] + other_ref[...]
    lines = total.shape[0]
    shape = (new_count, LANES)
    eye = iota((new_count, new_count), 0) == iota((new_count, new_count), 1)
    found = []
    for kind in range(2):
        place = (kind * groups + here) * new_count
        line = jnp.sum(
            jnp.where(iota((lines, LANES), 0) == place // LANES, total, 0.0), axis=0, keepdims=True
        )
        column = jnp.sum(
            jnp.where(iota(shape, 1) == iota(shape, 0) + place % LANES, line, 0.0),
            axis=1, keepdims=True,
        )
        found.append(jnp.sum(jnp.where(eye, column, 0.0), axis=0, keepdims=True))
    density_ref[...] = jnp.log(found[0] * (1.0 / total_heads))
    spread_ref[...] = found[1] / found[0]


def per_device(heads, new_heads, vectors, near_ids):
    head_dev, width = heads.shape
    new_count = new_heads.shape[0]
    near = near_ids.shape[1]
    groups = lax.axis_size("group")
    members = lax.axis_size("member")
    most = 2 * near // members
    slots = -(-most // PACK) * PACK

    partner_ids = from_partner(near_ids, "member", 1)
    partner_new = from_partner(new_heads, "group", 1)
    kept, head_sq, pair, ids = call(
        early_kernel,
        (
            jax.ShapeDtypeStruct(heads.shape, heads.dtype),
            jax.ShapeDtypeStruct((1, head_dev), jnp.float32),
            jax.ShapeDtypeStruct((2 * new_count, width), new_heads.dtype),
            jax.ShapeDtypeStruct(near_ids.shape, near_ids.dtype),
        ),
        (in_hbm(heads), in_hbm(new_heads), in_hbm(near_ids), partner_new),
        (heads.size * 2, heads.size * 2),
        scratch=[pltpu.SemaphoreType.DMA((6,))],
        spaces=[HBM, HBM, HBM, VMEM],
    )
    ids = jnp.concatenate([ids, partner_ids], axis=0)
    mask = 2
    while mask < members:
        ids = jnp.concatenate([ids, from_partner(ids, "member", mask)], axis=0)
        mask *= 2
    blocks = [pair]
    mask = 2
    while mask < groups:
        blocks.append(from_partner(jnp.concatenate(blocks, axis=0), "group", mask))
        mask *= 2

    lines = 2 * groups * new_count // LANES
    chunks = width // LANES
    extra = -(-PARTS * lines // PACK) * PACK
    message = call(
        functools.partial(message_kernel, groups, members, slots),
        jax.ShapeDtypeStruct((members, chunks * slots + extra, LANES), jnp.bfloat16),
        (ids, kept, head_sq, *blocks),
        (2 * (members * slots + groups * new_count) * head_dev * width, heads.size * 4),
    )
    message = lax.all_to_all(message, "member", 0, 0, tiled=True)

    coded = message[:, chunks * slots:chunks * slots + PARTS * lines, :].astype(jnp.float32)
    total = jnp.sum(coded.reshape(members * PARTS, lines, LANES), axis=0)
    mask = groups // 2
    while mask > 1:
        total = total + from_partner(total, "group", mask)
        mask //= 2
    density, spread = call(
        functools.partial(
            final_kernel, groups, new_count, float(head_dev * groups * members)
        ),
        (jax.ShapeDtypeStruct((1, new_count), jnp.float32),) * 2,
        (total, from_partner(total, "group", 1)),
        (lines * LANES, lines * LANES * 4),
    )
    reassign = call(
        functools.partial(near_kernel, most, slots, head_dev),
        jax.ShapeDtypeStruct((1, near, vectors.shape[1]), jnp.float32),
        (near_ids, message, vectors),
        (4 * near * vectors.shape[1] * width, vectors.size * 4),
    )
    return (density[0], spread[0], reassign)


def solution(mesh):
    placed = (
        P(("group", "member"), None),
        P("group", None),
        P(("group", "member"), None, None),
        P(("group", "member"), None),
    )
    return jax.shard_map(
        per_device,
        mesh=mesh,
        in_specs=placed,
        out_specs=(P("group"), P("group"), P(("group", "member"), None, None)),
        check_vma=False,
    )
```

```python
import functools

import jax
import jax.numpy as jnp
from jax import lax
from jax.experimental import pallas as pl
from jax.experimental.pallas import tpu as pltpu
from jax.sharding import PartitionSpec as P

VMEM = pltpu.MemorySpace.VMEM
HBM = pltpu.MemorySpace.HBM
LANES = 128
PACK = 16
PARTS = 3
LIMIT = 24 * 2**20


def from_partner(value, axis, mask):
    count = lax.axis_size(axis)
    return lax.ppermute(value, axis, [(source, source ^ mask) for source in range(count)])


def in_hbm(value):
    return pltpu.with_memory_space_constraint(value, HBM)


def call(body, shapes, operands, cost, scratch=(), spaces=None):
    return pl.pallas_call(
        body,
        out_shape=shapes,
        in_specs=[pl.BlockSpec(memory_space=space) for space in spaces or [VMEM] * len(operands)],
        out_specs=jax.tree.map(lambda unused: pl.BlockSpec(memory_space=VMEM), shapes),
        scratch_shapes=scratch,
        compiler_params=pltpu.CompilerParams(vmem_limit_bytes=LIMIT),
        cost_estimate=pl.CostEstimate(flops=cost[0], bytes_accessed=cost[1], transcendentals=0),
    )(*operands)


def iota(shape, dim):
    return lax.broadcasted_iota(jnp.int32, shape, dim)


def early_kernel(
    heads_ref, new_ref, ids_ref, other_ref, kept_ref, head_sq_ref, pair_ref, kept_ids_ref, sems
):
    head_dev, width = heads_ref.shape
    new_count = new_ref.shape[0]
    tiles = 4
    tile = head_dev // tiles
    parts = [pl.ds(i * tile, tile) for i in range(tiles)]
    copies = [
        pltpu.make_async_copy(heads_ref.at[part], kept_ref.at[part], sems.at[i])
        for i, part in enumerate(parts)
    ]
    copies += [
        pltpu.make_async_copy(new_ref, pair_ref.at[pl.ds(0, new_count)], sems.at[tiles]),
        pltpu.make_async_copy(ids_ref, kept_ids_ref, sems.at[tiles + 1]),
    ]
    for copy in copies:
        copy.start()
    pair_ref[new_count:, :] = other_ref[...]
    for i in range(tiles):
        copies[i].wait()
        for first in range(i * tile, (i + 1) * tile, LANES):
            block = jnp.square(kept_ref[first:first + LANES, :].astype(jnp.float32))
            folded = block[:, :LANES]
            for column in range(LANES, width, LANES):
                folded = folded + block[:, column:column + LANES]
            head_sq_ref[:, first:first + LANES] = jnp.sum(folded.T, axis=0, keepdims=True)
    for copy in copies[tiles:]:
        copy.wait()


def listed_rows(ids, me, slots, heads_ref):
    members, near = ids.shape
    head_dev = heads_ref.shape[0]
    local = ids - me * head_dev
    owned = (local >= 0) & (local < head_dev)
    earlier = (iota((near, near), 0) < iota((near, near), 1)).astype(jnp.bfloat16)
    rank = jnp.dot(owned.astype(jnp.bfloat16), earlier, preferred_element_type=jnp.float32)
    rank = jnp.where(owned, rank.astype(jnp.int32), -1)
    shape = (members, slots, near)
    pick = jnp.broadcast_to(rank[:, None, :], shape) == iota(shape, 1)
    wanted = jnp.sum(
        jnp.where(pick, jnp.broadcast_to(local[:, None, :] + 1, shape), 0), axis=2, keepdims=True
    ).reshape(members * slots, 1)
    onehot = (wanted == iota((members * slots, head_dev), 1) + 1).astype(jnp.bfloat16)
    return jnp.dot(
        onehot, heads_ref[...], preferred_element_type=jnp.float32
    ).astype(jnp.bfloat16)


def crowding(queries, heads_ref, head_sq_ref):
    head_dev, width = heads_ref.shape
    query_sq = jnp.sum(jnp.square(queries.astype(jnp.float32)), axis=1, keepdims=True)
    total_w = jnp.zeros((queries.shape[0], 1), jnp.float32)
    total_we = jnp.zeros((queries.shape[0], 1), jnp.float32)
    tile = 512
    for start in range(0, head_dev, tile):
        dots = lax.dot_general(
            queries, heads_ref[start:start + tile, :], (((1,), (1,)), ((), ())),
            preferred_element_type=jnp.float32,
        )
        head_sq = head_sq_ref[:, start:start + tile]
        excess = (query_sq + head_sq - 2.0 * dots) * (1.0 / width)
        inverse = 1.0 / (1.0 + excess)
        weight = inverse * inverse
        total_w = total_w + jnp.sum(weight, axis=1, keepdims=True)
        total_we = total_we + jnp.sum(weight * excess, axis=1, keepdims=True)
    return total_w, total_we


def crowd_kernel(groups, heads_ref, head_sq_ref, *refs):
    query_refs, sums_ref = refs[:-1], refs[-1]
    here = lax.axis_index("group")
    queries = jnp.concatenate([ref[...] for ref in query_refs], axis=0)
    new_count = queries.shape[0] // groups
    totals = crowding(queries, heads_ref, head_sq_ref)
    lane = iota((new_count, LANES), 1)
    row = iota((new_count, LANES), 0)
    line = iota(sums_ref.shape, 0)
    sums = jnp.zeros(sums_ref.shape, jnp.float32)
    for mask in range(groups):
        part = slice(mask * new_count, (mask + 1) * new_count)
        for kind in range(2):
            place = (kind * groups + (here ^ mask)) * new_count
            spread_out = jnp.where(lane == row + place % LANES, totals[kind][part], 0.0)
            spread_out = jnp.sum(spread_out, axis=0, keepdims=True)
            sums = sums + jnp.where(line == place // LANES, spread_out, 0.0)
    sums_ref[...] = sums


def gather_kernel(members, slots, ids_ref, heads_ref, unused, rows_ref):
    me = lax.axis_index("member")
    ids = jnp.concatenate([ids_ref[pl.ds(me ^ member, 1), :] for member in range(members)], axis=0)
    rows_ref[...] = listed_rows(ids, me, slots, heads_ref)


def pack_kernel(members, slots, rows_ref, mine_ref, other_ref, out_ref):
    chunks = rows_ref.shape[1] // LANES
    for member in range(members):
        for chunk in range(chunks):
            out_ref[member, chunk * slots:(chunk + 1) * slots, :] = rows_ref[
                member * slots:(member + 1) * slots, chunk * LANES:(chunk + 1) * LANES
            ]
    sums = mine_ref[...] + other_ref[...]
    coded = []
    for unused in range(PARTS):
        coded.append(sums.astype(jnp.bfloat16).astype(jnp.float32))
        sums = sums - coded[-1]
    missing = out_ref.shape[1] - chunks * slots - PARTS * sums.shape[0]
    if missing:
        coded.append(jnp.zeros((missing, LANES), jnp.float32))
    tail = jnp.concatenate(coded, axis=0).astype(jnp.bfloat16)
    for member in range(members):
        out_ref[member, chunks * slots:, :] = tail


def distances(slots, head_dev, ids_ref, listed_ref, vectors_ref, out_ref):
    near = ids_ref.shape[1]
    members = listed_ref.shape[0]
    block, width = vectors_ref.shape[1:]
    square = (near, near)
    owner_row = jnp.broadcast_to(lax.div(ids_ref[...], head_dev), square)
    eye = iota(square, 0) == iota(square, 1)
    owner = jnp.sum(jnp.where(eye, owner_row, 0), axis=1, keepdims=True)
    before = (owner_row == owner) & (iota(square, 1) < iota(square, 0))
    place = jnp.sum(before.astype(jnp.int32), axis=1, keepdims=True)
    source = owner * slots + place
    back = (source == iota((near, members * slots), 1)).astype(jnp.bfloat16)
    rows = []
    for chunk in range(width // LANES):
        part = listed_ref[:, chunk * slots:(chunk + 1) * slots, :].reshape(members * slots, LANES)
        rows.append(jnp.dot(back, part, preferred_element_type=jnp.float32))
    rows = jnp.concatenate(rows, axis=1)
    row_sq = jnp.sum(jnp.square(rows), axis=1, keepdims=True)
    vec = vectors_ref[0]
    vec_sq = jnp.sum(jnp.square(vec.astype(jnp.float32)), axis=1, keepdims=True)
    turned = iota((block, block), 0) == iota((block, block), 1)
    vec_sq = jnp.sum(jnp.where(turned, vec_sq, 0.0), axis=0, keepdims=True)
    dots = lax.dot_general(
        rows.astype(jnp.bfloat16), vec, (((1,), (1,)), ((), ())),
        preferred_element_type=jnp.float32,
    )
    out_ref[0] = (row_sq + vec_sq - 2.0 * dots) * (1.0 / width)


def tail_kernel(
    groups, slots, head_dev, total_heads, ids_ref, listed_ref, vectors_ref,
    density_ref, spread_ref, out_ref,
):
    distances(slots, head_dev, ids_ref, listed_ref, vectors_ref, out_ref)
    here = lax.axis_index("group")
    members = listed_ref.shape[0]
    new_count = density_ref.shape[1]
    lines = 2 * groups * new_count // LANES
    first = vectors_ref.shape[2] // LANES * slots
    coded = jnp.sum(listed_ref[:, first:, :].astype(jnp.float32), axis=0)
    total = sum(coded[part * lines:(part + 1) * lines] for part in range(PARTS))
    shape = (new_count, LANES)
    eye = iota((new_count, new_count), 0) == iota((new_count, new_count), 1)
    found = []
    for kind in range(2):
        place = (kind * groups + here) * new_count
        line = jnp.sum(
            jnp.where(iota((lines, LANES), 0) == place // LANES, total, 0.0), axis=0, keepdims=True
        )
        column = jnp.sum(
            jnp.where(iota(shape, 1) == iota(shape, 0) + place % LANES, line, 0.0),
            axis=1, keepdims=True,
        )
        found.append(jnp.sum(jnp.where(eye, column, 0.0), axis=0, keepdims=True))
    density_ref[...] = jnp.log(found[0] * (1.0 / total_heads))
    spread_ref[...] = found[1] / found[0]


def per_device(heads, new_heads, vectors, near_ids):
    head_dev, width = heads.shape
    new_count = new_heads.shape[0]
    near = near_ids.shape[1]
    groups = lax.axis_size("group")
    members = lax.axis_size("member")
    most = 2 * near // members
    slots = -(-most // PACK) * PACK

    partner_ids = from_partner(near_ids, "member", 1)
    partner_new = from_partner(new_heads, "group", 1)
    kept, head_sq, pair, ids = call(
        early_kernel,
        (
            jax.ShapeDtypeStruct(heads.shape, heads.dtype),
            jax.ShapeDtypeStruct((1, head_dev), jnp.float32),
            jax.ShapeDtypeStruct((2 * new_count, width), new_heads.dtype),
            jax.ShapeDtypeStruct(near_ids.shape, near_ids.dtype),
        ),
        (in_hbm(heads), in_hbm(new_heads), in_hbm(near_ids), partner_new),
        (heads.size * 2, heads.size * 2),
        scratch=[pltpu.SemaphoreType.DMA((6,))],
        spaces=[HBM, HBM, HBM, VMEM],
    )
    ids = jnp.concatenate([ids, partner_ids], axis=0)
    mask = 2
    while mask < members:
        ids = jnp.concatenate([ids, from_partner(ids, "member", mask)], axis=0)
        mask *= 2
    blocks = [pair]
    mask = 2
    while mask < groups:
        blocks.append(from_partner(jnp.concatenate(blocks, axis=0), "group", mask))
        mask *= 2

    lines = 2 * groups * new_count // LANES
    chunks = width // LANES
    extra = -(-PARTS * lines // PACK) * PACK
    sums = call(
        functools.partial(crowd_kernel, groups),
        jax.ShapeDtypeStruct((lines, LANES), jnp.float32),
        (kept, head_sq, *blocks),
        (2 * groups * new_count * head_dev * width, heads.size * 2),
    )
    mask = 1
    while mask < groups // 2:
        sums = sums + from_partner(sums, "group", mask)
        mask *= 2
    rows = call(
        functools.partial(gather_kernel, members, slots),
        jax.ShapeDtypeStruct((members * slots, width), jnp.bfloat16),
        (ids, kept, sums),
        (2 * members * slots * head_dev * width, heads.size * 2),
        spaces=[VMEM, VMEM, pl.ANY],
    )
    message = call(
        functools.partial(pack_kernel, members, slots),
        jax.ShapeDtypeStruct((members, chunks * slots + extra, LANES), jnp.bfloat16),
        (rows, sums, from_partner(sums, "group", mask)),
        (0, members * slots * width * 4),
    )
    message = lax.all_to_all(message, "member", 0, 0, tiled=True)

    density, spread, reassign = call(
        functools.partial(
            tail_kernel, groups, slots, head_dev, float(head_dev * groups * members)
        ),
        (
            jax.ShapeDtypeStruct((1, new_count), jnp.float32),
            jax.ShapeDtypeStruct((1, new_count), jnp.float32),
            jax.ShapeDtypeStruct((1, near, vectors.shape[1]), jnp.float32),
        ),
        (near_ids, message, vectors),
        (4 * near * vectors.shape[1] * width, vectors.size * 4),
    )
    return (density[0], spread[0], reassign)


def solution(mesh):
    placed = (
        P(("group", "member"), None),
        P("group", None),
        P(("group", "member"), None, None),
        P(("group", "member"), None),
    )
    return jax.shard_map(
        per_device,
        mesh=mesh,
        in_specs=placed,
        out_specs=(P("group"), P("group"), P(("group", "member"), None, None)),
        check_vma=False,
    )
```

```python
import functools

import jax
import jax.numpy as jnp
from jax import lax
from jax.experimental import pallas as pl
from jax.experimental.pallas import tpu as pltpu
from jax.sharding import PartitionSpec as P

VMEM = pltpu.MemorySpace.VMEM
HBM = pltpu.MemorySpace.HBM
LANES = 128
PACK = 16
PARTS = 3
LIMIT = 24 * 2**20


def from_partner(value, axis, mask):
    count = lax.axis_size(axis)
    return lax.ppermute(value, axis, [(source, source ^ mask) for source in range(count)])


def in_hbm(value):
    return pltpu.with_memory_space_constraint(value, HBM)


def call(body, shapes, operands, cost, scratch=(), spaces=None):
    return pl.pallas_call(
        body,
        out_shape=shapes,
        in_specs=[pl.BlockSpec(memory_space=space) for space in spaces or [VMEM] * len(operands)],
        out_specs=jax.tree.map(lambda unused: pl.BlockSpec(memory_space=VMEM), shapes),
        scratch_shapes=scratch,
        compiler_params=pltpu.CompilerParams(vmem_limit_bytes=LIMIT),
        cost_estimate=pl.CostEstimate(flops=cost[0], bytes_accessed=cost[1], transcendentals=0),
    )(*operands)


def iota(shape, dim):
    return lax.broadcasted_iota(jnp.int32, shape, dim)


def early_kernel(
    heads_ref, new_ref, ids_ref, other_ref, kept_ref, head_sq_ref, pair_ref, kept_ids_ref, sems
):
    head_dev, width = heads_ref.shape
    new_count = new_ref.shape[0]
    tiles = 4
    tile = head_dev // tiles
    parts = [pl.ds(i * tile, tile) for i in range(tiles)]
    copies = [
        pltpu.make_async_copy(heads_ref.at[part], kept_ref.at[part], sems.at[i])
        for i, part in enumerate(parts)
    ]
    copies += [
        pltpu.make_async_copy(new_ref, pair_ref.at[pl.ds(0, new_count)], sems.at[tiles]),
        pltpu.make_async_copy(ids_ref, kept_ids_ref, sems.at[tiles + 1]),
    ]
    for copy in copies:
        copy.start()
    pair_ref[new_count:, :] = other_ref[...]
    for i in range(tiles):
        copies[i].wait()
        for first in range(i * tile, (i + 1) * tile, LANES):
            block = jnp.square(kept_ref[first:first + LANES, :].astype(jnp.float32))
            folded = block[:, :LANES]
            for column in range(LANES, width, LANES):
                folded = folded + block[:, column:column + LANES]
            head_sq_ref[:, first:first + LANES] = jnp.sum(folded.T, axis=0, keepdims=True)
    for copy in copies[tiles:]:
        copy.wait()


def listed_rows(ids, me, slots, heads_ref):
    members, near = ids.shape
    head_dev = heads_ref.shape[0]
    local = ids - me * head_dev
    owned = (local >= 0) & (local < head_dev)
    earlier = (iota((near, near), 0) < iota((near, near), 1)).astype(jnp.bfloat16)
    rank = jnp.dot(owned.astype(jnp.bfloat16), earlier, preferred_element_type=jnp.float32)
    rank = jnp.where(owned, rank.astype(jnp.int32), -1)
    shape = (members, slots, near)
    pick = jnp.broadcast_to(rank[:, None, :], shape) == iota(shape, 1)
    wanted = jnp.sum(
        jnp.where(pick, jnp.broadcast_to(local[:, None, :] + 1, shape), 0), axis=2, keepdims=True
    ).reshape(members * slots, 1)
    onehot = (wanted == iota((members * slots, head_dev), 1) + 1).astype(jnp.bfloat16)
    return jnp.dot(
        onehot, heads_ref[...], preferred_element_type=jnp.float32
    ).astype(jnp.bfloat16)


def crowding(queries, heads_ref, head_sq_ref):
    head_dev, width = heads_ref.shape
    query_sq = jnp.sum(jnp.square(queries.astype(jnp.float32)), axis=1, keepdims=True)
    total_w = jnp.zeros((queries.shape[0], 1), jnp.float32)
    total_we = jnp.zeros((queries.shape[0], 1), jnp.float32)
    tile = 512
    for start in range(0, head_dev, tile):
        dots = lax.dot_general(
            queries, heads_ref[start:start + tile, :], (((1,), (1,)), ((), ())),
            preferred_element_type=jnp.float32,
        )
        head_sq = head_sq_ref[:, start:start + tile]
        excess = (query_sq + head_sq - 2.0 * dots) * (1.0 / width)
        inverse = 1.0 / (1.0 + excess)
        weight = inverse * inverse
        total_w = total_w + jnp.sum(weight, axis=1, keepdims=True)
        total_we = total_we + jnp.sum(weight * excess, axis=1, keepdims=True)
    return total_w, total_we


def crowd_kernel(groups, heads_ref, head_sq_ref, *refs):
    query_refs, sums_ref = refs[:-1], refs[-1]
    here = lax.axis_index("group")
    queries = jnp.concatenate([ref[...] for ref in query_refs], axis=0)
    new_count = queries.shape[0] // groups
    totals = crowding(queries, heads_ref, head_sq_ref)
    lane = iota((new_count, LANES), 1)
    row = iota((new_count, LANES), 0)
    line = iota(sums_ref.shape, 0)
    sums = jnp.zeros(sums_ref.shape, jnp.float32)
    for mask in range(groups):
        part = slice(mask * new_count, (mask + 1) * new_count)
        for kind in range(2):
            place = (kind * groups + (here ^ mask)) * new_count
            spread_out = jnp.where(lane == row + place % LANES, totals[kind][part], 0.0)
            spread_out = jnp.sum(spread_out, axis=0, keepdims=True)
            sums = sums + jnp.where(line == place // LANES, spread_out, 0.0)
    sums_ref[...] = sums


def gather_kernel(members, slots, near_ref, far_ref, heads_ref, unused, rows_ref, ids_ref):
    me = lax.axis_index("member")
    half = members // 2
    ids_ref[:half, :] = near_ref[...]
    ids_ref[half:, :] = far_ref[...]
    ids = jnp.concatenate([ids_ref[pl.ds(me ^ member, 1), :] for member in range(members)], axis=0)
    rows_ref[...] = listed_rows(ids, me, slots, heads_ref)


def pack_kernel(members, slots, rows_ref, mine_ref, other_ref, out_ref):
    chunks = rows_ref.shape[1] // LANES
    for member in range(members):
        for chunk in range(chunks):
            out_ref[member, chunk * slots:(chunk + 1) * slots, :] = rows_ref[
                member * slots:(member + 1) * slots, chunk * LANES:(chunk + 1) * LANES
            ]
    sums = mine_ref[...] + other_ref[...]
    coded = []
    for unused in range(PARTS):
        coded.append(sums.astype(jnp.bfloat16).astype(jnp.float32))
        sums = sums - coded[-1]
    missing = out_ref.shape[1] - chunks * slots - PARTS * sums.shape[0]
    if missing:
        coded.append(jnp.zeros((missing, LANES), jnp.float32))
    tail = jnp.concatenate(coded, axis=0).astype(jnp.bfloat16)
    for member in range(members):
        out_ref[member, chunks * slots:, :] = tail


def distances(slots, head_dev, ids_ref, listed_ref, vectors_ref, out_ref):
    near = ids_ref.shape[1]
    members = listed_ref.shape[0]
    block, width = vectors_ref.shape[1:]
    square = (near, near)
    owner_row = jnp.broadcast_to(lax.div(ids_ref[...], head_dev), square)
    eye = iota(square, 0) == iota(square, 1)
    owner = jnp.sum(jnp.where(eye, owner_row, 0), axis=1, keepdims=True)
    before = (owner_row == owner) & (iota(square, 1) < iota(square, 0))
    place = jnp.sum(before.astype(jnp.int32), axis=1, keepdims=True)
    source = owner * slots + place
    back = (source == iota((near, members * slots), 1)).astype(jnp.bfloat16)
    rows = []
    for chunk in range(width // LANES):
        part = listed_ref[:, chunk * slots:(chunk + 1) * slots, :].reshape(members * slots, LANES)
        rows.append(jnp.dot(back, part, preferred_element_type=jnp.float32))
    rows = jnp.concatenate(rows, axis=1)
    row_sq = jnp.sum(jnp.square(rows), axis=1, keepdims=True)
    vec = vectors_ref[0]
    vec_sq = jnp.sum(jnp.square(vec.astype(jnp.float32)), axis=1, keepdims=True)
    turned = iota((block, block), 0) == iota((block, block), 1)
    vec_sq = jnp.sum(jnp.where(turned, vec_sq, 0.0), axis=0, keepdims=True)
    dots = lax.dot_general(
        rows.astype(jnp.bfloat16), vec, (((1,), (1,)), ((), ())),
        preferred_element_type=jnp.float32,
    )
    out_ref[0] = (row_sq + vec_sq - 2.0 * dots) * (1.0 / width)


def tail_kernel(
    groups, slots, head_dev, total_heads, ids_ref, listed_ref, vectors_ref,
    density_ref, spread_ref, out_ref,
):
    distances(slots, head_dev, ids_ref, listed_ref, vectors_ref, out_ref)
    here = lax.axis_index("group")
    members = listed_ref.shape[0]
    new_count = density_ref.shape[1]
    lines = 2 * groups * new_count // LANES
    first = vectors_ref.shape[2] // LANES * slots
    coded = jnp.sum(listed_ref[:, first:, :].astype(jnp.float32), axis=0)
    total = sum(coded[part * lines:(part + 1) * lines] for part in range(PARTS))
    shape = (new_count, LANES)
    eye = iota((new_count, new_count), 0) == iota((new_count, new_count), 1)
    found = []
    for kind in range(2):
        place = (kind * groups + here) * new_count
        line = jnp.sum(
            jnp.where(iota((lines, LANES), 0) == place // LANES, total, 0.0), axis=0, keepdims=True
        )
        column = jnp.sum(
            jnp.where(iota(shape, 1) == iota(shape, 0) + place % LANES, line, 0.0),
            axis=1, keepdims=True,
        )
        found.append(jnp.sum(jnp.where(eye, column, 0.0), axis=0, keepdims=True))
    density_ref[...] = jnp.log(found[0] * (1.0 / total_heads))
    spread_ref[...] = found[1] / found[0]


def per_device(heads, new_heads, vectors, near_ids):
    head_dev, width = heads.shape
    new_count = new_heads.shape[0]
    near = near_ids.shape[1]
    groups = lax.axis_size("group")
    members = lax.axis_size("member")
    most = 2 * near // members
    slots = -(-most // PACK) * PACK

    partner_ids = from_partner(near_ids, "member", 1)
    partner_new = from_partner(new_heads, "group", 1)
    kept, head_sq, pair, ids = call(
        early_kernel,
        (
            jax.ShapeDtypeStruct(heads.shape, heads.dtype),
            jax.ShapeDtypeStruct((1, head_dev), jnp.float32),
            jax.ShapeDtypeStruct((2 * new_count, width), new_heads.dtype),
            jax.ShapeDtypeStruct(near_ids.shape, near_ids.dtype),
        ),
        (in_hbm(heads), in_hbm(new_heads), in_hbm(near_ids), partner_new),
        (heads.size * 2, heads.size * 2),
        scratch=[pltpu.SemaphoreType.DMA((6,))],
        spaces=[HBM, HBM, HBM, VMEM],
    )
    ids = jnp.concatenate([ids, partner_ids], axis=0)
    mask = 2
    while mask < members // 2:
        ids = jnp.concatenate([ids, from_partner(ids, "member", mask)], axis=0)
        mask *= 2
    far_ids = from_partner(ids, "member", mask)
    blocks = [pair]
    mask = 2
    while mask < groups:
        blocks.append(from_partner(jnp.concatenate(blocks, axis=0), "group", mask))
        mask *= 2

    lines = 2 * groups * new_count // LANES
    chunks = width // LANES
    extra = -(-PARTS * lines // PACK) * PACK
    sums = call(
        functools.partial(crowd_kernel, groups),
        jax.ShapeDtypeStruct((lines, LANES), jnp.float32),
        (kept, head_sq, *blocks),
        (2 * groups * new_count * head_dev * width, heads.size * 2),
    )
    mask = 1
    while mask < groups // 2:
        sums = sums + from_partner(sums, "group", mask)
        mask *= 2
    rows = call(
        functools.partial(gather_kernel, members, slots),
        jax.ShapeDtypeStruct((members * slots, width), jnp.bfloat16),
        (ids, far_ids, kept, sums),
        (2 * members * slots * head_dev * width, heads.size * 2),
        scratch=[pltpu.VMEM((members, near), jnp.int32)],
        spaces=[VMEM, VMEM, VMEM, pl.ANY],
    )
    message = call(
        functools.partial(pack_kernel, members, slots),
        jax.ShapeDtypeStruct((members, chunks * slots + extra, LANES), jnp.bfloat16),
        (rows, sums, from_partner(sums, "group", mask)),
        (0, members * slots * width * 4),
    )
    message = lax.all_to_all(message, "member", 0, 0, tiled=True)

    density, spread, reassign = call(
        functools.partial(
            tail_kernel, groups, slots, head_dev, float(head_dev * groups * members)
        ),
        (
            jax.ShapeDtypeStruct((1, new_count), jnp.float32),
            jax.ShapeDtypeStruct((1, new_count), jnp.float32),
            jax.ShapeDtypeStruct((1, near, vectors.shape[1]), jnp.float32),
        ),
        (near_ids, message, vectors),
        (4 * near * vectors.shape[1] * width, vectors.size * 4),
    )
    return (density[0], spread[0], reassign)


def solution(mesh):
    placed = (
        P(("group", "member"), None),
        P("group", None),
        P(("group", "member"), None, None),
        P(("group", "member"), None),
    )
    return jax.shard_map(
        per_device,
        mesh=mesh,
        in_specs=placed,
        out_specs=(P("group"), P("group"), P(("group", "member"), None, None)),
        check_vma=False,
    )
```

```python
import functools

import jax
import jax.numpy as jnp
from jax import lax
from jax.experimental import pallas as pl
from jax.experimental.pallas import tpu as pltpu
from jax.sharding import PartitionSpec as P

VMEM = pltpu.MemorySpace.VMEM
HBM = pltpu.MemorySpace.HBM
LANES = 128
PACK = 16
PARTS = 3
LIMIT = 24 * 2**20


def from_partner(value, axis, mask):
    count = lax.axis_size(axis)
    return lax.ppermute(value, axis, [(source, source ^ mask) for source in range(count)])


def in_hbm(value):
    return pltpu.with_memory_space_constraint(value, HBM)


def call(body, shapes, operands, cost, scratch=(), spaces=None):
    return pl.pallas_call(
        body,
        out_shape=shapes,
        in_specs=[pl.BlockSpec(memory_space=space) for space in spaces or [VMEM] * len(operands)],
        out_specs=jax.tree.map(lambda unused: pl.BlockSpec(memory_space=VMEM), shapes),
        scratch_shapes=scratch,
        compiler_params=pltpu.CompilerParams(vmem_limit_bytes=LIMIT),
        cost_estimate=pl.CostEstimate(flops=cost[0], bytes_accessed=cost[1], transcendentals=0),
    )(*operands)


def iota(shape, dim):
    return lax.broadcasted_iota(jnp.int32, shape, dim)


def early_kernel(
    heads_ref, new_ref, ids_ref, kept_ref, head_sq_ref, kept_new_ref, kept_ids_ref, sems
):
    head_dev, width = heads_ref.shape
    tiles = 4
    tile = head_dev // tiles
    parts = [pl.ds(i * tile, tile) for i in range(tiles)]
    copies = [
        pltpu.make_async_copy(heads_ref.at[part], kept_ref.at[part], sems.at[i])
        for i, part in enumerate(parts)
    ]
    copies += [
        pltpu.make_async_copy(new_ref, kept_new_ref, sems.at[tiles]),
        pltpu.make_async_copy(ids_ref, kept_ids_ref, sems.at[tiles + 1]),
    ]
    for copy in copies:
        copy.start()
    for i in range(tiles):
        copies[i].wait()
        for first in range(i * tile, (i + 1) * tile, LANES):
            block = jnp.square(kept_ref[first:first + LANES, :].astype(jnp.float32))
            folded = block[:, :LANES]
            for column in range(LANES, width, LANES):
                folded = folded + block[:, column:column + LANES]
            head_sq_ref[:, first:first + LANES] = jnp.sum(folded.T, axis=0, keepdims=True)
    for copy in copies[tiles:]:
        copy.wait()


def listed_rows(ids, me, slots, heads_ref):
    members, near = ids.shape
    head_dev = heads_ref.shape[0]
    local = ids - me * head_dev
    owned = (local >= 0) & (local < head_dev)
    earlier = (iota((near, near), 0) < iota((near, near), 1)).astype(jnp.bfloat16)
    rank = jnp.dot(owned.astype(jnp.bfloat16), earlier, preferred_element_type=jnp.float32)
    rank = jnp.where(owned, rank.astype(jnp.int32), -1)
    shape = (members, slots, near)
    pick = jnp.broadcast_to(rank[:, None, :], shape) == iota(shape, 1)
    wanted = jnp.sum(
        jnp.where(pick, jnp.broadcast_to(local[:, None, :] + 1, shape), 0), axis=2, keepdims=True
    ).reshape(members * slots, 1)
    onehot = (wanted == iota((members * slots, head_dev), 1) + 1).astype(jnp.bfloat16)
    return jnp.dot(
        onehot, heads_ref[...], preferred_element_type=jnp.float32
    ).astype(jnp.bfloat16)


def crowding(queries, heads_ref, head_sq_ref):
    head_dev, width = heads_ref.shape
    query_sq = jnp.sum(jnp.square(queries.astype(jnp.float32)), axis=1, keepdims=True)
    total_w = jnp.zeros((queries.shape[0], 1), jnp.float32)
    total_we = jnp.zeros((queries.shape[0], 1), jnp.float32)
    tile = 512
    for start in range(0, head_dev, tile):
        dots = lax.dot_general(
            queries, heads_ref[start:start + tile, :], (((1,), (1,)), ((), ())),
            preferred_element_type=jnp.float32,
        )
        head_sq = head_sq_ref[:, start:start + tile]
        excess = (query_sq + head_sq - 2.0 * dots) * (1.0 / width)
        inverse = 1.0 / (1.0 + excess)
        weight = inverse * inverse
        total_w = total_w + jnp.sum(weight, axis=1, keepdims=True)
        total_we = total_we + jnp.sum(weight * excess, axis=1, keepdims=True)
    return total_w, total_we


def crowd_kernel(groups, ids_ref, heads_ref, head_sq_ref, *refs):
    query_refs, (sums_ref, kept_ids_ref) = refs[:-2], refs[-2:]
    kept_ids_ref[...] = ids_ref[...]
    here = lax.axis_index("group")
    queries = jnp.concatenate([ref[...] for ref in query_refs], axis=0)
    new_count = queries.shape[0] // groups
    totals = crowding(queries, heads_ref, head_sq_ref)
    lane = iota((new_count, LANES), 1)
    row = iota((new_count, LANES), 0)
    line = iota(sums_ref.shape, 0)
    sums = jnp.zeros(sums_ref.shape, jnp.float32)
    for mask in range(groups):
        part = slice(mask * new_count, (mask + 1) * new_count)
        for kind in range(2):
            place = (kind * groups + (here ^ mask)) * new_count
            spread_out = jnp.where(lane == row + place % LANES, totals[kind][part], 0.0)
            spread_out = jnp.sum(spread_out, axis=0, keepdims=True)
            sums = sums + jnp.where(line == place // LANES, spread_out, 0.0)
    sums_ref[...] = sums


def gather_kernel(members, slots, near_ref, far_ref, heads_ref, unused, rows_ref, ids_ref):
    me = lax.axis_index("member")
    half = members // 2
    ids_ref[:half, :] = near_ref[...]
    ids_ref[half:, :] = far_ref[...]
    ids = jnp.concatenate([ids_ref[pl.ds(me ^ member, 1), :] for member in range(members)], axis=0)
    rows_ref[...] = listed_rows(ids, me, slots, heads_ref)


def pack_kernel(members, slots, rows_ref, mine_ref, other_ref, out_ref):
    chunks = rows_ref.shape[1] // LANES
    for member in range(members):
        for chunk in range(chunks):
            out_ref[member, chunk * slots:(chunk + 1) * slots, :] = rows_ref[
                member * slots:(member + 1) * slots, chunk * LANES:(chunk + 1) * LANES
            ]
    sums = mine_ref[...] + other_ref[...]
    coded = []
    for unused in range(PARTS):
        coded.append(sums.astype(jnp.bfloat16).astype(jnp.float32))
        sums = sums - coded[-1]
    missing = out_ref.shape[1] - chunks * slots - PARTS * sums.shape[0]
    if missing:
        coded.append(jnp.zeros((missing, LANES), jnp.float32))
    tail = jnp.concatenate(coded, axis=0).astype(jnp.bfloat16)
    for member in range(members):
        out_ref[member, chunks * slots:, :] = tail


def distances(slots, head_dev, ids_ref, listed_ref, vectors_ref, out_ref):
    near = ids_ref.shape[1]
    members = listed_ref.shape[0]
    block, width = vectors_ref.shape[1:]
    square = (near, near)
    owner_row = jnp.broadcast_to(lax.div(ids_ref[...], head_dev), square)
    eye = iota(square, 0) == iota(square, 1)
    owner = jnp.sum(jnp.where(eye, owner_row, 0), axis=1, keepdims=True)
    before = (owner_row == owner) & (iota(square, 1) < iota(square, 0))
    place = jnp.sum(before.astype(jnp.int32), axis=1, keepdims=True)
    source = owner * slots + place
    back = (source == iota((near, members * slots), 1)).astype(jnp.bfloat16)
    rows = []
    for chunk in range(width // LANES):
        part = listed_ref[:, chunk * slots:(chunk + 1) * slots, :].reshape(members * slots, LANES)
        rows.append(jnp.dot(back, part, preferred_element_type=jnp.float32))
    rows = jnp.concatenate(rows, axis=1)
    row_sq = jnp.sum(jnp.square(rows), axis=1, keepdims=True)
    vec = vectors_ref[0]
    vec_sq = jnp.sum(jnp.square(vec.astype(jnp.float32)), axis=1, keepdims=True)
    turned = iota((block, block), 0) == iota((block, block), 1)
    vec_sq = jnp.sum(jnp.where(turned, vec_sq, 0.0), axis=0, keepdims=True)
    dots = lax.dot_general(
        rows.astype(jnp.bfloat16), vec, (((1,), (1,)), ((), ())),
        preferred_element_type=jnp.float32,
    )
    out_ref[0] = (row_sq + vec_sq - 2.0 * dots) * (1.0 / width)


def tail_kernel(
    groups, slots, head_dev, total_heads, ids_ref, listed_ref, vectors_ref,
    density_ref, spread_ref, out_ref,
):
    distances(slots, head_dev, ids_ref, listed_ref, vectors_ref, out_ref)
    here = lax.axis_index("group")
    members = listed_ref.shape[0]
    new_count = density_ref.shape[1]
    lines = 2 * groups * new_count // LANES
    first = vectors_ref.shape[2] // LANES * slots
    coded = jnp.sum(listed_ref[:, first:, :].astype(jnp.float32), axis=0)
    total = sum(coded[part * lines:(part + 1) * lines] for part in range(PARTS))
    shape = (new_count, LANES)
    eye = iota((new_count, new_count), 0) == iota((new_count, new_count), 1)
    found = []
    for kind in range(2):
        place = (kind * groups + here) * new_count
        line = jnp.sum(
            jnp.where(iota((lines, LANES), 0) == place // LANES, total, 0.0), axis=0, keepdims=True
        )
        column = jnp.sum(
            jnp.where(iota(shape, 1) == iota(shape, 0) + place % LANES, line, 0.0),
            axis=1, keepdims=True,
        )
        found.append(jnp.sum(jnp.where(eye, column, 0.0), axis=0, keepdims=True))
    density_ref[...] = jnp.log(found[0] * (1.0 / total_heads))
    spread_ref[...] = found[1] / found[0]


def per_device(heads, new_heads, vectors, near_ids):
    head_dev, width = heads.shape
    new_count = new_heads.shape[0]
    near = near_ids.shape[1]
    groups = lax.axis_size("group")
    members = lax.axis_size("member")
    most = 2 * near // members
    slots = -(-most // PACK) * PACK

    partner_ids = from_partner(near_ids, "member", 1)
    others = [from_partner(new_heads, "group", mask) for mask in range(1, groups)]
    kept, head_sq, new_heads, ids = call(
        early_kernel,
        (
            jax.ShapeDtypeStruct(heads.shape, heads.dtype),
            jax.ShapeDtypeStruct((1, head_dev), jnp.float32),
            jax.ShapeDtypeStruct(new_heads.shape, new_heads.dtype),
            jax.ShapeDtypeStruct(near_ids.shape, near_ids.dtype),
        ),
        (in_hbm(heads), in_hbm(new_heads), in_hbm(near_ids)),
        (0, 0),
        scratch=[pltpu.SemaphoreType.DMA((6,))],
        spaces=[HBM, HBM, HBM],
    )
    ids = jnp.concatenate([ids, partner_ids], axis=0)
    lines = 2 * groups * new_count // LANES
    chunks = width // LANES
    extra = -(-PARTS * lines // PACK) * PACK
    sums, kept_ids = call(
        functools.partial(crowd_kernel, groups),
        (
            jax.ShapeDtypeStruct((lines, LANES), jnp.float32),
            jax.ShapeDtypeStruct(ids.shape, ids.dtype),
        ),
        (ids, kept, head_sq, new_heads, *others),
        (0, 0),
    )
    mask = 2
    while mask < members // 2:
        kept_ids = jnp.concatenate([kept_ids, from_partner(ids, "member", mask)], axis=0)
        ids = kept_ids
        mask *= 2
    far_ids = from_partner(ids, "member", mask)
    mask = 1
    while mask < groups // 2:
        sums = sums + from_partner(sums, "group", mask)
        mask *= 2
    rows = call(
        functools.partial(gather_kernel, members, slots),
        jax.ShapeDtypeStruct((members * slots, width), jnp.bfloat16),
        (ids, far_ids, kept, sums),
        (2 * members * slots * head_dev * width, heads.size * 2),
        scratch=[pltpu.VMEM((members, near), jnp.int32)],
        spaces=[VMEM, VMEM, VMEM, pl.ANY],
    )
    message = call(
        functools.partial(pack_kernel, members, slots),
        jax.ShapeDtypeStruct((members, chunks * slots + extra, LANES), jnp.bfloat16),
        (rows, sums, from_partner(sums, "group", mask)),
        (0, members * slots * width * 4),
    )
    message = lax.all_to_all(message, "member", 0, 0, tiled=True)

    density, spread, reassign = call(
        functools.partial(
            tail_kernel, groups, slots, head_dev, float(head_dev * groups * members)
        ),
        (
            jax.ShapeDtypeStruct((1, new_count), jnp.float32),
            jax.ShapeDtypeStruct((1, new_count), jnp.float32),
            jax.ShapeDtypeStruct((1, near, vectors.shape[1]), jnp.float32),
        ),
        (near_ids, message, vectors),
        (4 * near * vectors.shape[1] * width, vectors.size * 4),
    )
    return (density[0], spread[0], reassign)


def solution(mesh):
    placed = (
        P(("group", "member"), None),
        P("group", None),
        P(("group", "member"), None, None),
        P(("group", "member"), None),
    )
    return jax.shard_map(
        per_device,
        mesh=mesh,
        in_specs=placed,
        out_specs=(P("group"), P("group"), P(("group", "member"), None, None)),
        check_vma=False,
    )
```

```python
import functools

import jax
import jax.numpy as jnp
from jax import lax
from jax.experimental import pallas as pl
from jax.experimental.pallas import tpu as pltpu
from jax.sharding import PartitionSpec as P

VMEM = pltpu.MemorySpace.VMEM
HBM = pltpu.MemorySpace.HBM
LANES = 128
PACK = 16
PARTS = 3
LIMIT = 24 * 2**20


def from_partner(value, axis, mask):
    count = lax.axis_size(axis)
    return lax.ppermute(value, axis, [(source, source ^ mask) for source in range(count)])


def in_hbm(value):
    return pltpu.with_memory_space_constraint(value, HBM)


def call(body, shapes, operands, cost, scratch=(), spaces=None):
    return pl.pallas_call(
        body,
        out_shape=shapes,
        in_specs=[pl.BlockSpec(memory_space=space) for space in spaces or [VMEM] * len(operands)],
        out_specs=jax.tree.map(lambda unused: pl.BlockSpec(memory_space=VMEM), shapes),
        scratch_shapes=scratch,
        compiler_params=pltpu.CompilerParams(vmem_limit_bytes=LIMIT),
        cost_estimate=pl.CostEstimate(flops=cost[0], bytes_accessed=cost[1], transcendentals=0),
    )(*operands)


def iota(shape, dim):
    return lax.broadcasted_iota(jnp.int32, shape, dim)


def listed_rows(ids, me, slots, heads_ref):
    members, near = ids.shape
    head_dev = heads_ref.shape[0]
    local = ids - me * head_dev
    owned = (local >= 0) & (local < head_dev)
    earlier = (iota((near, near), 0) < iota((near, near), 1)).astype(jnp.bfloat16)
    rank = jnp.dot(owned.astype(jnp.bfloat16), earlier, preferred_element_type=jnp.float32)
    rank = jnp.where(owned, rank.astype(jnp.int32), -1)
    shape = (members, slots, near)
    pick = jnp.broadcast_to(rank[:, None, :], shape) == iota(shape, 1)
    wanted = jnp.sum(
        jnp.where(pick, jnp.broadcast_to(local[:, None, :] + 1, shape), 0), axis=2, keepdims=True
    ).reshape(members * slots, 1)
    onehot = (wanted == iota((members * slots, head_dev), 1) + 1).astype(jnp.bfloat16)
    return jnp.dot(
        onehot, heads_ref[...], preferred_element_type=jnp.float32
    ).astype(jnp.bfloat16)


def stage_kernel(ids_ref, kept_ref, sem):
    copy = pltpu.make_async_copy(ids_ref, kept_ref, sem)
    copy.start()
    copy.wait()


def squares(block):
    width = block.shape[1]
    block = jnp.square(block.astype(jnp.float32))
    folded = block[:, :LANES]
    for column in range(LANES, width, LANES):
        folded = folded + block[:, column:column + LANES]
    return jnp.sum(folded.T, axis=0, keepdims=True)


def crowd_kernel(groups, unused, heads_ref, new_ref, *refs):
    other_refs, (sums_ref, kept_ref, queries_ref, sems) = refs[:-4], refs[-4:]
    head_dev, width = heads_ref.shape
    new_count = new_ref.shape[0]
    tiles = sems.shape[0] - 1
    tile = head_dev // tiles
    parts = [pl.ds(i * tile, tile) for i in range(tiles)]
    new_copy = pltpu.make_async_copy(new_ref, queries_ref.at[pl.ds(0, new_count)], sems.at[tiles])
    new_copy.start()
    copies = [
        pltpu.make_async_copy(heads_ref.at[part], kept_ref.at[part], sems.at[i])
        for i, part in enumerate(parts)
    ]
    for copy in copies:
        copy.start()
    for i, ref in enumerate(other_refs):
        queries_ref[(i + 1) * new_count:(i + 2) * new_count, :] = ref[...]
    new_copy.wait()
    queries = queries_ref[...]
    query_sq = jnp.sum(jnp.square(queries.astype(jnp.float32)), axis=1, keepdims=True)
    total_w = jnp.zeros((groups * new_count, 1), jnp.float32)
    total_we = jnp.zeros((groups * new_count, 1), jnp.float32)
    for i, copy in enumerate(copies):
        copy.wait()
        first = i * tile
        head_sq = jnp.concatenate(
            [squares(kept_ref[row:row + LANES, :]) for row in range(first, first + tile, LANES)],
            axis=1,
        )
        dots = lax.dot_general(
            queries, kept_ref[first:first + tile, :], (((1,), (1,)), ((), ())),
            preferred_element_type=jnp.float32,
        )
        excess = (query_sq + head_sq - 2.0 * dots) * (1.0 / width)
        inverse = 1.0 / (1.0 + excess)
        weight = inverse * inverse
        total_w = total_w + jnp.sum(weight, axis=1, keepdims=True)
        total_we = total_we + jnp.sum(weight * excess, axis=1, keepdims=True)
    totals = (total_w, total_we)
    here = lax.axis_index("group")
    lane = iota((new_count, LANES), 1)
    row = iota((new_count, LANES), 0)
    line = iota(sums_ref.shape, 0)
    sums = jnp.zeros(sums_ref.shape, jnp.float32)
    for mask in range(groups):
        part = slice(mask * new_count, (mask + 1) * new_count)
        for kind in range(2):
            place = (kind * groups + (here ^ mask)) * new_count
            spread_out = jnp.where(lane == row + place % LANES, totals[kind][part], 0.0)
            spread_out = jnp.sum(spread_out, axis=0, keepdims=True)
            sums = sums + jnp.where(line == place // LANES, spread_out, 0.0)
    sums_ref[...] = sums


def join_kernel(mine_ref, other_ref, low_ref, high_ref, sums_ref, ids_ref):
    half = low_ref.shape[0]
    sums_ref[...] = mine_ref[...] + other_ref[...]
    ids_ref[:half, :] = low_ref[...]
    ids_ref[half:, :] = high_ref[...]


def gather_kernel(members, slots, near_ref, far_ref, heads_ref, unused, rows_ref, ids_ref):
    me = lax.axis_index("member")
    half = members // 2
    ids_ref[:half, :] = near_ref[...]
    ids_ref[half:, :] = far_ref[...]
    ids = jnp.concatenate([ids_ref[pl.ds(me ^ member, 1), :] for member in range(members)], axis=0)
    rows_ref[...] = listed_rows(ids, me, slots, heads_ref)


def pack_kernel(members, slots, rows_ref, mine_ref, other_ref, out_ref):
    chunks = rows_ref.shape[1] // LANES
    for member in range(members):
        for chunk in range(chunks):
            out_ref[member, chunk * slots:(chunk + 1) * slots, :] = rows_ref[
                member * slots:(member + 1) * slots, chunk * LANES:(chunk + 1) * LANES
            ]
    sums = mine_ref[...] + other_ref[...]
    coded = []
    for unused in range(PARTS):
        coded.append(sums.astype(jnp.bfloat16).astype(jnp.float32))
        sums = sums - coded[-1]
    missing = out_ref.shape[1] - chunks * slots - PARTS * sums.shape[0]
    if missing:
        coded.append(jnp.zeros((missing, LANES), jnp.float32))
    tail = jnp.concatenate(coded, axis=0).astype(jnp.bfloat16)
    for member in range(members):
        out_ref[member, chunks * slots:, :] = tail


def distances(slots, head_dev, ids_ref, listed_ref, vectors_ref, out_ref):
    near = ids_ref.shape[1]
    members = listed_ref.shape[0]
    block, width = vectors_ref.shape[1:]
    square = (near, near)
    owner_row = jnp.broadcast_to(lax.div(ids_ref[...], head_dev), square)
    eye = iota(square, 0) == iota(square, 1)
    owner = jnp.sum(jnp.where(eye, owner_row, 0), axis=1, keepdims=True)
    before = (owner_row == owner) & (iota(square, 1) < iota(square, 0))
    place = jnp.sum(before.astype(jnp.int32), axis=1, keepdims=True)
    source = owner * slots + place
    back = (source == iota((near, members * slots), 1)).astype(jnp.bfloat16)
    rows = []
    for chunk in range(width // LANES):
        part = listed_ref[:, chunk * slots:(chunk + 1) * slots, :].reshape(members * slots, LANES)
        rows.append(jnp.dot(back, part, preferred_element_type=jnp.float32))
    rows = jnp.concatenate(rows, axis=1)
    row_sq = jnp.sum(jnp.square(rows), axis=1, keepdims=True)
    vec = vectors_ref[0]
    vec_sq = jnp.sum(jnp.square(vec.astype(jnp.float32)), axis=1, keepdims=True)
    turned = iota((block, block), 0) == iota((block, block), 1)
    vec_sq = jnp.sum(jnp.where(turned, vec_sq, 0.0), axis=0, keepdims=True)
    dots = lax.dot_general(
        rows.astype(jnp.bfloat16), vec, (((1,), (1,)), ((), ())),
        preferred_element_type=jnp.float32,
    )
    out_ref[0] = (row_sq + vec_sq - 2.0 * dots) * (1.0 / width)


def tail_kernel(
    groups, slots, head_dev, total_heads, ids_ref, listed_ref, vectors_ref,
    density_ref, spread_ref, out_ref,
):
    distances(slots, head_dev, ids_ref, listed_ref, vectors_ref, out_ref)
    here = lax.axis_index("group")
    members = listed_ref.shape[0]
    new_count = density_ref.shape[1]
    lines = 2 * groups * new_count // LANES
    first = vectors_ref.shape[2] // LANES * slots
    coded = jnp.sum(listed_ref[:, first:, :].astype(jnp.float32), axis=0)
    total = sum(coded[part * lines:(part + 1) * lines] for part in range(PARTS))
    shape = (new_count, LANES)
    eye = iota((new_count, new_count), 0) == iota((new_count, new_count), 1)
    found = []
    for kind in range(2):
        place = (kind * groups + here) * new_count
        line = jnp.sum(
            jnp.where(iota((lines, LANES), 0) == place // LANES, total, 0.0), axis=0, keepdims=True
        )
        column = jnp.sum(
            jnp.where(iota(shape, 1) == iota(shape, 0) + place % LANES, line, 0.0),
            axis=1, keepdims=True,
        )
        found.append(jnp.sum(jnp.where(eye, column, 0.0), axis=0, keepdims=True))
    density_ref[...] = jnp.log(found[0] * (1.0 / total_heads))
    spread_ref[...] = found[1] / found[0]


def per_device(heads, new_heads, vectors, near_ids):
    head_dev, width = heads.shape
    new_count = new_heads.shape[0]
    near = near_ids.shape[1]
    groups = lax.axis_size("group")
    members = lax.axis_size("member")
    most = 2 * near // members
    slots = -(-most // PACK) * PACK

    partner_ids = from_partner(near_ids, "member", 1)
    others = [from_partner(new_heads, "group", mask) for mask in range(1, groups)]
    ids = call(
        stage_kernel,
        jax.ShapeDtypeStruct(near_ids.shape, near_ids.dtype),
        (in_hbm(near_ids),),
        (0, 0),
        scratch=[pltpu.SemaphoreType.DMA],
        spaces=[HBM],
    )
    ids = jnp.concatenate([ids, partner_ids], axis=0)
    lines = 2 * groups * new_count // LANES
    chunks = width // LANES
    extra = -(-PARTS * lines // PACK) * PACK
    sums, kept = call(
        functools.partial(crowd_kernel, groups),
        (
            jax.ShapeDtypeStruct((lines, LANES), jnp.float32),
            jax.ShapeDtypeStruct(heads.shape, heads.dtype),
        ),
        (ids, in_hbm(heads), in_hbm(new_heads), *others),
        (0, 0),
        scratch=[
            pltpu.VMEM((groups * new_count, width), new_heads.dtype),
            pltpu.SemaphoreType.DMA((5,)),
        ],
        spaces=[pl.ANY, HBM, HBM] + [VMEM] * len(others),
    )
    mask = 2
    while mask < members // 4:
        ids = jnp.concatenate([ids, from_partner(ids, "member", mask)], axis=0)
        mask *= 2
    sums, ids = call(
        join_kernel,
        (
            jax.ShapeDtypeStruct(sums.shape, sums.dtype),
            jax.ShapeDtypeStruct((2 * mask, near), ids.dtype),
        ),
        (sums, from_partner(sums, "group", 1), ids, from_partner(ids, "member", mask)),
        (0, 0),
    )
    far_ids = from_partner(ids, "member", 2 * mask)
    mask = 2
    while mask < groups // 2:
        sums = sums + from_partner(sums, "group", mask)
        mask *= 2
    rows = call(
        functools.partial(gather_kernel, members, slots),
        jax.ShapeDtypeStruct((members * slots, width), jnp.bfloat16),
        (ids, far_ids, kept, sums),
        (2 * members * slots * head_dev * width, heads.size * 2),
        scratch=[pltpu.VMEM((members, near), jnp.int32)],
        spaces=[VMEM, VMEM, VMEM, pl.ANY],
    )
    message = call(
        functools.partial(pack_kernel, members, slots),
        jax.ShapeDtypeStruct((members, chunks * slots + extra, LANES), jnp.bfloat16),
        (rows, sums, from_partner(sums, "group", mask)),
        (0, members * slots * width * 4),
    )
    message = lax.all_to_all(message, "member", 0, 0, tiled=True)

    density, spread, reassign = call(
        functools.partial(
            tail_kernel, groups, slots, head_dev, float(head_dev * groups * members)
        ),
        (
            jax.ShapeDtypeStruct((1, new_count), jnp.float32),
            jax.ShapeDtypeStruct((1, new_count), jnp.float32),
            jax.ShapeDtypeStruct((1, near, vectors.shape[1]), jnp.float32),
        ),
        (near_ids, message, vectors),
        (4 * near * vectors.shape[1] * width, vectors.size * 4),
    )
    return (density[0], spread[0], reassign)


def solution(mesh):
    placed = (
        P(("group", "member"), None),
        P("group", None),
        P(("group", "member"), None, None),
        P(("group", "member"), None),
    )
    return jax.shard_map(
        per_device,
        mesh=mesh,
        in_specs=placed,
        out_specs=(P("group"), P("group"), P(("group", "member"), None, None)),
        check_vma=False,
    )
```

```python
import functools

import jax
import jax.numpy as jnp
from jax import lax
from jax.experimental import pallas as pl
from jax.experimental.pallas import tpu as pltpu
from jax.sharding import PartitionSpec as P

VMEM = pltpu.MemorySpace.VMEM
HBM = pltpu.MemorySpace.HBM
LANES = 128
PACK = 16
PARTS = 3
LIMIT = 24 * 2**20


def from_partner(value, axis, mask):
    count = lax.axis_size(axis)
    return lax.ppermute(value, axis, [(source, source ^ mask) for source in range(count)])


def in_hbm(value):
    return pltpu.with_memory_space_constraint(value, HBM)


def call(body, shapes, operands, cost, scratch=(), spaces=None):
    return pl.pallas_call(
        body,
        out_shape=shapes,
        in_specs=[pl.BlockSpec(memory_space=space) for space in spaces or [VMEM] * len(operands)],
        out_specs=jax.tree.map(lambda unused: pl.BlockSpec(memory_space=VMEM), shapes),
        scratch_shapes=scratch,
        compiler_params=pltpu.CompilerParams(vmem_limit_bytes=LIMIT),
        cost_estimate=pl.CostEstimate(flops=cost[0], bytes_accessed=cost[1], transcendentals=0),
    )(*operands)


def iota(shape, dim):
    return lax.broadcasted_iota(jnp.int32, shape, dim)


def early_kernel(heads_ref, new_ref, ids_ref, kept_ref, kept_new_ref, kept_ids_ref, sems):
    pairs = [(heads_ref, kept_ref), (new_ref, kept_new_ref), (ids_ref, kept_ids_ref)]
    copies = [pltpu.make_async_copy(*pair, sems.at[i]) for i, pair in enumerate(pairs)]
    for copy in copies:
        copy.start()
    for copy in copies:
        copy.wait()


def squares(block):
    width = block.shape[1]
    block = jnp.square(block.astype(jnp.float32))
    folded = block[:, :LANES]
    for column in range(LANES, width, LANES):
        folded = folded + block[:, column:column + LANES]
    return jnp.sum(folded.T, axis=0, keepdims=True)


def listed_rows(ids, me, slots, heads_ref):
    members, near = ids.shape
    head_dev = heads_ref.shape[0]
    local = ids - me * head_dev
    owned = (local >= 0) & (local < head_dev)
    earlier = (iota((near, near), 0) < iota((near, near), 1)).astype(jnp.bfloat16)
    rank = jnp.dot(owned.astype(jnp.bfloat16), earlier, preferred_element_type=jnp.float32)
    rank = jnp.where(owned, rank.astype(jnp.int32), -1)
    shape = (members, slots, near)
    pick = jnp.broadcast_to(rank[:, None, :], shape) == iota(shape, 1)
    wanted = jnp.sum(
        jnp.where(pick, jnp.broadcast_to(local[:, None, :] + 1, shape), 0), axis=2, keepdims=True
    ).reshape(members * slots, 1)
    onehot = (wanted == iota((members * slots, head_dev), 1) + 1).astype(jnp.bfloat16)
    return jnp.dot(
        onehot, heads_ref[...], preferred_element_type=jnp.float32
    ).astype(jnp.bfloat16)


def crowding(queries, heads_ref):
    head_dev, width = heads_ref.shape
    query_sq = jnp.sum(jnp.square(queries.astype(jnp.float32)), axis=1, keepdims=True)
    total_w = jnp.zeros((queries.shape[0], 1), jnp.float32)
    total_we = jnp.zeros((queries.shape[0], 1), jnp.float32)
    tile = 512
    for start in range(0, head_dev, tile):
        dots = lax.dot_general(
            queries, heads_ref[start:start + tile, :], (((1,), (1,)), ((), ())),
            preferred_element_type=jnp.float32,
        )
        head_sq = jnp.concatenate(
            [squares(heads_ref[row:row + LANES, :]) for row in range(start, start + tile, LANES)],
            axis=1,
        )
        excess = (query_sq + head_sq - 2.0 * dots) * (1.0 / width)
        inverse = 1.0 / (1.0 + excess)
        weight = inverse * inverse
        total_w = total_w + jnp.sum(weight, axis=1, keepdims=True)
        total_we = total_we + jnp.sum(weight * excess, axis=1, keepdims=True)
    return total_w, total_we


def crowd_kernel(groups, unused, heads_ref, *refs):
    query_refs, sums_ref = refs[:-1], refs[-1]
    here = lax.axis_index("group")
    queries = jnp.concatenate([ref[...] for ref in query_refs], axis=0)
    new_count = queries.shape[0] // groups
    totals = crowding(queries, heads_ref)
    lane = iota((new_count, LANES), 1)
    row = iota((new_count, LANES), 0)
    line = iota(sums_ref.shape, 0)
    sums = jnp.zeros(sums_ref.shape, jnp.float32)
    for mask in range(groups):
        part = slice(mask * new_count, (mask + 1) * new_count)
        for kind in range(2):
            place = (kind * groups + (here ^ mask)) * new_count
            spread_out = jnp.where(lane == row + place % LANES, totals[kind][part], 0.0)
            spread_out = jnp.sum(spread_out, axis=0, keepdims=True)
            sums = sums + jnp.where(line == place // LANES, spread_out, 0.0)
    sums_ref[...] = sums


def join_kernel(mine_ref, other_ref, low_ref, high_ref, sums_ref, ids_ref):
    half = low_ref.shape[0]
    sums_ref[...] = mine_ref[...] + other_ref[...]
    ids_ref[:half, :] = low_ref[...]
    ids_ref[half:, :] = high_ref[...]


def gather_kernel(members, slots, near_ref, far_ref, heads_ref, unused, rows_ref, ids_ref):
    me = lax.axis_index("member")
    half = members // 2
    ids_ref[:half, :] = near_ref[...]
    ids_ref[half:, :] = far_ref[...]
    ids = jnp.concatenate([ids_ref[pl.ds(me ^ member, 1), :] for member in range(members)], axis=0)
    rows_ref[...] = listed_rows(ids, me, slots, heads_ref)


def pack_kernel(members, slots, rows_ref, mine_ref, other_ref, out_ref):
    chunks = rows_ref.shape[1] // LANES
    for member in range(members):
        for chunk in range(chunks):
            out_ref[member, chunk * slots:(chunk + 1) * slots, :] = rows_ref[
                member * slots:(member + 1) * slots, chunk * LANES:(chunk + 1) * LANES
            ]
    sums = mine_ref[...] + other_ref[...]
    coded = []
    for unused in range(PARTS):
        coded.append(sums.astype(jnp.bfloat16).astype(jnp.float32))
        sums = sums - coded[-1]
    missing = out_ref.shape[1] - chunks * slots - PARTS * sums.shape[0]
    if missing:
        coded.append(jnp.zeros((missing, LANES), jnp.float32))
    tail = jnp.concatenate(coded, axis=0).astype(jnp.bfloat16)
    for member in range(members):
        out_ref[member, chunks * slots:, :] = tail


def distances(slots, head_dev, ids_ref, listed_ref, vectors_ref, out_ref):
    near = ids_ref.shape[1]
    members = listed_ref.shape[0]
    block, width = vectors_ref.shape[1:]
    square = (near, near)
    owner_row = jnp.broadcast_to(lax.div(ids_ref[...], head_dev), square)
    eye = iota(square, 0) == iota(square, 1)
    owner = jnp.sum(jnp.where(eye, owner_row, 0), axis=1, keepdims=True)
    before = (owner_row == owner) & (iota(square, 1) < iota(square, 0))
    place = jnp.sum(before.astype(jnp.int32), axis=1, keepdims=True)
    source = owner * slots + place
    back = (source == iota((near, members * slots), 1)).astype(jnp.bfloat16)
    rows = []
    for chunk in range(width // LANES):
        part = listed_ref[:, chunk * slots:(chunk + 1) * slots, :].reshape(members * slots, LANES)
        rows.append(jnp.dot(back, part, preferred_element_type=jnp.float32))
    rows = jnp.concatenate(rows, axis=1)
    row_sq = jnp.sum(jnp.square(rows), axis=1, keepdims=True)
    vec = vectors_ref[0]
    vec_sq = jnp.sum(jnp.square(vec.astype(jnp.float32)), axis=1, keepdims=True)
    turned = iota((block, block), 0) == iota((block, block), 1)
    vec_sq = jnp.sum(jnp.where(turned, vec_sq, 0.0), axis=0, keepdims=True)
    dots = lax.dot_general(
        rows.astype(jnp.bfloat16), vec, (((1,), (1,)), ((), ())),
        preferred_element_type=jnp.float32,
    )
    out_ref[0] = (row_sq + vec_sq - 2.0 * dots) * (1.0 / width)


def tail_kernel(
    groups, slots, head_dev, total_heads, ids_ref, listed_ref, vectors_ref,
    density_ref, spread_ref, out_ref,
):
    distances(slots, head_dev, ids_ref, listed_ref, vectors_ref, out_ref)
    here = lax.axis_index("group")
    members = listed_ref.shape[0]
    new_count = density_ref.shape[1]
    lines = 2 * groups * new_count // LANES
    first = vectors_ref.shape[2] // LANES * slots
    coded = jnp.sum(listed_ref[:, first:, :].astype(jnp.float32), axis=0)
    total = sum(coded[part * lines:(part + 1) * lines] for part in range(PARTS))
    shape = (new_count, LANES)
    eye = iota((new_count, new_count), 0) == iota((new_count, new_count), 1)
    found = []
    for kind in range(2):
        place = (kind * groups + here) * new_count
        line = jnp.sum(
            jnp.where(iota((lines, LANES), 0) == place // LANES, total, 0.0), axis=0, keepdims=True
        )
        column = jnp.sum(
            jnp.where(iota(shape, 1) == iota(shape, 0) + place % LANES, line, 0.0),
            axis=1, keepdims=True,
        )
        found.append(jnp.sum(jnp.where(eye, column, 0.0), axis=0, keepdims=True))
    density_ref[...] = jnp.log(found[0] * (1.0 / total_heads))
    spread_ref[...] = found[1] / found[0]


def per_device(heads, new_heads, vectors, near_ids):
    head_dev, width = heads.shape
    new_count = new_heads.shape[0]
    near = near_ids.shape[1]
    groups = lax.axis_size("group")
    members = lax.axis_size("member")
    most = 2 * near // members
    slots = -(-most // PACK) * PACK

    partner_ids = from_partner(near_ids, "member", 1)
    others = [from_partner(new_heads, "group", mask) for mask in range(1, groups)]
    kept, new_heads, ids = call(
        early_kernel,
        (
            jax.ShapeDtypeStruct(heads.shape, heads.dtype),
            jax.ShapeDtypeStruct(new_heads.shape, new_heads.dtype),
            jax.ShapeDtypeStruct(near_ids.shape, near_ids.dtype),
        ),
        (in_hbm(heads), in_hbm(new_heads), in_hbm(near_ids)),
        (0, 0),
        scratch=[pltpu.SemaphoreType.DMA((3,))],
        spaces=[HBM, HBM, HBM],
    )
    ids = jnp.concatenate([ids, partner_ids], axis=0)
    lines = 2 * groups * new_count // LANES
    chunks = width // LANES
    extra = -(-PARTS * lines // PACK) * PACK
    sums = call(
        functools.partial(crowd_kernel, groups),
        jax.ShapeDtypeStruct((lines, LANES), jnp.float32),
        (ids, kept, new_heads, *others),
        (0, 0),
        spaces=[pl.ANY] + [VMEM] * (2 + len(others)),
    )
    mask = 2
    while mask < members // 4:
        ids = jnp.concatenate([ids, from_partner(ids, "member", mask)], axis=0)
        mask *= 2
    sums, ids = call(
        join_kernel,
        (
            jax.ShapeDtypeStruct(sums.shape, sums.dtype),
            jax.ShapeDtypeStruct((2 * mask, near), ids.dtype),
        ),
        (sums, from_partner(sums, "group", 1), ids, from_partner(ids, "member", mask)),
        (0, 0),
    )
    far_ids = from_partner(ids, "member", 2 * mask)
    mask = 2
    while mask < groups // 2:
        sums = sums + from_partner(sums, "group", mask)
        mask *= 2
    rows = call(
        functools.partial(gather_kernel, members, slots),
        jax.ShapeDtypeStruct((members * slots, width), jnp.bfloat16),
        (ids, far_ids, kept, sums),
        (2 * members * slots * head_dev * width, heads.size * 2),
        scratch=[pltpu.VMEM((members, near), jnp.int32)],
        spaces=[VMEM, VMEM, VMEM, pl.ANY],
    )
    message = call(
        functools.partial(pack_kernel, members, slots),
        jax.ShapeDtypeStruct((members, chunks * slots + extra, LANES), jnp.bfloat16),
        (rows, sums, from_partner(sums, "group", mask)),
        (0, members * slots * width * 4),
    )
    message = lax.all_to_all(message, "member", 0, 0, tiled=True)

    density, spread, reassign = call(
        functools.partial(
            tail_kernel, groups, slots, head_dev, float(head_dev * groups * members)
        ),
        (
            jax.ShapeDtypeStruct((1, new_count), jnp.float32),
            jax.ShapeDtypeStruct((1, new_count), jnp.float32),
            jax.ShapeDtypeStruct((1, near, vectors.shape[1]), jnp.float32),
        ),
        (near_ids, message, vectors),
        (4 * near * vectors.shape[1] * width, vectors.size * 4),
    )
    return (density[0], spread[0], reassign)


def solution(mesh):
    placed = (
        P(("group", "member"), None),
        P("group", None),
        P(("group", "member"), None, None),
        P(("group", "member"), None),
    )
    return jax.shard_map(
        per_device,
        mesh=mesh,
        in_specs=placed,
        out_specs=(P("group"), P("group"), P(("group", "member"), None, None)),
        check_vma=False,
    )
```

```python
import functools

import jax
import jax.numpy as jnp
from jax import lax
from jax.experimental import pallas as pl
from jax.experimental.pallas import tpu as pltpu
from jax.sharding import PartitionSpec as P

VMEM = pltpu.MemorySpace.VMEM
HBM = pltpu.MemorySpace.HBM
LANES = 128
PACK = 16
PARTS = 3
LIMIT = 24 * 2**20


def from_partner(value, axis, mask):
    count = lax.axis_size(axis)
    return lax.ppermute(value, axis, [(source, source ^ mask) for source in range(count)])


def on_odd(value, mask):
    groups, members = lax.axis_size("group"), lax.axis_size("member")
    pairs = [
        (group * members + member, group * members + (member ^ mask))
        for group in range(1, groups, 2) for member in range(members)
    ]
    return lax.ppermute(value, ("group", "member"), pairs)


def across_core(value, first):
    groups = lax.axis_size("group")
    return lax.ppermute(value, "group", [(group, group ^ 1) for group in range(first, groups, 2)])


def in_hbm(value):
    return pltpu.with_memory_space_constraint(value, HBM)


def call(body, shapes, operands, cost, scratch=(), spaces=None):
    return pl.pallas_call(
        body,
        out_shape=shapes,
        in_specs=[pl.BlockSpec(memory_space=space) for space in spaces or [VMEM] * len(operands)],
        out_specs=jax.tree.map(lambda unused: pl.BlockSpec(memory_space=VMEM), shapes),
        scratch_shapes=scratch,
        compiler_params=pltpu.CompilerParams(vmem_limit_bytes=LIMIT),
        cost_estimate=pl.CostEstimate(flops=cost[0], bytes_accessed=cost[1], transcendentals=0),
    )(*operands)


def iota(shape, dim):
    return lax.broadcasted_iota(jnp.int32, shape, dim)


def stage_kernel(ids_ref, kept_ref, sem):
    copy = pltpu.make_async_copy(ids_ref, kept_ref, sem)
    copy.start()
    copy.wait()


def early_kernel(heads_ref, new_ref, ids_ref, kept_ref, kept_new_ref, kept_ids_ref, sems):
    kept_ids_ref[...] = ids_ref[...]
    tiles = sems.shape[0] - 1
    tile = heads_ref.shape[0] // tiles
    parts = [pl.ds(i * tile, tile) for i in range(tiles)]
    pairs = [(heads_ref.at[part], kept_ref.at[part]) for part in parts]
    pairs.append((new_ref, kept_new_ref))
    copies = [pltpu.make_async_copy(*pair, sems.at[i]) for i, pair in enumerate(pairs)]
    for copy in copies:
        copy.start()
    for copy in copies:
        copy.wait()


def squares(block):
    width = block.shape[1]
    block = jnp.square(block.astype(jnp.float32))
    folded = block[:, :LANES]
    for column in range(LANES, width, LANES):
        folded = folded + block[:, column:column + LANES]
    return jnp.sum(folded.T, axis=0, keepdims=True)


def listed_rows(ids, me, slots, heads_ref):
    members, near = ids.shape
    head_dev = heads_ref.shape[0]
    local = ids - me * head_dev
    owned = (local >= 0) & (local < head_dev)
    earlier = (iota((near, near), 0) < iota((near, near), 1)).astype(jnp.bfloat16)
    rank = jnp.dot(owned.astype(jnp.bfloat16), earlier, preferred_element_type=jnp.float32)
    rank = jnp.where(owned, rank.astype(jnp.int32), -1)
    shape = (members, slots, near)
    pick = jnp.broadcast_to(rank[:, None, :], shape) == iota(shape, 1)
    wanted = jnp.sum(
        jnp.where(pick, jnp.broadcast_to(local[:, None, :] + 1, shape), 0), axis=2, keepdims=True
    ).reshape(members * slots, 1)
    onehot = (wanted == iota((members * slots, head_dev), 1) + 1).astype(jnp.bfloat16)
    return jnp.dot(
        onehot, heads_ref[...], preferred_element_type=jnp.float32
    ).astype(jnp.bfloat16)


def crowding(queries, heads_ref):
    head_dev, width = heads_ref.shape
    query_sq = jnp.sum(jnp.square(queries.astype(jnp.float32)), axis=1, keepdims=True)
    total_w = jnp.zeros((queries.shape[0], 1), jnp.float32)
    total_we = jnp.zeros((queries.shape[0], 1), jnp.float32)
    tile = 512
    for start in range(0, head_dev, tile):
        dots = lax.dot_general(
            queries, heads_ref[start:start + tile, :], (((1,), (1,)), ((), ())),
            preferred_element_type=jnp.float32,
        )
        head_sq = jnp.concatenate(
            [squares(heads_ref[row:row + LANES, :]) for row in range(start, start + tile, LANES)],
            axis=1,
        )
        excess = (query_sq + head_sq - 2.0 * dots) * (1.0 / width)
        inverse = 1.0 / (1.0 + excess)
        weight = inverse * inverse
        total_w = total_w + jnp.sum(weight, axis=1, keepdims=True)
        total_we = total_we + jnp.sum(weight * excess, axis=1, keepdims=True)
    return total_w, total_we


def crowd_kernel(groups, unused, heads_ref, *refs):
    query_refs, sums_ref = refs[:-1], refs[-1]
    here = lax.axis_index("group")
    queries = jnp.concatenate([ref[...] for ref in query_refs], axis=0)
    new_count = queries.shape[0] // groups
    totals = crowding(queries, heads_ref)
    lane = iota((new_count, LANES), 1)
    row = iota((new_count, LANES), 0)
    line = iota(sums_ref.shape, 0)
    sums = jnp.zeros(sums_ref.shape, jnp.float32)
    for mask in range(groups):
        part = slice(mask * new_count, (mask + 1) * new_count)
        for kind in range(2):
            place = (kind * groups + (here ^ mask)) * new_count
            spread_out = jnp.where(lane == row + place % LANES, totals[kind][part], 0.0)
            spread_out = jnp.sum(spread_out, axis=0, keepdims=True)
            sums = sums + jnp.where(line == place // LANES, spread_out, 0.0)
    sums_ref[...] = sums


def join_kernel(mine_ref, other_ref, low_ref, high_ref, sums_ref, ids_ref):
    half = low_ref.shape[0]
    sums_ref[...] = mine_ref[...] + other_ref[...]
    ids_ref[:half, :] = low_ref[...]
    ids_ref[half:, :] = high_ref[...]


def joined(mine, other, low, high):
    shapes = (
        jax.ShapeDtypeStruct(mine.shape, mine.dtype),
        jax.ShapeDtypeStruct((2 * low.shape[0], low.shape[1]), low.dtype),
    )
    return call(join_kernel, shapes, (mine, other, low, high), (0, 0))


def gather_kernel(members, slots, mine_ref, handed_ref, heads_ref, rows_ref):
    me = lax.axis_index("member")
    odd = lax.axis_index("group") % 2 == 1
    mine = [mine_ref[pl.ds(2 * (me ^ member), 1), :] for member in range(members)]
    handed = [handed_ref[pl.ds(2 * (me ^ member) + 1, 1), :] for member in range(members)]
    ids = jnp.where(odd, jnp.concatenate(mine, axis=0), jnp.concatenate(handed, axis=0))
    rows_ref[...] = listed_rows(ids, me, slots, heads_ref)


def pack_kernel(members, slots, rows_ref, sums_ref, out_ref):
    chunks = rows_ref.shape[1] // LANES
    for member in range(members):
        for chunk in range(chunks):
            out_ref[member, chunk * slots:(chunk + 1) * slots, :] = rows_ref[
                member * slots:(member + 1) * slots, chunk * LANES:(chunk + 1) * LANES
            ]
    sums = sums_ref[...]
    coded = []
    for unused in range(PARTS):
        coded.append(sums.astype(jnp.bfloat16).astype(jnp.float32))
        sums = sums - coded[-1]
    missing = out_ref.shape[1] - chunks * slots - PARTS * sums.shape[0]
    if missing:
        coded.append(jnp.zeros((missing, LANES), jnp.float32))
    tail = jnp.concatenate(coded, axis=0).astype(jnp.bfloat16)
    for member in range(members):
        out_ref[member, chunks * slots:, :] = tail


def distances(slots, head_dev, ids_ref, listed_ref, vectors_ref, out_ref):
    near = ids_ref.shape[1]
    members = listed_ref.shape[0]
    block, width = vectors_ref.shape[1:]
    square = (near, near)
    owner_row = jnp.broadcast_to(lax.div(ids_ref[...], head_dev), square)
    eye = iota(square, 0) == iota(square, 1)
    owner = jnp.sum(jnp.where(eye, owner_row, 0), axis=1, keepdims=True)
    before = (owner_row == owner) & (iota(square, 1) < iota(square, 0))
    place = jnp.sum(before.astype(jnp.int32), axis=1, keepdims=True)
    source = owner * slots + place
    back = (source == iota((near, members * slots), 1)).astype(jnp.bfloat16)
    rows = []
    for chunk in range(width // LANES):
        part = listed_ref[:, chunk * slots:(chunk + 1) * slots, :].reshape(members * slots, LANES)
        rows.append(jnp.dot(back, part, preferred_element_type=jnp.float32))
    rows = jnp.concatenate(rows, axis=1)
    row_sq = jnp.sum(jnp.square(rows), axis=1, keepdims=True)
    vec = vectors_ref[0]
    vec_sq = jnp.sum(jnp.square(vec.astype(jnp.float32)), axis=1, keepdims=True)
    turned = iota((block, block), 0) == iota((block, block), 1)
    vec_sq = jnp.sum(jnp.where(turned, vec_sq, 0.0), axis=0, keepdims=True)
    dots = lax.dot_general(
        rows.astype(jnp.bfloat16), vec, (((1,), (1,)), ((), ())),
        preferred_element_type=jnp.float32,
    )
    out_ref[0] = (row_sq + vec_sq - 2.0 * dots) * (1.0 / width)


def tail_kernel(
    groups, slots, head_dev, total_heads, ids_ref, listed_ref, vectors_ref,
    density_ref, spread_ref, out_ref,
):
    distances(slots, head_dev, ids_ref, listed_ref, vectors_ref, out_ref)
    here = lax.axis_index("group")
    members = listed_ref.shape[0]
    new_count = density_ref.shape[1]
    lines = 2 * groups * new_count // LANES
    first = vectors_ref.shape[2] // LANES * slots
    coded = jnp.sum(listed_ref[:, first:, :].astype(jnp.float32), axis=0)
    total = sum(coded[part * lines:(part + 1) * lines] for part in range(PARTS))
    shape = (new_count, LANES)
    eye = iota((new_count, new_count), 0) == iota((new_count, new_count), 1)
    found = []
    for kind in range(2):
        place = (kind * groups + here) * new_count
        line = jnp.sum(
            jnp.where(iota((lines, LANES), 0) == place // LANES, total, 0.0), axis=0, keepdims=True
        )
        column = jnp.sum(
            jnp.where(iota(shape, 1) == iota(shape, 0) + place % LANES, line, 0.0),
            axis=1, keepdims=True,
        )
        found.append(jnp.sum(jnp.where(eye, column, 0.0), axis=0, keepdims=True))
    density_ref[...] = jnp.log(found[0] * (1.0 / total_heads))
    spread_ref[...] = found[1] / found[0]


def per_device(heads, new_heads, vectors, near_ids):
    head_dev, width = heads.shape
    new_count = new_heads.shape[0]
    near = near_ids.shape[1]
    groups = lax.axis_size("group")
    members = lax.axis_size("member")
    most = 2 * near // members
    slots = -(-most // PACK) * PACK

    neighbour_ids = across_core(near_ids, 0)
    others = [from_partner(new_heads, "group", mask) for mask in range(1, groups)]
    ids = call(
        stage_kernel,
        jax.ShapeDtypeStruct(near_ids.shape, near_ids.dtype),
        (in_hbm(near_ids),),
        (0, 0),
        scratch=[pltpu.SemaphoreType.DMA],
        spaces=[HBM],
    )
    ids = jnp.concatenate([ids, neighbour_ids], axis=0)
    kept, new_heads, kept_ids = call(
        early_kernel,
        (
            jax.ShapeDtypeStruct(heads.shape, heads.dtype),
            jax.ShapeDtypeStruct(new_heads.shape, new_heads.dtype),
            jax.ShapeDtypeStruct(ids.shape, ids.dtype),
        ),
        (in_hbm(heads), in_hbm(new_heads), ids),
        (0, heads.size * 4),
        scratch=[pltpu.SemaphoreType.DMA((9,))],
        spaces=[HBM, HBM, VMEM],
    )
    ids = jnp.concatenate([kept_ids, on_odd(ids, 1)], axis=0)
    lines = 2 * groups * new_count // LANES
    chunks = width // LANES
    extra = -(-PARTS * lines // PACK) * PACK
    sums = call(
        functools.partial(crowd_kernel, groups),
        jax.ShapeDtypeStruct((lines, LANES), jnp.float32),
        (ids, kept, new_heads, *others),
        (0, 0),
        spaces=[pl.ANY] + [VMEM] * (2 + len(others)),
    )
    mask = 2
    while mask < members // 4:
        ids = jnp.concatenate([ids, on_odd(ids, mask)], axis=0)
        mask *= 2
    sums, ids = joined(sums, from_partner(sums, "group", 1), ids, on_odd(ids, mask))
    far_ids = on_odd(ids, 2 * mask)
    mask = 2
    while mask < groups // 2:
        sums = sums + from_partner(sums, "group", mask)
        mask *= 2
    sums, ids = joined(sums, from_partner(sums, "group", mask), ids, far_ids)
    rows = call(
        functools.partial(gather_kernel, members, slots),
        jax.ShapeDtypeStruct((members * slots, width), jnp.bfloat16),
        (ids, across_core(ids, 1), kept),
        (0, 0),
    )
    message = call(
        functools.partial(pack_kernel, members, slots),
        jax.ShapeDtypeStruct((members, chunks * slots + extra, LANES), jnp.bfloat16),
        (rows, sums),
        (0, 0),
    )
    message = lax.all_to_all(message, "member", 0, 0, tiled=True)

    density, spread, reassign = call(
        functools.partial(
            tail_kernel, groups, slots, head_dev, float(head_dev * groups * members)
        ),
        (
            jax.ShapeDtypeStruct((1, new_count), jnp.float32),
            jax.ShapeDtypeStruct((1, new_count), jnp.float32),
            jax.ShapeDtypeStruct((1, near, vectors.shape[1]), jnp.float32),
        ),
        (near_ids, message, vectors),
        (4 * near * vectors.shape[1] * width, vectors.size * 4),
    )
    return (density[0], spread[0], reassign)


def solution(mesh):
    placed = (
        P(("group", "member"), None),
        P("group", None),
        P(("group", "member"), None, None),
        P(("group", "member"), None),
    )
    return jax.shard_map(
        per_device,
        mesh=mesh,
        in_specs=placed,
        out_specs=(P("group"), P("group"), P(("group", "member"), None, None)),
        check_vma=False,
    )
```

```python
import functools

import jax
import jax.numpy as jnp
from jax import lax
from jax.experimental import pallas as pl
from jax.experimental.pallas import tpu as pltpu
from jax.sharding import PartitionSpec as P

VMEM = pltpu.MemorySpace.VMEM
HBM = pltpu.MemorySpace.HBM
LANES = 128
PACK = 16
PARTS = 3
LIMIT = 24 * 2**20


def from_partner(value, axis, mask):
    count = lax.axis_size(axis)
    return lax.ppermute(value, axis, [(source, source ^ mask) for source in range(count)])


def in_hbm(value):
    return pltpu.with_memory_space_constraint(value, HBM)


def call(body, shapes, operands, cost, scratch=(), spaces=None):
    return pl.pallas_call(
        body,
        out_shape=shapes,
        in_specs=[pl.BlockSpec(memory_space=space) for space in spaces or [VMEM] * len(operands)],
        out_specs=jax.tree.map(lambda unused: pl.BlockSpec(memory_space=VMEM), shapes),
        scratch_shapes=scratch,
        compiler_params=pltpu.CompilerParams(vmem_limit_bytes=LIMIT),
        cost_estimate=pl.CostEstimate(flops=cost[0], bytes_accessed=cost[1], transcendentals=0),
    )(*operands)


def iota(shape, dim):
    return lax.broadcasted_iota(jnp.int32, shape, dim)


def stage_kernel(ids_ref, kept_ref, sem):
    copy = pltpu.make_async_copy(ids_ref, kept_ref, sem)
    copy.start()
    copy.wait()


def early_kernel(heads_ref, new_ref, unused, kept_ref, head_sq_ref, kept_new_ref, sems):
    head_dev, width = heads_ref.shape
    tiles = 4
    tile = head_dev // tiles
    parts = [pl.ds(i * tile, tile) for i in range(tiles)]
    copies = [
        pltpu.make_async_copy(heads_ref.at[part], kept_ref.at[part], sems.at[i])
        for i, part in enumerate(parts)
    ]
    copies.append(pltpu.make_async_copy(new_ref, kept_new_ref, sems.at[tiles]))
    for copy in copies:
        copy.start()
    for i in range(tiles):
        copies[i].wait()
        for first in range(i * tile, (i + 1) * tile, LANES):
            block = jnp.square(kept_ref[first:first + LANES, :].astype(jnp.float32))
            folded = block[:, :LANES]
            for column in range(LANES, width, LANES):
                folded = folded + block[:, column:column + LANES]
            head_sq_ref[:, first:first + LANES] = jnp.sum(folded.T, axis=0, keepdims=True)
    for copy in copies[tiles:]:
        copy.wait()


def listed_rows(ids, me, slots, heads_ref):
    members, near = ids.shape
    head_dev = heads_ref.shape[0]
    local = ids - me * head_dev
    owned = (local >= 0) & (local < head_dev)
    earlier = (iota((near, near), 0) < iota((near, near), 1)).astype(jnp.bfloat16)
    rank = jnp.dot(owned.astype(jnp.bfloat16), earlier, preferred_element_type=jnp.float32)
    rank = jnp.where(owned, rank.astype(jnp.int32), -1)
    shape = (members, slots, near)
    pick = jnp.broadcast_to(rank[:, None, :], shape) == iota(shape, 1)
    wanted = jnp.sum(
        jnp.where(pick, jnp.broadcast_to(local[:, None, :] + 1, shape), 0), axis=2, keepdims=True
    ).reshape(members * slots, 1)
    onehot = (wanted == iota((members * slots, head_dev), 1) + 1).astype(jnp.bfloat16)
    return jnp.dot(
        onehot, heads_ref[...], preferred_element_type=jnp.float32
    ).astype(jnp.bfloat16)


def crowding(queries, heads_ref, head_sq_ref):
    head_dev, width = heads_ref.shape
    query_sq = jnp.sum(jnp.square(queries.astype(jnp.float32)), axis=1, keepdims=True)
    total_w = jnp.zeros((queries.shape[0], 1), jnp.float32)
    total_we = jnp.zeros((queries.shape[0], 1), jnp.float32)
    tile = 512
    for start in range(0, head_dev, tile):
        dots = lax.dot_general(
            queries, heads_ref[start:start + tile, :], (((1,), (1,)), ((), ())),
            preferred_element_type=jnp.float32,
        )
        head_sq = head_sq_ref[:, start:start + tile]
        excess = (query_sq + head_sq - 2.0 * dots) * (1.0 / width)
        inverse = 1.0 / (1.0 + excess)
        weight = inverse * inverse
        total_w = total_w + jnp.sum(weight, axis=1, keepdims=True)
        total_we = total_we + jnp.sum(weight * excess, axis=1, keepdims=True)
    return total_w, total_we


def crowd_kernel(groups, ids_ref, heads_ref, head_sq_ref, *refs):
    query_refs, (sums_ref, kept_ids_ref) = refs[:-2], refs[-2:]
    kept_ids_ref[...] = ids_ref[...]
    here = lax.axis_index("group")
    queries = jnp.concatenate([ref[...] for ref in query_refs], axis=0)
    new_count = queries.shape[0] // groups
    totals = crowding(queries, heads_ref, head_sq_ref)
    lane = iota((new_count, LANES), 1)
    row = iota((new_count, LANES), 0)
    line = iota(sums_ref.shape, 0)
    sums = jnp.zeros(sums_ref.shape, jnp.float32)
    for mask in range(groups):
        part = slice(mask * new_count, (mask + 1) * new_count)
        for kind in range(2):
            place = (kind * groups + (here ^ mask)) * new_count
            spread_out = jnp.where(lane == row + place % LANES, totals[kind][part], 0.0)
            spread_out = jnp.sum(spread_out, axis=0, keepdims=True)
            sums = sums + jnp.where(line == place // LANES, spread_out, 0.0)
    sums_ref[...] = sums


def gather_kernel(members, slots, near_ref, far_ref, heads_ref, unused, rows_ref, ids_ref):
    me = lax.axis_index("member")
    half = members // 2
    ids_ref[:half, :] = near_ref[...]
    ids_ref[half:, :] = far_ref[...]
    ids = jnp.concatenate([ids_ref[pl.ds(me ^ member, 1), :] for member in range(members)], axis=0)
    rows_ref[...] = listed_rows(ids, me, slots, heads_ref)


def pack_kernel(members, slots, rows_ref, mine_ref, other_ref, out_ref):
    chunks = rows_ref.shape[1] // LANES
    for member in range(members):
        for chunk in range(chunks):
            out_ref[member, chunk * slots:(chunk + 1) * slots, :] = rows_ref[
                member * slots:(member + 1) * slots, chunk * LANES:(chunk + 1) * LANES
            ]
    sums = mine_ref[...] + other_ref[...]
    coded = []
    for unused in range(PARTS):
        coded.append(sums.astype(jnp.bfloat16).astype(jnp.float32))
        sums = sums - coded[-1]
    missing = out_ref.shape[1] - chunks * slots - PARTS * sums.shape[0]
    if missing:
        coded.append(jnp.zeros((missing, LANES), jnp.float32))
    tail = jnp.concatenate(coded, axis=0).astype(jnp.bfloat16)
    for member in range(members):
        out_ref[member, chunks * slots:, :] = tail


def distances(slots, head_dev, ids_ref, listed_ref, vectors_ref, out_ref):
    near = ids_ref.shape[1]
    members = listed_ref.shape[0]
    block, width = vectors_ref.shape[1:]
    square = (near, near)
    owner_row = jnp.broadcast_to(lax.div(ids_ref[...], head_dev), square)
    eye = iota(square, 0) == iota(square, 1)
    owner = jnp.sum(jnp.where(eye, owner_row, 0), axis=1, keepdims=True)
    before = (owner_row == owner) & (iota(square, 1) < iota(square, 0))
    place = jnp.sum(before.astype(jnp.int32), axis=1, keepdims=True)
    source = owner * slots + place
    back = (source == iota((near, members * slots), 1)).astype(jnp.bfloat16)
    rows = []
    for chunk in range(width // LANES):
        part = listed_ref[:, chunk * slots:(chunk + 1) * slots, :].reshape(members * slots, LANES)
        rows.append(jnp.dot(back, part, preferred_element_type=jnp.float32))
    rows = jnp.concatenate(rows, axis=1)
    row_sq = jnp.sum(jnp.square(rows), axis=1, keepdims=True)
    vec = vectors_ref[0]
    vec_sq = jnp.sum(jnp.square(vec.astype(jnp.float32)), axis=1, keepdims=True)
    turned = iota((block, block), 0) == iota((block, block), 1)
    vec_sq = jnp.sum(jnp.where(turned, vec_sq, 0.0), axis=0, keepdims=True)
    dots = lax.dot_general(
        rows.astype(jnp.bfloat16), vec, (((1,), (1,)), ((), ())),
        preferred_element_type=jnp.float32,
    )
    out_ref[0] = (row_sq + vec_sq - 2.0 * dots) * (1.0 / width)


def tail_kernel(
    groups, slots, head_dev, total_heads, ids_ref, listed_ref, vectors_ref,
    density_ref, spread_ref, out_ref,
):
    distances(slots, head_dev, ids_ref, listed_ref, vectors_ref, out_ref)
    here = lax.axis_index("group")
    members = listed_ref.shape[0]
    new_count = density_ref.shape[1]
    lines = 2 * groups * new_count // LANES
    first = vectors_ref.shape[2] // LANES * slots
    coded = jnp.sum(listed_ref[:, first:, :].astype(jnp.float32), axis=0)
    total = sum(coded[part * lines:(part + 1) * lines] for part in range(PARTS))
    shape = (new_count, LANES)
    eye = iota((new_count, new_count), 0) == iota((new_count, new_count), 1)
    found = []
    for kind in range(2):
        place = (kind * groups + here) * new_count
        line = jnp.sum(
            jnp.where(iota((lines, LANES), 0) == place // LANES, total, 0.0), axis=0, keepdims=True
        )
        column = jnp.sum(
            jnp.where(iota(shape, 1) == iota(shape, 0) + place % LANES, line, 0.0),
            axis=1, keepdims=True,
        )
        found.append(jnp.sum(jnp.where(eye, column, 0.0), axis=0, keepdims=True))
    density_ref[...] = jnp.log(found[0] * (1.0 / total_heads))
    spread_ref[...] = found[1] / found[0]


def per_device(heads, new_heads, vectors, near_ids):
    head_dev, width = heads.shape
    new_count = new_heads.shape[0]
    near = near_ids.shape[1]
    groups = lax.axis_size("group")
    members = lax.axis_size("member")
    most = 2 * near // members
    slots = -(-most // PACK) * PACK

    partner_ids = from_partner(near_ids, "member", 1)
    others = [from_partner(new_heads, "group", mask) for mask in range(1, groups)]
    ids = call(
        stage_kernel,
        jax.ShapeDtypeStruct(near_ids.shape, near_ids.dtype),
        (in_hbm(near_ids),),
        (0, 0),
        scratch=[pltpu.SemaphoreType.DMA],
        spaces=[HBM],
    )
    ids = jnp.concatenate([ids, partner_ids], axis=0)
    kept, head_sq, new_heads = call(
        early_kernel,
        (
            jax.ShapeDtypeStruct(heads.shape, heads.dtype),
            jax.ShapeDtypeStruct((1, head_dev), jnp.float32),
            jax.ShapeDtypeStruct(new_heads.shape, new_heads.dtype),
        ),
        (in_hbm(heads), in_hbm(new_heads), ids),
        (0, 0),
        scratch=[pltpu.SemaphoreType.DMA((5,))],
        spaces=[HBM, HBM, pl.ANY],
    )
    lines = 2 * groups * new_count // LANES
    chunks = width // LANES
    extra = -(-PARTS * lines // PACK) * PACK
    sums, kept_ids = call(
        functools.partial(crowd_kernel, groups),
        (
            jax.ShapeDtypeStruct((lines, LANES), jnp.float32),
            jax.ShapeDtypeStruct(ids.shape, ids.dtype),
        ),
        (ids, kept, head_sq, new_heads, *others),
        (0, 0),
    )
    mask = 2
    while mask < members // 2:
        kept_ids = jnp.concatenate([kept_ids, from_partner(ids, "member", mask)], axis=0)
        ids = kept_ids
        mask *= 2
    far_ids = from_partner(ids, "member", mask)
    mask = 1
    while mask < groups // 2:
        sums = sums + from_partner(sums, "group", mask)
        mask *= 2
    rows = call(
        functools.partial(gather_kernel, members, slots),
        jax.ShapeDtypeStruct((members * slots, width), jnp.bfloat16),
        (ids, far_ids, kept, sums),
        (2 * members * slots * head_dev * width, heads.size * 2),
        scratch=[pltpu.VMEM((members, near), jnp.int32)],
        spaces=[VMEM, VMEM, VMEM, pl.ANY],
    )
    message = call(
        functools.partial(pack_kernel, members, slots),
        jax.ShapeDtypeStruct((members, chunks * slots + extra, LANES), jnp.bfloat16),
        (rows, sums, from_partner(sums, "group", mask)),
        (0, members * slots * width * 4),
    )
    message = lax.all_to_all(message, "member", 0, 0, tiled=True)

    density, spread, reassign = call(
        functools.partial(
            tail_kernel, groups, slots, head_dev, float(head_dev * groups * members)
        ),
        (
            jax.ShapeDtypeStruct((1, new_count), jnp.float32),
            jax.ShapeDtypeStruct((1, new_count), jnp.float32),
            jax.ShapeDtypeStruct((1, near, vectors.shape[1]), jnp.float32),
        ),
        (near_ids, message, vectors),
        (4 * near * vectors.shape[1] * width, vectors.size * 4),
    )
    return (density[0], spread[0], reassign)


def solution(mesh):
    placed = (
        P(("group", "member"), None),
        P("group", None),
        P(("group", "member"), None, None),
        P(("group", "member"), None),
    )
    return jax.shard_map(
        per_device,
        mesh=mesh,
        in_specs=placed,
        out_specs=(P("group"), P("group"), P(("group", "member"), None, None)),
        check_vma=False,
    )
```

```python
import functools

import jax
import jax.numpy as jnp
from jax import lax
from jax.experimental import pallas as pl
from jax.experimental.pallas import tpu as pltpu
from jax.sharding import PartitionSpec as P

VMEM = pltpu.MemorySpace.VMEM
HBM = pltpu.MemorySpace.HBM
LANES = 128
PACK = 16
TILE = 8
PARTS = 3
LIMIT = 24 * 2**20


def from_partner(value, axis, mask):
    count = lax.axis_size(axis)
    return lax.ppermute(value, axis, [(source, source ^ mask) for source in range(count)])


def in_hbm(value):
    return pltpu.with_memory_space_constraint(value, HBM)


def call(body, shapes, operands, cost, scratch=(), spaces=None):
    return pl.pallas_call(
        body,
        out_shape=shapes,
        in_specs=[pl.BlockSpec(memory_space=space) for space in spaces or [VMEM] * len(operands)],
        out_specs=jax.tree.map(lambda unused: pl.BlockSpec(memory_space=VMEM), shapes),
        scratch_shapes=scratch,
        compiler_params=pltpu.CompilerParams(vmem_limit_bytes=LIMIT),
        cost_estimate=pl.CostEstimate(flops=cost[0], bytes_accessed=cost[1], transcendentals=0),
    )(*operands)


def iota(shape, dim):
    return lax.broadcasted_iota(jnp.int32, shape, dim)


def stage_kernel(ids_ref, kept_ref, sem):
    copy = pltpu.make_async_copy(ids_ref, kept_ref, sem)
    copy.start()
    copy.wait()


def early_kernel(heads_ref, new_ref, unused, kept_ref, head_sq_ref, kept_new_ref, sems):
    head_dev, width = heads_ref.shape
    tiles = 4
    tile = head_dev // tiles
    parts = [pl.ds(i * tile, tile) for i in range(tiles)]
    copies = [
        pltpu.make_async_copy(heads_ref.at[part], kept_ref.at[part], sems.at[i])
        for i, part in enumerate(parts)
    ]
    copies.append(pltpu.make_async_copy(new_ref, kept_new_ref, sems.at[tiles]))
    for copy in copies:
        copy.start()
    for i in range(tiles):
        copies[i].wait()
        for first in range(i * tile, (i + 1) * tile, LANES):
            block = jnp.square(kept_ref[first:first + LANES, :].astype(jnp.float32))
            folded = block[:, :LANES]
            for column in range(LANES, width, LANES):
                folded = folded + block[:, column:column + LANES]
            head_sq_ref[:, first:first + LANES] = jnp.sum(folded.T, axis=0, keepdims=True)
    for copy in copies[tiles:]:
        copy.wait()


def listed_rows(ids, me, slots, heads_ref):
    members, near = ids.shape
    head_dev = heads_ref.shape[0]
    local = ids - me * head_dev
    owned = (local >= 0) & (local < head_dev)
    earlier = (iota((near, near), 0) < iota((near, near), 1)).astype(jnp.bfloat16)
    rank = jnp.dot(owned.astype(jnp.bfloat16), earlier, preferred_element_type=jnp.float32)
    rank = jnp.where(owned, rank.astype(jnp.int32), -1)
    shape = (members, slots, near)
    pick = jnp.broadcast_to(rank[:, None, :], shape) == iota(shape, 1)
    wanted = jnp.sum(
        jnp.where(pick, jnp.broadcast_to(local[:, None, :] + 1, shape), 0), axis=2, keepdims=True
    ).reshape(members * slots, 1)
    onehot = (wanted == iota((members * slots, head_dev), 1) + 1).astype(jnp.bfloat16)
    return jnp.dot(
        onehot, heads_ref[...], preferred_element_type=jnp.float32
    ).astype(jnp.bfloat16)


def crowding(queries, heads_ref, head_sq_ref):
    head_dev, width = heads_ref.shape
    query_sq = jnp.sum(jnp.square(queries.astype(jnp.float32)), axis=1, keepdims=True)
    total_w = jnp.zeros((queries.shape[0], 1), jnp.float32)
    total_we = jnp.zeros((queries.shape[0], 1), jnp.float32)
    tile = 512
    for start in range(0, head_dev, tile):
        dots = lax.dot_general(
            queries, heads_ref[start:start + tile, :], (((1,), (1,)), ((), ())),
            preferred_element_type=jnp.float32,
        )
        head_sq = head_sq_ref[:, start:start + tile]
        excess = (query_sq + head_sq - 2.0 * dots) * (1.0 / width)
        inverse = 1.0 / (1.0 + excess)
        weight = inverse * inverse
        total_w = total_w + jnp.sum(weight, axis=1, keepdims=True)
        total_we = total_we + jnp.sum(weight * excess, axis=1, keepdims=True)
    return total_w, total_we


def crowd_kernel(groups, ids_ref, heads_ref, head_sq_ref, *refs):
    query_refs, (sums_ref, kept_ids_ref) = refs[:-2], refs[-2:]
    kept_ids_ref[...] = ids_ref[...]
    here = lax.axis_index("group")
    queries = jnp.concatenate([ref[...] for ref in query_refs], axis=0)
    new_count = queries.shape[0] // groups
    totals = crowding(queries, heads_ref, head_sq_ref)
    lane = iota((new_count, LANES), 1)
    row = iota((new_count, LANES), 0)
    line = iota(sums_ref.shape, 0)
    sums = jnp.zeros(sums_ref.shape, jnp.float32)
    for mask in range(groups):
        part = slice(mask * new_count, (mask + 1) * new_count)
        for kind in range(2):
            place = (kind * groups + (here ^ mask)) * new_count
            spread_out = jnp.where(lane == row + place % LANES, totals[kind][part], 0.0)
            spread_out = jnp.sum(spread_out, axis=0, keepdims=True)
            sums = sums + jnp.where(line == place // LANES, spread_out, 0.0)
    sums_ref[...] = sums


def gather_kernel(members, slots, near_ref, far_ref, heads_ref, unused, rows_ref, ids_ref):
    me = lax.axis_index("member")
    half = members // 2
    ids_ref[:half, :] = near_ref[...]
    ids_ref[half:, :] = far_ref[...]
    ids = jnp.concatenate([ids_ref[pl.ds(me ^ member, 1), :] for member in range(members)], axis=0)
    rows_ref[...] = listed_rows(ids, me, slots, heads_ref)


def pack_kernel(members, slots, lines, rows_ref, mine_ref, other_ref, out_ref):
    chunks = rows_ref.shape[1] // LANES
    for member in range(members):
        for chunk in range(chunks):
            out_ref[member, chunk * slots:(chunk + 1) * slots, :] = rows_ref[
                member * slots:(member + 1) * slots, chunk * LANES:(chunk + 1) * LANES
            ]
    sums = (mine_ref[...] + other_ref[...])[:lines]
    coded = []
    for unused in range(PARTS):
        coded.append(sums.astype(jnp.bfloat16).astype(jnp.float32))
        sums = sums - coded[-1]
    missing = out_ref.shape[1] - chunks * slots - PARTS * lines
    if missing:
        coded.append(jnp.zeros((missing, LANES), jnp.float32))
    tail = jnp.concatenate(coded, axis=0).astype(jnp.bfloat16)
    for member in range(members):
        out_ref[member, chunks * slots:, :] = tail


def distances(slots, head_dev, ids_ref, listed_ref, vectors_ref, out_ref):
    near = ids_ref.shape[1]
    members = listed_ref.shape[0]
    block, width = vectors_ref.shape[1:]
    square = (near, near)
    owner_row = jnp.broadcast_to(lax.div(ids_ref[...], head_dev), square)
    eye = iota(square, 0) == iota(square, 1)
    owner = jnp.sum(jnp.where(eye, owner_row, 0), axis=1, keepdims=True)
    before = (owner_row == owner) & (iota(square, 1) < iota(square, 0))
    place = jnp.sum(before.astype(jnp.int32), axis=1, keepdims=True)
    source = owner * slots + place
    back = (source == iota((near, members * slots), 1)).astype(jnp.bfloat16)
    rows = []
    for chunk in range(width // LANES):
        part = listed_ref[:, chunk * slots:(chunk + 1) * slots, :].reshape(members * slots, LANES)
        rows.append(jnp.dot(back, part, preferred_element_type=jnp.float32))
    rows = jnp.concatenate(rows, axis=1)
    row_sq = jnp.sum(jnp.square(rows), axis=1, keepdims=True)
    vec = vectors_ref[0]
    vec_sq = jnp.sum(jnp.square(vec.astype(jnp.float32)), axis=1, keepdims=True)
    turned = iota((block, block), 0) == iota((block, block), 1)
    vec_sq = jnp.sum(jnp.where(turned, vec_sq, 0.0), axis=0, keepdims=True)
    dots = lax.dot_general(
        rows.astype(jnp.bfloat16), vec, (((1,), (1,)), ((), ())),
        preferred_element_type=jnp.float32,
    )
    out_ref[0] = (row_sq + vec_sq - 2.0 * dots) * (1.0 / width)


def tail_kernel(
    groups, slots, head_dev, total_heads, ids_ref, listed_ref, vectors_ref,
    density_ref, spread_ref, out_ref,
):
    distances(slots, head_dev, ids_ref, listed_ref, vectors_ref, out_ref)
    here = lax.axis_index("group")
    members = listed_ref.shape[0]
    new_count = density_ref.shape[1]
    lines = 2 * groups * new_count // LANES
    first = vectors_ref.shape[2] // LANES * slots
    coded = jnp.sum(listed_ref[:, first:, :].astype(jnp.float32), axis=0)
    total = sum(coded[part * lines:(part + 1) * lines] for part in range(PARTS))
    shape = (new_count, LANES)
    eye = iota((new_count, new_count), 0) == iota((new_count, new_count), 1)
    found = []
    for kind in range(2):
        place = (kind * groups + here) * new_count
        line = jnp.sum(
            jnp.where(iota((lines, LANES), 0) == place // LANES, total, 0.0), axis=0, keepdims=True
        )
        column = jnp.sum(
            jnp.where(iota(shape, 1) == iota(shape, 0) + place % LANES, line, 0.0),
            axis=1, keepdims=True,
        )
        found.append(jnp.sum(jnp.where(eye, column, 0.0), axis=0, keepdims=True))
    density_ref[...] = jnp.log(found[0] * (1.0 / total_heads))
    spread_ref[...] = found[1] / found[0]


def per_device(heads, new_heads, vectors, near_ids):
    head_dev, width = heads.shape
    new_count = new_heads.shape[0]
    near = near_ids.shape[1]
    groups = lax.axis_size("group")
    members = lax.axis_size("member")
    most = 2 * near // members
    slots = -(-most // PACK) * PACK

    partner_ids = from_partner(near_ids, "member", 1)
    others = [from_partner(new_heads, "group", mask) for mask in range(1, groups)]
    ids = call(
        stage_kernel,
        jax.ShapeDtypeStruct(near_ids.shape, near_ids.dtype),
        (in_hbm(near_ids),),
        (0, 0),
        scratch=[pltpu.SemaphoreType.DMA],
        spaces=[HBM],
    )
    ids = jnp.concatenate([ids, partner_ids], axis=0)
    kept, head_sq, new_heads = call(
        early_kernel,
        (
            jax.ShapeDtypeStruct(heads.shape, heads.dtype),
            jax.ShapeDtypeStruct((1, head_dev), jnp.float32),
            jax.ShapeDtypeStruct(new_heads.shape, new_heads.dtype),
        ),
        (in_hbm(heads), in_hbm(new_heads), ids),
        (0, 0),
        scratch=[pltpu.SemaphoreType.DMA((5,))],
        spaces=[HBM, HBM, pl.ANY],
    )
    lines = 2 * groups * new_count // LANES
    chunks = width // LANES
    extra = -(-PARTS * lines // TILE) * TILE
    sums, kept_ids = call(
        functools.partial(crowd_kernel, groups),
        (
            jax.ShapeDtypeStruct((-(-lines // TILE) * TILE, LANES), jnp.float32),
            jax.ShapeDtypeStruct(ids.shape, ids.dtype),
        ),
        (ids, kept, head_sq, new_heads, *others),
        (0, 0),
    )
    mask = 2
    while mask < members // 2:
        kept_ids = jnp.concatenate([kept_ids, from_partner(ids, "member", mask)], axis=0)
        ids = kept_ids
        mask *= 2
    far_ids = from_partner(ids, "member", mask)
    mask = 1
    while mask < groups // 2:
        sums = sums + from_partner(sums, "group", mask)
        mask *= 2
    rows = call(
        functools.partial(gather_kernel, members, slots),
        jax.ShapeDtypeStruct((members * slots, width), jnp.bfloat16),
        (ids, far_ids, kept, sums),
        (2 * members * slots * head_dev * width, heads.size * 2),
        scratch=[pltpu.VMEM((members, near), jnp.int32)],
        spaces=[VMEM, VMEM, VMEM, pl.ANY],
    )
    message = call(
        functools.partial(pack_kernel, members, slots, lines),
        jax.ShapeDtypeStruct((members, chunks * slots + extra, LANES), jnp.bfloat16),
        (rows, sums, from_partner(sums, "group", mask)),
        (0, members * slots * width * 4),
    )
    message = lax.all_to_all(message, "member", 0, 0, tiled=True)

    density, spread, reassign = call(
        functools.partial(
            tail_kernel, groups, slots, head_dev, float(head_dev * groups * members)
        ),
        (
            jax.ShapeDtypeStruct((1, new_count), jnp.float32),
            jax.ShapeDtypeStruct((1, new_count), jnp.float32),
            jax.ShapeDtypeStruct((1, near, vectors.shape[1]), jnp.float32),
        ),
        (near_ids, message, vectors),
        (4 * near * vectors.shape[1] * width, vectors.size * 4),
    )
    return (density[0], spread[0], reassign)


def solution(mesh):
    placed = (
        P(("group", "member"), None),
        P("group", None),
        P(("group", "member"), None, None),
        P(("group", "member"), None),
    )
    return jax.shard_map(
        per_device,
        mesh=mesh,
        in_specs=placed,
        out_specs=(P("group"), P("group"), P(("group", "member"), None, None)),
        check_vma=False,
    )
```

```python
import functools

import jax
import jax.numpy as jnp
from jax import lax
from jax.experimental import pallas as pl
from jax.experimental.pallas import tpu as pltpu
from jax.sharding import PartitionSpec as P

VMEM = pltpu.MemorySpace.VMEM
HBM = pltpu.MemorySpace.HBM
LANES = 128
PACK = 16
TILE = 8
PARTS = 3
LIMIT = 24 * 2**20


def from_partner(value, axis, mask):
    count = lax.axis_size(axis)
    return lax.ppermute(value, axis, [(source, source ^ mask) for source in range(count)])


def ring(members):
    return [*range(0, members, 2), *range(members - 1, 0, -2)]


def ring_place(member, members):
    return jnp.where(member % 2 == 0, member // 2, members - 1 - member // 2)


def in_hbm(value):
    return pltpu.with_memory_space_constraint(value, HBM)


def call(body, shapes, operands, cost, scratch=(), spaces=None):
    return pl.pallas_call(
        body,
        out_shape=shapes,
        in_specs=[pl.BlockSpec(memory_space=space) for space in spaces or [VMEM] * len(operands)],
        out_specs=jax.tree.map(lambda unused: pl.BlockSpec(memory_space=VMEM), shapes),
        scratch_shapes=scratch,
        compiler_params=pltpu.CompilerParams(vmem_limit_bytes=LIMIT),
        cost_estimate=pl.CostEstimate(flops=cost[0], bytes_accessed=cost[1], transcendentals=0),
    )(*operands)


def iota(shape, dim):
    return lax.broadcasted_iota(jnp.int32, shape, dim)


def stage_kernel(ids_ref, kept_ref, sem):
    copy = pltpu.make_async_copy(ids_ref, kept_ref, sem)
    copy.start()
    copy.wait()


def early_kernel(heads_ref, new_ref, unused, kept_ref, head_sq_ref, kept_new_ref, sems):
    head_dev, width = heads_ref.shape
    tiles = 4
    tile = head_dev // tiles
    parts = [pl.ds(i * tile, tile) for i in range(tiles)]
    copies = [
        pltpu.make_async_copy(heads_ref.at[part], kept_ref.at[part], sems.at[i])
        for i, part in enumerate(parts)
    ]
    copies.append(pltpu.make_async_copy(new_ref, kept_new_ref, sems.at[tiles]))
    for copy in copies:
        copy.start()
    for i in range(tiles):
        copies[i].wait()
        for first in range(i * tile, (i + 1) * tile, LANES):
            block = jnp.square(kept_ref[first:first + LANES, :].astype(jnp.float32))
            folded = block[:, :LANES]
            for column in range(LANES, width, LANES):
                folded = folded + block[:, column:column + LANES]
            head_sq_ref[:, first:first + LANES] = jnp.sum(folded.T, axis=0, keepdims=True)
    for copy in copies[tiles:]:
        copy.wait()


def listed_rows(ids, me, slots, heads_ref):
    members, near = ids.shape
    head_dev = heads_ref.shape[0]
    local = ids - me * head_dev
    owned = (local >= 0) & (local < head_dev)
    earlier = (iota((near, near), 0) < iota((near, near), 1)).astype(jnp.bfloat16)
    rank = jnp.dot(owned.astype(jnp.bfloat16), earlier, preferred_element_type=jnp.float32)
    rank = jnp.where(owned, rank.astype(jnp.int32), -1)
    shape = (members, slots, near)
    pick = jnp.broadcast_to(rank[:, None, :], shape) == iota(shape, 1)
    wanted = jnp.sum(
        jnp.where(pick, jnp.broadcast_to(local[:, None, :] + 1, shape), 0), axis=2, keepdims=True
    ).reshape(members * slots, 1)
    onehot = (wanted == iota((members * slots, head_dev), 1) + 1).astype(jnp.bfloat16)
    return jnp.dot(
        onehot, heads_ref[...], preferred_element_type=jnp.float32
    ).astype(jnp.bfloat16)


def crowding(queries, heads_ref, head_sq_ref):
    head_dev, width = heads_ref.shape
    query_sq = jnp.sum(jnp.square(queries.astype(jnp.float32)), axis=1, keepdims=True)
    total_w = jnp.zeros((queries.shape[0], 1), jnp.float32)
    total_we = jnp.zeros((queries.shape[0], 1), jnp.float32)
    tile = 512
    for start in range(0, head_dev, tile):
        dots = lax.dot_general(
            queries, heads_ref[start:start + tile, :], (((1,), (1,)), ((), ())),
            preferred_element_type=jnp.float32,
        )
        head_sq = head_sq_ref[:, start:start + tile]
        excess = (query_sq + head_sq - 2.0 * dots) * (1.0 / width)
        inverse = 1.0 / (1.0 + excess)
        weight = inverse * inverse
        total_w = total_w + jnp.sum(weight, axis=1, keepdims=True)
        total_we = total_we + jnp.sum(weight * excess, axis=1, keepdims=True)
    return total_w, total_we


def crowd_kernel(groups, ids_ref, heads_ref, head_sq_ref, *refs):
    query_refs, (sums_ref, kept_ids_ref) = refs[:-2], refs[-2:]
    kept_ids_ref[...] = ids_ref[...]
    here = lax.axis_index("group")
    queries = jnp.concatenate([ref[...] for ref in query_refs], axis=0)
    new_count = queries.shape[0] // groups
    totals = crowding(queries, heads_ref, head_sq_ref)
    lane = iota((new_count, LANES), 1)
    row = iota((new_count, LANES), 0)
    line = iota(sums_ref.shape, 0)
    sums = jnp.zeros(sums_ref.shape, jnp.float32)
    for mask in range(groups):
        part = slice(mask * new_count, (mask + 1) * new_count)
        for kind in range(2):
            place = (kind * groups + (here ^ mask)) * new_count
            spread_out = jnp.where(lane == row + place % LANES, totals[kind][part], 0.0)
            spread_out = jnp.sum(spread_out, axis=0, keepdims=True)
            sums = sums + jnp.where(line == place // LANES, spread_out, 0.0)
    sums_ref[...] = sums


def gather_kernel(members, slots, near_ref, far_ref, heads_ref, unused, rows_ref, ids_ref):
    me = lax.axis_index("member")
    half = members // 2
    ids_ref[:half, :] = near_ref[...]
    ids_ref[half:, :] = far_ref[...]
    ids = jnp.concatenate([ids_ref[pl.ds(me ^ member, 1), :] for member in ring(members)], axis=0)
    rows_ref[...] = listed_rows(ids, me, slots, heads_ref)


def pack_kernel(members, slots, lines, rows_ref, mine_ref, other_ref, out_ref):
    chunks = rows_ref.shape[1] // LANES
    for member in range(members):
        for chunk in range(chunks):
            out_ref[member, chunk * slots:(chunk + 1) * slots, :] = rows_ref[
                member * slots:(member + 1) * slots, chunk * LANES:(chunk + 1) * LANES
            ]
    sums = (mine_ref[...] + other_ref[...])[:lines]
    coded = []
    for unused in range(PARTS):
        coded.append(sums.astype(jnp.bfloat16).astype(jnp.float32))
        sums = sums - coded[-1]
    missing = out_ref.shape[1] - chunks * slots - PARTS * lines
    if missing:
        coded.append(jnp.zeros((missing, LANES), jnp.float32))
    tail = jnp.concatenate(coded, axis=0).astype(jnp.bfloat16)
    for member in range(members):
        out_ref[member, chunks * slots:, :] = tail


def distances(slots, head_dev, ids_ref, listed_ref, vectors_ref, out_ref):
    near = ids_ref.shape[1]
    members = listed_ref.shape[0]
    block, width = vectors_ref.shape[1:]
    square = (near, near)
    owner_row = jnp.broadcast_to(lax.div(ids_ref[...], head_dev), square)
    eye = iota(square, 0) == iota(square, 1)
    owner = jnp.sum(jnp.where(eye, owner_row, 0), axis=1, keepdims=True)
    before = (owner_row == owner) & (iota(square, 1) < iota(square, 0))
    place = jnp.sum(before.astype(jnp.int32), axis=1, keepdims=True)
    source = ring_place(owner, members) * slots + place
    back = (source == iota((near, members * slots), 1)).astype(jnp.bfloat16)
    rows = []
    for chunk in range(width // LANES):
        part = listed_ref[:, chunk * slots:(chunk + 1) * slots, :].reshape(members * slots, LANES)
        rows.append(jnp.dot(back, part, preferred_element_type=jnp.float32))
    rows = jnp.concatenate(rows, axis=1)
    row_sq = jnp.sum(jnp.square(rows), axis=1, keepdims=True)
    vec = vectors_ref[0]
    vec_sq = jnp.sum(jnp.square(vec.astype(jnp.float32)), axis=1, keepdims=True)
    turned = iota((block, block), 0) == iota((block, block), 1)
    vec_sq = jnp.sum(jnp.where(turned, vec_sq, 0.0), axis=0, keepdims=True)
    dots = lax.dot_general(
        rows.astype(jnp.bfloat16), vec, (((1,), (1,)), ((), ())),
        preferred_element_type=jnp.float32,
    )
    out_ref[0] = (row_sq + vec_sq - 2.0 * dots) * (1.0 / width)


def tail_kernel(
    groups, slots, head_dev, total_heads, ids_ref, listed_ref, vectors_ref,
    density_ref, spread_ref, out_ref,
):
    distances(slots, head_dev, ids_ref, listed_ref, vectors_ref, out_ref)
    here = lax.axis_index("group")
    members = listed_ref.shape[0]
    new_count = density_ref.shape[1]
    lines = 2 * groups * new_count // LANES
    first = vectors_ref.shape[2] // LANES * slots
    coded = jnp.sum(listed_ref[:, first:, :].astype(jnp.float32), axis=0)
    total = sum(coded[part * lines:(part + 1) * lines] for part in range(PARTS))
    shape = (new_count, LANES)
    eye = iota((new_count, new_count), 0) == iota((new_count, new_count), 1)
    found = []
    for kind in range(2):
        place = (kind * groups + here) * new_count
        line = jnp.sum(
            jnp.where(iota((lines, LANES), 0) == place // LANES, total, 0.0), axis=0, keepdims=True
        )
        column = jnp.sum(
            jnp.where(iota(shape, 1) == iota(shape, 0) + place % LANES, line, 0.0),
            axis=1, keepdims=True,
        )
        found.append(jnp.sum(jnp.where(eye, column, 0.0), axis=0, keepdims=True))
    density_ref[...] = jnp.log(found[0] * (1.0 / total_heads))
    spread_ref[...] = found[1] / found[0]


def per_device(heads, new_heads, vectors, near_ids):
    head_dev, width = heads.shape
    new_count = new_heads.shape[0]
    near = near_ids.shape[1]
    groups = lax.axis_size("group")
    members = lax.axis_size("member")
    most = 2 * near // members
    slots = -(-most // PACK) * PACK

    partner_ids = from_partner(near_ids, "member", 1)
    others = [from_partner(new_heads, "group", mask) for mask in range(1, groups)]
    ids = call(
        stage_kernel,
        jax.ShapeDtypeStruct(near_ids.shape, near_ids.dtype),
        (in_hbm(near_ids),),
        (0, 0),
        scratch=[pltpu.SemaphoreType.DMA],
        spaces=[HBM],
    )
    ids = jnp.concatenate([ids, partner_ids], axis=0)
    kept, head_sq, new_heads = call(
        early_kernel,
        (
            jax.ShapeDtypeStruct(heads.shape, heads.dtype),
            jax.ShapeDtypeStruct((1, head_dev), jnp.float32),
            jax.ShapeDtypeStruct(new_heads.shape, new_heads.dtype),
        ),
        (in_hbm(heads), in_hbm(new_heads), ids),
        (0, 0),
        scratch=[pltpu.SemaphoreType.DMA((5,))],
        spaces=[HBM, HBM, pl.ANY],
    )
    lines = 2 * groups * new_count // LANES
    chunks = width // LANES
    extra = -(-PARTS * lines // TILE) * TILE
    sums, kept_ids = call(
        functools.partial(crowd_kernel, groups),
        (
            jax.ShapeDtypeStruct((-(-lines // TILE) * TILE, LANES), jnp.float32),
            jax.ShapeDtypeStruct(ids.shape, ids.dtype),
        ),
        (ids, kept, head_sq, new_heads, *others),
        (0, 0),
    )
    mask = 2
    while mask < members // 2:
        kept_ids = jnp.concatenate([kept_ids, from_partner(ids, "member", mask)], axis=0)
        ids = kept_ids
        mask *= 2
    far_ids = from_partner(ids, "member", mask)
    mask = 1
    while mask < groups // 2:
        sums = sums + from_partner(sums, "group", mask)
        mask *= 2
    rows = call(
        functools.partial(gather_kernel, members, slots),
        jax.ShapeDtypeStruct((members * slots, width), jnp.bfloat16),
        (ids, far_ids, kept, sums),
        (2 * members * slots * head_dev * width, heads.size * 2),
        scratch=[pltpu.VMEM((members, near), jnp.int32)],
        spaces=[VMEM, VMEM, VMEM, pl.ANY],
    )
    message = call(
        functools.partial(pack_kernel, members, slots, lines),
        jax.ShapeDtypeStruct((members, chunks * slots + extra, LANES), jnp.bfloat16),
        (rows, sums, from_partner(sums, "group", mask)),
        (0, members * slots * width * 4),
    )
    message = lax.all_to_all(
        message, "member", 0, 0, tiled=True, axis_index_groups=[ring(members)]
    )

    density, spread, reassign = call(
        functools.partial(
            tail_kernel, groups, slots, head_dev, float(head_dev * groups * members)
        ),
        (
            jax.ShapeDtypeStruct((1, new_count), jnp.float32),
            jax.ShapeDtypeStruct((1, new_count), jnp.float32),
            jax.ShapeDtypeStruct((1, near, vectors.shape[1]), jnp.float32),
        ),
        (near_ids, message, vectors),
        (4 * near * vectors.shape[1] * width, vectors.size * 4),
    )
    return (density[0], spread[0], reassign)


def solution(mesh):
    placed = (
        P(("group", "member"), None),
        P("group", None),
        P(("group", "member"), None, None),
        P(("group", "member"), None),
    )
    return jax.shard_map(
        per_device,
        mesh=mesh,
        in_specs=placed,
        out_specs=(P("group"), P("group"), P(("group", "member"), None, None)),
        check_vma=False,
    )
```

```python
import functools

import jax
import jax.numpy as jnp
from jax import lax
from jax.experimental import pallas as pl
from jax.experimental.pallas import tpu as pltpu
from jax.sharding import PartitionSpec as P

VMEM = pltpu.MemorySpace.VMEM
HBM = pltpu.MemorySpace.HBM
LANES = 128
PACK = 16
TILE = 8
PARTS = 3
LIMIT = 24 * 2**20


def from_partner(value, axis, mask):
    count = lax.axis_size(axis)
    return lax.ppermute(value, axis, [(source, source ^ mask) for source in range(count)])


def turned(members):
    return [member ^ (members // 2) for member in range(members)]


def in_hbm(value):
    return pltpu.with_memory_space_constraint(value, HBM)


def call(body, shapes, operands, cost, scratch=(), spaces=None):
    return pl.pallas_call(
        body,
        out_shape=shapes,
        in_specs=[pl.BlockSpec(memory_space=space) for space in spaces or [VMEM] * len(operands)],
        out_specs=jax.tree.map(lambda unused: pl.BlockSpec(memory_space=VMEM), shapes),
        scratch_shapes=scratch,
        compiler_params=pltpu.CompilerParams(vmem_limit_bytes=LIMIT),
        cost_estimate=pl.CostEstimate(flops=cost[0], bytes_accessed=cost[1], transcendentals=0),
    )(*operands)


def iota(shape, dim):
    return lax.broadcasted_iota(jnp.int32, shape, dim)


def stage_kernel(ids_ref, kept_ref, sem):
    copy = pltpu.make_async_copy(ids_ref, kept_ref, sem)
    copy.start()
    copy.wait()


def early_kernel(heads_ref, new_ref, unused, kept_ref, head_sq_ref, kept_new_ref, sems):
    head_dev, width = heads_ref.shape
    tiles = 4
    tile = head_dev // tiles
    parts = [pl.ds(i * tile, tile) for i in range(tiles)]
    copies = [
        pltpu.make_async_copy(heads_ref.at[part], kept_ref.at[part], sems.at[i])
        for i, part in enumerate(parts)
    ]
    copies.append(pltpu.make_async_copy(new_ref, kept_new_ref, sems.at[tiles]))
    for copy in copies:
        copy.start()
    for i in range(tiles):
        copies[i].wait()
        for first in range(i * tile, (i + 1) * tile, LANES):
            block = jnp.square(kept_ref[first:first + LANES, :].astype(jnp.float32))
            folded = block[:, :LANES]
            for column in range(LANES, width, LANES):
                folded = folded + block[:, column:column + LANES]
            head_sq_ref[:, first:first + LANES] = jnp.sum(folded.T, axis=0, keepdims=True)
    for copy in copies[tiles:]:
        copy.wait()


def listed_rows(ids, me, slots, heads_ref):
    members, near = ids.shape
    head_dev = heads_ref.shape[0]
    local = ids - me * head_dev
    owned = (local >= 0) & (local < head_dev)
    earlier = (iota((near, near), 0) < iota((near, near), 1)).astype(jnp.bfloat16)
    rank = jnp.dot(owned.astype(jnp.bfloat16), earlier, preferred_element_type=jnp.float32)
    rank = jnp.where(owned, rank.astype(jnp.int32), -1)
    shape = (members, slots, near)
    pick = jnp.broadcast_to(rank[:, None, :], shape) == iota(shape, 1)
    wanted = jnp.sum(
        jnp.where(pick, jnp.broadcast_to(local[:, None, :] + 1, shape), 0), axis=2, keepdims=True
    ).reshape(members * slots, 1)
    onehot = (wanted == iota((members * slots, head_dev), 1) + 1).astype(jnp.bfloat16)
    return jnp.dot(
        onehot, heads_ref[...], preferred_element_type=jnp.float32
    ).astype(jnp.bfloat16)


def crowding(queries, heads_ref, head_sq_ref):
    head_dev, width = heads_ref.shape
    query_sq = jnp.sum(jnp.square(queries.astype(jnp.float32)), axis=1, keepdims=True)
    total_w = jnp.zeros((queries.shape[0], 1), jnp.float32)
    total_we = jnp.zeros((queries.shape[0], 1), jnp.float32)
    tile = 512
    for start in range(0, head_dev, tile):
        dots = lax.dot_general(
            queries, heads_ref[start:start + tile, :], (((1,), (1,)), ((), ())),
            preferred_element_type=jnp.float32,
        )
        head_sq = head_sq_ref[:, start:start + tile]
        excess = (query_sq + head_sq - 2.0 * dots) * (1.0 / width)
        inverse = 1.0 / (1.0 + excess)
        weight = inverse * inverse
        total_w = total_w + jnp.sum(weight, axis=1, keepdims=True)
        total_we = total_we + jnp.sum(weight * excess, axis=1, keepdims=True)
    return total_w, total_we


def crowd_kernel(groups, ids_ref, heads_ref, head_sq_ref, *refs):
    query_refs, (sums_ref, kept_ids_ref) = refs[:-2], refs[-2:]
    kept_ids_ref[...] = ids_ref[...]
    here = lax.axis_index("group")
    queries = jnp.concatenate([ref[...] for ref in query_refs], axis=0)
    new_count = queries.shape[0] // groups
    totals = crowding(queries, heads_ref, head_sq_ref)
    lane = iota((new_count, LANES), 1)
    row = iota((new_count, LANES), 0)
    line = iota(sums_ref.shape, 0)
    sums = jnp.zeros(sums_ref.shape, jnp.float32)
    for mask in range(groups):
        part = slice(mask * new_count, (mask + 1) * new_count)
        for kind in range(2):
            place = (kind * groups + (here ^ mask)) * new_count
            spread_out = jnp.where(lane == row + place % LANES, totals[kind][part], 0.0)
            spread_out = jnp.sum(spread_out, axis=0, keepdims=True)
            sums = sums + jnp.where(line == place // LANES, spread_out, 0.0)
    sums_ref[...] = sums


def gather_kernel(members, slots, near_ref, far_ref, heads_ref, unused, rows_ref, ids_ref):
    me = lax.axis_index("member")
    half = members // 2
    ids_ref[:half, :] = near_ref[...]
    ids_ref[half:, :] = far_ref[...]
    ids = jnp.concatenate([ids_ref[pl.ds(me ^ member, 1), :] for member in turned(members)], axis=0)
    rows_ref[...] = listed_rows(ids, me, slots, heads_ref)


def pack_kernel(members, slots, lines, rows_ref, mine_ref, other_ref, out_ref):
    chunks = rows_ref.shape[1] // LANES
    for member in range(members):
        for chunk in range(chunks):
            out_ref[member, chunk * slots:(chunk + 1) * slots, :] = rows_ref[
                member * slots:(member + 1) * slots, chunk * LANES:(chunk + 1) * LANES
            ]
    sums = (mine_ref[...] + other_ref[...])[:lines]
    coded = []
    for unused in range(PARTS):
        coded.append(sums.astype(jnp.bfloat16).astype(jnp.float32))
        sums = sums - coded[-1]
    missing = out_ref.shape[1] - chunks * slots - PARTS * lines
    if missing:
        coded.append(jnp.zeros((missing, LANES), jnp.float32))
    tail = jnp.concatenate(coded, axis=0).astype(jnp.bfloat16)
    for member in range(members):
        out_ref[member, chunks * slots:, :] = tail


def distances(slots, head_dev, ids_ref, listed_ref, vectors_ref, out_ref):
    near = ids_ref.shape[1]
    members = listed_ref.shape[0]
    block, width = vectors_ref.shape[1:]
    square = (near, near)
    owner_row = jnp.broadcast_to(lax.div(ids_ref[...], head_dev), square)
    eye = iota(square, 0) == iota(square, 1)
    owner = jnp.sum(jnp.where(eye, owner_row, 0), axis=1, keepdims=True)
    before = (owner_row == owner) & (iota(square, 1) < iota(square, 0))
    place = jnp.sum(before.astype(jnp.int32), axis=1, keepdims=True)
    source = (owner ^ (members // 2)) * slots + place
    back = (source == iota((near, members * slots), 1)).astype(jnp.bfloat16)
    rows = []
    for chunk in range(width // LANES):
        part = listed_ref[:, chunk * slots:(chunk + 1) * slots, :].reshape(members * slots, LANES)
        rows.append(jnp.dot(back, part, preferred_element_type=jnp.float32))
    rows = jnp.concatenate(rows, axis=1)
    row_sq = jnp.sum(jnp.square(rows), axis=1, keepdims=True)
    vec = vectors_ref[0]
    vec_sq = jnp.sum(jnp.square(vec.astype(jnp.float32)), axis=1, keepdims=True)
    diagonal = iota((block, block), 0) == iota((block, block), 1)
    vec_sq = jnp.sum(jnp.where(diagonal, vec_sq, 0.0), axis=0, keepdims=True)
    dots = lax.dot_general(
        rows.astype(jnp.bfloat16), vec, (((1,), (1,)), ((), ())),
        preferred_element_type=jnp.float32,
    )
    out_ref[0] = (row_sq + vec_sq - 2.0 * dots) * (1.0 / width)


def tail_kernel(
    groups, slots, head_dev, total_heads, ids_ref, listed_ref, vectors_ref,
    density_ref, spread_ref, out_ref,
):
    distances(slots, head_dev, ids_ref, listed_ref, vectors_ref, out_ref)
    here = lax.axis_index("group")
    members = listed_ref.shape[0]
    new_count = density_ref.shape[1]
    lines = 2 * groups * new_count // LANES
    first = vectors_ref.shape[2] // LANES * slots
    coded = jnp.sum(listed_ref[:, first:, :].astype(jnp.float32), axis=0)
    total = sum(coded[part * lines:(part + 1) * lines] for part in range(PARTS))
    shape = (new_count, LANES)
    eye = iota((new_count, new_count), 0) == iota((new_count, new_count), 1)
    found = []
    for kind in range(2):
        place = (kind * groups + here) * new_count
        line = jnp.sum(
            jnp.where(iota((lines, LANES), 0) == place // LANES, total, 0.0), axis=0, keepdims=True
        )
        column = jnp.sum(
            jnp.where(iota(shape, 1) == iota(shape, 0) + place % LANES, line, 0.0),
            axis=1, keepdims=True,
        )
        found.append(jnp.sum(jnp.where(eye, column, 0.0), axis=0, keepdims=True))
    density_ref[...] = jnp.log(found[0] * (1.0 / total_heads))
    spread_ref[...] = found[1] / found[0]


def per_device(heads, new_heads, vectors, near_ids):
    head_dev, width = heads.shape
    new_count = new_heads.shape[0]
    near = near_ids.shape[1]
    groups = lax.axis_size("group")
    members = lax.axis_size("member")
    most = 2 * near // members
    slots = -(-most // PACK) * PACK

    partner_ids = from_partner(near_ids, "member", 1)
    others = [from_partner(new_heads, "group", mask) for mask in range(1, groups)]
    ids = call(
        stage_kernel,
        jax.ShapeDtypeStruct(near_ids.shape, near_ids.dtype),
        (in_hbm(near_ids),),
        (0, 0),
        scratch=[pltpu.SemaphoreType.DMA],
        spaces=[HBM],
    )
    ids = jnp.concatenate([ids, partner_ids], axis=0)
    kept, head_sq, new_heads = call(
        early_kernel,
        (
            jax.ShapeDtypeStruct(heads.shape, heads.dtype),
            jax.ShapeDtypeStruct((1, head_dev), jnp.float32),
            jax.ShapeDtypeStruct(new_heads.shape, new_heads.dtype),
        ),
        (in_hbm(heads), in_hbm(new_heads), ids),
        (0, 0),
        scratch=[pltpu.SemaphoreType.DMA((5,))],
        spaces=[HBM, HBM, pl.ANY],
    )
    lines = 2 * groups * new_count // LANES
    chunks = width // LANES
    extra = -(-PARTS * lines // TILE) * TILE
    sums, kept_ids = call(
        functools.partial(crowd_kernel, groups),
        (
            jax.ShapeDtypeStruct((-(-lines // TILE) * TILE, LANES), jnp.float32),
            jax.ShapeDtypeStruct(ids.shape, ids.dtype),
        ),
        (ids, kept, head_sq, new_heads, *others),
        (0, 0),
    )
    mask = 2
    while mask < members // 2:
        kept_ids = jnp.concatenate([kept_ids, from_partner(ids, "member", mask)], axis=0)
        ids = kept_ids
        mask *= 2
    far_ids = from_partner(ids, "member", mask)
    mask = 1
    while mask < groups // 2:
        sums = sums + from_partner(sums, "group", mask)
        mask *= 2
    rows = call(
        functools.partial(gather_kernel, members, slots),
        jax.ShapeDtypeStruct((members * slots, width), jnp.bfloat16),
        (ids, far_ids, kept, sums),
        (2 * members * slots * head_dev * width, heads.size * 2),
        scratch=[pltpu.VMEM((members, near), jnp.int32)],
        spaces=[VMEM, VMEM, VMEM, pl.ANY],
    )
    message = call(
        functools.partial(pack_kernel, members, slots, lines),
        jax.ShapeDtypeStruct((members, chunks * slots + extra, LANES), jnp.bfloat16),
        (rows, sums, from_partner(sums, "group", mask)),
        (0, members * slots * width * 4),
    )
    message = lax.all_to_all(
        message, "member", 0, 0, tiled=True, axis_index_groups=[turned(members)]
    )

    density, spread, reassign = call(
        functools.partial(
            tail_kernel, groups, slots, head_dev, float(head_dev * groups * members)
        ),
        (
            jax.ShapeDtypeStruct((1, new_count), jnp.float32),
            jax.ShapeDtypeStruct((1, new_count), jnp.float32),
            jax.ShapeDtypeStruct((1, near, vectors.shape[1]), jnp.float32),
        ),
        (near_ids, message, vectors),
        (4 * near * vectors.shape[1] * width, vectors.size * 4),
    )
    return (density[0], spread[0], reassign)


def solution(mesh):
    placed = (
        P(("group", "member"), None),
        P("group", None),
        P(("group", "member"), None, None),
        P(("group", "member"), None),
    )
    return jax.shard_map(
        per_device,
        mesh=mesh,
        in_specs=placed,
        out_specs=(P("group"), P("group"), P(("group", "member"), None, None)),
        check_vma=False,
    )
```

```python
import functools

import jax
import jax.numpy as jnp
from jax import lax
from jax.experimental import pallas as pl
from jax.experimental.pallas import tpu as pltpu
from jax.sharding import PartitionSpec as P

VMEM = pltpu.MemorySpace.VMEM
HBM = pltpu.MemorySpace.HBM
LANES = 128
PACK = 16
TILE = 8
PARTS = 3
LIMIT = 24 * 2**20


def from_partner(value, axis, mask):
    count = lax.axis_size(axis)
    return lax.ppermute(value, axis, [(source, source ^ mask) for source in range(count)])


def turned(members):
    return [member ^ (members // 2 + 1) for member in range(members)]


def in_hbm(value):
    return pltpu.with_memory_space_constraint(value, HBM)


def call(body, shapes, operands, cost, scratch=(), spaces=None):
    return pl.pallas_call(
        body,
        out_shape=shapes,
        in_specs=[pl.BlockSpec(memory_space=space) for space in spaces or [VMEM] * len(operands)],
        out_specs=jax.tree.map(lambda unused: pl.BlockSpec(memory_space=VMEM), shapes),
        scratch_shapes=scratch,
        compiler_params=pltpu.CompilerParams(vmem_limit_bytes=LIMIT),
        cost_estimate=pl.CostEstimate(flops=cost[0], bytes_accessed=cost[1], transcendentals=0),
    )(*operands)


def iota(shape, dim):
    return lax.broadcasted_iota(jnp.int32, shape, dim)


def stage_kernel(ids_ref, kept_ref, sem):
    copy = pltpu.make_async_copy(ids_ref, kept_ref, sem)
    copy.start()
    copy.wait()


def early_kernel(heads_ref, new_ref, unused, kept_ref, head_sq_ref, kept_new_ref, sems):
    head_dev, width = heads_ref.shape
    tiles = 4
    tile = head_dev // tiles
    parts = [pl.ds(i * tile, tile) for i in range(tiles)]
    copies = [
        pltpu.make_async_copy(heads_ref.at[part], kept_ref.at[part], sems.at[i])
        for i, part in enumerate(parts)
    ]
    copies.append(pltpu.make_async_copy(new_ref, kept_new_ref, sems.at[tiles]))
    for copy in copies:
        copy.start()
    for i in range(tiles):
        copies[i].wait()
        for first in range(i * tile, (i + 1) * tile, LANES):
            block = jnp.square(kept_ref[first:first + LANES, :].astype(jnp.float32))
            folded = block[:, :LANES]
            for column in range(LANES, width, LANES):
                folded = folded + block[:, column:column + LANES]
            head_sq_ref[:, first:first + LANES] = jnp.sum(folded.T, axis=0, keepdims=True)
    for copy in copies[tiles:]:
        copy.wait()


def listed_rows(ids, me, slots, heads_ref):
    members, near = ids.shape
    head_dev = heads_ref.shape[0]
    local = ids - me * head_dev
    owned = (local >= 0) & (local < head_dev)
    earlier = (iota((near, near), 0) < iota((near, near), 1)).astype(jnp.bfloat16)
    rank = jnp.dot(owned.astype(jnp.bfloat16), earlier, preferred_element_type=jnp.float32)
    rank = jnp.where(owned, rank.astype(jnp.int32), -1)
    shape = (members, slots, near)
    pick = jnp.broadcast_to(rank[:, None, :], shape) == iota(shape, 1)
    wanted = jnp.sum(
        jnp.where(pick, jnp.broadcast_to(local[:, None, :] + 1, shape), 0), axis=2, keepdims=True
    ).reshape(members * slots, 1)
    onehot = (wanted == iota((members * slots, head_dev), 1) + 1).astype(jnp.bfloat16)
    return jnp.dot(
        onehot, heads_ref[...], preferred_element_type=jnp.float32
    ).astype(jnp.bfloat16)


def crowding(queries, heads_ref, head_sq_ref):
    head_dev, width = heads_ref.shape
    query_sq = jnp.sum(jnp.square(queries.astype(jnp.float32)), axis=1, keepdims=True)
    total_w = jnp.zeros((queries.shape[0], 1), jnp.float32)
    total_we = jnp.zeros((queries.shape[0], 1), jnp.float32)
    tile = 512
    for start in range(0, head_dev, tile):
        dots = lax.dot_general(
            queries, heads_ref[start:start + tile, :], (((1,), (1,)), ((), ())),
            preferred_element_type=jnp.float32,
        )
        head_sq = head_sq_ref[:, start:start + tile]
        excess = (query_sq + head_sq - 2.0 * dots) * (1.0 / width)
        inverse = 1.0 / (1.0 + excess)
        weight = inverse * inverse
        total_w = total_w + jnp.sum(weight, axis=1, keepdims=True)
        total_we = total_we + jnp.sum(weight * excess, axis=1, keepdims=True)
    return total_w, total_we


def crowd_kernel(groups, ids_ref, heads_ref, head_sq_ref, *refs):
    query_refs, (sums_ref, kept_ids_ref) = refs[:-2], refs[-2:]
    kept_ids_ref[...] = ids_ref[...]
    here = lax.axis_index("group")
    queries = jnp.concatenate([ref[...] for ref in query_refs], axis=0)
    new_count = queries.shape[0] // groups
    totals = crowding(queries, heads_ref, head_sq_ref)
    lane = iota((new_count, LANES), 1)
    row = iota((new_count, LANES), 0)
    line = iota(sums_ref.shape, 0)
    sums = jnp.zeros(sums_ref.shape, jnp.float32)
    for mask in range(groups):
        part = slice(mask * new_count, (mask + 1) * new_count)
        for kind in range(2):
            place = (kind * groups + (here ^ mask)) * new_count
            spread_out = jnp.where(lane == row + place % LANES, totals[kind][part], 0.0)
            spread_out = jnp.sum(spread_out, axis=0, keepdims=True)
            sums = sums + jnp.where(line == place // LANES, spread_out, 0.0)
    sums_ref[...] = sums


def gather_kernel(members, slots, near_ref, far_ref, heads_ref, unused, rows_ref, ids_ref):
    me = lax.axis_index("member")
    half = members // 2
    ids_ref[:half, :] = near_ref[...]
    ids_ref[half:, :] = far_ref[...]
    ids = jnp.concatenate([ids_ref[pl.ds(me ^ member, 1), :] for member in turned(members)], axis=0)
    rows_ref[...] = listed_rows(ids, me, slots, heads_ref)


def pack_kernel(members, slots, lines, rows_ref, mine_ref, other_ref, out_ref):
    chunks = rows_ref.shape[1] // LANES
    for member in range(members):
        for chunk in range(chunks):
            out_ref[member, chunk * slots:(chunk + 1) * slots, :] = rows_ref[
                member * slots:(member + 1) * slots, chunk * LANES:(chunk + 1) * LANES
            ]
    sums = (mine_ref[...] + other_ref[...])[:lines]
    coded = []
    for unused in range(PARTS):
        coded.append(sums.astype(jnp.bfloat16).astype(jnp.float32))
        sums = sums - coded[-1]
    missing = out_ref.shape[1] - chunks * slots - PARTS * lines
    if missing:
        coded.append(jnp.zeros((missing, LANES), jnp.float32))
    tail = jnp.concatenate(coded, axis=0).astype(jnp.bfloat16)
    for member in range(members):
        out_ref[member, chunks * slots:, :] = tail


def distances(slots, head_dev, ids_ref, listed_ref, vectors_ref, out_ref):
    near = ids_ref.shape[1]
    members = listed_ref.shape[0]
    block, width = vectors_ref.shape[1:]
    square = (near, near)
    owner_row = jnp.broadcast_to(lax.div(ids_ref[...], head_dev), square)
    eye = iota(square, 0) == iota(square, 1)
    owner = jnp.sum(jnp.where(eye, owner_row, 0), axis=1, keepdims=True)
    before = (owner_row == owner) & (iota(square, 1) < iota(square, 0))
    place = jnp.sum(before.astype(jnp.int32), axis=1, keepdims=True)
    source = (owner ^ (members // 2 + 1)) * slots + place
    back = (source == iota((near, members * slots), 1)).astype(jnp.bfloat16)
    rows = []
    for chunk in range(width // LANES):
        part = listed_ref[:, chunk * slots:(chunk + 1) * slots, :].reshape(members * slots, LANES)
        rows.append(jnp.dot(back, part, preferred_element_type=jnp.float32))
    rows = jnp.concatenate(rows, axis=1)
    row_sq = jnp.sum(jnp.square(rows), axis=1, keepdims=True)
    vec = vectors_ref[0]
    vec_sq = jnp.sum(jnp.square(vec.astype(jnp.float32)), axis=1, keepdims=True)
    diagonal = iota((block, block), 0) == iota((block, block), 1)
    vec_sq = jnp.sum(jnp.where(diagonal, vec_sq, 0.0), axis=0, keepdims=True)
    dots = lax.dot_general(
        rows.astype(jnp.bfloat16), vec, (((1,), (1,)), ((), ())),
        preferred_element_type=jnp.float32,
    )
    out_ref[0] = (row_sq + vec_sq - 2.0 * dots) * (1.0 / width)


def tail_kernel(
    groups, slots, head_dev, total_heads, ids_ref, listed_ref, vectors_ref,
    density_ref, spread_ref, out_ref,
):
    distances(slots, head_dev, ids_ref, listed_ref, vectors_ref, out_ref)
    here = lax.axis_index("group")
    members = listed_ref.shape[0]
    new_count = density_ref.shape[1]
    lines = 2 * groups * new_count // LANES
    first = vectors_ref.shape[2] // LANES * slots
    coded = jnp.sum(listed_ref[:, first:, :].astype(jnp.float32), axis=0)
    total = sum(coded[part * lines:(part + 1) * lines] for part in range(PARTS))
    shape = (new_count, LANES)
    eye = iota((new_count, new_count), 0) == iota((new_count, new_count), 1)
    found = []
    for kind in range(2):
        place = (kind * groups + here) * new_count
        line = jnp.sum(
            jnp.where(iota((lines, LANES), 0) == place // LANES, total, 0.0), axis=0, keepdims=True
        )
        column = jnp.sum(
            jnp.where(iota(shape, 1) == iota(shape, 0) + place % LANES, line, 0.0),
            axis=1, keepdims=True,
        )
        found.append(jnp.sum(jnp.where(eye, column, 0.0), axis=0, keepdims=True))
    density_ref[...] = jnp.log(found[0] * (1.0 / total_heads))
    spread_ref[...] = found[1] / found[0]


def per_device(heads, new_heads, vectors, near_ids):
    head_dev, width = heads.shape
    new_count = new_heads.shape[0]
    near = near_ids.shape[1]
    groups = lax.axis_size("group")
    members = lax.axis_size("member")
    most = 2 * near // members
    slots = -(-most // PACK) * PACK

    partner_ids = from_partner(near_ids, "member", 1)
    others = [from_partner(new_heads, "group", mask) for mask in range(1, groups)]
    ids = call(
        stage_kernel,
        jax.ShapeDtypeStruct(near_ids.shape, near_ids.dtype),
        (in_hbm(near_ids),),
        (0, 0),
        scratch=[pltpu.SemaphoreType.DMA],
        spaces=[HBM],
    )
    ids = jnp.concatenate([ids, partner_ids], axis=0)
    kept, head_sq, new_heads = call(
        early_kernel,
        (
            jax.ShapeDtypeStruct(heads.shape, heads.dtype),
            jax.ShapeDtypeStruct((1, head_dev), jnp.float32),
            jax.ShapeDtypeStruct(new_heads.shape, new_heads.dtype),
        ),
        (in_hbm(heads), in_hbm(new_heads), ids),
        (0, 0),
        scratch=[pltpu.SemaphoreType.DMA((5,))],
        spaces=[HBM, HBM, pl.ANY],
    )
    lines = 2 * groups * new_count // LANES
    chunks = width // LANES
    extra = -(-PARTS * lines // TILE) * TILE
    sums, kept_ids = call(
        functools.partial(crowd_kernel, groups),
        (
            jax.ShapeDtypeStruct((-(-lines // TILE) * TILE, LANES), jnp.float32),
            jax.ShapeDtypeStruct(ids.shape, ids.dtype),
        ),
        (ids, kept, head_sq, new_heads, *others),
        (0, 0),
    )
    mask = 2
    while mask < members // 2:
        kept_ids = jnp.concatenate([kept_ids, from_partner(ids, "member", mask)], axis=0)
        ids = kept_ids
        mask *= 2
    far_ids = from_partner(ids, "member", mask)
    mask = 1
    while mask < groups // 2:
        sums = sums + from_partner(sums, "group", mask)
        mask *= 2
    rows = call(
        functools.partial(gather_kernel, members, slots),
        jax.ShapeDtypeStruct((members * slots, width), jnp.bfloat16),
        (ids, far_ids, kept, sums),
        (2 * members * slots * head_dev * width, heads.size * 2),
        scratch=[pltpu.VMEM((members, near), jnp.int32)],
        spaces=[VMEM, VMEM, VMEM, pl.ANY],
    )
    message = call(
        functools.partial(pack_kernel, members, slots, lines),
        jax.ShapeDtypeStruct((members, chunks * slots + extra, LANES), jnp.bfloat16),
        (rows, sums, from_partner(sums, "group", mask)),
        (0, members * slots * width * 4),
    )
    message = lax.all_to_all(
        message, "member", 0, 0, tiled=True, axis_index_groups=[turned(members)]
    )

    density, spread, reassign = call(
        functools.partial(
            tail_kernel, groups, slots, head_dev, float(head_dev * groups * members)
        ),
        (
            jax.ShapeDtypeStruct((1, new_count), jnp.float32),
            jax.ShapeDtypeStruct((1, new_count), jnp.float32),
            jax.ShapeDtypeStruct((1, near, vectors.shape[1]), jnp.float32),
        ),
        (near_ids, message, vectors),
        (4 * near * vectors.shape[1] * width, vectors.size * 4),
    )
    return (density[0], spread[0], reassign)


def solution(mesh):
    placed = (
        P(("group", "member"), None),
        P("group", None),
        P(("group", "member"), None, None),
        P(("group", "member"), None),
    )
    return jax.shard_map(
        per_device,
        mesh=mesh,
        in_specs=placed,
        out_specs=(P("group"), P("group"), P(("group", "member"), None, None)),
        check_vma=False,
    )
```

```python
import functools

import jax
import jax.numpy as jnp
from jax import lax
from jax.experimental import pallas as pl
from jax.experimental.pallas import tpu as pltpu
from jax.sharding import PartitionSpec as P

VMEM = pltpu.MemorySpace.VMEM
HBM = pltpu.MemorySpace.HBM
LANES = 128
PACK = 16
TILE = 8
PARTS = 3
LIMIT = 24 * 2**20


def from_partner(value, axis, mask):
    count = lax.axis_size(axis)
    return lax.ppermute(value, axis, [(source, source ^ mask) for source in range(count)])


def turned(members):
    return [member ^ (members // 2) for member in range(members)]


def in_hbm(value):
    return pltpu.with_memory_space_constraint(value, HBM)


def call(body, shapes, operands, cost, scratch=(), spaces=None):
    return pl.pallas_call(
        body,
        out_shape=shapes,
        in_specs=[pl.BlockSpec(memory_space=space) for space in spaces or [VMEM] * len(operands)],
        out_specs=jax.tree.map(lambda unused: pl.BlockSpec(memory_space=VMEM), shapes),
        scratch_shapes=scratch,
        compiler_params=pltpu.CompilerParams(vmem_limit_bytes=LIMIT),
        cost_estimate=pl.CostEstimate(flops=cost[0], bytes_accessed=cost[1], transcendentals=0),
    )(*operands)


def iota(shape, dim):
    return lax.broadcasted_iota(jnp.int32, shape, dim)


def stage_kernel(ids_ref, kept_ref, sem):
    copy = pltpu.make_async_copy(ids_ref, kept_ref, sem)
    copy.start()
    copy.wait()


def early_kernel(heads_ref, new_ref, unused, kept_ref, head_sq_ref, kept_new_ref, sems):
    head_dev, width = heads_ref.shape
    tiles = 4
    tile = head_dev // tiles
    parts = [pl.ds(i * tile, tile) for i in range(tiles)]
    copies = [
        pltpu.make_async_copy(heads_ref.at[part], kept_ref.at[part], sems.at[i])
        for i, part in enumerate(parts)
    ]
    copies.append(pltpu.make_async_copy(new_ref, kept_new_ref, sems.at[tiles]))
    for copy in copies:
        copy.start()
    for i in range(tiles):
        copies[i].wait()
        for first in range(i * tile, (i + 1) * tile, LANES):
            block = jnp.square(kept_ref[first:first + LANES, :].astype(jnp.float32))
            folded = block[:, :LANES]
            for column in range(LANES, width, LANES):
                folded = folded + block[:, column:column + LANES]
            head_sq_ref[:, first:first + LANES] = jnp.sum(folded.T, axis=0, keepdims=True)
    for copy in copies[tiles:]:
        copy.wait()


def listed_rows(ids, me, slots, heads_ref):
    members, near = ids.shape
    head_dev = heads_ref.shape[0]
    local = ids - me * head_dev
    owned = (local >= 0) & (local < head_dev)
    earlier = (iota((near, near), 0) < iota((near, near), 1)).astype(jnp.bfloat16)
    rank = jnp.dot(owned.astype(jnp.bfloat16), earlier, preferred_element_type=jnp.float32)
    rank = jnp.where(owned, rank.astype(jnp.int32), -1)
    shape = (members, slots, near)
    pick = jnp.broadcast_to(rank[:, None, :], shape) == iota(shape, 1)
    wanted = jnp.sum(
        jnp.where(pick, jnp.broadcast_to(local[:, None, :] + 1, shape), 0), axis=2, keepdims=True
    ).reshape(members * slots, 1)
    rows = None
    tile = 512
    for start in range(0, head_dev, tile):
        onehot = wanted == iota((members * slots, tile), 1) + (start + 1)
        part = jnp.dot(
            onehot.astype(jnp.bfloat16), heads_ref[start:start + tile, :],
            preferred_element_type=jnp.float32,
        )
        rows = part if rows is None else rows + part
    return rows.astype(jnp.bfloat16)


def crowding(queries, heads_ref, head_sq_ref):
    head_dev, width = heads_ref.shape
    query_sq = jnp.sum(jnp.square(queries.astype(jnp.float32)), axis=1, keepdims=True)
    total_w = jnp.zeros((queries.shape[0], LANES), jnp.float32)
    total_we = jnp.zeros((queries.shape[0], LANES), jnp.float32)
    tile = 512
    for start in range(0, head_dev, tile):
        dots = lax.dot_general(
            queries, heads_ref[start:start + tile, :], (((1,), (1,)), ((), ())),
            preferred_element_type=jnp.float32,
        )
        head_sq = head_sq_ref[:, start:start + tile]
        excess = (query_sq + head_sq - 2.0 * dots) * (1.0 / width)
        inverse = 1.0 / (1.0 + excess)
        weight = inverse * inverse
        weighted = weight * excess
        for column in range(0, tile, LANES):
            total_w = total_w + weight[:, column:column + LANES]
            total_we = total_we + weighted[:, column:column + LANES]
    total_w = jnp.sum(total_w, axis=1, keepdims=True)
    total_we = jnp.sum(total_we, axis=1, keepdims=True)
    return total_w, total_we


def crowd_kernel(groups, ids_ref, heads_ref, head_sq_ref, *refs):
    query_refs, (sums_ref, kept_ids_ref) = refs[:-2], refs[-2:]
    kept_ids_ref[...] = ids_ref[...]
    here = lax.axis_index("group")
    queries = jnp.concatenate([ref[...] for ref in query_refs], axis=0)
    new_count = queries.shape[0] // groups
    totals = crowding(queries, heads_ref, head_sq_ref)
    shape = (groups * new_count, LANES)
    row = iota(shape, 0)
    place = (here ^ (row // new_count)) * new_count + row % new_count
    sums_ref[...] = jnp.zeros(sums_ref.shape, jnp.float32)
    lines = 2 * groups * new_count // LANES
    for line in range(lines):
        lane = iota(shape, 1) + line * LANES
        spread_out = jnp.where(lane == place, totals[0], 0.0) + jnp.where(
            lane == place + groups * new_count, totals[1], 0.0
        )
        sums_ref[line:line + 1, :] = jnp.sum(spread_out, axis=0, keepdims=True)


def gather_kernel(members, slots, near_ref, far_ref, heads_ref, unused, rows_ref, ids_ref):
    me = lax.axis_index("member")
    half = members // 2
    ids_ref[:half, :] = near_ref[...]
    ids_ref[half:, :] = far_ref[...]
    ids = jnp.concatenate([ids_ref[pl.ds(me ^ member, 1), :] for member in turned(members)], axis=0)
    rows_ref[...] = listed_rows(ids, me, slots, heads_ref)


def pack_kernel(members, slots, lines, rows_ref, mine_ref, other_ref, out_ref):
    chunks = rows_ref.shape[1] // LANES
    for member in range(members):
        for chunk in range(chunks):
            out_ref[member, chunk * slots:(chunk + 1) * slots, :] = rows_ref[
                member * slots:(member + 1) * slots, chunk * LANES:(chunk + 1) * LANES
            ]
    sums = (mine_ref[...] + other_ref[...])[:lines]
    coded = []
    for unused in range(PARTS):
        coded.append(sums.astype(jnp.bfloat16).astype(jnp.float32))
        sums = sums - coded[-1]
    missing = out_ref.shape[1] - chunks * slots - PARTS * lines
    if missing:
        coded.append(jnp.zeros((missing, LANES), jnp.float32))
    tail = jnp.concatenate(coded, axis=0).astype(jnp.bfloat16)
    for member in range(members):
        out_ref[member, chunks * slots:, :] = tail


def prepare_kernel(members, slots, head_dev, ids_ref, vectors_ref, unused, back_ref, vec_sq_ref):
    near = ids_ref.shape[1]
    block = vectors_ref.shape[1]
    square = (near, near)
    owner_row = jnp.broadcast_to(lax.div(ids_ref[...], head_dev), square)
    eye = iota(square, 0) == iota(square, 1)
    owner = jnp.sum(jnp.where(eye, owner_row, 0), axis=1, keepdims=True)
    before = (owner_row == owner) & (iota(square, 1) < iota(square, 0))
    place = jnp.sum(before.astype(jnp.int32), axis=1, keepdims=True)
    source = (owner ^ (members // 2)) * slots + place
    back_ref[...] = (source == iota(back_ref.shape, 1)).astype(jnp.bfloat16)
    vec_sq = jnp.sum(jnp.square(vectors_ref[0].astype(jnp.float32)), axis=1, keepdims=True)
    diagonal = iota((block, block), 0) == iota((block, block), 1)
    vec_sq_ref[...] = jnp.sum(jnp.where(diagonal, vec_sq, 0.0), axis=0, keepdims=True)


def distances(slots, back_ref, vec_sq_ref, listed_ref, vectors_ref, out_ref):
    members = listed_ref.shape[0]
    width = vectors_ref.shape[2]
    rows = []
    for chunk in range(width // LANES):
        part = listed_ref[:, chunk * slots:(chunk + 1) * slots, :].reshape(members * slots, LANES)
        rows.append(jnp.dot(back_ref[...], part, preferred_element_type=jnp.float32))
    rows = jnp.concatenate(rows, axis=1)
    row_sq = jnp.sum(jnp.square(rows), axis=1, keepdims=True)
    dots = lax.dot_general(
        rows.astype(jnp.bfloat16), vectors_ref[0], (((1,), (1,)), ((), ())),
        preferred_element_type=jnp.float32,
    )
    out_ref[0] = (row_sq + vec_sq_ref[...] - 2.0 * dots) * (1.0 / width)


def tail_kernel(
    groups, slots, total_heads, back_ref, vec_sq_ref, listed_ref, vectors_ref,
    density_ref, spread_ref, out_ref,
):
    distances(slots, back_ref, vec_sq_ref, listed_ref, vectors_ref, out_ref)
    here = lax.axis_index("group")
    members = listed_ref.shape[0]
    new_count = density_ref.shape[1]
    lines = 2 * groups * new_count // LANES
    first = vectors_ref.shape[2] // LANES * slots
    coded = jnp.sum(listed_ref[:, first:, :].astype(jnp.float32), axis=0)
    total = sum(coded[part * lines:(part + 1) * lines] for part in range(PARTS))
    shape = (new_count, LANES)
    eye = iota((new_count, new_count), 0) == iota((new_count, new_count), 1)
    found = []
    for kind in range(2):
        place = (kind * groups + here) * new_count
        line = jnp.sum(
            jnp.where(iota((lines, LANES), 0) == place // LANES, total, 0.0), axis=0, keepdims=True
        )
        column = jnp.sum(
            jnp.where(iota(shape, 1) == iota(shape, 0) + place % LANES, line, 0.0),
            axis=1, keepdims=True,
        )
        found.append(jnp.sum(jnp.where(eye, column, 0.0), axis=0, keepdims=True))
    density_ref[...] = jnp.log(found[0] * (1.0 / total_heads))
    spread_ref[...] = found[1] / found[0]


def per_device(heads, new_heads, vectors, near_ids):
    head_dev, width = heads.shape
    new_count = new_heads.shape[0]
    near = near_ids.shape[1]
    groups = lax.axis_size("group")
    members = lax.axis_size("member")
    most = 2 * near // members
    slots = -(-most // PACK) * PACK

    partner_ids = from_partner(near_ids, "member", 1)
    others = [from_partner(new_heads, "group", mask) for mask in range(1, groups)]
    ids = call(
        stage_kernel,
        jax.ShapeDtypeStruct(near_ids.shape, near_ids.dtype),
        (in_hbm(near_ids),),
        (0, 0),
        scratch=[pltpu.SemaphoreType.DMA],
        spaces=[HBM],
    )
    ids = jnp.concatenate([ids, partner_ids], axis=0)
    kept, head_sq, new_heads = call(
        early_kernel,
        (
            jax.ShapeDtypeStruct(heads.shape, heads.dtype),
            jax.ShapeDtypeStruct((1, head_dev), jnp.float32),
            jax.ShapeDtypeStruct(new_heads.shape, new_heads.dtype),
        ),
        (in_hbm(heads), in_hbm(new_heads), ids),
        (0, 0),
        scratch=[pltpu.SemaphoreType.DMA((5,))],
        spaces=[HBM, HBM, pl.ANY],
    )
    lines = 2 * groups * new_count // LANES
    chunks = width // LANES
    extra = -(-PARTS * lines // TILE) * TILE
    sums, kept_ids = call(
        functools.partial(crowd_kernel, groups),
        (
            jax.ShapeDtypeStruct((-(-lines // TILE) * TILE, LANES), jnp.float32),
            jax.ShapeDtypeStruct(ids.shape, ids.dtype),
        ),
        (ids, kept, head_sq, new_heads, *others),
        (0, 0),
    )
    mask = 2
    while mask < members // 2:
        kept_ids = jnp.concatenate([kept_ids, from_partner(ids, "member", mask)], axis=0)
        ids = kept_ids
        mask *= 2
    far_ids = from_partner(ids, "member", mask)
    mask = 1
    while mask < groups // 2:
        sums = sums + from_partner(sums, "group", mask)
        mask *= 2
    rows = call(
        functools.partial(gather_kernel, members, slots),
        jax.ShapeDtypeStruct((members * slots, width), jnp.bfloat16),
        (ids, far_ids, kept, sums),
        (2 * members * slots * head_dev * width, heads.size * 2),
        scratch=[pltpu.VMEM((members, near), jnp.int32)],
        spaces=[VMEM, VMEM, VMEM, pl.ANY],
    )
    message = call(
        functools.partial(pack_kernel, members, slots, lines),
        jax.ShapeDtypeStruct((members, chunks * slots + extra, LANES), jnp.bfloat16),
        (rows, sums, from_partner(sums, "group", mask)),
        (0, members * slots * width * 4),
    )
    sent = message
    message = lax.all_to_all(
        sent, "member", 0, 0, tiled=True, axis_index_groups=[turned(members)]
    )

    back, vec_sq = call(
        functools.partial(prepare_kernel, members, slots, head_dev),
        (
            jax.ShapeDtypeStruct((near, members * slots), jnp.bfloat16),
            jax.ShapeDtypeStruct((1, vectors.shape[1]), jnp.float32),
        ),
        (near_ids, vectors, sent),
        (vectors.size * 2, vectors.size * 2),
        spaces=[VMEM, VMEM, pl.ANY],
    )
    density, spread, reassign = call(
        functools.partial(
            tail_kernel, groups, slots, float(head_dev * groups * members)
        ),
        (
            jax.ShapeDtypeStruct((1, new_count), jnp.float32),
            jax.ShapeDtypeStruct((1, new_count), jnp.float32),
            jax.ShapeDtypeStruct((1, near, vectors.shape[1]), jnp.float32),
        ),
        (back, vec_sq, message, vectors),
        (4 * near * vectors.shape[1] * width, vectors.size * 4),
    )
    return (density[0], spread[0], reassign)


def solution(mesh):
    placed = (
        P(("group", "member"), None),
        P("group", None),
        P(("group", "member"), None, None),
        P(("group", "member"), None),
    )
    return jax.shard_map(
        per_device,
        mesh=mesh,
        in_specs=placed,
        out_specs=(P("group"), P("group"), P(("group", "member"), None, None)),
        check_vma=False,
    )
```

```python
import functools

import jax
import jax.numpy as jnp
from jax import lax
from jax.experimental import pallas as pl
from jax.experimental.pallas import tpu as pltpu
from jax.sharding import PartitionSpec as P

VMEM = pltpu.MemorySpace.VMEM
HBM = pltpu.MemorySpace.HBM
LANES = 128
PACK = 16
TILE = 8
PARTS = 3
LIMIT = 24 * 2**20


def from_partner(value, axis, mask):
    count = lax.axis_size(axis)
    return lax.ppermute(value, axis, [(source, source ^ mask) for source in range(count)])


def middle_first(members):
    return [members // 2] + [member for member in range(members) if member != members // 2]


def first_middle(member, members):
    middle = members // 2
    return jnp.where(member == middle, 0, jnp.where(member < middle, member + 1, member))


def in_hbm(value):
    return pltpu.with_memory_space_constraint(value, HBM)


def call(body, shapes, operands, cost, scratch=(), spaces=None):
    return pl.pallas_call(
        body,
        out_shape=shapes,
        in_specs=[pl.BlockSpec(memory_space=space) for space in spaces or [VMEM] * len(operands)],
        out_specs=jax.tree.map(lambda unused: pl.BlockSpec(memory_space=VMEM), shapes),
        scratch_shapes=scratch,
        compiler_params=pltpu.CompilerParams(vmem_limit_bytes=LIMIT),
        cost_estimate=pl.CostEstimate(flops=cost[0], bytes_accessed=cost[1], transcendentals=0),
    )(*operands)


def iota(shape, dim):
    return lax.broadcasted_iota(jnp.int32, shape, dim)


def stage_kernel(ids_ref, kept_ref, sem):
    copy = pltpu.make_async_copy(ids_ref, kept_ref, sem)
    copy.start()
    copy.wait()


def early_kernel(heads_ref, new_ref, unused, kept_ref, head_sq_ref, kept_new_ref, sems):
    head_dev, width = heads_ref.shape
    tiles = 4
    tile = head_dev // tiles
    parts = [pl.ds(i * tile, tile) for i in range(tiles)]
    copies = [
        pltpu.make_async_copy(heads_ref.at[part], kept_ref.at[part], sems.at[i])
        for i, part in enumerate(parts)
    ]
    copies.append(pltpu.make_async_copy(new_ref, kept_new_ref, sems.at[tiles]))
    for copy in copies:
        copy.start()
    for i in range(tiles):
        copies[i].wait()
        for first in range(i * tile, (i + 1) * tile, LANES):
            block = jnp.square(kept_ref[first:first + LANES, :].astype(jnp.float32))
            folded = block[:, :LANES]
            for column in range(LANES, width, LANES):
                folded = folded + block[:, column:column + LANES]
            head_sq_ref[:, first:first + LANES] = jnp.sum(folded.T, axis=0, keepdims=True)
    for copy in copies[tiles:]:
        copy.wait()


def listed_rows(ids, me, slots, heads_ref):
    members, near = ids.shape
    head_dev = heads_ref.shape[0]
    local = ids - me * head_dev
    owned = (local >= 0) & (local < head_dev)
    earlier = (iota((near, near), 0) < iota((near, near), 1)).astype(jnp.bfloat16)
    rank = jnp.dot(owned.astype(jnp.bfloat16), earlier, preferred_element_type=jnp.float32)
    rank = jnp.where(owned, rank.astype(jnp.int32), -1)
    shape = (members, slots, near)
    pick = jnp.broadcast_to(rank[:, None, :], shape) == iota(shape, 1)
    wanted = jnp.sum(
        jnp.where(pick, jnp.broadcast_to(local[:, None, :] + 1, shape), 0), axis=2, keepdims=True
    ).reshape(members * slots, 1)
    onehot = (wanted == iota((members * slots, head_dev), 1) + 1).astype(jnp.bfloat16)
    return jnp.dot(
        onehot, heads_ref[...], preferred_element_type=jnp.float32
    ).astype(jnp.bfloat16)


def crowding(queries, heads_ref, head_sq_ref):
    head_dev, width = heads_ref.shape
    query_sq = jnp.sum(jnp.square(queries.astype(jnp.float32)), axis=1, keepdims=True)
    total_w = jnp.zeros((queries.shape[0], 1), jnp.float32)
    total_we = jnp.zeros((queries.shape[0], 1), jnp.float32)
    tile = 512
    for start in range(0, head_dev, tile):
        dots = lax.dot_general(
            queries, heads_ref[start:start + tile, :], (((1,), (1,)), ((), ())),
            preferred_element_type=jnp.float32,
        )
        head_sq = head_sq_ref[:, start:start + tile]
        excess = (query_sq + head_sq - 2.0 * dots) * (1.0 / width)
        inverse = 1.0 / (1.0 + excess)
        weight = inverse * inverse
        total_w = total_w + jnp.sum(weight, axis=1, keepdims=True)
        total_we = total_we + jnp.sum(weight * excess, axis=1, keepdims=True)
    return total_w, total_we


def crowd_kernel(groups, ids_ref, heads_ref, head_sq_ref, *refs):
    query_refs, (sums_ref, kept_ids_ref) = refs[:-2], refs[-2:]
    kept_ids_ref[...] = ids_ref[...]
    here = lax.axis_index("group")
    queries = jnp.concatenate([ref[...] for ref in query_refs], axis=0)
    new_count = queries.shape[0] // groups
    totals = crowding(queries, heads_ref, head_sq_ref)
    lane = iota((new_count, LANES), 1)
    row = iota((new_count, LANES), 0)
    line = iota(sums_ref.shape, 0)
    sums = jnp.zeros(sums_ref.shape, jnp.float32)
    for mask in range(groups):
        part = slice(mask * new_count, (mask + 1) * new_count)
        for kind in range(2):
            place = (kind * groups + (here ^ mask)) * new_count
            spread_out = jnp.where(lane == row + place % LANES, totals[kind][part], 0.0)
            spread_out = jnp.sum(spread_out, axis=0, keepdims=True)
            sums = sums + jnp.where(line == place // LANES, spread_out, 0.0)
    sums_ref[...] = sums


def gather_kernel(members, slots, near_ref, far_ref, heads_ref, unused, rows_ref, ids_ref):
    me = lax.axis_index("member")
    half = members // 2
    ids_ref[:half, :] = near_ref[...]
    ids_ref[half:, :] = far_ref[...]
    ids = jnp.concatenate([ids_ref[pl.ds(me ^ member, 1), :] for member in middle_first(members)], axis=0)
    rows_ref[...] = listed_rows(ids, me, slots, heads_ref)


def pack_kernel(members, slots, lines, rows_ref, mine_ref, other_ref, out_ref):
    chunks = rows_ref.shape[1] // LANES
    for member in range(members):
        for chunk in range(chunks):
            out_ref[member, chunk * slots:(chunk + 1) * slots, :] = rows_ref[
                member * slots:(member + 1) * slots, chunk * LANES:(chunk + 1) * LANES
            ]
    sums = (mine_ref[...] + other_ref[...])[:lines]
    coded = []
    for unused in range(PARTS):
        coded.append(sums.astype(jnp.bfloat16).astype(jnp.float32))
        sums = sums - coded[-1]
    missing = out_ref.shape[1] - chunks * slots - PARTS * lines
    if missing:
        coded.append(jnp.zeros((missing, LANES), jnp.float32))
    tail = jnp.concatenate(coded, axis=0).astype(jnp.bfloat16)
    for member in range(members):
        out_ref[member, chunks * slots:, :] = tail


def prepare_kernel(members, slots, head_dev, ids_ref, vectors_ref, unused, back_ref, vec_sq_ref):
    near = ids_ref.shape[1]
    block = vectors_ref.shape[1]
    square = (near, near)
    owner_row = jnp.broadcast_to(lax.div(ids_ref[...], head_dev), square)
    eye = iota(square, 0) == iota(square, 1)
    owner = jnp.sum(jnp.where(eye, owner_row, 0), axis=1, keepdims=True)
    before = (owner_row == owner) & (iota(square, 1) < iota(square, 0))
    place = jnp.sum(before.astype(jnp.int32), axis=1, keepdims=True)
    source = first_middle(owner, members) * slots + place
    back_ref[...] = (source == iota(back_ref.shape, 1)).astype(jnp.bfloat16)
    vec_sq = jnp.sum(jnp.square(vectors_ref[0].astype(jnp.float32)), axis=1, keepdims=True)
    diagonal = iota((block, block), 0) == iota((block, block), 1)
    vec_sq_ref[...] = jnp.sum(jnp.where(diagonal, vec_sq, 0.0), axis=0, keepdims=True)


def distances(slots, back_ref, vec_sq_ref, listed_ref, vectors_ref, out_ref):
    members = listed_ref.shape[0]
    width = vectors_ref.shape[2]
    rows = []
    for chunk in range(width // LANES):
        part = listed_ref[:, chunk * slots:(chunk + 1) * slots, :].reshape(members * slots, LANES)
        rows.append(jnp.dot(back_ref[...], part, preferred_element_type=jnp.float32))
    rows = jnp.concatenate(rows, axis=1)
    row_sq = jnp.sum(jnp.square(rows), axis=1, keepdims=True)
    dots = lax.dot_general(
        rows.astype(jnp.bfloat16), vectors_ref[0], (((1,), (1,)), ((), ())),
        preferred_element_type=jnp.float32,
    )
    out_ref[0] = (row_sq + vec_sq_ref[...] - 2.0 * dots) * (1.0 / width)


def tail_kernel(
    groups, slots, total_heads, back_ref, vec_sq_ref, listed_ref, vectors_ref,
    density_ref, spread_ref, out_ref,
):
    distances(slots, back_ref, vec_sq_ref, listed_ref, vectors_ref, out_ref)
    here = lax.axis_index("group")
    members = listed_ref.shape[0]
    new_count = density_ref.shape[1]
    lines = 2 * groups * new_count // LANES
    first = vectors_ref.shape[2] // LANES * slots
    coded = jnp.sum(listed_ref[:, first:, :].astype(jnp.float32), axis=0)
    total = sum(coded[part * lines:(part + 1) * lines] for part in range(PARTS))
    shape = (new_count, LANES)
    eye = iota((new_count, new_count), 0) == iota((new_count, new_count), 1)
    found = []
    for kind in range(2):
        place = (kind * groups + here) * new_count
        line = jnp.sum(
            jnp.where(iota((lines, LANES), 0) == place // LANES, total, 0.0), axis=0, keepdims=True
        )
        column = jnp.sum(
            jnp.where(iota(shape, 1) == iota(shape, 0) + place % LANES, line, 0.0),
            axis=1, keepdims=True,
        )
        found.append(jnp.sum(jnp.where(eye, column, 0.0), axis=0, keepdims=True))
    density_ref[...] = jnp.log(found[0] * (1.0 / total_heads))
    spread_ref[...] = found[1] / found[0]


def per_device(heads, new_heads, vectors, near_ids):
    head_dev, width = heads.shape
    new_count = new_heads.shape[0]
    near = near_ids.shape[1]
    groups = lax.axis_size("group")
    members = lax.axis_size("member")
    most = 2 * near // members
    slots = -(-most // PACK) * PACK

    partner_ids = from_partner(near_ids, "member", 1)
    others = [from_partner(new_heads, "group", mask) for mask in range(1, groups)]
    ids = call(
        stage_kernel,
        jax.ShapeDtypeStruct(near_ids.shape, near_ids.dtype),
        (in_hbm(near_ids),),
        (0, 0),
        scratch=[pltpu.SemaphoreType.DMA],
        spaces=[HBM],
    )
    ids = jnp.concatenate([ids, partner_ids], axis=0)
    kept, head_sq, new_heads = call(
        early_kernel,
        (
            jax.ShapeDtypeStruct(heads.shape, heads.dtype),
            jax.ShapeDtypeStruct((1, head_dev), jnp.float32),
            jax.ShapeDtypeStruct(new_heads.shape, new_heads.dtype),
        ),
        (in_hbm(heads), in_hbm(new_heads), ids),
        (0, 0),
        scratch=[pltpu.SemaphoreType.DMA((5,))],
        spaces=[HBM, HBM, pl.ANY],
    )
    lines = 2 * groups * new_count // LANES
    chunks = width // LANES
    extra = -(-PARTS * lines // TILE) * TILE
    sums, kept_ids = call(
        functools.partial(crowd_kernel, groups),
        (
            jax.ShapeDtypeStruct((-(-lines // TILE) * TILE, LANES), jnp.float32),
            jax.ShapeDtypeStruct(ids.shape, ids.dtype),
        ),
        (ids, kept, head_sq, new_heads, *others),
        (0, 0),
    )
    mask = 2
    while mask < members // 2:
        kept_ids = jnp.concatenate([kept_ids, from_partner(ids, "member", mask)], axis=0)
        ids = kept_ids
        mask *= 2
    far_ids = from_partner(ids, "member", mask)
    mask = 1
    while mask < groups // 2:
        sums = sums + from_partner(sums, "group", mask)
        mask *= 2
    back, vec_sq = call(
        functools.partial(prepare_kernel, members, slots, head_dev),
        (
            jax.ShapeDtypeStruct((near, members * slots), jnp.bfloat16),
            jax.ShapeDtypeStruct((1, vectors.shape[1]), jnp.float32),
        ),
        (near_ids, vectors, sums),
        (0, 0),
        spaces=[VMEM, VMEM, pl.ANY],
    )
    rows = call(
        functools.partial(gather_kernel, members, slots),
        jax.ShapeDtypeStruct((members * slots, width), jnp.bfloat16),
        (ids, far_ids, kept, back),
        (2 * members * slots * head_dev * width, heads.size * 2),
        scratch=[pltpu.VMEM((members, near), jnp.int32)],
        spaces=[VMEM, VMEM, VMEM, pl.ANY],
    )
    message = call(
        functools.partial(pack_kernel, members, slots, lines),
        jax.ShapeDtypeStruct((members, chunks * slots + extra, LANES), jnp.bfloat16),
        (rows, sums, from_partner(sums, "group", mask)),
        (0, members * slots * width * 4),
    )
    message = lax.all_to_all(
        message, "member", 0, 0, tiled=True, axis_index_groups=[middle_first(members)]
    )

    density, spread, reassign = call(
        functools.partial(
            tail_kernel, groups, slots, float(head_dev * groups * members)
        ),
        (
            jax.ShapeDtypeStruct((1, new_count), jnp.float32),
            jax.ShapeDtypeStruct((1, new_count), jnp.float32),
            jax.ShapeDtypeStruct((1, near, vectors.shape[1]), jnp.float32),
        ),
        (back, vec_sq, message, vectors),
        (4 * near * vectors.shape[1] * width, vectors.size * 4),
    )
    return (density[0], spread[0], reassign)


def solution(mesh):
    placed = (
        P(("group", "member"), None),
        P("group", None),
        P(("group", "member"), None, None),
        P(("group", "member"), None),
    )
    return jax.shard_map(
        per_device,
        mesh=mesh,
        in_specs=placed,
        out_specs=(P("group"), P("group"), P(("group", "member"), None, None)),
        check_vma=False,
    )
```

```python
import functools

import jax
import jax.numpy as jnp
from jax import lax
from jax.experimental import pallas as pl
from jax.experimental.pallas import tpu as pltpu
from jax.sharding import PartitionSpec as P

VMEM = pltpu.MemorySpace.VMEM
HBM = pltpu.MemorySpace.HBM
LANES = 128
PACK = 16
TILE = 8
PARTS = 3
LIMIT = 24 * 2**20


def from_partner(value, axis, mask):
    count = lax.axis_size(axis)
    return lax.ppermute(value, axis, [(source, source ^ mask) for source in range(count)])


def middle_first(members):
    middle = members // 2 + 1
    return [middle] + [member for member in range(members) if member != middle]


def first_middle(member, members):
    middle = members // 2 + 1
    return jnp.where(member == middle, 0, jnp.where(member < middle, member + 1, member))


def in_hbm(value):
    return pltpu.with_memory_space_constraint(value, HBM)


def call(body, shapes, operands, cost, scratch=(), spaces=None):
    return pl.pallas_call(
        body,
        out_shape=shapes,
        in_specs=[pl.BlockSpec(memory_space=space) for space in spaces or [VMEM] * len(operands)],
        out_specs=jax.tree.map(lambda unused: pl.BlockSpec(memory_space=VMEM), shapes),
        scratch_shapes=scratch,
        compiler_params=pltpu.CompilerParams(vmem_limit_bytes=LIMIT),
        cost_estimate=pl.CostEstimate(flops=cost[0], bytes_accessed=cost[1], transcendentals=0),
    )(*operands)


def iota(shape, dim):
    return lax.broadcasted_iota(jnp.int32, shape, dim)


def stage_kernel(ids_ref, kept_ref, sem):
    copy = pltpu.make_async_copy(ids_ref, kept_ref, sem)
    copy.start()
    copy.wait()


def early_kernel(heads_ref, new_ref, unused, kept_ref, head_sq_ref, kept_new_ref, sems):
    head_dev, width = heads_ref.shape
    tiles = sems.shape[0] - 1
    tile = head_dev // tiles
    parts = [pl.ds(i * tile, tile) for i in range(tiles)]
    copies = [
        pltpu.make_async_copy(heads_ref.at[part], kept_ref.at[part], sems.at[i])
        for i, part in enumerate(parts)
    ]
    copies.append(pltpu.make_async_copy(new_ref, kept_new_ref, sems.at[tiles]))
    for copy in copies:
        copy.start()
    for i in range(tiles):
        copies[i].wait()
        for first in range(i * tile, (i + 1) * tile, LANES):
            block = jnp.square(kept_ref[first:first + LANES, :].astype(jnp.float32))
            folded = block[:, :LANES]
            for column in range(LANES, width, LANES):
                folded = folded + block[:, column:column + LANES]
            head_sq_ref[:, first:first + LANES] = jnp.sum(folded.T, axis=0, keepdims=True)
    for copy in copies[tiles:]:
        copy.wait()


def listed_rows(ids, me, slots, heads_ref):
    members, near = ids.shape
    head_dev = heads_ref.shape[0]
    local = ids - me * head_dev
    owned = (local >= 0) & (local < head_dev)
    earlier = (iota((near, near), 0) < iota((near, near), 1)).astype(jnp.bfloat16)
    rank = jnp.dot(owned.astype(jnp.bfloat16), earlier, preferred_element_type=jnp.float32)
    rank = jnp.where(owned, rank.astype(jnp.int32), -1)
    shape = (members, slots, near)
    pick = jnp.broadcast_to(rank[:, None, :], shape) == iota(shape, 1)
    wanted = jnp.sum(
        jnp.where(pick, jnp.broadcast_to(local[:, None, :] + 1, shape), 0), axis=2, keepdims=True
    ).reshape(members * slots, 1)
    onehot = (wanted == iota((members * slots, head_dev), 1) + 1).astype(jnp.bfloat16)
    return jnp.dot(
        onehot, heads_ref[...], preferred_element_type=jnp.float32
    ).astype(jnp.bfloat16)


def crowding(queries, heads_ref, head_sq_ref):
    head_dev, width = heads_ref.shape
    query_sq = jnp.sum(jnp.square(queries.astype(jnp.float32)), axis=1, keepdims=True)
    total_w = jnp.zeros((queries.shape[0], 1), jnp.float32)
    total_we = jnp.zeros((queries.shape[0], 1), jnp.float32)
    tile = 512
    for start in range(0, head_dev, tile):
        dots = lax.dot_general(
            queries, heads_ref[start:start + tile, :], (((1,), (1,)), ((), ())),
            preferred_element_type=jnp.float32,
        )
        head_sq = head_sq_ref[:, start:start + tile]
        excess = (query_sq + head_sq - 2.0 * dots) * (1.0 / width)
        inverse = 1.0 / (1.0 + excess)
        weight = inverse * inverse
        total_w = total_w + jnp.sum(weight, axis=1, keepdims=True)
        total_we = total_we + jnp.sum(weight * excess, axis=1, keepdims=True)
    return total_w, total_we


def crowd_kernel(groups, ids_ref, heads_ref, head_sq_ref, *refs):
    query_refs, (sums_ref, kept_ids_ref) = refs[:-2], refs[-2:]
    kept_ids_ref[...] = ids_ref[...]
    here = lax.axis_index("group")
    queries = jnp.concatenate([ref[...] for ref in query_refs], axis=0)
    new_count = queries.shape[0] // groups
    totals = crowding(queries, heads_ref, head_sq_ref)
    lane = iota((new_count, LANES), 1)
    row = iota((new_count, LANES), 0)
    line = iota(sums_ref.shape, 0)
    sums = jnp.zeros(sums_ref.shape, jnp.float32)
    for mask in range(groups):
        part = slice(mask * new_count, (mask + 1) * new_count)
        for kind in range(2):
            place = (kind * groups + (here ^ mask)) * new_count
            spread_out = jnp.where(lane == row + place % LANES, totals[kind][part], 0.0)
            spread_out = jnp.sum(spread_out, axis=0, keepdims=True)
            sums = sums + jnp.where(line == place // LANES, spread_out, 0.0)
    sums_ref[...] = sums


def gather_kernel(members, slots, near_ref, far_ref, heads_ref, unused, rows_ref, ids_ref):
    me = lax.axis_index("member")
    half = members // 2
    ids_ref[:half, :] = near_ref[...]
    ids_ref[half:, :] = far_ref[...]
    ids = jnp.concatenate([ids_ref[pl.ds(me ^ member, 1), :] for member in middle_first(members)], axis=0)
    rows_ref[...] = listed_rows(ids, me, slots, heads_ref)


def pack_kernel(members, slots, lines, rows_ref, mine_ref, other_ref, out_ref):
    chunks = rows_ref.shape[1] // LANES
    for member in range(members):
        for chunk in range(chunks):
            out_ref[member, chunk * slots:(chunk + 1) * slots, :] = rows_ref[
                member * slots:(member + 1) * slots, chunk * LANES:(chunk + 1) * LANES
            ]
    sums = (mine_ref[...] + other_ref[...])[:lines]
    coded = []
    for unused in range(PARTS):
        coded.append(sums.astype(jnp.bfloat16).astype(jnp.float32))
        sums = sums - coded[-1]
    missing = out_ref.shape[1] - chunks * slots - PARTS * lines
    if missing:
        coded.append(jnp.zeros((missing, LANES), jnp.float32))
    tail = jnp.concatenate(coded, axis=0).astype(jnp.bfloat16)
    for member in range(members):
        out_ref[member, chunks * slots:, :] = tail


def prepare_kernel(members, slots, head_dev, ids_ref, vectors_ref, unused, back_ref, vec_sq_ref):
    near = ids_ref.shape[1]
    block = vectors_ref.shape[1]
    square = (near, near)
    owner_row = jnp.broadcast_to(lax.div(ids_ref[...], head_dev), square)
    eye = iota(square, 0) == iota(square, 1)
    owner = jnp.sum(jnp.where(eye, owner_row, 0), axis=1, keepdims=True)
    before = (owner_row == owner) & (iota(square, 1) < iota(square, 0))
    place = jnp.sum(before.astype(jnp.int32), axis=1, keepdims=True)
    source = first_middle(owner, members) * slots + place
    back_ref[...] = (source == iota(back_ref.shape, 1)).astype(jnp.bfloat16)
    vec_sq = jnp.sum(jnp.square(vectors_ref[0].astype(jnp.float32)), axis=1, keepdims=True)
    diagonal = iota((block, block), 0) == iota((block, block), 1)
    vec_sq_ref[...] = jnp.sum(jnp.where(diagonal, vec_sq, 0.0), axis=0, keepdims=True)


def distances(slots, back_ref, vec_sq_ref, listed_ref, vectors_ref, out_ref):
    members = listed_ref.shape[0]
    width = vectors_ref.shape[2]
    rows = []
    for chunk in range(width // LANES):
        part = listed_ref[:, chunk * slots:(chunk + 1) * slots, :].reshape(members * slots, LANES)
        rows.append(jnp.dot(back_ref[...], part, preferred_element_type=jnp.float32))
    rows = jnp.concatenate(rows, axis=1)
    row_sq = jnp.sum(jnp.square(rows), axis=1, keepdims=True)
    dots = lax.dot_general(
        rows.astype(jnp.bfloat16), vectors_ref[0], (((1,), (1,)), ((), ())),
        preferred_element_type=jnp.float32,
    )
    out_ref[0] = (row_sq + vec_sq_ref[...] - 2.0 * dots) * (1.0 / width)


def tail_kernel(
    groups, slots, total_heads, back_ref, vec_sq_ref, listed_ref, vectors_ref,
    density_ref, spread_ref, out_ref,
):
    distances(slots, back_ref, vec_sq_ref, listed_ref, vectors_ref, out_ref)
    here = lax.axis_index("group")
    members = listed_ref.shape[0]
    new_count = density_ref.shape[1]
    lines = 2 * groups * new_count // LANES
    first = vectors_ref.shape[2] // LANES * slots
    coded = jnp.sum(listed_ref[:, first:, :].astype(jnp.float32), axis=0)
    total = sum(coded[part * lines:(part + 1) * lines] for part in range(PARTS))
    shape = (new_count, LANES)
    eye = iota((new_count, new_count), 0) == iota((new_count, new_count), 1)
    found = []
    for kind in range(2):
        place = (kind * groups + here) * new_count
        line = jnp.sum(
            jnp.where(iota((lines, LANES), 0) == place // LANES, total, 0.0), axis=0, keepdims=True
        )
        column = jnp.sum(
            jnp.where(iota(shape, 1) == iota(shape, 0) + place % LANES, line, 0.0),
            axis=1, keepdims=True,
        )
        found.append(jnp.sum(jnp.where(eye, column, 0.0), axis=0, keepdims=True))
    density_ref[...] = jnp.log(found[0] * (1.0 / total_heads))
    spread_ref[...] = found[1] / found[0]


def per_device(heads, new_heads, vectors, near_ids):
    head_dev, width = heads.shape
    new_count = new_heads.shape[0]
    near = near_ids.shape[1]
    groups = lax.axis_size("group")
    members = lax.axis_size("member")
    most = 2 * near // members
    slots = -(-most // PACK) * PACK

    partner_ids = from_partner(near_ids, "member", 1)
    others = [from_partner(new_heads, "group", mask) for mask in range(1, groups)]
    ids = call(
        stage_kernel,
        jax.ShapeDtypeStruct(near_ids.shape, near_ids.dtype),
        (in_hbm(near_ids),),
        (0, 0),
        scratch=[pltpu.SemaphoreType.DMA],
        spaces=[HBM],
    )
    ids = jnp.concatenate([ids, partner_ids], axis=0)
    kept, head_sq, new_heads = call(
        early_kernel,
        (
            jax.ShapeDtypeStruct(heads.shape, heads.dtype),
            jax.ShapeDtypeStruct((1, head_dev), jnp.float32),
            jax.ShapeDtypeStruct(new_heads.shape, new_heads.dtype),
        ),
        (in_hbm(heads), in_hbm(new_heads), ids),
        (0, 0),
        scratch=[pltpu.SemaphoreType.DMA((9,))],
        spaces=[HBM, HBM, pl.ANY],
    )
    lines = 2 * groups * new_count // LANES
    chunks = width // LANES
    extra = -(-PARTS * lines // TILE) * TILE
    sums, kept_ids = call(
        functools.partial(crowd_kernel, groups),
        (
            jax.ShapeDtypeStruct((-(-lines // TILE) * TILE, LANES), jnp.float32),
            jax.ShapeDtypeStruct(ids.shape, ids.dtype),
        ),
        (ids, kept, head_sq, new_heads, *others),
        (0, 0),
    )
    mask = 2
    while mask < members // 2:
        kept_ids = jnp.concatenate([kept_ids, from_partner(ids, "member", mask)], axis=0)
        ids = kept_ids
        mask *= 2
    far_ids = from_partner(ids, "member", mask)
    mask = 1
    while mask < groups // 2:
        sums = sums + from_partner(sums, "group", mask)
        mask *= 2
    back, vec_sq = call(
        functools.partial(prepare_kernel, members, slots, head_dev),
        (
            jax.ShapeDtypeStruct((near, members * slots), jnp.bfloat16),
            jax.ShapeDtypeStruct((1, vectors.shape[1]), jnp.float32),
        ),
        (near_ids, vectors, sums),
        (0, 0),
        spaces=[VMEM, VMEM, pl.ANY],
    )
    rows = call(
        functools.partial(gather_kernel, members, slots),
        jax.ShapeDtypeStruct((members * slots, width), jnp.bfloat16),
        (ids, far_ids, kept, back),
        (2 * members * slots * head_dev * width, heads.size * 2),
        scratch=[pltpu.VMEM((members, near), jnp.int32)],
        spaces=[VMEM, VMEM, VMEM, pl.ANY],
    )
    message = call(
        functools.partial(pack_kernel, members, slots, lines),
        jax.ShapeDtypeStruct((members, chunks * slots + extra, LANES), jnp.bfloat16),
        (rows, sums, from_partner(sums, "group", mask)),
        (0, members * slots * width * 4),
    )
    message = lax.all_to_all(
        message, "member", 0, 0, tiled=True, axis_index_groups=[middle_first(members)]
    )

    density, spread, reassign = call(
        functools.partial(
            tail_kernel, groups, slots, float(head_dev * groups * members)
        ),
        (
            jax.ShapeDtypeStruct((1, new_count), jnp.float32),
            jax.ShapeDtypeStruct((1, new_count), jnp.float32),
            jax.ShapeDtypeStruct((1, near, vectors.shape[1]), jnp.float32),
        ),
        (back, vec_sq, message, vectors),
        (4 * near * vectors.shape[1] * width, vectors.size * 4),
    )
    return (density[0], spread[0], reassign)


def solution(mesh):
    placed = (
        P(("group", "member"), None),
        P("group", None),
        P(("group", "member"), None, None),
        P(("group", "member"), None),
    )
    return jax.shard_map(
        per_device,
        mesh=mesh,
        in_specs=placed,
        out_specs=(P("group"), P("group"), P(("group", "member"), None, None)),
        check_vma=False,
    )
```

```python
import functools

import jax
import jax.numpy as jnp
from jax import lax
from jax.experimental import pallas as pl
from jax.experimental.pallas import tpu as pltpu
from jax.sharding import PartitionSpec as P

VMEM = pltpu.MemorySpace.VMEM
HBM = pltpu.MemorySpace.HBM
LANES = 128
PACK = 16
TILE = 8
PARTS = 3
LIMIT = 24 * 2**20


def from_partner(value, axis, mask):
    count = lax.axis_size(axis)
    return lax.ppermute(value, axis, [(source, source ^ mask) for source in range(count)])


def middle_first(members):
    return [members // 2] + [member for member in range(members) if member != members // 2]


def first_middle(member, members):
    middle = members // 2
    return jnp.where(member == middle, 0, jnp.where(member < middle, member + 1, member))


def in_hbm(value):
    return pltpu.with_memory_space_constraint(value, HBM)


def call(body, shapes, operands, cost, scratch=(), spaces=None):
    return pl.pallas_call(
        body,
        out_shape=shapes,
        in_specs=[pl.BlockSpec(memory_space=space) for space in spaces or [VMEM] * len(operands)],
        out_specs=jax.tree.map(lambda unused: pl.BlockSpec(memory_space=VMEM), shapes),
        scratch_shapes=scratch,
        compiler_params=pltpu.CompilerParams(vmem_limit_bytes=LIMIT),
        cost_estimate=pl.CostEstimate(flops=cost[0], bytes_accessed=cost[1], transcendentals=0),
    )(*operands)


def iota(shape, dim):
    return lax.broadcasted_iota(jnp.int32, shape, dim)


def stage_kernel(ids_ref, kept_ref, sem):
    copy = pltpu.make_async_copy(ids_ref, kept_ref, sem)
    copy.start()
    copy.wait()


def early_kernel(heads_ref, new_ref, unused, kept_ref, head_sq_ref, kept_new_ref, sems):
    head_dev, width = heads_ref.shape
    tiles = 4
    tile = head_dev // tiles
    parts = [pl.ds(i * tile, tile) for i in range(tiles)]
    copies = [
        pltpu.make_async_copy(heads_ref.at[part], kept_ref.at[part], sems.at[i])
        for i, part in enumerate(parts)
    ]
    copies.append(pltpu.make_async_copy(new_ref, kept_new_ref, sems.at[tiles]))
    for copy in copies:
        copy.start()
    for i in range(tiles):
        copies[i].wait()
        for first in range(i * tile, (i + 1) * tile, LANES):
            block = jnp.square(kept_ref[first:first + LANES, :].astype(jnp.float32))
            folded = block[:, :LANES]
            for column in range(LANES, width, LANES):
                folded = folded + block[:, column:column + LANES]
            head_sq_ref[first:first + LANES, :] = jnp.sum(folded, axis=1, keepdims=True)
    for copy in copies[tiles:]:
        copy.wait()


def listed_rows(ids, me, slots, heads_ref):
    members, near = ids.shape
    head_dev = heads_ref.shape[0]
    local = ids - me * head_dev
    owned = (local >= 0) & (local < head_dev)
    earlier = (iota((near, near), 0) < iota((near, near), 1)).astype(jnp.bfloat16)
    rank = jnp.dot(owned.astype(jnp.bfloat16), earlier, preferred_element_type=jnp.float32)
    rank = jnp.where(owned, rank.astype(jnp.int32), -1)
    shape = (members, slots, near)
    pick = jnp.broadcast_to(rank[:, None, :], shape) == iota(shape, 1)
    wanted = jnp.sum(
        jnp.where(pick, jnp.broadcast_to(local[:, None, :] + 1, shape), 0), axis=2, keepdims=True
    ).reshape(members * slots, 1)
    onehot = (wanted == iota((members * slots, head_dev), 1) + 1).astype(jnp.bfloat16)
    return jnp.dot(
        onehot, heads_ref[...], preferred_element_type=jnp.float32
    ).astype(jnp.bfloat16)


def turned(vector):
    count = max(vector.shape)
    diagonal = iota((count, count), 0) == iota((count, count), 1)
    return jnp.sum(jnp.where(diagonal, vector, 0.0), axis=vector.shape.index(count), keepdims=True)


def crowding(queries, heads_ref, head_sq_ref):
    head_dev, width = heads_ref.shape
    query_sq = turned(jnp.sum(jnp.square(queries.astype(jnp.float32)), axis=1, keepdims=True))
    total_w = jnp.zeros((TILE, queries.shape[0]), jnp.float32)
    total_we = jnp.zeros((TILE, queries.shape[0]), jnp.float32)
    tile = 256
    for start in range(0, head_dev, tile):
        dots = lax.dot_general(
            heads_ref[start:start + tile, :], queries, (((1,), (1,)), ((), ())),
            preferred_element_type=jnp.float32,
        )
        excess = (query_sq + head_sq_ref[start:start + tile, :] - 2.0 * dots) * (1.0 / width)
        inverse = 1.0 / (1.0 + excess)
        weight = inverse * inverse
        weighted = weight * excess
        for row in range(0, tile, TILE):
            total_w = total_w + weight[row:row + TILE, :]
            total_we = total_we + weighted[row:row + TILE, :]
    total_w = jnp.sum(total_w, axis=0, keepdims=True)
    total_we = jnp.sum(total_we, axis=0, keepdims=True)
    return turned(total_w), turned(total_we)


def crowd_kernel(groups, ids_ref, heads_ref, head_sq_ref, *refs):
    query_refs, (sums_ref, kept_ids_ref) = refs[:-2], refs[-2:]
    kept_ids_ref[...] = ids_ref[...]
    here = lax.axis_index("group")
    queries = jnp.concatenate([ref[...] for ref in query_refs], axis=0)
    new_count = queries.shape[0] // groups
    totals = crowding(queries, heads_ref, head_sq_ref)
    lane = iota((new_count, LANES), 1)
    row = iota((new_count, LANES), 0)
    line = iota(sums_ref.shape, 0)
    sums = jnp.zeros(sums_ref.shape, jnp.float32)
    for mask in range(groups):
        part = slice(mask * new_count, (mask + 1) * new_count)
        for kind in range(2):
            place = (kind * groups + (here ^ mask)) * new_count
            spread_out = jnp.where(lane == row + place % LANES, totals[kind][part], 0.0)
            spread_out = jnp.sum(spread_out, axis=0, keepdims=True)
            sums = sums + jnp.where(line == place // LANES, spread_out, 0.0)
    sums_ref[...] = sums


def gather_kernel(members, slots, near_ref, far_ref, heads_ref, unused, rows_ref, ids_ref):
    me = lax.axis_index("member")
    half = members // 2
    ids_ref[:half, :] = near_ref[...]
    ids_ref[half:, :] = far_ref[...]
    ids = jnp.concatenate([ids_ref[pl.ds(me ^ member, 1), :] for member in middle_first(members)], axis=0)
    rows_ref[...] = listed_rows(ids, me, slots, heads_ref)


def pack_kernel(members, slots, lines, rows_ref, mine_ref, other_ref, out_ref):
    chunks = rows_ref.shape[1] // LANES
    for member in range(members):
        for chunk in range(chunks):
            out_ref[member, chunk * slots:(chunk + 1) * slots, :] = rows_ref[
                member * slots:(member + 1) * slots, chunk * LANES:(chunk + 1) * LANES
            ]
    sums = (mine_ref[...] + other_ref[...])[:lines]
    coded = []
    for unused in range(PARTS):
        coded.append(sums.astype(jnp.bfloat16).astype(jnp.float32))
        sums = sums - coded[-1]
    missing = out_ref.shape[1] - chunks * slots - PARTS * lines
    if missing:
        coded.append(jnp.zeros((missing, LANES), jnp.float32))
    tail = jnp.concatenate(coded, axis=0).astype(jnp.bfloat16)
    for member in range(members):
        out_ref[member, chunks * slots:, :] = tail


def prepare_kernel(members, slots, head_dev, ids_ref, vectors_ref, unused, back_ref, vec_sq_ref):
    near = ids_ref.shape[1]
    block = vectors_ref.shape[1]
    square = (near, near)
    owner_row = jnp.broadcast_to(lax.div(ids_ref[...], head_dev), square)
    eye = iota(square, 0) == iota(square, 1)
    owner = jnp.sum(jnp.where(eye, owner_row, 0), axis=1, keepdims=True)
    before = (owner_row == owner) & (iota(square, 1) < iota(square, 0))
    place = jnp.sum(before.astype(jnp.int32), axis=1, keepdims=True)
    source = first_middle(owner, members) * slots + place
    back_ref[...] = (source == iota(back_ref.shape, 1)).astype(jnp.bfloat16)
    vec_sq = jnp.sum(jnp.square(vectors_ref[0].astype(jnp.float32)), axis=1, keepdims=True)
    diagonal = iota((block, block), 0) == iota((block, block), 1)
    vec_sq_ref[...] = jnp.sum(jnp.where(diagonal, vec_sq, 0.0), axis=0, keepdims=True)


def distances(slots, back_ref, vec_sq_ref, listed_ref, vectors_ref, out_ref):
    members = listed_ref.shape[0]
    width = vectors_ref.shape[2]
    rows = []
    for chunk in range(width // LANES):
        part = listed_ref[:, chunk * slots:(chunk + 1) * slots, :].reshape(members * slots, LANES)
        rows.append(jnp.dot(back_ref[...], part, preferred_element_type=jnp.float32))
    rows = jnp.concatenate(rows, axis=1)
    row_sq = jnp.sum(jnp.square(rows), axis=1, keepdims=True)
    dots = lax.dot_general(
        rows.astype(jnp.bfloat16), vectors_ref[0], (((1,), (1,)), ((), ())),
        preferred_element_type=jnp.float32,
    )
    out_ref[0] = (row_sq + vec_sq_ref[...] - 2.0 * dots) * (1.0 / width)


def tail_kernel(
    groups, slots, total_heads, back_ref, vec_sq_ref, listed_ref, vectors_ref,
    density_ref, spread_ref, out_ref,
):
    distances(slots, back_ref, vec_sq_ref, listed_ref, vectors_ref, out_ref)
    here = lax.axis_index("group")
    members = listed_ref.shape[0]
    new_count = density_ref.shape[1]
    lines = 2 * groups * new_count // LANES
    first = vectors_ref.shape[2] // LANES * slots
    coded = jnp.sum(listed_ref[:, first:, :].astype(jnp.float32), axis=0)
    total = sum(coded[part * lines:(part + 1) * lines] for part in range(PARTS))
    shape = (new_count, LANES)
    eye = iota((new_count, new_count), 0) == iota((new_count, new_count), 1)
    found = []
    for kind in range(2):
        place = (kind * groups + here) * new_count
        line = jnp.sum(
            jnp.where(iota((lines, LANES), 0) == place // LANES, total, 0.0), axis=0, keepdims=True
        )
        column = jnp.sum(
            jnp.where(iota(shape, 1) == iota(shape, 0) + place % LANES, line, 0.0),
            axis=1, keepdims=True,
        )
        found.append(jnp.sum(jnp.where(eye, column, 0.0), axis=0, keepdims=True))
    density_ref[...] = jnp.log(found[0] * (1.0 / total_heads))
    spread_ref[...] = found[1] / found[0]


def per_device(heads, new_heads, vectors, near_ids):
    head_dev, width = heads.shape
    new_count = new_heads.shape[0]
    near = near_ids.shape[1]
    groups = lax.axis_size("group")
    members = lax.axis_size("member")
    most = 2 * near // members
    slots = -(-most // PACK) * PACK

    partner_ids = from_partner(near_ids, "member", 1)
    others = [from_partner(new_heads, "group", mask) for mask in range(1, groups)]
    ids = call(
        stage_kernel,
        jax.ShapeDtypeStruct(near_ids.shape, near_ids.dtype),
        (in_hbm(near_ids),),
        (0, 0),
        scratch=[pltpu.SemaphoreType.DMA],
        spaces=[HBM],
    )
    ids = jnp.concatenate([ids, partner_ids], axis=0)
    kept, head_sq, new_heads = call(
        early_kernel,
        (
            jax.ShapeDtypeStruct(heads.shape, heads.dtype),
            jax.ShapeDtypeStruct((head_dev, 1), jnp.float32),
            jax.ShapeDtypeStruct(new_heads.shape, new_heads.dtype),
        ),
        (in_hbm(heads), in_hbm(new_heads), ids),
        (0, 0),
        scratch=[pltpu.SemaphoreType.DMA((5,))],
        spaces=[HBM, HBM, pl.ANY],
    )
    lines = 2 * groups * new_count // LANES
    chunks = width // LANES
    extra = -(-PARTS * lines // TILE) * TILE
    sums, kept_ids = call(
        functools.partial(crowd_kernel, groups),
        (
            jax.ShapeDtypeStruct((-(-lines // TILE) * TILE, LANES), jnp.float32),
            jax.ShapeDtypeStruct(ids.shape, ids.dtype),
        ),
        (ids, kept, head_sq, new_heads, *others),
        (0, 0),
    )
    mask = 2
    while mask < members // 2:
        kept_ids = jnp.concatenate([kept_ids, from_partner(ids, "member", mask)], axis=0)
        ids = kept_ids
        mask *= 2
    far_ids = from_partner(ids, "member", mask)
    mask = 1
    while mask < groups // 2:
        sums = sums + from_partner(sums, "group", mask)
        mask *= 2
    back, vec_sq = call(
        functools.partial(prepare_kernel, members, slots, head_dev),
        (
            jax.ShapeDtypeStruct((near, members * slots), jnp.bfloat16),
            jax.ShapeDtypeStruct((1, vectors.shape[1]), jnp.float32),
        ),
        (near_ids, vectors, sums),
        (0, 0),
        spaces=[VMEM, VMEM, pl.ANY],
    )
    rows = call(
        functools.partial(gather_kernel, members, slots),
        jax.ShapeDtypeStruct((members * slots, width), jnp.bfloat16),
        (ids, far_ids, kept, back),
        (2 * members * slots * head_dev * width, heads.size * 2),
        scratch=[pltpu.VMEM((members, near), jnp.int32)],
        spaces=[VMEM, VMEM, VMEM, pl.ANY],
    )
    message = call(
        functools.partial(pack_kernel, members, slots, lines),
        jax.ShapeDtypeStruct((members, chunks * slots + extra, LANES), jnp.bfloat16),
        (rows, sums, from_partner(sums, "group", mask)),
        (0, members * slots * width * 4),
    )
    message = lax.all_to_all(
        message, "member", 0, 0, tiled=True, axis_index_groups=[middle_first(members)]
    )

    density, spread, reassign = call(
        functools.partial(
            tail_kernel, groups, slots, float(head_dev * groups * members)
        ),
        (
            jax.ShapeDtypeStruct((1, new_count), jnp.float32),
            jax.ShapeDtypeStruct((1, new_count), jnp.float32),
            jax.ShapeDtypeStruct((1, near, vectors.shape[1]), jnp.float32),
        ),
        (back, vec_sq, message, vectors),
        (4 * near * vectors.shape[1] * width, vectors.size * 4),
    )
    return (density[0], spread[0], reassign)


def solution(mesh):
    placed = (
        P(("group", "member"), None),
        P("group", None),
        P(("group", "member"), None, None),
        P(("group", "member"), None),
    )
    return jax.shard_map(
        per_device,
        mesh=mesh,
        in_specs=placed,
        out_specs=(P("group"), P("group"), P(("group", "member"), None, None)),
        check_vma=False,
    )
```

```python
import functools

import jax
import jax.numpy as jnp
from jax import lax
from jax.experimental import pallas as pl
from jax.experimental.pallas import tpu as pltpu
from jax.sharding import PartitionSpec as P

VMEM = pltpu.MemorySpace.VMEM
HBM = pltpu.MemorySpace.HBM
LANES = 128
PACK = 16
TILE = 8
PARTS = 3
LIMIT = 24 * 2**20


def from_partner(value, axis, mask):
    count = lax.axis_size(axis)
    return lax.ppermute(value, axis, [(source, source ^ mask) for source in range(count)])


def middle_first(members):
    return [members // 2] + [member for member in range(members) if member != members // 2]


def first_middle(member, members):
    middle = members // 2
    return jnp.where(member == middle, 0, jnp.where(member < middle, member + 1, member))


def in_hbm(value):
    return pltpu.with_memory_space_constraint(value, HBM)


def call(body, shapes, operands, cost, scratch=(), spaces=None):
    return pl.pallas_call(
        body,
        out_shape=shapes,
        in_specs=[pl.BlockSpec(memory_space=space) for space in spaces or [VMEM] * len(operands)],
        out_specs=jax.tree.map(lambda unused: pl.BlockSpec(memory_space=VMEM), shapes),
        scratch_shapes=scratch,
        compiler_params=pltpu.CompilerParams(vmem_limit_bytes=LIMIT),
        cost_estimate=pl.CostEstimate(flops=cost[0], bytes_accessed=cost[1], transcendentals=0),
    )(*operands)


def iota(shape, dim):
    return lax.broadcasted_iota(jnp.int32, shape, dim)


def stage_kernel(ids_ref, kept_ref, sem):
    copy = pltpu.make_async_copy(ids_ref, kept_ref, sem)
    copy.start()
    copy.wait()


def early_kernel(heads_ref, new_ref, unused, kept_ref, head_sq_ref, kept_new_ref, sems):
    head_dev, width = heads_ref.shape
    tiles = 4
    tile = head_dev // tiles
    parts = [pl.ds(i * tile, tile) for i in range(tiles)]
    copies = [
        pltpu.make_async_copy(heads_ref.at[part], kept_ref.at[part], sems.at[i])
        for i, part in enumerate(parts)
    ]
    copies.append(pltpu.make_async_copy(new_ref, kept_new_ref, sems.at[tiles]))
    for copy in copies:
        copy.start()
    for i in range(tiles):
        copies[i].wait()
        for first in range(i * tile, (i + 1) * tile, LANES):
            block = jnp.square(kept_ref[first:first + LANES, :].astype(jnp.float32))
            folded = block[:, :LANES]
            for column in range(LANES, width, LANES):
                folded = folded + block[:, column:column + LANES]
            head_sq_ref[:, first:first + LANES] = jnp.sum(folded.T, axis=0, keepdims=True)
    for copy in copies[tiles:]:
        copy.wait()


def listed_rows(ids, me, slots, heads_ref):
    members, near = ids.shape
    head_dev = heads_ref.shape[0]
    local = ids - me * head_dev
    owned = (local >= 0) & (local < head_dev)
    earlier = (iota((near, near), 0) < iota((near, near), 1)).astype(jnp.bfloat16)
    rank = jnp.dot(owned.astype(jnp.bfloat16), earlier, preferred_element_type=jnp.float32)
    rank = jnp.where(owned, rank.astype(jnp.int32), -1)
    shape = (members, slots, near)
    pick = jnp.broadcast_to(rank[:, None, :], shape) == iota(shape, 1)
    wanted = jnp.sum(
        jnp.where(pick, jnp.broadcast_to(local[:, None, :] + 1, shape), 0), axis=2, keepdims=True
    ).reshape(members * slots, 1)
    onehot = (wanted == iota((members * slots, head_dev), 1) + 1).astype(jnp.bfloat16)
    return jnp.dot(
        onehot, heads_ref[...], preferred_element_type=jnp.float32
    ).astype(jnp.bfloat16)


def crowding(queries, heads_ref, head_sq_ref):
    head_dev, width = heads_ref.shape
    query_sq = jnp.sum(jnp.square(queries.astype(jnp.float32)), axis=1, keepdims=True)
    total_w = jnp.zeros((queries.shape[0], 1), jnp.float32)
    total_we = jnp.zeros((queries.shape[0], 1), jnp.float32)
    tile = 512
    for start in range(0, head_dev, tile):
        dots = lax.dot_general(
            queries, heads_ref[start:start + tile, :], (((1,), (1,)), ((), ())),
            preferred_element_type=jnp.float32,
        )
        head_sq = head_sq_ref[:, start:start + tile]
        excess = (query_sq + head_sq - 2.0 * dots) * (1.0 / width)
        inverse = 1.0 / (1.0 + excess)
        weight = inverse * inverse
        total_w = total_w + jnp.sum(weight, axis=1, keepdims=True)
        total_we = total_we + jnp.sum(weight * excess, axis=1, keepdims=True)
    return total_w, total_we


def crowd_kernel(groups, ids_ref, heads_ref, head_sq_ref, *refs):
    query_refs, (sums_ref, kept_ids_ref) = refs[:-2], refs[-2:]
    kept_ids_ref[...] = ids_ref[...]
    here = lax.axis_index("group")
    queries = jnp.concatenate([ref[...] for ref in query_refs], axis=0)
    new_count = queries.shape[0] // groups
    totals = crowding(queries, heads_ref, head_sq_ref)
    lane = iota((new_count, LANES), 1)
    row = iota((new_count, LANES), 0)
    line = iota(sums_ref.shape, 0)
    sums = jnp.zeros(sums_ref.shape, jnp.float32)
    for mask in range(groups):
        part = slice(mask * new_count, (mask + 1) * new_count)
        for kind in range(2):
            place = (kind * groups + (here ^ mask)) * new_count
            spread_out = jnp.where(lane == row + place % LANES, totals[kind][part], 0.0)
            spread_out = jnp.sum(spread_out, axis=0, keepdims=True)
            sums = sums + jnp.where(line == place // LANES, spread_out, 0.0)
    sums_ref[...] = sums


def gather_kernel(members, slots, near_ref, far_ref, heads_ref, unused, rows_ref, ids_ref):
    me = lax.axis_index("member")
    half = members // 2
    ids_ref[:half, :] = near_ref[...]
    ids_ref[half:, :] = far_ref[...]
    ids = jnp.concatenate([ids_ref[pl.ds(me ^ member, 1), :] for member in middle_first(members)], axis=0)
    rows_ref[...] = listed_rows(ids, me, slots, heads_ref)


def pack_kernel(members, slots, lines, rows_ref, mine_ref, other_ref, out_ref):
    chunks = rows_ref.shape[1] // LANES
    for member in range(members):
        for chunk in range(chunks):
            out_ref[member, chunk * slots:(chunk + 1) * slots, :] = rows_ref[
                member * slots:(member + 1) * slots, chunk * LANES:(chunk + 1) * LANES
            ]
    sums = (mine_ref[...] + other_ref[...])[:lines]
    coded = []
    for unused in range(PARTS):
        coded.append(sums.astype(jnp.bfloat16).astype(jnp.float32))
        sums = sums - coded[-1]
    missing = out_ref.shape[1] - chunks * slots - PARTS * lines
    if missing:
        coded.append(jnp.zeros((missing, LANES), jnp.float32))
    tail = jnp.concatenate(coded, axis=0).astype(jnp.bfloat16)
    for member in range(members):
        out_ref[member, chunks * slots:, :] = tail


def prepare_kernel(members, slots, head_dev, ids_ref, vectors_ref, unused, back_ref, vec_sq_ref):
    near = ids_ref.shape[1]
    block = vectors_ref.shape[1]
    square = (near, near)
    owner_row = jnp.broadcast_to(lax.div(ids_ref[...], head_dev), square)
    eye = iota(square, 0) == iota(square, 1)
    owner = jnp.sum(jnp.where(eye, owner_row, 0), axis=1, keepdims=True)
    before = (owner_row == owner) & (iota(square, 1) < iota(square, 0))
    place = jnp.sum(before.astype(jnp.int32), axis=1, keepdims=True)
    source = first_middle(owner, members) * slots + place
    back_ref[...] = (source == iota(back_ref.shape, 1)).astype(jnp.bfloat16)
    vec_sq = jnp.sum(jnp.square(vectors_ref[0].astype(jnp.float32)), axis=1, keepdims=True)
    diagonal = iota((block, block), 0) == iota((block, block), 1)
    vec_sq_ref[...] = jnp.sum(jnp.where(diagonal, vec_sq, 0.0), axis=0, keepdims=True)


def distances(slots, back_ref, vec_sq_ref, listed_ref, vectors_ref, out_ref):
    members = listed_ref.shape[0]
    width = vectors_ref.shape[2]
    rows = []
    for chunk in range(width // LANES):
        part = listed_ref[:, chunk * slots:(chunk + 1) * slots, :].reshape(members * slots, LANES)
        rows.append(jnp.dot(back_ref[...], part, preferred_element_type=jnp.float32))
    rows = jnp.concatenate(rows, axis=1)
    row_sq = jnp.sum(jnp.square(rows), axis=1, keepdims=True)
    dots = lax.dot_general(
        rows.astype(jnp.bfloat16), vectors_ref[0], (((1,), (1,)), ((), ())),
        preferred_element_type=jnp.float32,
    )
    out_ref[0] = (row_sq + vec_sq_ref[...] - 2.0 * dots) * (1.0 / width)


def tail_kernel(
    groups, slots, total_heads, back_ref, vec_sq_ref, listed_ref, vectors_ref,
    density_ref, spread_ref, out_ref,
):
    distances(slots, back_ref, vec_sq_ref, listed_ref, vectors_ref, out_ref)
    here = lax.axis_index("group")
    members = listed_ref.shape[0]
    new_count = density_ref.shape[1]
    lines = 2 * groups * new_count // LANES
    first = vectors_ref.shape[2] // LANES * slots
    coded = jnp.sum(listed_ref[:, first:, :].astype(jnp.float32), axis=0)
    total = sum(coded[part * lines:(part + 1) * lines] for part in range(PARTS))
    shape = (new_count, LANES)
    eye = iota((new_count, new_count), 0) == iota((new_count, new_count), 1)
    found = []
    for kind in range(2):
        place = (kind * groups + here) * new_count
        line = jnp.sum(
            jnp.where(iota((lines, LANES), 0) == place // LANES, total, 0.0), axis=0, keepdims=True
        )
        column = jnp.sum(
            jnp.where(iota(shape, 1) == iota(shape, 0) + place % LANES, line, 0.0),
            axis=1, keepdims=True,
        )
        found.append(jnp.sum(jnp.where(eye, column, 0.0), axis=0, keepdims=True))
    density_ref[...] = jnp.log(found[0] * (1.0 / total_heads))
    spread_ref[...] = found[1] / found[0]


def per_device(heads, new_heads, vectors, near_ids):
    head_dev, width = heads.shape
    new_count = new_heads.shape[0]
    near = near_ids.shape[1]
    groups = lax.axis_size("group")
    members = lax.axis_size("member")
    most = 2 * near // members
    slots = -(-most // PACK) * PACK

    partner_ids = from_partner(near_ids, "member", 1)
    others = [from_partner(new_heads, "group", mask) for mask in range(1, groups)]
    ids = call(
        stage_kernel,
        jax.ShapeDtypeStruct(near_ids.shape, near_ids.dtype),
        (in_hbm(near_ids),),
        (0, 0),
        scratch=[pltpu.SemaphoreType.DMA],
        spaces=[HBM],
    )
    ids = jnp.concatenate([ids, partner_ids], axis=0)
    kept, head_sq, new_heads = call(
        early_kernel,
        (
            jax.ShapeDtypeStruct(heads.shape, heads.dtype),
            jax.ShapeDtypeStruct((1, head_dev), jnp.float32),
            jax.ShapeDtypeStruct(new_heads.shape, new_heads.dtype),
        ),
        (in_hbm(heads), in_hbm(new_heads), ids),
        (0, 0),
        scratch=[pltpu.SemaphoreType.DMA((5,))],
        spaces=[HBM, HBM, pl.ANY],
    )
    lines = 2 * groups * new_count // LANES
    chunks = width // LANES
    extra = -(-PARTS * lines // PACK) * PACK
    sums, kept_ids = call(
        functools.partial(crowd_kernel, groups),
        (
            jax.ShapeDtypeStruct((-(-lines // TILE) * TILE, LANES), jnp.float32),
            jax.ShapeDtypeStruct(ids.shape, ids.dtype),
        ),
        (ids, kept, head_sq, new_heads, *others),
        (0, 0),
    )
    mask = 2
    while mask < members // 2:
        kept_ids = jnp.concatenate([kept_ids, from_partner(ids, "member", mask)], axis=0)
        ids = kept_ids
        mask *= 2
    far_ids = from_partner(ids, "member", mask)
    mask = 1
    while mask < groups // 2:
        sums = sums + from_partner(sums, "group", mask)
        mask *= 2
    back, vec_sq = call(
        functools.partial(prepare_kernel, members, slots, head_dev),
        (
            jax.ShapeDtypeStruct((near, members * slots), jnp.bfloat16),
            jax.ShapeDtypeStruct((1, vectors.shape[1]), jnp.float32),
        ),
        (near_ids, vectors, sums),
        (0, 0),
        spaces=[VMEM, VMEM, pl.ANY],
    )
    rows = call(
        functools.partial(gather_kernel, members, slots),
        jax.ShapeDtypeStruct((members * slots, width), jnp.bfloat16),
        (ids, far_ids, kept, back),
        (2 * members * slots * head_dev * width, heads.size * 2),
        scratch=[pltpu.VMEM((members, near), jnp.int32)],
        spaces=[VMEM, VMEM, VMEM, pl.ANY],
    )
    message = call(
        functools.partial(pack_kernel, members, slots, lines),
        jax.ShapeDtypeStruct((members, chunks * slots + extra, LANES), jnp.bfloat16),
        (rows, sums, from_partner(sums, "group", mask)),
        (0, members * slots * width * 4),
    )
    message = lax.all_to_all(
        message, "member", 0, 0, tiled=True, axis_index_groups=[middle_first(members)]
    )

    density, spread, reassign = call(
        functools.partial(
            tail_kernel, groups, slots, float(head_dev * groups * members)
        ),
        (
            jax.ShapeDtypeStruct((1, new_count), jnp.float32),
            jax.ShapeDtypeStruct((1, new_count), jnp.float32),
            jax.ShapeDtypeStruct((1, near, vectors.shape[1]), jnp.float32),
        ),
        (back, vec_sq, message, vectors),
        (4 * near * vectors.shape[1] * width, vectors.size * 4),
    )
    return (density[0], spread[0], reassign)


def solution(mesh):
    placed = (
        P(("group", "member"), None),
        P("group", None),
        P(("group", "member"), None, None),
        P(("group", "member"), None),
    )
    return jax.shard_map(
        per_device,
        mesh=mesh,
        in_specs=placed,
        out_specs=(P("group"), P("group"), P(("group", "member"), None, None)),
        check_vma=False,
    )
```

```python
import functools

import jax
import jax.numpy as jnp
from jax import lax
from jax.experimental import pallas as pl
from jax.experimental.pallas import tpu as pltpu
from jax.sharding import PartitionSpec as P

VMEM = pltpu.MemorySpace.VMEM
HBM = pltpu.MemorySpace.HBM
LANES = 128
PACK = 16
TILE = 8
PARTS = 3
LIMIT = 24 * 2**20


def from_partner(value, axis, mask):
    count = lax.axis_size(axis)
    return lax.ppermute(value, axis, [(source, source ^ mask) for source in range(count)])


def middle_first(members):
    return [members // 2] + [member for member in range(members) if member != members // 2]


def first_middle(member, members):
    middle = members // 2
    return jnp.where(member == middle, 0, jnp.where(member < middle, member + 1, member))


def in_hbm(value):
    return pltpu.with_memory_space_constraint(value, HBM)


def call(body, shapes, operands, cost, scratch=(), spaces=None):
    return pl.pallas_call(
        body,
        out_shape=shapes,
        in_specs=[pl.BlockSpec(memory_space=space) for space in spaces or [VMEM] * len(operands)],
        out_specs=jax.tree.map(lambda unused: pl.BlockSpec(memory_space=VMEM), shapes),
        scratch_shapes=scratch,
        compiler_params=pltpu.CompilerParams(vmem_limit_bytes=LIMIT),
        cost_estimate=pl.CostEstimate(flops=cost[0], bytes_accessed=cost[1], transcendentals=0),
    )(*operands)


def iota(shape, dim):
    return lax.broadcasted_iota(jnp.int32, shape, dim)


def stage_kernel(ids_ref, kept_ref, sem):
    copy = pltpu.make_async_copy(ids_ref, kept_ref, sem)
    copy.start()
    copy.wait()


def early_kernel(heads_ref, new_ref, unused, kept_ref, head_sq_ref, kept_new_ref, sems):
    head_dev, width = heads_ref.shape
    tiles = 4
    tile = head_dev // tiles
    parts = [pl.ds(i * tile, tile) for i in range(tiles)]
    copies = [
        pltpu.make_async_copy(heads_ref.at[part], kept_ref.at[part], sems.at[i])
        for i, part in enumerate(parts)
    ]
    copies.append(pltpu.make_async_copy(new_ref, kept_new_ref, sems.at[tiles]))
    for copy in copies:
        copy.start()
    for i in range(tiles):
        copies[i].wait()
        for first in range(i * tile, (i + 1) * tile, LANES):
            block = jnp.square(kept_ref[first:first + LANES, :].astype(jnp.float32))
            folded = block[:, :LANES]
            for column in range(LANES, width, LANES):
                folded = folded + block[:, column:column + LANES]
            head_sq_ref[:, first:first + LANES] = jnp.sum(folded.T, axis=0, keepdims=True)
    for copy in copies[tiles:]:
        copy.wait()


def listed_rows(ids, me, slots, heads_ref):
    members, near = ids.shape
    head_dev = heads_ref.shape[0]
    local = ids - me * head_dev
    owned = (local >= 0) & (local < head_dev)
    earlier = (iota((near, near), 0) < iota((near, near), 1)).astype(jnp.bfloat16)
    rank = jnp.dot(owned.astype(jnp.bfloat16), earlier, preferred_element_type=jnp.float32)
    rank = jnp.where(owned, rank.astype(jnp.int32), -1)
    shape = (members, slots, near)
    pick = jnp.broadcast_to(rank[:, None, :], shape) == iota(shape, 1)
    wanted = jnp.sum(
        jnp.where(pick, jnp.broadcast_to(local[:, None, :] + 1, shape), 0), axis=2, keepdims=True
    ).reshape(members * slots, 1)
    onehot = (wanted == iota((members * slots, head_dev), 1) + 1).astype(jnp.bfloat16)
    return jnp.dot(
        onehot, heads_ref[...], preferred_element_type=jnp.float32
    ).astype(jnp.bfloat16)


def crowding(queries, heads_ref, head_sq_ref):
    head_dev, width = heads_ref.shape
    query_sq = jnp.sum(jnp.square(queries.astype(jnp.float32)), axis=1, keepdims=True)
    total_w = jnp.zeros((queries.shape[0], 1), jnp.float32)
    total_we = jnp.zeros((queries.shape[0], 1), jnp.float32)
    tile = 512
    for start in range(0, head_dev, tile):
        dots = lax.dot_general(
            queries, heads_ref[start:start + tile, :], (((1,), (1,)), ((), ())),
            preferred_element_type=jnp.float32,
        )
        head_sq = head_sq_ref[:, start:start + tile]
        excess = (query_sq + head_sq - 2.0 * dots) * (1.0 / width)
        inverse = 1.0 / (1.0 + excess)
        weight = inverse * inverse
        total_w = total_w + jnp.sum(weight, axis=1, keepdims=True)
        total_we = total_we + jnp.sum(weight * excess, axis=1, keepdims=True)
    return total_w, total_we


def crowd_kernel(groups, ids_ref, heads_ref, head_sq_ref, *refs):
    query_refs, (sums_ref, kept_ids_ref) = refs[:-2], refs[-2:]
    kept_ids_ref[...] = ids_ref[...]
    here = lax.axis_index("group")
    queries = jnp.concatenate([ref[...] for ref in query_refs], axis=0)
    new_count = queries.shape[0] // groups
    totals = crowding(queries, heads_ref, head_sq_ref)
    lane = iota((new_count, LANES), 1)
    row = iota((new_count, LANES), 0)
    line = iota(sums_ref.shape, 0)
    sums = jnp.zeros(sums_ref.shape, jnp.float32)
    for mask in range(groups):
        part = slice(mask * new_count, (mask + 1) * new_count)
        for kind in range(2):
            place = (kind * groups + (here ^ mask)) * new_count
            spread_out = jnp.where(lane == row + place % LANES, totals[kind][part], 0.0)
            spread_out = jnp.sum(spread_out, axis=0, keepdims=True)
            sums = sums + jnp.where(line == place // LANES, spread_out, 0.0)
    sums_ref[...] = sums


def gather_kernel(members, slots, near_ref, far_ref, heads_ref, unused, rows_ref, ids_ref):
    me = lax.axis_index("member")
    half = members // 2
    ids_ref[:half, :] = near_ref[...]
    ids_ref[half:, :] = far_ref[...]
    ids = jnp.concatenate([ids_ref[pl.ds(me ^ member, 1), :] for member in middle_first(members)], axis=0)
    rows_ref[...] = listed_rows(ids, me, slots, heads_ref)


def pack_kernel(members, slots, lines, rows_ref, mine_ref, other_ref, out_ref):
    chunks = rows_ref.shape[1] // LANES
    sums = (mine_ref[...] + other_ref[...])[:lines]
    coded = []
    for unused in range(PARTS):
        coded.append(sums.astype(jnp.bfloat16).astype(jnp.float32))
        sums = sums - coded[-1]
    missing = out_ref.shape[1] - chunks * slots - PARTS * lines
    if missing:
        coded.append(jnp.zeros((missing, LANES), jnp.float32))
    tail = jnp.concatenate(coded, axis=0).astype(jnp.bfloat16)
    for member in range(members):
        part = slice(member * slots, (member + 1) * slots)
        pieces = [rows_ref[part, chunk * LANES:(chunk + 1) * LANES] for chunk in range(chunks)]
        out_ref[member] = jnp.concatenate([*pieces, tail], axis=0)


def prepare_kernel(members, slots, head_dev, ids_ref, vectors_ref, unused, back_ref, vec_sq_ref):
    near = ids_ref.shape[1]
    block = vectors_ref.shape[1]
    square = (near, near)
    owner_row = jnp.broadcast_to(lax.div(ids_ref[...], head_dev), square)
    eye = iota(square, 0) == iota(square, 1)
    owner = jnp.sum(jnp.where(eye, owner_row, 0), axis=1, keepdims=True)
    before = (owner_row == owner) & (iota(square, 1) < iota(square, 0))
    place = jnp.sum(before.astype(jnp.int32), axis=1, keepdims=True)
    source = first_middle(owner, members) * slots + place
    back_ref[...] = (source == iota(back_ref.shape, 1)).astype(jnp.bfloat16)
    vec_sq = jnp.sum(jnp.square(vectors_ref[0].astype(jnp.float32)), axis=1, keepdims=True)
    diagonal = iota((block, block), 0) == iota((block, block), 1)
    vec_sq_ref[...] = jnp.sum(jnp.where(diagonal, vec_sq, 0.0), axis=0, keepdims=True)


def distances(slots, back_ref, vec_sq_ref, listed, vectors_ref, out_ref):
    members = listed.shape[0]
    width = vectors_ref.shape[2]
    rows = []
    for chunk in range(width // LANES):
        part = listed[:, chunk * slots:(chunk + 1) * slots, :].reshape(members * slots, LANES)
        rows.append(jnp.dot(back_ref[...], part, preferred_element_type=jnp.float32))
    rows = jnp.concatenate(rows, axis=1)
    row_sq = jnp.sum(jnp.square(rows), axis=1, keepdims=True)
    dots = lax.dot_general(
        rows.astype(jnp.bfloat16), vectors_ref[0], (((1,), (1,)), ((), ())),
        preferred_element_type=jnp.float32,
    )
    out_ref[0] = (row_sq + vec_sq_ref[...] - 2.0 * dots) * (1.0 / width)


def tail_kernel(
    groups, slots, total_heads, back_ref, vec_sq_ref, listed_ref, vectors_ref,
    density_ref, spread_ref, out_ref,
):
    listed = listed_ref[...]
    distances(slots, back_ref, vec_sq_ref, listed, vectors_ref, out_ref)
    here = lax.axis_index("group")
    members = listed_ref.shape[0]
    new_count = density_ref.shape[1]
    lines = 2 * groups * new_count // LANES
    first = vectors_ref.shape[2] // LANES * slots
    coded = jnp.sum(listed[:, first:, :].astype(jnp.float32), axis=0)
    total = sum(coded[part * lines:(part + 1) * lines] for part in range(PARTS))
    shape = (new_count, LANES)
    eye = iota((new_count, new_count), 0) == iota((new_count, new_count), 1)
    found = []
    for kind in range(2):
        place = (kind * groups + here) * new_count
        line = jnp.sum(
            jnp.where(iota((lines, LANES), 0) == place // LANES, total, 0.0), axis=0, keepdims=True
        )
        column = jnp.sum(
            jnp.where(iota(shape, 1) == iota(shape, 0) + place % LANES, line, 0.0),
            axis=1, keepdims=True,
        )
        found.append(jnp.sum(jnp.where(eye, column, 0.0), axis=0, keepdims=True))
    density_ref[...] = jnp.log(found[0] * (1.0 / total_heads))
    spread_ref[...] = found[1] / found[0]


def per_device(heads, new_heads, vectors, near_ids):
    head_dev, width = heads.shape
    new_count = new_heads.shape[0]
    near = near_ids.shape[1]
    groups = lax.axis_size("group")
    members = lax.axis_size("member")
    most = 2 * near // members
    slots = -(-most // PACK) * PACK

    partner_ids = from_partner(near_ids, "member", 1)
    others = [from_partner(new_heads, "group", mask) for mask in range(1, groups)]
    ids = call(
        stage_kernel,
        jax.ShapeDtypeStruct(near_ids.shape, near_ids.dtype),
        (in_hbm(near_ids),),
        (0, 0),
        scratch=[pltpu.SemaphoreType.DMA],
        spaces=[HBM],
    )
    ids = jnp.concatenate([ids, partner_ids], axis=0)
    kept, head_sq, new_heads = call(
        early_kernel,
        (
            jax.ShapeDtypeStruct(heads.shape, heads.dtype),
            jax.ShapeDtypeStruct((1, head_dev), jnp.float32),
            jax.ShapeDtypeStruct(new_heads.shape, new_heads.dtype),
        ),
        (in_hbm(heads), in_hbm(new_heads), ids),
        (0, 0),
        scratch=[pltpu.SemaphoreType.DMA((5,))],
        spaces=[HBM, HBM, pl.ANY],
    )
    lines = 2 * groups * new_count // LANES
    chunks = width // LANES
    extra = -(-PARTS * lines // TILE) * TILE
    sums, kept_ids = call(
        functools.partial(crowd_kernel, groups),
        (
            jax.ShapeDtypeStruct((-(-lines // TILE) * TILE, LANES), jnp.float32),
            jax.ShapeDtypeStruct(ids.shape, ids.dtype),
        ),
        (ids, kept, head_sq, new_heads, *others),
        (0, 0),
    )
    mask = 2
    while mask < members // 2:
        kept_ids = jnp.concatenate([kept_ids, from_partner(ids, "member", mask)], axis=0)
        ids = kept_ids
        mask *= 2
    far_ids = from_partner(ids, "member", mask)
    mask = 1
    while mask < groups // 2:
        sums = sums + from_partner(sums, "group", mask)
        mask *= 2
    back, vec_sq = call(
        functools.partial(prepare_kernel, members, slots, head_dev),
        (
            jax.ShapeDtypeStruct((near, members * slots), jnp.bfloat16),
            jax.ShapeDtypeStruct((1, vectors.shape[1]), jnp.float32),
        ),
        (near_ids, vectors, sums),
        (0, 0),
        spaces=[VMEM, VMEM, pl.ANY],
    )
    rows = call(
        functools.partial(gather_kernel, members, slots),
        jax.ShapeDtypeStruct((members * slots, width), jnp.bfloat16),
        (ids, far_ids, kept, back),
        (2 * members * slots * head_dev * width, heads.size * 2),
        scratch=[pltpu.VMEM((members, near), jnp.int32)],
        spaces=[VMEM, VMEM, VMEM, pl.ANY],
    )
    message = call(
        functools.partial(pack_kernel, members, slots, lines),
        jax.ShapeDtypeStruct((members, chunks * slots + extra, LANES), jnp.bfloat16),
        (rows, sums, from_partner(sums, "group", mask)),
        (0, members * slots * width * 4),
    )
    message = lax.all_to_all(
        message, "member", 0, 0, tiled=True, axis_index_groups=[middle_first(members)]
    )

    density, spread, reassign = call(
        functools.partial(
            tail_kernel, groups, slots, float(head_dev * groups * members)
        ),
        (
            jax.ShapeDtypeStruct((1, new_count), jnp.float32),
            jax.ShapeDtypeStruct((1, new_count), jnp.float32),
            jax.ShapeDtypeStruct((1, near, vectors.shape[1]), jnp.float32),
        ),
        (back, vec_sq, message, vectors),
        (4 * near * vectors.shape[1] * width, vectors.size * 4),
    )
    return (density[0], spread[0], reassign)


def solution(mesh):
    placed = (
        P(("group", "member"), None),
        P("group", None),
        P(("group", "member"), None, None),
        P(("group", "member"), None),
    )
    return jax.shard_map(
        per_device,
        mesh=mesh,
        in_specs=placed,
        out_specs=(P("group"), P("group"), P(("group", "member"), None, None)),
        check_vma=False,
    )
```

```python
import functools

import jax
import jax.numpy as jnp
from jax import lax
from jax.experimental import pallas as pl
from jax.experimental.pallas import tpu as pltpu
from jax.sharding import PartitionSpec as P

VMEM = pltpu.MemorySpace.VMEM
HBM = pltpu.MemorySpace.HBM
LANES = 128
PACK = 16
TILE = 8
PARTS = 3
LIMIT = 24 * 2**20


def from_partner(value, axis, mask):
    count = lax.axis_size(axis)
    return lax.ppermute(value, axis, [(source, source ^ mask) for source in range(count)])


def by_turns(members):
    half = members // 2
    return [place // 2 + (half if place % 2 == 0 else 0) for place in range(members)]


def turn_of(member, members):
    half = members // 2
    return jnp.where(member < half, 2 * member + 1, 2 * (member - half))


def in_hbm(value):
    return pltpu.with_memory_space_constraint(value, HBM)


def call(body, shapes, operands, cost, scratch=(), spaces=None):
    return pl.pallas_call(
        body,
        out_shape=shapes,
        in_specs=[pl.BlockSpec(memory_space=space) for space in spaces or [VMEM] * len(operands)],
        out_specs=jax.tree.map(lambda unused: pl.BlockSpec(memory_space=VMEM), shapes),
        scratch_shapes=scratch,
        compiler_params=pltpu.CompilerParams(vmem_limit_bytes=LIMIT),
        cost_estimate=pl.CostEstimate(flops=cost[0], bytes_accessed=cost[1], transcendentals=0),
    )(*operands)


def iota(shape, dim):
    return lax.broadcasted_iota(jnp.int32, shape, dim)


def stage_kernel(ids_ref, kept_ref, sem):
    copy = pltpu.make_async_copy(ids_ref, kept_ref, sem)
    copy.start()
    copy.wait()


def early_kernel(heads_ref, new_ref, unused, kept_ref, head_sq_ref, kept_new_ref, sems):
    head_dev, width = heads_ref.shape
    tiles = 4
    tile = head_dev // tiles
    parts = [pl.ds(i * tile, tile) for i in range(tiles)]
    copies = [
        pltpu.make_async_copy(heads_ref.at[part], kept_ref.at[part], sems.at[i])
        for i, part in enumerate(parts)
    ]
    copies.append(pltpu.make_async_copy(new_ref, kept_new_ref, sems.at[tiles]))
    for copy in copies:
        copy.start()
    for i in range(tiles):
        copies[i].wait()
        for first in range(i * tile, (i + 1) * tile, LANES):
            block = jnp.square(kept_ref[first:first + LANES, :].astype(jnp.float32))
            folded = block[:, :LANES]
            for column in range(LANES, width, LANES):
                folded = folded + block[:, column:column + LANES]
            head_sq_ref[:, first:first + LANES] = jnp.sum(folded.T, axis=0, keepdims=True)
    for copy in copies[tiles:]:
        copy.wait()


def listed_rows(ids, me, slots, heads_ref):
    members, near = ids.shape
    head_dev = heads_ref.shape[0]
    local = ids - me * head_dev
    owned = (local >= 0) & (local < head_dev)
    earlier = (iota((near, near), 0) < iota((near, near), 1)).astype(jnp.bfloat16)
    rank = jnp.dot(owned.astype(jnp.bfloat16), earlier, preferred_element_type=jnp.float32)
    rank = jnp.where(owned, rank.astype(jnp.int32), -1)
    shape = (members, slots, near)
    pick = jnp.broadcast_to(rank[:, None, :], shape) == iota(shape, 1)
    wanted = jnp.sum(
        jnp.where(pick, jnp.broadcast_to(local[:, None, :] + 1, shape), 0), axis=2, keepdims=True
    ).reshape(members * slots, 1)
    onehot = (wanted == iota((members * slots, head_dev), 1) + 1).astype(jnp.bfloat16)
    return jnp.dot(
        onehot, heads_ref[...], preferred_element_type=jnp.float32
    ).astype(jnp.bfloat16)


def crowding(queries, heads_ref, head_sq_ref):
    head_dev, width = heads_ref.shape
    query_sq = jnp.sum(jnp.square(queries.astype(jnp.float32)), axis=1, keepdims=True)
    total_w = jnp.zeros((queries.shape[0], 1), jnp.float32)
    total_we = jnp.zeros((queries.shape[0], 1), jnp.float32)
    tile = 512
    for start in range(0, head_dev, tile):
        dots = lax.dot_general(
            queries, heads_ref[start:start + tile, :], (((1,), (1,)), ((), ())),
            preferred_element_type=jnp.float32,
        )
        head_sq = head_sq_ref[:, start:start + tile]
        excess = (query_sq + head_sq - 2.0 * dots) * (1.0 / width)
        inverse = 1.0 / (1.0 + excess)
        weight = inverse * inverse
        total_w = total_w + jnp.sum(weight, axis=1, keepdims=True)
        total_we = total_we + jnp.sum(weight * excess, axis=1, keepdims=True)
    return total_w, total_we


def crowd_kernel(groups, ids_ref, heads_ref, head_sq_ref, *refs):
    query_refs, (sums_ref, kept_ids_ref) = refs[:-2], refs[-2:]
    kept_ids_ref[...] = ids_ref[...]
    here = lax.axis_index("group")
    queries = jnp.concatenate([ref[...] for ref in query_refs], axis=0)
    new_count = queries.shape[0] // groups
    totals = crowding(queries, heads_ref, head_sq_ref)
    lane = iota((new_count, LANES), 1)
    row = iota((new_count, LANES), 0)
    line = iota(sums_ref.shape, 0)
    sums = jnp.zeros(sums_ref.shape, jnp.float32)
    for mask in range(groups):
        part = slice(mask * new_count, (mask + 1) * new_count)
        for kind in range(2):
            place = (kind * groups + (here ^ mask)) * new_count
            spread_out = jnp.where(lane == row + place % LANES, totals[kind][part], 0.0)
            spread_out = jnp.sum(spread_out, axis=0, keepdims=True)
            sums = sums + jnp.where(line == place // LANES, spread_out, 0.0)
    sums_ref[...] = sums


def gather_kernel(members, slots, near_ref, far_ref, heads_ref, unused, rows_ref, ids_ref):
    me = lax.axis_index("member")
    half = members // 2
    ids_ref[:half, :] = near_ref[...]
    ids_ref[half:, :] = far_ref[...]
    ids = jnp.concatenate([ids_ref[pl.ds(me ^ member, 1), :] for member in by_turns(members)], axis=0)
    rows_ref[...] = listed_rows(ids, me, slots, heads_ref)


def pack_kernel(members, slots, lines, rows_ref, mine_ref, other_ref, out_ref):
    chunks = rows_ref.shape[1] // LANES
    sums = (mine_ref[...] + other_ref[...])[:lines]
    coded = []
    for unused in range(PARTS):
        coded.append(sums.astype(jnp.bfloat16).astype(jnp.float32))
        sums = sums - coded[-1]
    missing = out_ref.shape[1] - chunks * slots - PARTS * lines
    if missing:
        coded.append(jnp.zeros((missing, LANES), jnp.float32))
    tail = jnp.concatenate(coded, axis=0).astype(jnp.bfloat16)
    for member in range(members):
        part = slice(member * slots, (member + 1) * slots)
        pieces = [rows_ref[part, chunk * LANES:(chunk + 1) * LANES] for chunk in range(chunks)]
        out_ref[member] = jnp.concatenate([*pieces, tail], axis=0)


def prepare_kernel(members, slots, head_dev, ids_ref, vectors_ref, unused, back_ref, vec_sq_ref):
    near = ids_ref.shape[1]
    block = vectors_ref.shape[1]
    square = (near, near)
    owner_row = jnp.broadcast_to(lax.div(ids_ref[...], head_dev), square)
    eye = iota(square, 0) == iota(square, 1)
    owner = jnp.sum(jnp.where(eye, owner_row, 0), axis=1, keepdims=True)
    before = (owner_row == owner) & (iota(square, 1) < iota(square, 0))
    place = jnp.sum(before.astype(jnp.int32), axis=1, keepdims=True)
    source = turn_of(owner, members) * slots + place
    back_ref[...] = (source == iota(back_ref.shape, 1)).astype(jnp.bfloat16)
    vec_sq = jnp.sum(jnp.square(vectors_ref[0].astype(jnp.float32)), axis=1, keepdims=True)
    diagonal = iota((block, block), 0) == iota((block, block), 1)
    vec_sq_ref[...] = jnp.sum(jnp.where(diagonal, vec_sq, 0.0), axis=0, keepdims=True)


def distances(slots, back_ref, vec_sq_ref, listed, vectors_ref, out_ref):
    members = listed.shape[0]
    width = vectors_ref.shape[2]
    rows = []
    for chunk in range(width // LANES):
        part = listed[:, chunk * slots:(chunk + 1) * slots, :].reshape(members * slots, LANES)
        rows.append(jnp.dot(back_ref[...], part, preferred_element_type=jnp.float32))
    rows = jnp.concatenate(rows, axis=1)
    row_sq = jnp.sum(jnp.square(rows), axis=1, keepdims=True)
    dots = lax.dot_general(
        rows.astype(jnp.bfloat16), vectors_ref[0], (((1,), (1,)), ((), ())),
        preferred_element_type=jnp.float32,
    )
    out_ref[0] = (row_sq + vec_sq_ref[...] - 2.0 * dots) * (1.0 / width)


def tail_kernel(
    groups, slots, total_heads, back_ref, vec_sq_ref, listed_ref, vectors_ref,
    density_ref, spread_ref, out_ref,
):
    listed = listed_ref[...]
    distances(slots, back_ref, vec_sq_ref, listed, vectors_ref, out_ref)
    here = lax.axis_index("group")
    members = listed_ref.shape[0]
    new_count = density_ref.shape[1]
    lines = 2 * groups * new_count // LANES
    first = vectors_ref.shape[2] // LANES * slots
    coded = jnp.sum(listed[:, first:, :].astype(jnp.float32), axis=0)
    total = sum(coded[part * lines:(part + 1) * lines] for part in range(PARTS))
    shape = (new_count, LANES)
    eye = iota((new_count, new_count), 0) == iota((new_count, new_count), 1)
    found = []
    for kind in range(2):
        place = (kind * groups + here) * new_count
        line = jnp.sum(
            jnp.where(iota((lines, LANES), 0) == place // LANES, total, 0.0), axis=0, keepdims=True
        )
        column = jnp.sum(
            jnp.where(iota(shape, 1) == iota(shape, 0) + place % LANES, line, 0.0),
            axis=1, keepdims=True,
        )
        found.append(jnp.sum(jnp.where(eye, column, 0.0), axis=0, keepdims=True))
    density_ref[...] = jnp.log(found[0] * (1.0 / total_heads))
    spread_ref[...] = found[1] / found[0]


def per_device(heads, new_heads, vectors, near_ids):
    head_dev, width = heads.shape
    new_count = new_heads.shape[0]
    near = near_ids.shape[1]
    groups = lax.axis_size("group")
    members = lax.axis_size("member")
    most = 2 * near // members
    slots = -(-most // PACK) * PACK

    partner_ids = from_partner(near_ids, "member", 1)
    others = [from_partner(new_heads, "group", mask) for mask in range(1, groups)]
    ids = call(
        stage_kernel,
        jax.ShapeDtypeStruct(near_ids.shape, near_ids.dtype),
        (in_hbm(near_ids),),
        (0, 0),
        scratch=[pltpu.SemaphoreType.DMA],
        spaces=[HBM],
    )
    ids = jnp.concatenate([ids, partner_ids], axis=0)
    kept, head_sq, new_heads = call(
        early_kernel,
        (
            jax.ShapeDtypeStruct(heads.shape, heads.dtype),
            jax.ShapeDtypeStruct((1, head_dev), jnp.float32),
            jax.ShapeDtypeStruct(new_heads.shape, new_heads.dtype),
        ),
        (in_hbm(heads), in_hbm(new_heads), ids),
        (0, 0),
        scratch=[pltpu.SemaphoreType.DMA((5,))],
        spaces=[HBM, HBM, pl.ANY],
    )
    lines = 2 * groups * new_count // LANES
    chunks = width // LANES
    extra = -(-PARTS * lines // TILE) * TILE
    sums, kept_ids = call(
        functools.partial(crowd_kernel, groups),
        (
            jax.ShapeDtypeStruct((-(-lines // TILE) * TILE, LANES), jnp.float32),
            jax.ShapeDtypeStruct(ids.shape, ids.dtype),
        ),
        (ids, kept, head_sq, new_heads, *others),
        (0, 0),
    )
    mask = 2
    while mask < members // 2:
        kept_ids = jnp.concatenate([kept_ids, from_partner(ids, "member", mask)], axis=0)
        ids = kept_ids
        mask *= 2
    far_ids = from_partner(ids, "member", mask)
    mask = 1
    while mask < groups // 2:
        sums = sums + from_partner(sums, "group", mask)
        mask *= 2
    back, vec_sq = call(
        functools.partial(prepare_kernel, members, slots, head_dev),
        (
            jax.ShapeDtypeStruct((near, members * slots), jnp.bfloat16),
            jax.ShapeDtypeStruct((1, vectors.shape[1]), jnp.float32),
        ),
        (near_ids, vectors, sums),
        (0, 0),
        spaces=[VMEM, VMEM, pl.ANY],
    )
    rows = call(
        functools.partial(gather_kernel, members, slots),
        jax.ShapeDtypeStruct((members * slots, width), jnp.bfloat16),
        (ids, far_ids, kept, back),
        (2 * members * slots * head_dev * width, heads.size * 2),
        scratch=[pltpu.VMEM((members, near), jnp.int32)],
        spaces=[VMEM, VMEM, VMEM, pl.ANY],
    )
    message = call(
        functools.partial(pack_kernel, members, slots, lines),
        jax.ShapeDtypeStruct((members, chunks * slots + extra, LANES), jnp.bfloat16),
        (rows, sums, from_partner(sums, "group", mask)),
        (0, members * slots * width * 4),
    )
    message = lax.all_to_all(
        message, "member", 0, 0, tiled=True, axis_index_groups=[by_turns(members)]
    )

    density, spread, reassign = call(
        functools.partial(
            tail_kernel, groups, slots, float(head_dev * groups * members)
        ),
        (
            jax.ShapeDtypeStruct((1, new_count), jnp.float32),
            jax.ShapeDtypeStruct((1, new_count), jnp.float32),
            jax.ShapeDtypeStruct((1, near, vectors.shape[1]), jnp.float32),
        ),
        (back, vec_sq, message, vectors),
        (4 * near * vectors.shape[1] * width, vectors.size * 4),
    )
    return (density[0], spread[0], reassign)


def solution(mesh):
    placed = (
        P(("group", "member"), None),
        P("group", None),
        P(("group", "member"), None, None),
        P(("group", "member"), None),
    )
    return jax.shard_map(
        per_device,
        mesh=mesh,
        in_specs=placed,
        out_specs=(P("group"), P("group"), P(("group", "member"), None, None)),
        check_vma=False,
    )
```

```python
import functools

import jax
import jax.numpy as jnp
from jax import lax
from jax.experimental import pallas as pl
from jax.experimental.pallas import tpu as pltpu
from jax.sharding import PartitionSpec as P

VMEM = pltpu.MemorySpace.VMEM
HBM = pltpu.MemorySpace.HBM
LANES = 128
PACK = 16
TILE = 8
PARTS = 3
LIMIT = 24 * 2**20


def from_partner(value, axis, mask):
    count = lax.axis_size(axis)
    return lax.ppermute(value, axis, [(source, source ^ mask) for source in range(count)])


def by_turns(members):
    half = members // 2
    order = [place // 2 + (half if place % 2 == 0 else 0) for place in range(members)]
    return [order[2], order[1], order[0], *order[3:]]


def turn_of(member, members):
    half = members // 2
    high = member - half
    return jnp.where(member < half, 2 * member + 1, 2 * jnp.where(high < 2, 1 - high, high))


def in_hbm(value):
    return pltpu.with_memory_space_constraint(value, HBM)


def call(body, shapes, operands, cost, scratch=(), spaces=None):
    return pl.pallas_call(
        body,
        out_shape=shapes,
        in_specs=[pl.BlockSpec(memory_space=space) for space in spaces or [VMEM] * len(operands)],
        out_specs=jax.tree.map(lambda unused: pl.BlockSpec(memory_space=VMEM), shapes),
        scratch_shapes=scratch,
        compiler_params=pltpu.CompilerParams(vmem_limit_bytes=LIMIT),
        cost_estimate=pl.CostEstimate(flops=cost[0], bytes_accessed=cost[1], transcendentals=0),
    )(*operands)


def iota(shape, dim):
    return lax.broadcasted_iota(jnp.int32, shape, dim)


def stage_kernel(ids_ref, kept_ref, sem):
    copy = pltpu.make_async_copy(ids_ref, kept_ref, sem)
    copy.start()
    copy.wait()


def early_kernel(heads_ref, new_ref, unused, kept_ref, head_sq_ref, kept_new_ref, sems):
    head_dev, width = heads_ref.shape
    tiles = 4
    tile = head_dev // tiles
    parts = [pl.ds(i * tile, tile) for i in range(tiles)]
    copies = [
        pltpu.make_async_copy(heads_ref.at[part], kept_ref.at[part], sems.at[i])
        for i, part in enumerate(parts)
    ]
    copies.append(pltpu.make_async_copy(new_ref, kept_new_ref, sems.at[tiles]))
    for copy in copies:
        copy.start()
    for i in range(tiles):
        copies[i].wait()
        for first in range(i * tile, (i + 1) * tile, LANES):
            block = jnp.square(kept_ref[first:first + LANES, :].astype(jnp.float32))
            folded = block[:, :LANES]
            for column in range(LANES, width, LANES):
                folded = folded + block[:, column:column + LANES]
            head_sq_ref[:, first:first + LANES] = jnp.sum(folded.T, axis=0, keepdims=True)
    for copy in copies[tiles:]:
        copy.wait()


def listed_rows(ids, me, slots, heads_ref):
    members, near = ids.shape
    head_dev = heads_ref.shape[0]
    local = ids - me * head_dev
    owned = (local >= 0) & (local < head_dev)
    earlier = (iota((near, near), 0) < iota((near, near), 1)).astype(jnp.bfloat16)
    rank = jnp.dot(owned.astype(jnp.bfloat16), earlier, preferred_element_type=jnp.float32)
    rank = jnp.where(owned, rank.astype(jnp.int32), -1)
    shape = (members, slots, near)
    pick = jnp.broadcast_to(rank[:, None, :], shape) == iota(shape, 1)
    wanted = jnp.sum(
        jnp.where(pick, jnp.broadcast_to(local[:, None, :] + 1, shape), 0), axis=2, keepdims=True
    ).reshape(members * slots, 1)
    onehot = (wanted == iota((members * slots, head_dev), 1) + 1).astype(jnp.bfloat16)
    return jnp.dot(
        onehot, heads_ref[...], preferred_element_type=jnp.float32
    ).astype(jnp.bfloat16)


def crowding(queries, heads_ref, head_sq_ref):
    head_dev, width = heads_ref.shape
    query_sq = jnp.sum(jnp.square(queries.astype(jnp.float32)), axis=1, keepdims=True)
    total_w = jnp.zeros((queries.shape[0], 1), jnp.float32)
    total_we = jnp.zeros((queries.shape[0], 1), jnp.float32)
    tile = 512
    for start in range(0, head_dev, tile):
        dots = lax.dot_general(
            queries, heads_ref[start:start + tile, :], (((1,), (1,)), ((), ())),
            preferred_element_type=jnp.float32,
        )
        head_sq = head_sq_ref[:, start:start + tile]
        excess = (query_sq + head_sq - 2.0 * dots) * (1.0 / width)
        inverse = 1.0 / (1.0 + excess)
        weight = inverse * inverse
        total_w = total_w + jnp.sum(weight, axis=1, keepdims=True)
        total_we = total_we + jnp.sum(weight * excess, axis=1, keepdims=True)
    return total_w, total_we


def crowd_kernel(groups, ids_ref, heads_ref, head_sq_ref, *refs):
    query_refs, (sums_ref, kept_ids_ref) = refs[:-2], refs[-2:]
    kept_ids_ref[...] = ids_ref[...]
    here = lax.axis_index("group")
    queries = jnp.concatenate([ref[...] for ref in query_refs], axis=0)
    new_count = queries.shape[0] // groups
    totals = crowding(queries, heads_ref, head_sq_ref)
    lane = iota((new_count, LANES), 1)
    row = iota((new_count, LANES), 0)
    line = iota(sums_ref.shape, 0)
    sums = jnp.zeros(sums_ref.shape, jnp.float32)
    for mask in range(groups):
        part = slice(mask * new_count, (mask + 1) * new_count)
        for kind in range(2):
            place = (kind * groups + (here ^ mask)) * new_count
            spread_out = jnp.where(lane == row + place % LANES, totals[kind][part], 0.0)
            spread_out = jnp.sum(spread_out, axis=0, keepdims=True)
            sums = sums + jnp.where(line == place // LANES, spread_out, 0.0)
    sums_ref[...] = sums


def gather_kernel(members, slots, near_ref, far_ref, heads_ref, unused, rows_ref, ids_ref):
    me = lax.axis_index("member")
    half = members // 2
    ids_ref[:half, :] = near_ref[...]
    ids_ref[half:, :] = far_ref[...]
    ids = jnp.concatenate([ids_ref[pl.ds(me ^ member, 1), :] for member in by_turns(members)], axis=0)
    rows_ref[...] = listed_rows(ids, me, slots, heads_ref)


def pack_kernel(members, slots, lines, rows_ref, mine_ref, other_ref, out_ref):
    chunks = rows_ref.shape[1] // LANES
    sums = (mine_ref[...] + other_ref[...])[:lines]
    coded = []
    for unused in range(PARTS):
        coded.append(sums.astype(jnp.bfloat16).astype(jnp.float32))
        sums = sums - coded[-1]
    missing = out_ref.shape[1] - chunks * slots - PARTS * lines
    if missing:
        coded.append(jnp.zeros((missing, LANES), jnp.float32))
    tail = jnp.concatenate(coded, axis=0).astype(jnp.bfloat16)
    for member in range(members):
        part = slice(member * slots, (member + 1) * slots)
        pieces = [rows_ref[part, chunk * LANES:(chunk + 1) * LANES] for chunk in range(chunks)]
        out_ref[member] = jnp.concatenate([*pieces, tail], axis=0)


def prepare_kernel(members, slots, head_dev, ids_ref, vectors_ref, unused, back_ref, vec_sq_ref):
    near = ids_ref.shape[1]
    block = vectors_ref.shape[1]
    square = (near, near)
    owner_row = jnp.broadcast_to(lax.div(ids_ref[...], head_dev), square)
    eye = iota(square, 0) == iota(square, 1)
    owner = jnp.sum(jnp.where(eye, owner_row, 0), axis=1, keepdims=True)
    before = (owner_row == owner) & (iota(square, 1) < iota(square, 0))
    place = jnp.sum(before.astype(jnp.int32), axis=1, keepdims=True)
    source = turn_of(owner, members) * slots + place
    back_ref[...] = (source == iota(back_ref.shape, 1)).astype(jnp.bfloat16)
    vec_sq = jnp.sum(jnp.square(vectors_ref[0].astype(jnp.float32)), axis=1, keepdims=True)
    diagonal = iota((block, block), 0) == iota((block, block), 1)
    vec_sq_ref[...] = jnp.sum(jnp.where(diagonal, vec_sq, 0.0), axis=0, keepdims=True)


def distances(slots, back_ref, vec_sq_ref, listed, vectors_ref, out_ref):
    members = listed.shape[0]
    width = vectors_ref.shape[2]
    rows = []
    for chunk in range(width // LANES):
        part = listed[:, chunk * slots:(chunk + 1) * slots, :].reshape(members * slots, LANES)
        rows.append(jnp.dot(back_ref[...], part, preferred_element_type=jnp.float32))
    rows = jnp.concatenate(rows, axis=1)
    row_sq = jnp.sum(jnp.square(rows), axis=1, keepdims=True)
    dots = lax.dot_general(
        rows.astype(jnp.bfloat16), vectors_ref[0], (((1,), (1,)), ((), ())),
        preferred_element_type=jnp.float32,
    )
    out_ref[0] = (row_sq + vec_sq_ref[...] - 2.0 * dots) * (1.0 / width)


def tail_kernel(
    groups, slots, total_heads, back_ref, vec_sq_ref, listed_ref, vectors_ref,
    density_ref, spread_ref, out_ref,
):
    listed = listed_ref[...]
    distances(slots, back_ref, vec_sq_ref, listed, vectors_ref, out_ref)
    here = lax.axis_index("group")
    members = listed_ref.shape[0]
    new_count = density_ref.shape[1]
    lines = 2 * groups * new_count // LANES
    first = vectors_ref.shape[2] // LANES * slots
    coded = jnp.sum(listed[:, first:, :].astype(jnp.float32), axis=0)
    total = sum(coded[part * lines:(part + 1) * lines] for part in range(PARTS))
    shape = (new_count, LANES)
    eye = iota((new_count, new_count), 0) == iota((new_count, new_count), 1)
    found = []
    for kind in range(2):
        place = (kind * groups + here) * new_count
        line = jnp.sum(
            jnp.where(iota((lines, LANES), 0) == place // LANES, total, 0.0), axis=0, keepdims=True
        )
        column = jnp.sum(
            jnp.where(iota(shape, 1) == iota(shape, 0) + place % LANES, line, 0.0),
            axis=1, keepdims=True,
        )
        found.append(jnp.sum(jnp.where(eye, column, 0.0), axis=0, keepdims=True))
    density_ref[...] = jnp.log(found[0] * (1.0 / total_heads))
    spread_ref[...] = found[1] / found[0]


def per_device(heads, new_heads, vectors, near_ids):
    head_dev, width = heads.shape
    new_count = new_heads.shape[0]
    near = near_ids.shape[1]
    groups = lax.axis_size("group")
    members = lax.axis_size("member")
    most = 2 * near // members
    slots = -(-most // PACK) * PACK

    partner_ids = from_partner(near_ids, "member", 1)
    others = [from_partner(new_heads, "group", mask) for mask in range(1, groups)]
    ids = call(
        stage_kernel,
        jax.ShapeDtypeStruct(near_ids.shape, near_ids.dtype),
        (in_hbm(near_ids),),
        (0, 0),
        scratch=[pltpu.SemaphoreType.DMA],
        spaces=[HBM],
    )
    ids = jnp.concatenate([ids, partner_ids], axis=0)
    kept, head_sq, new_heads = call(
        early_kernel,
        (
            jax.ShapeDtypeStruct(heads.shape, heads.dtype),
            jax.ShapeDtypeStruct((1, head_dev), jnp.float32),
            jax.ShapeDtypeStruct(new_heads.shape, new_heads.dtype),
        ),
        (in_hbm(heads), in_hbm(new_heads), ids),
        (0, 0),
        scratch=[pltpu.SemaphoreType.DMA((5,))],
        spaces=[HBM, HBM, pl.ANY],
    )
    lines = 2 * groups * new_count // LANES
    chunks = width // LANES
    extra = -(-PARTS * lines // TILE) * TILE
    sums, kept_ids = call(
        functools.partial(crowd_kernel, groups),
        (
            jax.ShapeDtypeStruct((-(-lines // TILE) * TILE, LANES), jnp.float32),
            jax.ShapeDtypeStruct(ids.shape, ids.dtype),
        ),
        (ids, kept, head_sq, new_heads, *others),
        (0, 0),
    )
    mask = 2
    while mask < members // 2:
        kept_ids = jnp.concatenate([kept_ids, from_partner(ids, "member", mask)], axis=0)
        ids = kept_ids
        mask *= 2
    far_ids = from_partner(ids, "member", mask)
    mask = 1
    while mask < groups // 2:
        sums = sums + from_partner(sums, "group", mask)
        mask *= 2
    back, vec_sq = call(
        functools.partial(prepare_kernel, members, slots, head_dev),
        (
            jax.ShapeDtypeStruct((near, members * slots), jnp.bfloat16),
            jax.ShapeDtypeStruct((1, vectors.shape[1]), jnp.float32),
        ),
        (near_ids, vectors, sums),
        (0, 0),
        spaces=[VMEM, VMEM, pl.ANY],
    )
    rows = call(
        functools.partial(gather_kernel, members, slots),
        jax.ShapeDtypeStruct((members * slots, width), jnp.bfloat16),
        (ids, far_ids, kept, back),
        (2 * members * slots * head_dev * width, heads.size * 2),
        scratch=[pltpu.VMEM((members, near), jnp.int32)],
        spaces=[VMEM, VMEM, VMEM, pl.ANY],
    )
    message = call(
        functools.partial(pack_kernel, members, slots, lines),
        jax.ShapeDtypeStruct((members, chunks * slots + extra, LANES), jnp.bfloat16),
        (rows, sums, from_partner(sums, "group", mask)),
        (0, members * slots * width * 4),
    )
    message = lax.all_to_all(
        message, "member", 0, 0, tiled=True, axis_index_groups=[by_turns(members)]
    )

    density, spread, reassign = call(
        functools.partial(
            tail_kernel, groups, slots, float(head_dev * groups * members)
        ),
        (
            jax.ShapeDtypeStruct((1, new_count), jnp.float32),
            jax.ShapeDtypeStruct((1, new_count), jnp.float32),
            jax.ShapeDtypeStruct((1, near, vectors.shape[1]), jnp.float32),
        ),
        (back, vec_sq, message, vectors),
        (4 * near * vectors.shape[1] * width, vectors.size * 4),
    )
    return (density[0], spread[0], reassign)


def solution(mesh):
    placed = (
        P(("group", "member"), None),
        P("group", None),
        P(("group", "member"), None, None),
        P(("group", "member"), None),
    )
    return jax.shard_map(
        per_device,
        mesh=mesh,
        in_specs=placed,
        out_specs=(P("group"), P("group"), P(("group", "member"), None, None)),
        check_vma=False,
    )
```

```python
import functools

import jax
import jax.numpy as jnp
from jax import lax
from jax.experimental import pallas as pl
from jax.experimental.pallas import tpu as pltpu
from jax.sharding import PartitionSpec as P

VMEM = pltpu.MemorySpace.VMEM
HBM = pltpu.MemorySpace.HBM
LANES = 128
PACK = 16
TILE = 8
PARTS = 3
LIMIT = 24 * 2**20


def from_partner(value, axis, mask):
    count = lax.axis_size(axis)
    return lax.ppermute(value, axis, [(source, source ^ mask) for source in range(count)])


def by_turns(members):
    half = members // 2
    order = [half, 0]
    for low in range(half - 1, 0, -1):
        order += [half + low, low]
    return order


def turn_of(member, members):
    half = members // 2
    low = member % half
    return jnp.where(low == 0, 0, 2 * (half - low)) + jnp.where(member < half, 1, 0)


def in_hbm(value):
    return pltpu.with_memory_space_constraint(value, HBM)


def call(body, shapes, operands, cost, scratch=(), spaces=None):
    return pl.pallas_call(
        body,
        out_shape=shapes,
        in_specs=[pl.BlockSpec(memory_space=space) for space in spaces or [VMEM] * len(operands)],
        out_specs=jax.tree.map(lambda unused: pl.BlockSpec(memory_space=VMEM), shapes),
        scratch_shapes=scratch,
        compiler_params=pltpu.CompilerParams(vmem_limit_bytes=LIMIT),
        cost_estimate=pl.CostEstimate(flops=cost[0], bytes_accessed=cost[1], transcendentals=0),
    )(*operands)


def iota(shape, dim):
    return lax.broadcasted_iota(jnp.int32, shape, dim)


def stage_kernel(ids_ref, kept_ref, sem):
    copy = pltpu.make_async_copy(ids_ref, kept_ref, sem)
    copy.start()
    copy.wait()


def early_kernel(heads_ref, new_ref, unused, kept_ref, head_sq_ref, kept_new_ref, sems):
    head_dev, width = heads_ref.shape
    tiles = 4
    tile = head_dev // tiles
    parts = [pl.ds(i * tile, tile) for i in range(tiles)]
    copies = [
        pltpu.make_async_copy(heads_ref.at[part], kept_ref.at[part], sems.at[i])
        for i, part in enumerate(parts)
    ]
    copies.append(pltpu.make_async_copy(new_ref, kept_new_ref, sems.at[tiles]))
    for copy in copies:
        copy.start()
    for i in range(tiles):
        copies[i].wait()
        for first in range(i * tile, (i + 1) * tile, LANES):
            block = jnp.square(kept_ref[first:first + LANES, :].astype(jnp.float32))
            folded = block[:, :LANES]
            for column in range(LANES, width, LANES):
                folded = folded + block[:, column:column + LANES]
            head_sq_ref[:, first:first + LANES] = jnp.sum(folded.T, axis=0, keepdims=True)
    for copy in copies[tiles:]:
        copy.wait()


def listed_rows(ids, me, slots, heads_ref):
    members, near = ids.shape
    head_dev = heads_ref.shape[0]
    local = ids - me * head_dev
    owned = (local >= 0) & (local < head_dev)
    earlier = (iota((near, near), 0) < iota((near, near), 1)).astype(jnp.bfloat16)
    rank = jnp.dot(owned.astype(jnp.bfloat16), earlier, preferred_element_type=jnp.float32)
    rank = jnp.where(owned, rank.astype(jnp.int32), -1)
    shape = (members, slots, near)
    pick = jnp.broadcast_to(rank[:, None, :], shape) == iota(shape, 1)
    wanted = jnp.sum(
        jnp.where(pick, jnp.broadcast_to(local[:, None, :] + 1, shape), 0), axis=2, keepdims=True
    ).reshape(members * slots, 1)
    onehot = (wanted == iota((members * slots, head_dev), 1) + 1).astype(jnp.bfloat16)
    return jnp.dot(
        onehot, heads_ref[...], preferred_element_type=jnp.float32
    ).astype(jnp.bfloat16)


def crowding(queries, heads_ref, head_sq_ref):
    head_dev, width = heads_ref.shape
    query_sq = jnp.sum(jnp.square(queries.astype(jnp.float32)), axis=1, keepdims=True)
    total_w = jnp.zeros((queries.shape[0], 1), jnp.float32)
    total_we = jnp.zeros((queries.shape[0], 1), jnp.float32)
    tile = 512
    for start in range(0, head_dev, tile):
        dots = lax.dot_general(
            queries, heads_ref[start:start + tile, :], (((1,), (1,)), ((), ())),
            preferred_element_type=jnp.float32,
        )
        head_sq = head_sq_ref[:, start:start + tile]
        excess = (query_sq + head_sq - 2.0 * dots) * (1.0 / width)
        inverse = 1.0 / (1.0 + excess)
        weight = inverse * inverse
        total_w = total_w + jnp.sum(weight, axis=1, keepdims=True)
        total_we = total_we + jnp.sum(weight * excess, axis=1, keepdims=True)
    return total_w, total_we


def crowd_kernel(groups, ids_ref, heads_ref, head_sq_ref, *refs):
    query_refs, (sums_ref, kept_ids_ref) = refs[:-2], refs[-2:]
    kept_ids_ref[...] = ids_ref[...]
    here = lax.axis_index("group")
    queries = jnp.concatenate([ref[...] for ref in query_refs], axis=0)
    new_count = queries.shape[0] // groups
    totals = crowding(queries, heads_ref, head_sq_ref)
    lane = iota((new_count, LANES), 1)
    row = iota((new_count, LANES), 0)
    line = iota(sums_ref.shape, 0)
    sums = jnp.zeros(sums_ref.shape, jnp.float32)
    for mask in range(groups):
        part = slice(mask * new_count, (mask + 1) * new_count)
        for kind in range(2):
            place = (kind * groups + (here ^ mask)) * new_count
            spread_out = jnp.where(lane == row + place % LANES, totals[kind][part], 0.0)
            spread_out = jnp.sum(spread_out, axis=0, keepdims=True)
            sums = sums + jnp.where(line == place // LANES, spread_out, 0.0)
    sums_ref[...] = sums


def gather_kernel(members, slots, near_ref, far_ref, heads_ref, unused, rows_ref, ids_ref):
    me = lax.axis_index("member")
    half = members // 2
    ids_ref[:half, :] = near_ref[...]
    ids_ref[half:, :] = far_ref[...]
    ids = jnp.concatenate([ids_ref[pl.ds(me ^ member, 1), :] for member in by_turns(members)], axis=0)
    rows_ref[...] = listed_rows(ids, me, slots, heads_ref)


def pack_kernel(members, slots, lines, rows_ref, mine_ref, other_ref, out_ref):
    chunks = rows_ref.shape[1] // LANES
    sums = (mine_ref[...] + other_ref[...])[:lines]
    coded = []
    for unused in range(PARTS):
        coded.append(sums.astype(jnp.bfloat16).astype(jnp.float32))
        sums = sums - coded[-1]
    missing = out_ref.shape[1] - chunks * slots - PARTS * lines
    if missing:
        coded.append(jnp.zeros((missing, LANES), jnp.float32))
    tail = jnp.concatenate(coded, axis=0).astype(jnp.bfloat16)
    for member in range(members):
        part = slice(member * slots, (member + 1) * slots)
        pieces = [rows_ref[part, chunk * LANES:(chunk + 1) * LANES] for chunk in range(chunks)]
        out_ref[member] = jnp.concatenate([*pieces, tail], axis=0)


def prepare_kernel(members, slots, head_dev, ids_ref, vectors_ref, unused, back_ref, vec_sq_ref):
    near = ids_ref.shape[1]
    block = vectors_ref.shape[1]
    square = (near, near)
    owner_row = jnp.broadcast_to(lax.div(ids_ref[...], head_dev), square)
    eye = iota(square, 0) == iota(square, 1)
    owner = jnp.sum(jnp.where(eye, owner_row, 0), axis=1, keepdims=True)
    before = (owner_row == owner) & (iota(square, 1) < iota(square, 0))
    place = jnp.sum(before.astype(jnp.int32), axis=1, keepdims=True)
    source = turn_of(owner, members) * slots + place
    back_ref[...] = (source == iota(back_ref.shape, 1)).astype(jnp.bfloat16)
    vec_sq = jnp.sum(jnp.square(vectors_ref[0].astype(jnp.float32)), axis=1, keepdims=True)
    diagonal = iota((block, block), 0) == iota((block, block), 1)
    vec_sq_ref[...] = jnp.sum(jnp.where(diagonal, vec_sq, 0.0), axis=0, keepdims=True)


def distances(slots, back_ref, vec_sq_ref, listed, vectors_ref, out_ref):
    members = listed.shape[0]
    width = vectors_ref.shape[2]
    rows = []
    for chunk in range(width // LANES):
        part = listed[:, chunk * slots:(chunk + 1) * slots, :].reshape(members * slots, LANES)
        rows.append(jnp.dot(back_ref[...], part, preferred_element_type=jnp.float32))
    rows = jnp.concatenate(rows, axis=1)
    row_sq = jnp.sum(jnp.square(rows), axis=1, keepdims=True)
    dots = lax.dot_general(
        rows.astype(jnp.bfloat16), vectors_ref[0], (((1,), (1,)), ((), ())),
        preferred_element_type=jnp.float32,
    )
    out_ref[0] = (row_sq + vec_sq_ref[...] - 2.0 * dots) * (1.0 / width)


def tail_kernel(
    groups, slots, total_heads, back_ref, vec_sq_ref, listed_ref, vectors_ref,
    density_ref, spread_ref, out_ref,
):
    listed = listed_ref[...]
    distances(slots, back_ref, vec_sq_ref, listed, vectors_ref, out_ref)
    here = lax.axis_index("group")
    members = listed_ref.shape[0]
    new_count = density_ref.shape[1]
    lines = 2 * groups * new_count // LANES
    first = vectors_ref.shape[2] // LANES * slots
    coded = jnp.sum(listed[:, first:, :].astype(jnp.float32), axis=0)
    total = sum(coded[part * lines:(part + 1) * lines] for part in range(PARTS))
    shape = (new_count, LANES)
    eye = iota((new_count, new_count), 0) == iota((new_count, new_count), 1)
    found = []
    for kind in range(2):
        place = (kind * groups + here) * new_count
        line = jnp.sum(
            jnp.where(iota((lines, LANES), 0) == place // LANES, total, 0.0), axis=0, keepdims=True
        )
        column = jnp.sum(
            jnp.where(iota(shape, 1) == iota(shape, 0) + place % LANES, line, 0.0),
            axis=1, keepdims=True,
        )
        found.append(jnp.sum(jnp.where(eye, column, 0.0), axis=0, keepdims=True))
    density_ref[...] = jnp.log(found[0] * (1.0 / total_heads))
    spread_ref[...] = found[1] / found[0]


def per_device(heads, new_heads, vectors, near_ids):
    head_dev, width = heads.shape
    new_count = new_heads.shape[0]
    near = near_ids.shape[1]
    groups = lax.axis_size("group")
    members = lax.axis_size("member")
    most = 2 * near // members
    slots = -(-most // PACK) * PACK

    partner_ids = from_partner(near_ids, "member", 1)
    others = [from_partner(new_heads, "group", mask) for mask in range(1, groups)]
    ids = call(
        stage_kernel,
        jax.ShapeDtypeStruct(near_ids.shape, near_ids.dtype),
        (in_hbm(near_ids),),
        (0, 0),
        scratch=[pltpu.SemaphoreType.DMA],
        spaces=[HBM],
    )
    ids = jnp.concatenate([ids, partner_ids], axis=0)
    kept, head_sq, new_heads = call(
        early_kernel,
        (
            jax.ShapeDtypeStruct(heads.shape, heads.dtype),
            jax.ShapeDtypeStruct((1, head_dev), jnp.float32),
            jax.ShapeDtypeStruct(new_heads.shape, new_heads.dtype),
        ),
        (in_hbm(heads), in_hbm(new_heads), ids),
        (0, 0),
        scratch=[pltpu.SemaphoreType.DMA((5,))],
        spaces=[HBM, HBM, pl.ANY],
    )
    lines = 2 * groups * new_count // LANES
    chunks = width // LANES
    extra = -(-PARTS * lines // TILE) * TILE
    sums, kept_ids = call(
        functools.partial(crowd_kernel, groups),
        (
            jax.ShapeDtypeStruct((-(-lines // TILE) * TILE, LANES), jnp.float32),
            jax.ShapeDtypeStruct(ids.shape, ids.dtype),
        ),
        (ids, kept, head_sq, new_heads, *others),
        (0, 0),
    )
    mask = 2
    while mask < members // 2:
        kept_ids = jnp.concatenate([kept_ids, from_partner(ids, "member", mask)], axis=0)
        ids = kept_ids
        mask *= 2
    far_ids = from_partner(ids, "member", mask)
    mask = 1
    while mask < groups // 2:
        sums = sums + from_partner(sums, "group", mask)
        mask *= 2
    back, vec_sq = call(
        functools.partial(prepare_kernel, members, slots, head_dev),
        (
            jax.ShapeDtypeStruct((near, members * slots), jnp.bfloat16),
            jax.ShapeDtypeStruct((1, vectors.shape[1]), jnp.float32),
        ),
        (near_ids, vectors, sums),
        (0, 0),
        spaces=[VMEM, VMEM, pl.ANY],
    )
    rows = call(
        functools.partial(gather_kernel, members, slots),
        jax.ShapeDtypeStruct((members * slots, width), jnp.bfloat16),
        (ids, far_ids, kept, back),
        (2 * members * slots * head_dev * width, heads.size * 2),
        scratch=[pltpu.VMEM((members, near), jnp.int32)],
        spaces=[VMEM, VMEM, VMEM, pl.ANY],
    )
    message = call(
        functools.partial(pack_kernel, members, slots, lines),
        jax.ShapeDtypeStruct((members, chunks * slots + extra, LANES), jnp.bfloat16),
        (rows, sums, from_partner(sums, "group", mask)),
        (0, members * slots * width * 4),
    )
    message = lax.all_to_all(
        message, "member", 0, 0, tiled=True, axis_index_groups=[by_turns(members)]
    )

    density, spread, reassign = call(
        functools.partial(
            tail_kernel, groups, slots, float(head_dev * groups * members)
        ),
        (
            jax.ShapeDtypeStruct((1, new_count), jnp.float32),
            jax.ShapeDtypeStruct((1, new_count), jnp.float32),
            jax.ShapeDtypeStruct((1, near, vectors.shape[1]), jnp.float32),
        ),
        (back, vec_sq, message, vectors),
        (4 * near * vectors.shape[1] * width, vectors.size * 4),
    )
    return (density[0], spread[0], reassign)


def solution(mesh):
    placed = (
        P(("group", "member"), None),
        P("group", None),
        P(("group", "member"), None, None),
        P(("group", "member"), None),
    )
    return jax.shard_map(
        per_device,
        mesh=mesh,
        in_specs=placed,
        out_specs=(P("group"), P("group"), P(("group", "member"), None, None)),
        check_vma=False,
    )
```

```python
import functools

import jax
import jax.numpy as jnp
from jax import lax
from jax.experimental import pallas as pl
from jax.experimental.pallas import tpu as pltpu
from jax.sharding import PartitionSpec as P

VMEM = pltpu.MemorySpace.VMEM
HBM = pltpu.MemorySpace.HBM
LANES = 128
PACK = 16
TILE = 8
PARTS = 3
LIMIT = 24 * 2**20


def from_partner(value, axis, mask):
    count = lax.axis_size(axis)
    return lax.ppermute(value, axis, [(source, source ^ mask) for source in range(count)])


def downward(members):
    return [(members // 2 - place) % members for place in range(members)]


def down_place(member, members):
    return (members + members // 2 - member) % members


def in_hbm(value):
    return pltpu.with_memory_space_constraint(value, HBM)


def call(body, shapes, operands, cost, scratch=(), spaces=None):
    return pl.pallas_call(
        body,
        out_shape=shapes,
        in_specs=[pl.BlockSpec(memory_space=space) for space in spaces or [VMEM] * len(operands)],
        out_specs=jax.tree.map(lambda unused: pl.BlockSpec(memory_space=VMEM), shapes),
        scratch_shapes=scratch,
        compiler_params=pltpu.CompilerParams(vmem_limit_bytes=LIMIT),
        cost_estimate=pl.CostEstimate(flops=cost[0], bytes_accessed=cost[1], transcendentals=0),
    )(*operands)


def iota(shape, dim):
    return lax.broadcasted_iota(jnp.int32, shape, dim)


def stage_kernel(ids_ref, kept_ref, sem):
    copy = pltpu.make_async_copy(ids_ref, kept_ref, sem)
    copy.start()
    copy.wait()


def early_kernel(heads_ref, new_ref, unused, kept_ref, head_sq_ref, kept_new_ref, sems):
    head_dev, width = heads_ref.shape
    tiles = 4
    tile = head_dev // tiles
    parts = [pl.ds(i * tile, tile) for i in range(tiles)]
    copies = [
        pltpu.make_async_copy(heads_ref.at[part], kept_ref.at[part], sems.at[i])
        for i, part in enumerate(parts)
    ]
    copies.append(pltpu.make_async_copy(new_ref, kept_new_ref, sems.at[tiles]))
    for copy in copies:
        copy.start()
    for i in range(tiles):
        copies[i].wait()
        for first in range(i * tile, (i + 1) * tile, LANES):
            block = jnp.square(kept_ref[first:first + LANES, :].astype(jnp.float32))
            folded = block[:, :LANES]
            for column in range(LANES, width, LANES):
                folded = folded + block[:, column:column + LANES]
            head_sq_ref[:, first:first + LANES] = jnp.sum(folded.T, axis=0, keepdims=True)
    for copy in copies[tiles:]:
        copy.wait()


def listed_rows(ids, me, slots, heads_ref):
    members, near = ids.shape
    head_dev = heads_ref.shape[0]
    local = ids - me * head_dev
    owned = (local >= 0) & (local < head_dev)
    earlier = (iota((near, near), 0) < iota((near, near), 1)).astype(jnp.bfloat16)
    rank = jnp.dot(owned.astype(jnp.bfloat16), earlier, preferred_element_type=jnp.float32)
    rank = jnp.where(owned, rank.astype(jnp.int32), -1)
    shape = (members, slots, near)
    pick = jnp.broadcast_to(rank[:, None, :], shape) == iota(shape, 1)
    wanted = jnp.sum(
        jnp.where(pick, jnp.broadcast_to(local[:, None, :] + 1, shape), 0), axis=2, keepdims=True
    ).reshape(members * slots, 1)
    onehot = (wanted == iota((members * slots, head_dev), 1) + 1).astype(jnp.bfloat16)
    return jnp.dot(
        onehot, heads_ref[...], preferred_element_type=jnp.float32
    ).astype(jnp.bfloat16)


def crowding(queries, heads_ref, head_sq_ref):
    head_dev, width = heads_ref.shape
    query_sq = jnp.sum(jnp.square(queries.astype(jnp.float32)), axis=1, keepdims=True)
    total_w = jnp.zeros((queries.shape[0], 1), jnp.float32)
    total_we = jnp.zeros((queries.shape[0], 1), jnp.float32)
    tile = 512
    for start in range(0, head_dev, tile):
        dots = lax.dot_general(
            queries, heads_ref[start:start + tile, :], (((1,), (1,)), ((), ())),
            preferred_element_type=jnp.float32,
        )
        head_sq = head_sq_ref[:, start:start + tile]
        excess = (query_sq + head_sq - 2.0 * dots) * (1.0 / width)
        inverse = 1.0 / (1.0 + excess)
        weight = inverse * inverse
        total_w = total_w + jnp.sum(weight, axis=1, keepdims=True)
        total_we = total_we + jnp.sum(weight * excess, axis=1, keepdims=True)
    return total_w, total_we


def crowd_kernel(groups, ids_ref, heads_ref, head_sq_ref, *refs):
    query_refs, (sums_ref, kept_ids_ref) = refs[:-2], refs[-2:]
    kept_ids_ref[...] = ids_ref[...]
    here = lax.axis_index("group")
    queries = jnp.concatenate([ref[...] for ref in query_refs], axis=0)
    new_count = queries.shape[0] // groups
    totals = crowding(queries, heads_ref, head_sq_ref)
    lane = iota((new_count, LANES), 1)
    row = iota((new_count, LANES), 0)
    line = iota(sums_ref.shape, 0)
    sums = jnp.zeros(sums_ref.shape, jnp.float32)
    for mask in range(groups):
        part = slice(mask * new_count, (mask + 1) * new_count)
        for kind in range(2):
            place = (kind * groups + (here ^ mask)) * new_count
            spread_out = jnp.where(lane == row + place % LANES, totals[kind][part], 0.0)
            spread_out = jnp.sum(spread_out, axis=0, keepdims=True)
            sums = sums + jnp.where(line == place // LANES, spread_out, 0.0)
    sums_ref[...] = sums


def gather_kernel(members, slots, near_ref, far_ref, heads_ref, unused, rows_ref, ids_ref):
    me = lax.axis_index("member")
    half = members // 2
    ids_ref[:half, :] = near_ref[...]
    ids_ref[half:, :] = far_ref[...]
    ids = jnp.concatenate([ids_ref[pl.ds(me ^ member, 1), :] for member in downward(members)], axis=0)
    rows_ref[...] = listed_rows(ids, me, slots, heads_ref)


def pack_kernel(members, slots, lines, rows_ref, mine_ref, other_ref, out_ref):
    chunks = rows_ref.shape[1] // LANES
    sums = (mine_ref[...] + other_ref[...])[:lines]
    coded = []
    for unused in range(PARTS):
        coded.append(sums.astype(jnp.bfloat16).astype(jnp.float32))
        sums = sums - coded[-1]
    missing = out_ref.shape[1] - chunks * slots - PARTS * lines
    if missing:
        coded.append(jnp.zeros((missing, LANES), jnp.float32))
    tail = jnp.concatenate(coded, axis=0).astype(jnp.bfloat16)
    for member in range(members):
        part = slice(member * slots, (member + 1) * slots)
        pieces = [rows_ref[part, chunk * LANES:(chunk + 1) * LANES] for chunk in range(chunks)]
        out_ref[member] = jnp.concatenate([*pieces, tail], axis=0)


def prepare_kernel(members, slots, head_dev, ids_ref, vectors_ref, unused, back_ref, vec_sq_ref):
    near = ids_ref.shape[1]
    block = vectors_ref.shape[1]
    square = (near, near)
    owner_row = jnp.broadcast_to(lax.div(ids_ref[...], head_dev), square)
    eye = iota(square, 0) == iota(square, 1)
    owner = jnp.sum(jnp.where(eye, owner_row, 0), axis=1, keepdims=True)
    before = (owner_row == owner) & (iota(square, 1) < iota(square, 0))
    place = jnp.sum(before.astype(jnp.int32), axis=1, keepdims=True)
    source = down_place(owner, members) * slots + place
    back_ref[...] = (source == iota(back_ref.shape, 1)).astype(jnp.bfloat16)
    vec_sq = jnp.sum(jnp.square(vectors_ref[0].astype(jnp.float32)), axis=1, keepdims=True)
    diagonal = iota((block, block), 0) == iota((block, block), 1)
    vec_sq_ref[...] = jnp.sum(jnp.where(diagonal, vec_sq, 0.0), axis=0, keepdims=True)


def distances(slots, back_ref, vec_sq_ref, listed, vectors_ref, out_ref):
    members = listed.shape[0]
    width = vectors_ref.shape[2]
    rows = []
    for chunk in range(width // LANES):
        part = listed[:, chunk * slots:(chunk + 1) * slots, :].reshape(members * slots, LANES)
        rows.append(jnp.dot(back_ref[...], part, preferred_element_type=jnp.float32))
    rows = jnp.concatenate(rows, axis=1)
    row_sq = jnp.sum(jnp.square(rows), axis=1, keepdims=True)
    dots = lax.dot_general(
        rows.astype(jnp.bfloat16), vectors_ref[0], (((1,), (1,)), ((), ())),
        preferred_element_type=jnp.float32,
    )
    out_ref[0] = (row_sq + vec_sq_ref[...] - 2.0 * dots) * (1.0 / width)


def tail_kernel(
    groups, slots, total_heads, back_ref, vec_sq_ref, listed_ref, vectors_ref,
    density_ref, spread_ref, out_ref,
):
    listed = listed_ref[...]
    distances(slots, back_ref, vec_sq_ref, listed, vectors_ref, out_ref)
    here = lax.axis_index("group")
    members = listed_ref.shape[0]
    new_count = density_ref.shape[1]
    lines = 2 * groups * new_count // LANES
    first = vectors_ref.shape[2] // LANES * slots
    coded = jnp.sum(listed[:, first:, :].astype(jnp.float32), axis=0)
    total = sum(coded[part * lines:(part + 1) * lines] for part in range(PARTS))
    shape = (new_count, LANES)
    eye = iota((new_count, new_count), 0) == iota((new_count, new_count), 1)
    found = []
    for kind in range(2):
        place = (kind * groups + here) * new_count
        line = jnp.sum(
            jnp.where(iota((lines, LANES), 0) == place // LANES, total, 0.0), axis=0, keepdims=True
        )
        column = jnp.sum(
            jnp.where(iota(shape, 1) == iota(shape, 0) + place % LANES, line, 0.0),
            axis=1, keepdims=True,
        )
        found.append(jnp.sum(jnp.where(eye, column, 0.0), axis=0, keepdims=True))
    density_ref[...] = jnp.log(found[0] * (1.0 / total_heads))
    spread_ref[...] = found[1] / found[0]


def per_device(heads, new_heads, vectors, near_ids):
    head_dev, width = heads.shape
    new_count = new_heads.shape[0]
    near = near_ids.shape[1]
    groups = lax.axis_size("group")
    members = lax.axis_size("member")
    most = 2 * near // members
    slots = -(-most // PACK) * PACK

    partner_ids = from_partner(near_ids, "member", 1)
    others = [from_partner(new_heads, "group", mask) for mask in range(1, groups)]
    ids = call(
        stage_kernel,
        jax.ShapeDtypeStruct(near_ids.shape, near_ids.dtype),
        (in_hbm(near_ids),),
        (0, 0),
        scratch=[pltpu.SemaphoreType.DMA],
        spaces=[HBM],
    )
    ids = jnp.concatenate([ids, partner_ids], axis=0)
    kept, head_sq, new_heads = call(
        early_kernel,
        (
            jax.ShapeDtypeStruct(heads.shape, heads.dtype),
            jax.ShapeDtypeStruct((1, head_dev), jnp.float32),
            jax.ShapeDtypeStruct(new_heads.shape, new_heads.dtype),
        ),
        (in_hbm(heads), in_hbm(new_heads), ids),
        (0, 0),
        scratch=[pltpu.SemaphoreType.DMA((5,))],
        spaces=[HBM, HBM, pl.ANY],
    )
    lines = 2 * groups * new_count // LANES
    chunks = width // LANES
    extra = -(-PARTS * lines // TILE) * TILE
    sums, kept_ids = call(
        functools.partial(crowd_kernel, groups),
        (
            jax.ShapeDtypeStruct((-(-lines // TILE) * TILE, LANES), jnp.float32),
            jax.ShapeDtypeStruct(ids.shape, ids.dtype),
        ),
        (ids, kept, head_sq, new_heads, *others),
        (0, 0),
    )
    mask = 2
    while mask < members // 2:
        kept_ids = jnp.concatenate([kept_ids, from_partner(ids, "member", mask)], axis=0)
        ids = kept_ids
        mask *= 2
    far_ids = from_partner(ids, "member", mask)
    mask = 1
    while mask < groups // 2:
        sums = sums + from_partner(sums, "group", mask)
        mask *= 2
    back, vec_sq = call(
        functools.partial(prepare_kernel, members, slots, head_dev),
        (
            jax.ShapeDtypeStruct((near, members * slots), jnp.bfloat16),
            jax.ShapeDtypeStruct((1, vectors.shape[1]), jnp.float32),
        ),
        (near_ids, vectors, sums),
        (0, 0),
        spaces=[VMEM, VMEM, pl.ANY],
    )
    rows = call(
        functools.partial(gather_kernel, members, slots),
        jax.ShapeDtypeStruct((members * slots, width), jnp.bfloat16),
        (ids, far_ids, kept, back),
        (2 * members * slots * head_dev * width, heads.size * 2),
        scratch=[pltpu.VMEM((members, near), jnp.int32)],
        spaces=[VMEM, VMEM, VMEM, pl.ANY],
    )
    message = call(
        functools.partial(pack_kernel, members, slots, lines),
        jax.ShapeDtypeStruct((members, chunks * slots + extra, LANES), jnp.bfloat16),
        (rows, sums, from_partner(sums, "group", mask)),
        (0, members * slots * width * 4),
    )
    message = lax.all_to_all(
        message, "member", 0, 0, tiled=True, axis_index_groups=[downward(members)]
    )

    density, spread, reassign = call(
        functools.partial(
            tail_kernel, groups, slots, float(head_dev * groups * members)
        ),
        (
            jax.ShapeDtypeStruct((1, new_count), jnp.float32),
            jax.ShapeDtypeStruct((1, new_count), jnp.float32),
            jax.ShapeDtypeStruct((1, near, vectors.shape[1]), jnp.float32),
        ),
        (back, vec_sq, message, vectors),
        (4 * near * vectors.shape[1] * width, vectors.size * 4),
    )
    return (density[0], spread[0], reassign)


def solution(mesh):
    placed = (
        P(("group", "member"), None),
        P("group", None),
        P(("group", "member"), None, None),
        P(("group", "member"), None),
    )
    return jax.shard_map(
        per_device,
        mesh=mesh,
        in_specs=placed,
        out_specs=(P("group"), P("group"), P(("group", "member"), None, None)),
        check_vma=False,
    )
```

```python
import functools

import jax
import jax.numpy as jnp
from jax import lax
from jax.experimental import pallas as pl
from jax.experimental.pallas import tpu as pltpu
from jax.sharding import PartitionSpec as P

VMEM = pltpu.MemorySpace.VMEM
HBM = pltpu.MemorySpace.HBM
LANES = 128
PACK = 16
TILE = 8
PARTS = 3
LIMIT = 24 * 2**20


def from_partner(value, axis, mask):
    count = lax.axis_size(axis)
    return lax.ppermute(value, axis, [(source, source ^ mask) for source in range(count)])


def by_turns(members):
    half = members // 2
    order = [half, 0]
    for low in range(half - 1, 0, -1):
        order += [half + low, low]
    return order[-2:] + order[:-2]


def turn_of(member, members):
    half = members // 2
    low = member % half
    return 2 * ((half + 1 - low) % half) + jnp.where(member < half, 1, 0)


def in_hbm(value):
    return pltpu.with_memory_space_constraint(value, HBM)


def call(body, shapes, operands, cost, scratch=(), spaces=None):
    return pl.pallas_call(
        body,
        out_shape=shapes,
        in_specs=[pl.BlockSpec(memory_space=space) for space in spaces or [VMEM] * len(operands)],
        out_specs=jax.tree.map(lambda unused: pl.BlockSpec(memory_space=VMEM), shapes),
        scratch_shapes=scratch,
        compiler_params=pltpu.CompilerParams(vmem_limit_bytes=LIMIT),
        cost_estimate=pl.CostEstimate(flops=cost[0], bytes_accessed=cost[1], transcendentals=0),
    )(*operands)


def iota(shape, dim):
    return lax.broadcasted_iota(jnp.int32, shape, dim)


def stage_kernel(ids_ref, kept_ref, sem):
    copy = pltpu.make_async_copy(ids_ref, kept_ref, sem)
    copy.start()
    copy.wait()


def early_kernel(heads_ref, new_ref, unused, kept_ref, head_sq_ref, kept_new_ref, sems):
    head_dev, width = heads_ref.shape
    tiles = 4
    tile = head_dev // tiles
    parts = [pl.ds(i * tile, tile) for i in range(tiles)]
    copies = [
        pltpu.make_async_copy(heads_ref.at[part], kept_ref.at[part], sems.at[i])
        for i, part in enumerate(parts)
    ]
    copies.append(pltpu.make_async_copy(new_ref, kept_new_ref, sems.at[tiles]))
    for copy in copies:
        copy.start()
    for i in range(tiles):
        copies[i].wait()
        for first in range(i * tile, (i + 1) * tile, LANES):
            block = jnp.square(kept_ref[first:first + LANES, :].astype(jnp.float32))
            folded = block[:, :LANES]
            for column in range(LANES, width, LANES):
                folded = folded + block[:, column:column + LANES]
            head_sq_ref[:, first:first + LANES] = jnp.sum(folded.T, axis=0, keepdims=True)
    for copy in copies[tiles:]:
        copy.wait()


def listed_rows(ids, me, slots, heads_ref):
    members, near = ids.shape
    head_dev = heads_ref.shape[0]
    local = ids - me * head_dev
    owned = (local >= 0) & (local < head_dev)
    earlier = (iota((near, near), 0) < iota((near, near), 1)).astype(jnp.bfloat16)
    rank = jnp.dot(owned.astype(jnp.bfloat16), earlier, preferred_element_type=jnp.float32)
    rank = jnp.where(owned, rank.astype(jnp.int32), -1)
    shape = (members, slots, near)
    pick = jnp.broadcast_to(rank[:, None, :], shape) == iota(shape, 1)
    wanted = jnp.sum(
        jnp.where(pick, jnp.broadcast_to(local[:, None, :] + 1, shape), 0), axis=2, keepdims=True
    ).reshape(members * slots, 1)
    onehot = (wanted == iota((members * slots, head_dev), 1) + 1).astype(jnp.bfloat16)
    return jnp.dot(
        onehot, heads_ref[...], preferred_element_type=jnp.float32
    ).astype(jnp.bfloat16)


def crowding(queries, heads_ref, head_sq_ref):
    head_dev, width = heads_ref.shape
    query_sq = jnp.sum(jnp.square(queries.astype(jnp.float32)), axis=1, keepdims=True)
    total_w = jnp.zeros((queries.shape[0], 1), jnp.float32)
    total_we = jnp.zeros((queries.shape[0], 1), jnp.float32)
    tile = 512
    for start in range(0, head_dev, tile):
        dots = lax.dot_general(
            queries, heads_ref[start:start + tile, :], (((1,), (1,)), ((), ())),
            preferred_element_type=jnp.float32,
        )
        head_sq = head_sq_ref[:, start:start + tile]
        excess = (query_sq + head_sq - 2.0 * dots) * (1.0 / width)
        inverse = 1.0 / (1.0 + excess)
        weight = inverse * inverse
        total_w = total_w + jnp.sum(weight, axis=1, keepdims=True)
        total_we = total_we + jnp.sum(weight * excess, axis=1, keepdims=True)
    return total_w, total_we


def crowd_kernel(groups, ids_ref, heads_ref, head_sq_ref, *refs):
    query_refs, (sums_ref, kept_ids_ref) = refs[:-2], refs[-2:]
    kept_ids_ref[...] = ids_ref[...]
    here = lax.axis_index("group")
    queries = jnp.concatenate([ref[...] for ref in query_refs], axis=0)
    new_count = queries.shape[0] // groups
    totals = crowding(queries, heads_ref, head_sq_ref)
    lane = iota((new_count, LANES), 1)
    row = iota((new_count, LANES), 0)
    line = iota(sums_ref.shape, 0)
    sums = jnp.zeros(sums_ref.shape, jnp.float32)
    for mask in range(groups):
        part = slice(mask * new_count, (mask + 1) * new_count)
        for kind in range(2):
            place = (kind * groups + (here ^ mask)) * new_count
            spread_out = jnp.where(lane == row + place % LANES, totals[kind][part], 0.0)
            spread_out = jnp.sum(spread_out, axis=0, keepdims=True)
            sums = sums + jnp.where(line == place // LANES, spread_out, 0.0)
    sums_ref[...] = sums


def gather_kernel(members, slots, near_ref, far_ref, heads_ref, unused, rows_ref, ids_ref):
    me = lax.axis_index("member")
    half = members // 2
    ids_ref[:half, :] = near_ref[...]
    ids_ref[half:, :] = far_ref[...]
    ids = jnp.concatenate([ids_ref[pl.ds(me ^ member, 1), :] for member in by_turns(members)], axis=0)
    rows_ref[...] = listed_rows(ids, me, slots, heads_ref)


def pack_kernel(members, slots, lines, rows_ref, mine_ref, other_ref, out_ref):
    chunks = rows_ref.shape[1] // LANES
    sums = (mine_ref[...] + other_ref[...])[:lines]
    coded = []
    for unused in range(PARTS):
        coded.append(sums.astype(jnp.bfloat16).astype(jnp.float32))
        sums = sums - coded[-1]
    missing = out_ref.shape[1] - chunks * slots - PARTS * lines
    if missing:
        coded.append(jnp.zeros((missing, LANES), jnp.float32))
    tail = jnp.concatenate(coded, axis=0).astype(jnp.bfloat16)
    for member in range(members):
        part = slice(member * slots, (member + 1) * slots)
        pieces = [rows_ref[part, chunk * LANES:(chunk + 1) * LANES] for chunk in range(chunks)]
        out_ref[member] = jnp.concatenate([*pieces, tail], axis=0)


def prepare_kernel(members, slots, head_dev, ids_ref, vectors_ref, unused, back_ref, vec_sq_ref):
    near = ids_ref.shape[1]
    block = vectors_ref.shape[1]
    square = (near, near)
    owner_row = jnp.broadcast_to(lax.div(ids_ref[...], head_dev), square)
    eye = iota(square, 0) == iota(square, 1)
    owner = jnp.sum(jnp.where(eye, owner_row, 0), axis=1, keepdims=True)
    before = (owner_row == owner) & (iota(square, 1) < iota(square, 0))
    place = jnp.sum(before.astype(jnp.int32), axis=1, keepdims=True)
    source = turn_of(owner, members) * slots + place
    back_ref[...] = (source == iota(back_ref.shape, 1)).astype(jnp.bfloat16)
    vec_sq = jnp.sum(jnp.square(vectors_ref[0].astype(jnp.float32)), axis=1, keepdims=True)
    diagonal = iota((block, block), 0) == iota((block, block), 1)
    vec_sq_ref[...] = jnp.sum(jnp.where(diagonal, vec_sq, 0.0), axis=0, keepdims=True)


def distances(slots, back_ref, vec_sq_ref, listed, vectors_ref, out_ref):
    members = listed.shape[0]
    width = vectors_ref.shape[2]
    rows = []
    for chunk in range(width // LANES):
        part = listed[:, chunk * slots:(chunk + 1) * slots, :].reshape(members * slots, LANES)
        rows.append(jnp.dot(back_ref[...], part, preferred_element_type=jnp.float32))
    rows = jnp.concatenate(rows, axis=1)
    row_sq = jnp.sum(jnp.square(rows), axis=1, keepdims=True)
    dots = lax.dot_general(
        rows.astype(jnp.bfloat16), vectors_ref[0], (((1,), (1,)), ((), ())),
        preferred_element_type=jnp.float32,
    )
    out_ref[0] = (row_sq + vec_sq_ref[...] - 2.0 * dots) * (1.0 / width)


def tail_kernel(
    groups, slots, total_heads, back_ref, vec_sq_ref, listed_ref, vectors_ref,
    density_ref, spread_ref, out_ref,
):
    listed = listed_ref[...]
    distances(slots, back_ref, vec_sq_ref, listed, vectors_ref, out_ref)
    here = lax.axis_index("group")
    members = listed_ref.shape[0]
    new_count = density_ref.shape[1]
    lines = 2 * groups * new_count // LANES
    first = vectors_ref.shape[2] // LANES * slots
    coded = jnp.sum(listed[:, first:, :].astype(jnp.float32), axis=0)
    total = sum(coded[part * lines:(part + 1) * lines] for part in range(PARTS))
    shape = (new_count, LANES)
    eye = iota((new_count, new_count), 0) == iota((new_count, new_count), 1)
    found = []
    for kind in range(2):
        place = (kind * groups + here) * new_count
        line = jnp.sum(
            jnp.where(iota((lines, LANES), 0) == place // LANES, total, 0.0), axis=0, keepdims=True
        )
        column = jnp.sum(
            jnp.where(iota(shape, 1) == iota(shape, 0) + place % LANES, line, 0.0),
            axis=1, keepdims=True,
        )
        found.append(jnp.sum(jnp.where(eye, column, 0.0), axis=0, keepdims=True))
    density_ref[...] = jnp.log(found[0] * (1.0 / total_heads))
    spread_ref[...] = found[1] / found[0]


def per_device(heads, new_heads, vectors, near_ids):
    head_dev, width = heads.shape
    new_count = new_heads.shape[0]
    near = near_ids.shape[1]
    groups = lax.axis_size("group")
    members = lax.axis_size("member")
    most = 2 * near // members
    slots = -(-most // PACK) * PACK

    partner_ids = from_partner(near_ids, "member", 1)
    others = [from_partner(new_heads, "group", mask) for mask in range(1, groups)]
    ids = call(
        stage_kernel,
        jax.ShapeDtypeStruct(near_ids.shape, near_ids.dtype),
        (in_hbm(near_ids),),
        (0, 0),
        scratch=[pltpu.SemaphoreType.DMA],
        spaces=[HBM],
    )
    ids = jnp.concatenate([ids, partner_ids], axis=0)
    kept, head_sq, new_heads = call(
        early_kernel,
        (
            jax.ShapeDtypeStruct(heads.shape, heads.dtype),
            jax.ShapeDtypeStruct((1, head_dev), jnp.float32),
            jax.ShapeDtypeStruct(new_heads.shape, new_heads.dtype),
        ),
        (in_hbm(heads), in_hbm(new_heads), ids),
        (0, 0),
        scratch=[pltpu.SemaphoreType.DMA((5,))],
        spaces=[HBM, HBM, pl.ANY],
    )
    lines = 2 * groups * new_count // LANES
    chunks = width // LANES
    extra = -(-PARTS * lines // TILE) * TILE
    sums, kept_ids = call(
        functools.partial(crowd_kernel, groups),
        (
            jax.ShapeDtypeStruct((-(-lines // TILE) * TILE, LANES), jnp.float32),
            jax.ShapeDtypeStruct(ids.shape, ids.dtype),
        ),
        (ids, kept, head_sq, new_heads, *others),
        (0, 0),
    )
    mask = 2
    while mask < members // 2:
        kept_ids = jnp.concatenate([kept_ids, from_partner(ids, "member", mask)], axis=0)
        ids = kept_ids
        mask *= 2
    far_ids = from_partner(ids, "member", mask)
    mask = 1
    while mask < groups // 2:
        sums = sums + from_partner(sums, "group", mask)
        mask *= 2
    back, vec_sq = call(
        functools.partial(prepare_kernel, members, slots, head_dev),
        (
            jax.ShapeDtypeStruct((near, members * slots), jnp.bfloat16),
            jax.ShapeDtypeStruct((1, vectors.shape[1]), jnp.float32),
        ),
        (near_ids, vectors, sums),
        (0, 0),
        spaces=[VMEM, VMEM, pl.ANY],
    )
    rows = call(
        functools.partial(gather_kernel, members, slots),
        jax.ShapeDtypeStruct((members * slots, width), jnp.bfloat16),
        (ids, far_ids, kept, back),
        (2 * members * slots * head_dev * width, heads.size * 2),
        scratch=[pltpu.VMEM((members, near), jnp.int32)],
        spaces=[VMEM, VMEM, VMEM, pl.ANY],
    )
    message = call(
        functools.partial(pack_kernel, members, slots, lines),
        jax.ShapeDtypeStruct((members, chunks * slots + extra, LANES), jnp.bfloat16),
        (rows, sums, from_partner(sums, "group", mask)),
        (0, members * slots * width * 4),
    )
    message = lax.all_to_all(
        message, "member", 0, 0, tiled=True, axis_index_groups=[by_turns(members)]
    )

    density, spread, reassign = call(
        functools.partial(
            tail_kernel, groups, slots, float(head_dev * groups * members)
        ),
        (
            jax.ShapeDtypeStruct((1, new_count), jnp.float32),
            jax.ShapeDtypeStruct((1, new_count), jnp.float32),
            jax.ShapeDtypeStruct((1, near, vectors.shape[1]), jnp.float32),
        ),
        (back, vec_sq, message, vectors),
        (4 * near * vectors.shape[1] * width, vectors.size * 4),
    )
    return (density[0], spread[0], reassign)


def solution(mesh):
    placed = (
        P(("group", "member"), None),
        P("group", None),
        P(("group", "member"), None, None),
        P(("group", "member"), None),
    )
    return jax.shard_map(
        per_device,
        mesh=mesh,
        in_specs=placed,
        out_specs=(P("group"), P("group"), P(("group", "member"), None, None)),
        check_vma=False,
    )
```

```python
import functools

import jax
import jax.numpy as jnp
from jax import lax
from jax.experimental import pallas as pl
from jax.experimental.pallas import tpu as pltpu
from jax.sharding import PartitionSpec as P

VMEM = pltpu.MemorySpace.VMEM
HBM = pltpu.MemorySpace.HBM
LANES = 128
PACK = 16
TILE = 8
PARTS = 3
LIMIT = 24 * 2**20


def from_partner(value, axis, mask):
    count = lax.axis_size(axis)
    return lax.ppermute(value, axis, [(source, source ^ mask) for source in range(count)])


def by_turns(members):
    half = members // 2
    order = [half, 0]
    for low in range(half - 1, 0, -1):
        order += [half + low, low]
    return order


def turn_of(member, members):
    half = members // 2
    low = member % half
    return jnp.where(low == 0, 0, 2 * (half - low)) + jnp.where(member < half, 1, 0)


def in_hbm(value):
    return pltpu.with_memory_space_constraint(value, HBM)


def call(body, shapes, operands, cost, scratch=(), spaces=None, outs=None):
    return pl.pallas_call(
        body,
        out_shape=shapes,
        in_specs=[pl.BlockSpec(memory_space=space) for space in spaces or [VMEM] * len(operands)],
        out_specs=outs or jax.tree.map(lambda unused: pl.BlockSpec(memory_space=VMEM), shapes),
        scratch_shapes=scratch,
        compiler_params=pltpu.CompilerParams(vmem_limit_bytes=LIMIT),
        cost_estimate=pl.CostEstimate(flops=cost[0], bytes_accessed=cost[1], transcendentals=0),
    )(*operands)


def iota(shape, dim):
    return lax.broadcasted_iota(jnp.int32, shape, dim)


def stage_kernel(ids_ref, kept_ref, sem):
    copy = pltpu.make_async_copy(ids_ref, kept_ref, sem)
    copy.start()
    copy.wait()


def early_kernel(heads_ref, new_ref, unused, kept_ref, head_sq_ref, kept_new_ref, sems):
    head_dev, width = heads_ref.shape
    tiles = 4
    tile = head_dev // tiles
    parts = [pl.ds(i * tile, tile) for i in range(tiles)]
    copies = [
        pltpu.make_async_copy(heads_ref.at[part], kept_ref.at[part], sems.at[i])
        for i, part in enumerate(parts)
    ]
    copies.append(pltpu.make_async_copy(new_ref, kept_new_ref, sems.at[tiles]))
    for copy in copies:
        copy.start()
    for i in range(tiles):
        copies[i].wait()
        for first in range(i * tile, (i + 1) * tile, LANES):
            block = jnp.square(kept_ref[first:first + LANES, :].astype(jnp.float32))
            folded = block[:, :LANES]
            for column in range(LANES, width, LANES):
                folded = folded + block[:, column:column + LANES]
            head_sq_ref[:, first:first + LANES] = jnp.sum(folded.T, axis=0, keepdims=True)
    for copy in copies[tiles:]:
        copy.wait()


def listed_rows(ids, me, slots, heads_ref):
    members, near = ids.shape
    head_dev = heads_ref.shape[0]
    local = ids - me * head_dev
    owned = (local >= 0) & (local < head_dev)
    earlier = (iota((near, near), 0) < iota((near, near), 1)).astype(jnp.bfloat16)
    rank = jnp.dot(owned.astype(jnp.bfloat16), earlier, preferred_element_type=jnp.float32)
    rank = jnp.where(owned, rank.astype(jnp.int32), -1)
    shape = (members, slots, near)
    pick = jnp.broadcast_to(rank[:, None, :], shape) == iota(shape, 1)
    wanted = jnp.sum(
        jnp.where(pick, jnp.broadcast_to(local[:, None, :] + 1, shape), 0), axis=2, keepdims=True
    ).reshape(members * slots, 1)
    onehot = (wanted == iota((members * slots, head_dev), 1) + 1).astype(jnp.bfloat16)
    return jnp.dot(
        onehot, heads_ref[...], preferred_element_type=jnp.float32
    ).astype(jnp.bfloat16)


def crowding(queries, heads_ref, head_sq_ref):
    head_dev, width = heads_ref.shape
    query_sq = jnp.sum(jnp.square(queries.astype(jnp.float32)), axis=1, keepdims=True)
    total_w = jnp.zeros((queries.shape[0], 1), jnp.float32)
    total_we = jnp.zeros((queries.shape[0], 1), jnp.float32)
    tile = 512
    for start in range(0, head_dev, tile):
        dots = lax.dot_general(
            queries, heads_ref[start:start + tile, :], (((1,), (1,)), ((), ())),
            preferred_element_type=jnp.float32,
        )
        head_sq = head_sq_ref[:, start:start + tile]
        excess = (query_sq + head_sq - 2.0 * dots) * (1.0 / width)
        inverse = 1.0 / (1.0 + excess)
        weight = inverse * inverse
        total_w = total_w + jnp.sum(weight, axis=1, keepdims=True)
        total_we = total_we + jnp.sum(weight * excess, axis=1, keepdims=True)
    return total_w, total_we


def crowd_kernel(groups, ids_ref, heads_ref, head_sq_ref, *refs):
    query_refs, (sums_ref, kept_ids_ref) = refs[:-2], refs[-2:]
    kept_ids_ref[...] = ids_ref[...]
    here = lax.axis_index("group")
    queries = jnp.concatenate([ref[...] for ref in query_refs], axis=0)
    new_count = queries.shape[0] // groups
    totals = crowding(queries, heads_ref, head_sq_ref)
    lane = iota((new_count, LANES), 1)
    row = iota((new_count, LANES), 0)
    line = iota(sums_ref.shape, 0)
    sums = jnp.zeros(sums_ref.shape, jnp.float32)
    for mask in range(groups):
        part = slice(mask * new_count, (mask + 1) * new_count)
        for kind in range(2):
            place = (kind * groups + (here ^ mask)) * new_count
            spread_out = jnp.where(lane == row + place % LANES, totals[kind][part], 0.0)
            spread_out = jnp.sum(spread_out, axis=0, keepdims=True)
            sums = sums + jnp.where(line == place // LANES, spread_out, 0.0)
    sums_ref[...] = sums


def gather_kernel(members, slots, near_ref, far_ref, heads_ref, unused, rows_ref, ids_ref):
    me = lax.axis_index("member")
    half = members // 2
    ids_ref[:half, :] = near_ref[...]
    ids_ref[half:, :] = far_ref[...]
    ids = jnp.concatenate([ids_ref[pl.ds(me ^ member, 1), :] for member in by_turns(members)], axis=0)
    rows_ref[...] = listed_rows(ids, me, slots, heads_ref)


def pack_kernel(members, slots, lines, rows_ref, mine_ref, other_ref, out_ref):
    chunks = rows_ref.shape[1] // LANES
    sums = (mine_ref[...] + other_ref[...])[:lines]
    coded = []
    for unused in range(PARTS):
        coded.append(sums.astype(jnp.bfloat16).astype(jnp.float32))
        sums = sums - coded[-1]
    missing = out_ref.shape[1] - chunks * slots - PARTS * lines
    if missing:
        coded.append(jnp.zeros((missing, LANES), jnp.float32))
    tail = jnp.concatenate(coded, axis=0).astype(jnp.bfloat16)
    for member in range(members):
        part = slice(member * slots, (member + 1) * slots)
        pieces = [rows_ref[part, chunk * LANES:(chunk + 1) * LANES] for chunk in range(chunks)]
        out_ref[member] = jnp.concatenate([*pieces, tail], axis=0)


def prepare_kernel(members, slots, head_dev, ids_ref, vectors_ref, unused, back_ref, vec_sq_ref):
    near = ids_ref.shape[1]
    block = vectors_ref.shape[1]
    square = (near, near)
    owner_row = jnp.broadcast_to(lax.div(ids_ref[...], head_dev), square)
    eye = iota(square, 0) == iota(square, 1)
    owner = jnp.sum(jnp.where(eye, owner_row, 0), axis=1, keepdims=True)
    before = (owner_row == owner) & (iota(square, 1) < iota(square, 0))
    place = jnp.sum(before.astype(jnp.int32), axis=1, keepdims=True)
    source = turn_of(owner, members) * slots + place
    back_ref[...] = (source == iota(back_ref.shape, 1)).astype(jnp.bfloat16)
    vec_sq = jnp.sum(jnp.square(vectors_ref[0].astype(jnp.float32)), axis=1, keepdims=True)
    diagonal = iota((block, block), 0) == iota((block, block), 1)
    vec_sq_ref[...] = jnp.sum(jnp.where(diagonal, vec_sq, 0.0), axis=0, keepdims=True)


def distances(slots, back_ref, vec_sq_ref, listed, vectors_ref, out_ref):
    members = listed.shape[0]
    width = vectors_ref.shape[2]
    rows = []
    for chunk in range(width // LANES):
        part = listed[:, chunk * slots:(chunk + 1) * slots, :].reshape(members * slots, LANES)
        rows.append(jnp.dot(back_ref[...], part, preferred_element_type=jnp.float32))
    rows = jnp.concatenate(rows, axis=1)
    row_sq = jnp.sum(jnp.square(rows), axis=1, keepdims=True)
    dots = lax.dot_general(
        rows.astype(jnp.bfloat16), vectors_ref[0], (((1,), (1,)), ((), ())),
        preferred_element_type=jnp.float32,
    )
    out_ref[0] = (row_sq + vec_sq_ref[...] - 2.0 * dots) * (1.0 / width)


def tail_kernel(
    groups, slots, total_heads, back_ref, vec_sq_ref, listed_ref, vectors_ref,
    density_ref, spread_ref, out_ref, made_ref, sem,
):
    listed = listed_ref[...]
    distances(slots, back_ref, vec_sq_ref, listed, vectors_ref, made_ref)
    copy = pltpu.make_async_copy(made_ref, out_ref, sem)
    copy.start()
    here = lax.axis_index("group")
    members = listed_ref.shape[0]
    new_count = density_ref.shape[1]
    lines = 2 * groups * new_count // LANES
    first = vectors_ref.shape[2] // LANES * slots
    coded = jnp.sum(listed[:, first:, :].astype(jnp.float32), axis=0)
    total = sum(coded[part * lines:(part + 1) * lines] for part in range(PARTS))
    shape = (new_count, LANES)
    eye = iota((new_count, new_count), 0) == iota((new_count, new_count), 1)
    found = []
    for kind in range(2):
        place = (kind * groups + here) * new_count
        line = jnp.sum(
            jnp.where(iota((lines, LANES), 0) == place // LANES, total, 0.0), axis=0, keepdims=True
        )
        column = jnp.sum(
            jnp.where(iota(shape, 1) == iota(shape, 0) + place % LANES, line, 0.0),
            axis=1, keepdims=True,
        )
        found.append(jnp.sum(jnp.where(eye, column, 0.0), axis=0, keepdims=True))
    density_ref[...] = jnp.log(found[0] * (1.0 / total_heads))
    spread_ref[...] = found[1] / found[0]
    copy.wait()


def per_device(heads, new_heads, vectors, near_ids):
    head_dev, width = heads.shape
    new_count = new_heads.shape[0]
    near = near_ids.shape[1]
    groups = lax.axis_size("group")
    members = lax.axis_size("member")
    most = 2 * near // members
    slots = -(-most // PACK) * PACK

    partner_ids = from_partner(near_ids, "member", 1)
    others = [from_partner(new_heads, "group", mask) for mask in range(1, groups)]
    ids = call(
        stage_kernel,
        jax.ShapeDtypeStruct(near_ids.shape, near_ids.dtype),
        (in_hbm(near_ids),),
        (0, 0),
        scratch=[pltpu.SemaphoreType.DMA],
        spaces=[HBM],
    )
    ids = jnp.concatenate([ids, partner_ids], axis=0)
    kept, head_sq, new_heads = call(
        early_kernel,
        (
            jax.ShapeDtypeStruct(heads.shape, heads.dtype),
            jax.ShapeDtypeStruct((1, head_dev), jnp.float32),
            jax.ShapeDtypeStruct(new_heads.shape, new_heads.dtype),
        ),
        (in_hbm(heads), in_hbm(new_heads), ids),
        (0, 0),
        scratch=[pltpu.SemaphoreType.DMA((5,))],
        spaces=[HBM, HBM, pl.ANY],
    )
    lines = 2 * groups * new_count // LANES
    chunks = width // LANES
    extra = -(-PARTS * lines // TILE) * TILE
    sums, kept_ids = call(
        functools.partial(crowd_kernel, groups),
        (
            jax.ShapeDtypeStruct((-(-lines // TILE) * TILE, LANES), jnp.float32),
            jax.ShapeDtypeStruct(ids.shape, ids.dtype),
        ),
        (ids, kept, head_sq, new_heads, *others),
        (0, 0),
    )
    mask = 2
    while mask < members // 2:
        kept_ids = jnp.concatenate([kept_ids, from_partner(ids, "member", mask)], axis=0)
        ids = kept_ids
        mask *= 2
    far_ids = from_partner(ids, "member", mask)
    mask = 1
    while mask < groups // 2:
        sums = sums + from_partner(sums, "group", mask)
        mask *= 2
    back, vec_sq = call(
        functools.partial(prepare_kernel, members, slots, head_dev),
        (
            jax.ShapeDtypeStruct((near, members * slots), jnp.bfloat16),
            jax.ShapeDtypeStruct((1, vectors.shape[1]), jnp.float32),
        ),
        (near_ids, vectors, sums),
        (0, 0),
        spaces=[VMEM, VMEM, pl.ANY],
    )
    rows = call(
        functools.partial(gather_kernel, members, slots),
        jax.ShapeDtypeStruct((members * slots, width), jnp.bfloat16),
        (ids, far_ids, kept, back),
        (2 * members * slots * head_dev * width, heads.size * 2),
        scratch=[pltpu.VMEM((members, near), jnp.int32)],
        spaces=[VMEM, VMEM, VMEM, pl.ANY],
    )
    message = call(
        functools.partial(pack_kernel, members, slots, lines),
        jax.ShapeDtypeStruct((members, chunks * slots + extra, LANES), jnp.bfloat16),
        (rows, sums, from_partner(sums, "group", mask)),
        (0, members * slots * width * 4),
    )
    message = lax.all_to_all(
        message, "member", 0, 0, tiled=True, axis_index_groups=[by_turns(members)]
    )

    density, spread, reassign = call(
        functools.partial(
            tail_kernel, groups, slots, float(head_dev * groups * members)
        ),
        (
            jax.ShapeDtypeStruct((1, new_count), jnp.float32),
            jax.ShapeDtypeStruct((1, new_count), jnp.float32),
            jax.ShapeDtypeStruct((1, near, vectors.shape[1]), jnp.float32),
        ),
        (back, vec_sq, message, vectors),
        (4 * near * vectors.shape[1] * width, vectors.size * 4),
        scratch=[
            pltpu.VMEM((1, near, vectors.shape[1]), jnp.float32), pltpu.SemaphoreType.DMA
        ],
        outs=tuple(pl.BlockSpec(memory_space=space) for space in (VMEM, VMEM, HBM)),
    )
    return (density[0], spread[0], reassign)


def solution(mesh):
    placed = (
        P(("group", "member"), None),
        P("group", None),
        P(("group", "member"), None, None),
        P(("group", "member"), None),
    )
    return jax.shard_map(
        per_device,
        mesh=mesh,
        in_specs=placed,
        out_specs=(P("group"), P("group"), P(("group", "member"), None, None)),
        check_vma=False,
    )
```

```python
import functools

import jax
import jax.numpy as jnp
from jax import lax
from jax.experimental import pallas as pl
from jax.experimental.pallas import tpu as pltpu
from jax.sharding import PartitionSpec as P

VMEM = pltpu.MemorySpace.VMEM
HBM = pltpu.MemorySpace.HBM
LANES = 128
PACK = 16
TILE = 8
PARTS = 3
LIMIT = 24 * 2**20


def from_partner(value, axis, mask):
    count = lax.axis_size(axis)
    return lax.ppermute(value, axis, [(source, source ^ mask) for source in range(count)])


def by_turns(members):
    half = members // 2
    order = [half, 0]
    for low in range(half - 1, 0, -1):
        order += [half + low, low]
    return order[:2] + order[4:6] + order[2:4] + order[6:]


def turn_of(member, members):
    half = members // 2
    low = member % half
    pair = jnp.where(low == 0, 0, half - low)
    pair = jnp.where(pair == 1, 2, jnp.where(pair == 2, 1, pair))
    return 2 * pair + jnp.where(member < half, 1, 0)


def in_hbm(value):
    return pltpu.with_memory_space_constraint(value, HBM)


def call(body, shapes, operands, cost, scratch=(), spaces=None):
    return pl.pallas_call(
        body,
        out_shape=shapes,
        in_specs=[pl.BlockSpec(memory_space=space) for space in spaces or [VMEM] * len(operands)],
        out_specs=jax.tree.map(lambda unused: pl.BlockSpec(memory_space=VMEM), shapes),
        scratch_shapes=scratch,
        compiler_params=pltpu.CompilerParams(vmem_limit_bytes=LIMIT),
        cost_estimate=pl.CostEstimate(flops=cost[0], bytes_accessed=cost[1], transcendentals=0),
    )(*operands)


def iota(shape, dim):
    return lax.broadcasted_iota(jnp.int32, shape, dim)


def stage_kernel(ids_ref, kept_ref, sem):
    copy = pltpu.make_async_copy(ids_ref, kept_ref, sem)
    copy.start()
    copy.wait()


def early_kernel(heads_ref, new_ref, unused, kept_ref, head_sq_ref, kept_new_ref, sems):
    head_dev, width = heads_ref.shape
    tiles = 4
    tile = head_dev // tiles
    parts = [pl.ds(i * tile, tile) for i in range(tiles)]
    copies = [
        pltpu.make_async_copy(heads_ref.at[part], kept_ref.at[part], sems.at[i])
        for i, part in enumerate(parts)
    ]
    copies.append(pltpu.make_async_copy(new_ref, kept_new_ref, sems.at[tiles]))
    for copy in copies:
        copy.start()
    for i in range(tiles):
        copies[i].wait()
        for first in range(i * tile, (i + 1) * tile, LANES):
            block = jnp.square(kept_ref[first:first + LANES, :].astype(jnp.float32))
            folded = block[:, :LANES]
            for column in range(LANES, width, LANES):
                folded = folded + block[:, column:column + LANES]
            head_sq_ref[:, first:first + LANES] = jnp.sum(folded.T, axis=0, keepdims=True)
    for copy in copies[tiles:]:
        copy.wait()


def listed_rows(ids, me, slots, heads_ref):
    members, near = ids.shape
    head_dev = heads_ref.shape[0]
    local = ids - me * head_dev
    owned = (local >= 0) & (local < head_dev)
    earlier = (iota((near, near), 0) < iota((near, near), 1)).astype(jnp.bfloat16)
    rank = jnp.dot(owned.astype(jnp.bfloat16), earlier, preferred_element_type=jnp.float32)
    rank = jnp.where(owned, rank.astype(jnp.int32), -1)
    shape = (members, slots, near)
    pick = jnp.broadcast_to(rank[:, None, :], shape) == iota(shape, 1)
    wanted = jnp.sum(
        jnp.where(pick, jnp.broadcast_to(local[:, None, :] + 1, shape), 0), axis=2, keepdims=True
    ).reshape(members * slots, 1)
    onehot = (wanted == iota((members * slots, head_dev), 1) + 1).astype(jnp.bfloat16)
    return jnp.dot(
        onehot, heads_ref[...], preferred_element_type=jnp.float32
    ).astype(jnp.bfloat16)


def crowding(queries, heads_ref, head_sq_ref):
    head_dev, width = heads_ref.shape
    query_sq = jnp.sum(jnp.square(queries.astype(jnp.float32)), axis=1, keepdims=True)
    total_w = jnp.zeros((queries.shape[0], 1), jnp.float32)
    total_we = jnp.zeros((queries.shape[0], 1), jnp.float32)
    tile = 512
    for start in range(0, head_dev, tile):
        dots = lax.dot_general(
            queries, heads_ref[start:start + tile, :], (((1,), (1,)), ((), ())),
            preferred_element_type=jnp.float32,
        )
        head_sq = head_sq_ref[:, start:start + tile]
        excess = (query_sq + head_sq - 2.0 * dots) * (1.0 / width)
        inverse = 1.0 / (1.0 + excess)
        weight = inverse * inverse
        total_w = total_w + jnp.sum(weight, axis=1, keepdims=True)
        total_we = total_we + jnp.sum(weight * excess, axis=1, keepdims=True)
    return total_w, total_we


def crowd_kernel(groups, ids_ref, heads_ref, head_sq_ref, *refs):
    query_refs, (sums_ref, kept_ids_ref) = refs[:-2], refs[-2:]
    kept_ids_ref[...] = ids_ref[...]
    here = lax.axis_index("group")
    queries = jnp.concatenate([ref[...] for ref in query_refs], axis=0)
    new_count = queries.shape[0] // groups
    totals = crowding(queries, heads_ref, head_sq_ref)
    lane = iota((new_count, LANES), 1)
    row = iota((new_count, LANES), 0)
    line = iota(sums_ref.shape, 0)
    sums = jnp.zeros(sums_ref.shape, jnp.float32)
    for mask in range(groups):
        part = slice(mask * new_count, (mask + 1) * new_count)
        for kind in range(2):
            place = (kind * groups + (here ^ mask)) * new_count
            spread_out = jnp.where(lane == row + place % LANES, totals[kind][part], 0.0)
            spread_out = jnp.sum(spread_out, axis=0, keepdims=True)
            sums = sums + jnp.where(line == place // LANES, spread_out, 0.0)
    sums_ref[...] = sums


def gather_kernel(members, slots, near_ref, far_ref, heads_ref, unused, rows_ref, ids_ref):
    me = lax.axis_index("member")
    half = members // 2
    ids_ref[:half, :] = near_ref[...]
    ids_ref[half:, :] = far_ref[...]
    ids = jnp.concatenate([ids_ref[pl.ds(me ^ member, 1), :] for member in by_turns(members)], axis=0)
    rows_ref[...] = listed_rows(ids, me, slots, heads_ref)


def pack_kernel(members, slots, lines, rows_ref, mine_ref, other_ref, out_ref):
    chunks = rows_ref.shape[1] // LANES
    sums = (mine_ref[...] + other_ref[...])[:lines]
    coded = []
    for unused in range(PARTS):
        coded.append(sums.astype(jnp.bfloat16).astype(jnp.float32))
        sums = sums - coded[-1]
    missing = out_ref.shape[1] - chunks * slots - PARTS * lines
    if missing:
        coded.append(jnp.zeros((missing, LANES), jnp.float32))
    tail = jnp.concatenate(coded, axis=0).astype(jnp.bfloat16)
    for member in range(members):
        part = slice(member * slots, (member + 1) * slots)
        pieces = [rows_ref[part, chunk * LANES:(chunk + 1) * LANES] for chunk in range(chunks)]
        out_ref[member] = jnp.concatenate([*pieces, tail], axis=0)


def prepare_kernel(members, slots, head_dev, ids_ref, vectors_ref, unused, back_ref, vec_sq_ref):
    near = ids_ref.shape[1]
    block = vectors_ref.shape[1]
    square = (near, near)
    owner_row = jnp.broadcast_to(lax.div(ids_ref[...], head_dev), square)
    eye = iota(square, 0) == iota(square, 1)
    owner = jnp.sum(jnp.where(eye, owner_row, 0), axis=1, keepdims=True)
    before = (owner_row == owner) & (iota(square, 1) < iota(square, 0))
    place = jnp.sum(before.astype(jnp.int32), axis=1, keepdims=True)
    source = turn_of(owner, members) * slots + place
    back_ref[...] = (source == iota(back_ref.shape, 1)).astype(jnp.bfloat16)
    vec_sq = jnp.sum(jnp.square(vectors_ref[0].astype(jnp.float32)), axis=1, keepdims=True)
    diagonal = iota((block, block), 0) == iota((block, block), 1)
    vec_sq_ref[...] = jnp.sum(jnp.where(diagonal, vec_sq, 0.0), axis=0, keepdims=True)


def distances(slots, back_ref, vec_sq_ref, listed, vectors_ref, out_ref):
    members = listed.shape[0]
    width = vectors_ref.shape[2]
    rows = []
    for chunk in range(width // LANES):
        part = listed[:, chunk * slots:(chunk + 1) * slots, :].reshape(members * slots, LANES)
        rows.append(jnp.dot(back_ref[...], part, preferred_element_type=jnp.float32))
    rows = jnp.concatenate(rows, axis=1)
    row_sq = jnp.sum(jnp.square(rows), axis=1, keepdims=True)
    dots = lax.dot_general(
        rows.astype(jnp.bfloat16), vectors_ref[0], (((1,), (1,)), ((), ())),
        preferred_element_type=jnp.float32,
    )
    out_ref[0] = (row_sq + vec_sq_ref[...] - 2.0 * dots) * (1.0 / width)


def tail_kernel(
    groups, slots, total_heads, back_ref, vec_sq_ref, listed_ref, vectors_ref,
    density_ref, spread_ref, out_ref,
):
    listed = listed_ref[...]
    distances(slots, back_ref, vec_sq_ref, listed, vectors_ref, out_ref)
    here = lax.axis_index("group")
    members = listed_ref.shape[0]
    new_count = density_ref.shape[1]
    lines = 2 * groups * new_count // LANES
    first = vectors_ref.shape[2] // LANES * slots
    coded = jnp.sum(listed[:, first:, :].astype(jnp.float32), axis=0)
    total = sum(coded[part * lines:(part + 1) * lines] for part in range(PARTS))
    shape = (new_count, LANES)
    eye = iota((new_count, new_count), 0) == iota((new_count, new_count), 1)
    found = []
    for kind in range(2):
        place = (kind * groups + here) * new_count
        line = jnp.sum(
            jnp.where(iota((lines, LANES), 0) == place // LANES, total, 0.0), axis=0, keepdims=True
        )
        column = jnp.sum(
            jnp.where(iota(shape, 1) == iota(shape, 0) + place % LANES, line, 0.0),
            axis=1, keepdims=True,
        )
        found.append(jnp.sum(jnp.where(eye, column, 0.0), axis=0, keepdims=True))
    density_ref[...] = jnp.log(found[0] * (1.0 / total_heads))
    spread_ref[...] = found[1] / found[0]


def per_device(heads, new_heads, vectors, near_ids):
    head_dev, width = heads.shape
    new_count = new_heads.shape[0]
    near = near_ids.shape[1]
    groups = lax.axis_size("group")
    members = lax.axis_size("member")
    most = 2 * near // members
    slots = -(-most // PACK) * PACK

    partner_ids = from_partner(near_ids, "member", 1)
    others = [from_partner(new_heads, "group", mask) for mask in range(1, groups)]
    ids = call(
        stage_kernel,
        jax.ShapeDtypeStruct(near_ids.shape, near_ids.dtype),
        (in_hbm(near_ids),),
        (0, 0),
        scratch=[pltpu.SemaphoreType.DMA],
        spaces=[HBM],
    )
    ids = jnp.concatenate([ids, partner_ids], axis=0)
    kept, head_sq, new_heads = call(
        early_kernel,
        (
            jax.ShapeDtypeStruct(heads.shape, heads.dtype),
            jax.ShapeDtypeStruct((1, head_dev), jnp.float32),
            jax.ShapeDtypeStruct(new_heads.shape, new_heads.dtype),
        ),
        (in_hbm(heads), in_hbm(new_heads), ids),
        (0, 0),
        scratch=[pltpu.SemaphoreType.DMA((5,))],
        spaces=[HBM, HBM, pl.ANY],
    )
    lines = 2 * groups * new_count // LANES
    chunks = width // LANES
    extra = -(-PARTS * lines // TILE) * TILE
    sums, kept_ids = call(
        functools.partial(crowd_kernel, groups),
        (
            jax.ShapeDtypeStruct((-(-lines // TILE) * TILE, LANES), jnp.float32),
            jax.ShapeDtypeStruct(ids.shape, ids.dtype),
        ),
        (ids, kept, head_sq, new_heads, *others),
        (0, 0),
    )
    mask = 2
    while mask < members // 2:
        kept_ids = jnp.concatenate([kept_ids, from_partner(ids, "member", mask)], axis=0)
        ids = kept_ids
        mask *= 2
    far_ids = from_partner(ids, "member", mask)
    mask = 1
    while mask < groups // 2:
        sums = sums + from_partner(sums, "group", mask)
        mask *= 2
    back, vec_sq = call(
        functools.partial(prepare_kernel, members, slots, head_dev),
        (
            jax.ShapeDtypeStruct((near, members * slots), jnp.bfloat16),
            jax.ShapeDtypeStruct((1, vectors.shape[1]), jnp.float32),
        ),
        (near_ids, vectors, sums),
        (0, 0),
        spaces=[VMEM, VMEM, pl.ANY],
    )
    rows = call(
        functools.partial(gather_kernel, members, slots),
        jax.ShapeDtypeStruct((members * slots, width), jnp.bfloat16),
        (ids, far_ids, kept, back),
        (2 * members * slots * head_dev * width, heads.size * 2),
        scratch=[pltpu.VMEM((members, near), jnp.int32)],
        spaces=[VMEM, VMEM, VMEM, pl.ANY],
    )
    message = call(
        functools.partial(pack_kernel, members, slots, lines),
        jax.ShapeDtypeStruct((members, chunks * slots + extra, LANES), jnp.bfloat16),
        (rows, sums, from_partner(sums, "group", mask)),
        (0, members * slots * width * 4),
    )
    message = lax.all_to_all(
        message, "member", 0, 0, tiled=True, axis_index_groups=[by_turns(members)]
    )

    density, spread, reassign = call(
        functools.partial(
            tail_kernel, groups, slots, float(head_dev * groups * members)
        ),
        (
            jax.ShapeDtypeStruct((1, new_count), jnp.float32),
            jax.ShapeDtypeStruct((1, new_count), jnp.float32),
            jax.ShapeDtypeStruct((1, near, vectors.shape[1]), jnp.float32),
        ),
        (back, vec_sq, message, vectors),
        (4 * near * vectors.shape[1] * width, vectors.size * 4),
    )
    return (density[0], spread[0], reassign)


def solution(mesh):
    placed = (
        P(("group", "member"), None),
        P("group", None),
        P(("group", "member"), None, None),
        P(("group", "member"), None),
    )
    return jax.shard_map(
        per_device,
        mesh=mesh,
        in_specs=placed,
        out_specs=(P("group"), P("group"), P(("group", "member"), None, None)),
        check_vma=False,
    )
```

```python
import functools

import jax
import jax.numpy as jnp
from jax import lax
from jax.experimental import pallas as pl
from jax.experimental.pallas import tpu as pltpu
from jax.sharding import PartitionSpec as P

VMEM = pltpu.MemorySpace.VMEM
HBM = pltpu.MemorySpace.HBM
LANES = 128
PACK = 16
TILE = 8
PARTS = 3
LIMIT = 24 * 2**20


def from_partner(value, axis, mask):
    count = lax.axis_size(axis)
    return lax.ppermute(value, axis, [(source, source ^ mask) for source in range(count)])


def by_turns(members):
    half = members // 2
    order = [half, 0]
    for low in range(half - 1, 0, -1):
        order += [half + low, low]
    return order


def turn_of(member, members):
    half = members // 2
    low = member % half
    return jnp.where(low == 0, 0, 2 * (half - low)) + jnp.where(member < half, 1, 0)


def in_hbm(value):
    return pltpu.with_memory_space_constraint(value, HBM)


def call(body, shapes, operands, cost, scratch=(), spaces=None):
    return pl.pallas_call(
        body,
        out_shape=shapes,
        in_specs=[pl.BlockSpec(memory_space=space) for space in spaces or [VMEM] * len(operands)],
        out_specs=jax.tree.map(lambda unused: pl.BlockSpec(memory_space=VMEM), shapes),
        scratch_shapes=scratch,
        compiler_params=pltpu.CompilerParams(vmem_limit_bytes=LIMIT),
        cost_estimate=pl.CostEstimate(flops=cost[0], bytes_accessed=cost[1], transcendentals=0),
    )(*operands)


def iota(shape, dim):
    return lax.broadcasted_iota(jnp.int32, shape, dim)


def stage_kernel(ids_ref, kept_ref, sem):
    copy = pltpu.make_async_copy(ids_ref, kept_ref, sem)
    copy.start()
    copy.wait()


def early_kernel(heads_ref, new_ref, unused, kept_ref, head_sq_ref, kept_new_ref, sems):
    head_dev, width = heads_ref.shape
    tiles = 2
    tile = head_dev // tiles
    parts = [pl.ds(i * tile, tile) for i in range(tiles)]
    copies = [
        pltpu.make_async_copy(heads_ref.at[part], kept_ref.at[part], sems.at[i])
        for i, part in enumerate(parts)
    ]
    copies.append(pltpu.make_async_copy(new_ref, kept_new_ref, sems.at[tiles]))
    for copy in copies:
        copy.start()
    for i in range(tiles):
        copies[i].wait()
        for first in range(i * tile, (i + 1) * tile, LANES):
            block = jnp.square(kept_ref[first:first + LANES, :].astype(jnp.float32))
            folded = block[:, :LANES]
            for column in range(LANES, width, LANES):
                folded = folded + block[:, column:column + LANES]
            head_sq_ref[:, first:first + LANES] = jnp.sum(folded.T, axis=0, keepdims=True)
    for copy in copies[tiles:]:
        copy.wait()


def listed_rows(ids, me, slots, heads_ref):
    members, near = ids.shape
    head_dev = heads_ref.shape[0]
    local = ids - me * head_dev
    owned = (local >= 0) & (local < head_dev)
    earlier = (iota((near, near), 0) < iota((near, near), 1)).astype(jnp.bfloat16)
    rank = jnp.dot(owned.astype(jnp.bfloat16), earlier, preferred_element_type=jnp.float32)
    rank = jnp.where(owned, rank.astype(jnp.int32), -1)
    shape = (members, slots, near)
    pick = jnp.broadcast_to(rank[:, None, :], shape) == iota(shape, 1)
    wanted = jnp.sum(
        jnp.where(pick, jnp.broadcast_to(local[:, None, :] + 1, shape), 0), axis=2, keepdims=True
    ).reshape(members * slots, 1)
    onehot = (wanted == iota((members * slots, head_dev), 1) + 1).astype(jnp.bfloat16)
    return jnp.dot(
        onehot, heads_ref[...], preferred_element_type=jnp.float32
    ).astype(jnp.bfloat16)


def crowding(queries, heads_ref, head_sq_ref):
    head_dev, width = heads_ref.shape
    query_sq = jnp.sum(jnp.square(queries.astype(jnp.float32)), axis=1, keepdims=True)
    total_w = jnp.zeros((queries.shape[0], 1), jnp.float32)
    total_we = jnp.zeros((queries.shape[0], 1), jnp.float32)
    tile = 512
    for start in range(0, head_dev, tile):
        dots = lax.dot_general(
            queries, heads_ref[start:start + tile, :], (((1,), (1,)), ((), ())),
            preferred_element_type=jnp.float32,
        )
        head_sq = head_sq_ref[:, start:start + tile]
        excess = (query_sq + head_sq - 2.0 * dots) * (1.0 / width)
        inverse = 1.0 / (1.0 + excess)
        weight = inverse * inverse
        total_w = total_w + jnp.sum(weight, axis=1, keepdims=True)
        total_we = total_we + jnp.sum(weight * excess, axis=1, keepdims=True)
    return total_w, total_we


def crowd_kernel(groups, ids_ref, heads_ref, head_sq_ref, *refs):
    query_refs, (sums_ref, kept_ids_ref) = refs[:-2], refs[-2:]
    kept_ids_ref[...] = ids_ref[...]
    here = lax.axis_index("group")
    queries = jnp.concatenate([ref[...] for ref in query_refs], axis=0)
    new_count = queries.shape[0] // groups
    totals = crowding(queries, heads_ref, head_sq_ref)
    lane = iota((new_count, LANES), 1)
    row = iota((new_count, LANES), 0)
    line = iota(sums_ref.shape, 0)
    sums = jnp.zeros(sums_ref.shape, jnp.float32)
    for mask in range(groups):
        part = slice(mask * new_count, (mask + 1) * new_count)
        for kind in range(2):
            place = (kind * groups + (here ^ mask)) * new_count
            spread_out = jnp.where(lane == row + place % LANES, totals[kind][part], 0.0)
            spread_out = jnp.sum(spread_out, axis=0, keepdims=True)
            sums = sums + jnp.where(line == place // LANES, spread_out, 0.0)
    sums_ref[...] = sums


def gather_kernel(members, slots, near_ref, far_ref, heads_ref, unused, rows_ref, ids_ref):
    me = lax.axis_index("member")
    half = members // 2
    ids_ref[:half, :] = near_ref[...]
    ids_ref[half:, :] = far_ref[...]
    ids = jnp.concatenate([ids_ref[pl.ds(me ^ member, 1), :] for member in by_turns(members)], axis=0)
    rows_ref[...] = listed_rows(ids, me, slots, heads_ref)


def pack_kernel(members, slots, lines, rows_ref, mine_ref, other_ref, out_ref):
    chunks = rows_ref.shape[1] // LANES
    sums = (mine_ref[...] + other_ref[...])[:lines]
    coded = []
    for unused in range(PARTS):
        coded.append(sums.astype(jnp.bfloat16).astype(jnp.float32))
        sums = sums - coded[-1]
    missing = out_ref.shape[1] - chunks * slots - PARTS * lines
    if missing:
        coded.append(jnp.zeros((missing, LANES), jnp.float32))
    tail = jnp.concatenate(coded, axis=0).astype(jnp.bfloat16)
    for member in range(members):
        part = slice(member * slots, (member + 1) * slots)
        pieces = [rows_ref[part, chunk * LANES:(chunk + 1) * LANES] for chunk in range(chunks)]
        out_ref[member] = jnp.concatenate([*pieces, tail], axis=0)


def prepare_kernel(members, slots, head_dev, ids_ref, vectors_ref, unused, back_ref, vec_sq_ref):
    near = ids_ref.shape[1]
    block = vectors_ref.shape[1]
    square = (near, near)
    owner_row = jnp.broadcast_to(lax.div(ids_ref[...], head_dev), square)
    eye = iota(square, 0) == iota(square, 1)
    owner = jnp.sum(jnp.where(eye, owner_row, 0), axis=1, keepdims=True)
    before = (owner_row == owner) & (iota(square, 1) < iota(square, 0))
    place = jnp.sum(before.astype(jnp.int32), axis=1, keepdims=True)
    source = turn_of(owner, members) * slots + place
    back_ref[...] = (source == iota(back_ref.shape, 1)).astype(jnp.bfloat16)
    vec_sq = jnp.sum(jnp.square(vectors_ref[0].astype(jnp.float32)), axis=1, keepdims=True)
    diagonal = iota((block, block), 0) == iota((block, block), 1)
    vec_sq_ref[...] = jnp.sum(jnp.where(diagonal, vec_sq, 0.0), axis=0, keepdims=True)


def distances(slots, back_ref, vec_sq_ref, listed, vectors_ref, out_ref):
    members = listed.shape[0]
    width = vectors_ref.shape[2]
    rows = []
    for chunk in range(width // LANES):
        part = listed[:, chunk * slots:(chunk + 1) * slots, :].reshape(members * slots, LANES)
        rows.append(jnp.dot(back_ref[...], part, preferred_element_type=jnp.float32))
    rows = jnp.concatenate(rows, axis=1)
    row_sq = jnp.sum(jnp.square(rows), axis=1, keepdims=True)
    dots = lax.dot_general(
        rows.astype(jnp.bfloat16), vectors_ref[0], (((1,), (1,)), ((), ())),
        preferred_element_type=jnp.float32,
    )
    out_ref[0] = (row_sq + vec_sq_ref[...] - 2.0 * dots) * (1.0 / width)


def tail_kernel(
    groups, slots, total_heads, back_ref, vec_sq_ref, listed_ref, vectors_ref,
    density_ref, spread_ref, out_ref,
):
    listed = listed_ref[...]
    distances(slots, back_ref, vec_sq_ref, listed, vectors_ref, out_ref)
    here = lax.axis_index("group")
    members = listed_ref.shape[0]
    new_count = density_ref.shape[1]
    lines = 2 * groups * new_count // LANES
    first = vectors_ref.shape[2] // LANES * slots
    coded = jnp.sum(listed[:, first:, :].astype(jnp.float32), axis=0)
    total = sum(coded[part * lines:(part + 1) * lines] for part in range(PARTS))
    shape = (new_count, LANES)
    eye = iota((new_count, new_count), 0) == iota((new_count, new_count), 1)
    found = []
    for kind in range(2):
        place = (kind * groups + here) * new_count
        line = jnp.sum(
            jnp.where(iota((lines, LANES), 0) == place // LANES, total, 0.0), axis=0, keepdims=True
        )
        column = jnp.sum(
            jnp.where(iota(shape, 1) == iota(shape, 0) + place % LANES, line, 0.0),
            axis=1, keepdims=True,
        )
        found.append(jnp.sum(jnp.where(eye, column, 0.0), axis=0, keepdims=True))
    density_ref[...] = jnp.log(found[0] * (1.0 / total_heads))
    spread_ref[...] = found[1] / found[0]


def per_device(heads, new_heads, vectors, near_ids):
    head_dev, width = heads.shape
    new_count = new_heads.shape[0]
    near = near_ids.shape[1]
    groups = lax.axis_size("group")
    members = lax.axis_size("member")
    most = 2 * near // members
    slots = -(-most // PACK) * PACK

    partner_ids = from_partner(near_ids, "member", 1)
    others = [from_partner(new_heads, "group", mask) for mask in range(1, groups)]
    ids = call(
        stage_kernel,
        jax.ShapeDtypeStruct(near_ids.shape, near_ids.dtype),
        (in_hbm(near_ids),),
        (0, 0),
        scratch=[pltpu.SemaphoreType.DMA],
        spaces=[HBM],
    )
    ids = jnp.concatenate([ids, partner_ids], axis=0)
    kept, head_sq, new_heads = call(
        early_kernel,
        (
            jax.ShapeDtypeStruct(heads.shape, heads.dtype),
            jax.ShapeDtypeStruct((1, head_dev), jnp.float32),
            jax.ShapeDtypeStruct(new_heads.shape, new_heads.dtype),
        ),
        (in_hbm(heads), in_hbm(new_heads), ids),
        (0, 0),
        scratch=[pltpu.SemaphoreType.DMA((3,))],
        spaces=[HBM, HBM, pl.ANY],
    )
    lines = 2 * groups * new_count // LANES
    chunks = width // LANES
    extra = -(-PARTS * lines // TILE) * TILE
    sums, kept_ids = call(
        functools.partial(crowd_kernel, groups),
        (
            jax.ShapeDtypeStruct((-(-lines // TILE) * TILE, LANES), jnp.float32),
            jax.ShapeDtypeStruct(ids.shape, ids.dtype),
        ),
        (ids, kept, head_sq, new_heads, *others),
        (0, 0),
    )
    mask = 2
    while mask < members // 2:
        kept_ids = jnp.concatenate([kept_ids, from_partner(ids, "member", mask)], axis=0)
        ids = kept_ids
        mask *= 2
    far_ids = from_partner(ids, "member", mask)
    mask = 1
    while mask < groups // 2:
        sums = sums + from_partner(sums, "group", mask)
        mask *= 2
    back, vec_sq = call(
        functools.partial(prepare_kernel, members, slots, head_dev),
        (
            jax.ShapeDtypeStruct((near, members * slots), jnp.bfloat16),
            jax.ShapeDtypeStruct((1, vectors.shape[1]), jnp.float32),
        ),
        (near_ids, vectors, sums),
        (0, 0),
        spaces=[VMEM, VMEM, pl.ANY],
    )
    rows = call(
        functools.partial(gather_kernel, members, slots),
        jax.ShapeDtypeStruct((members * slots, width), jnp.bfloat16),
        (ids, far_ids, kept, back),
        (2 * members * slots * head_dev * width, heads.size * 2),
        scratch=[pltpu.VMEM((members, near), jnp.int32)],
        spaces=[VMEM, VMEM, VMEM, pl.ANY],
    )
    message = call(
        functools.partial(pack_kernel, members, slots, lines),
        jax.ShapeDtypeStruct((members, chunks * slots + extra, LANES), jnp.bfloat16),
        (rows, sums, from_partner(sums, "group", mask)),
        (0, members * slots * width * 4),
    )
    message = lax.all_to_all(
        message, "member", 0, 0, tiled=True, axis_index_groups=[by_turns(members)]
    )

    density, spread, reassign = call(
        functools.partial(
            tail_kernel, groups, slots, float(head_dev * groups * members)
        ),
        (
            jax.ShapeDtypeStruct((1, new_count), jnp.float32),
            jax.ShapeDtypeStruct((1, new_count), jnp.float32),
            jax.ShapeDtypeStruct((1, near, vectors.shape[1]), jnp.float32),
        ),
        (back, vec_sq, message, vectors),
        (4 * near * vectors.shape[1] * width, vectors.size * 4),
    )
    return (density[0], spread[0], reassign)


def solution(mesh):
    placed = (
        P(("group", "member"), None),
        P("group", None),
        P(("group", "member"), None, None),
        P(("group", "member"), None),
    )
    return jax.shard_map(
        per_device,
        mesh=mesh,
        in_specs=placed,
        out_specs=(P("group"), P("group"), P(("group", "member"), None, None)),
        check_vma=False,
    )
```
